32 devices in a mesh: dp: 16 (over z, x, core), group: 2 (over y).
Axes of the slice: x: 2, y: 2, z: 4, core: 2. Of those that a mesh axis runs over, the one named last changes fastest.
Arguments:
- patches: bfloat16 [4, 8192, 512], P('group', 'dp'), may hold values from -6 to 6
- cotangents: bfloat16 [4, 8192, 512], P('group', 'dp'), may hold values from -6 to 6
- newton_counts: int32 [4, 2], P('group'), may hold values from 2 to 4
Outputs:
- update: bfloat16 [4, 512, 512], P(None, 'dp')
The draws below stay inside these ranges and needn't reach their ends.
All inputs are finite; a program needn't handle non-finite values.
Results may differ from the reference program's by a relative error of at most 0.012.
The reference program's roundings to bfloat16 on the way count: a program that leaves them out, or rounds other values in their place, can miss the bound.
Values may be sent and summed in bfloat16 or wider, within the bound.
No kernel may reach another device: no remote copies, remote signals or barrier semaphores. Data moves between devices by JAX's collectives and lax.ppermute only.
A program may use at most 64 MiB of HBM per device.

```python
import jax
import jax.numpy as jnp
from jax import lax

B = 512
MAXIT = 4
NBLK = 4
PIX = 8192


def with_ends(array, stream_key, low, top_value):
    longest = array.shape.index(max(array.shape))
    spots = []
    for shift in (0, 1):
        where = [jax.random.randint(jax.random.fold_in(stream_key, axis), (), 0, length) for axis, length in enumerate(array.shape)]
        where[longest] = (where[longest] + shift) % array.shape[longest]
        spots.append(tuple(where))
    return array.at[spots[0]].set(low).at[spots[1]].set(top_value)


def with_spikes(result, stream_key, source, target, parts, factor):
    def block_of(position):
        return (jnp.arange(result.shape[position]) // (result.shape[position] // parts)).reshape((-1,) + (1,) * (result.ndim - 1 - position))

    near = jax.random.permutation(stream_key, parts)[block_of(target)]
    far = (block_of(target) + parts // 2) % parts
    return jnp.where((block_of(source) == near) | (block_of(source) == far), factor * result, result)


def block_levels(own_key, extent, cuts, least, high):
    def one(axis_at, shards_of):
        steps = jax.random.uniform(jax.random.fold_in(jax.random.fold_in(own_key, 6), axis_at), (shards_of,), jnp.float32, least / len(cuts), high / len(cuts))
        return jnp.repeat(jnp.exp(steps), extent[axis_at] // shards_of).reshape((-1,) + (1,) * (len(extent) - axis_at - 1))

    factor_of = one(*cuts[0])
    for cut in cuts[1:]:
        factor_of = factor_of * one(*cut)
    return factor_of


def gaussian(own_key, dims, scale, bound, split=(), kind=jnp.bfloat16):
    drawn = scale * jax.random.normal(own_key, dims, jnp.float32)
    if split:
        drawn = drawn * block_levels(own_key, dims, split, -0.22, 0.18)
    return jnp.clip(drawn, -bound, bound).astype(kind)


def gaussian_with(key, dims, scale, reach, split, heavy, kind=jnp.bfloat16):
    entries = scale * jax.random.normal(key, dims, jnp.float32)
    if split:
        entries = entries * block_levels(key, dims, split, -0.22, 0.18)
    return jnp.clip(with_spikes(entries, jax.random.fold_in(key, 3), *heavy), -reach, reach).astype(kind)


def setup_inputs(seed: int = 0) -> dict:
    arg_keys = jax.random.split(jax.random.key(seed), 4)
    return {
        "patches": gaussian_with(arg_keys[0], (NBLK, PIX, B), 1.0, 6.0, ((0, 2), (1, 16)), (1, 2, 16, 2.0)),
        "cotangents": gaussian(arg_keys[1], (NBLK, PIX, B), 1.0, 6.0, ((0, 2), (1, 16))),
        "newton_counts": with_ends(jax.random.randint(arg_keys[2], (NBLK, 2), 2, MAXIT + 1), jax.random.fold_in(arg_keys[2], 1), 2, MAXIT).astype(jnp.int32),
    }


def half_dot(left_mat, right_mat):
    return jnp.dot(left_mat.astype(jnp.bfloat16), right_mat.astype(jnp.bfloat16), preferred_element_type=jnp.float32)

def newton_root(matrix, count):
    order = matrix.shape[0]
    eye = jnp.eye(order, dtype=jnp.float32)
    scale = 5.0 / (2.0 * jnp.sqrt(jnp.sum(matrix * matrix)))
    start = (scale ** 0.25 * eye, scale * matrix)

    def sweep(index, carry):
        current, moment = carry
        factor = (5.0 * eye - moment) / 4.0
        square = half_dot(factor, factor)
        fourth = half_dot(square, square)
        return (half_dot(current, factor), half_dot(fourth, moment))
    final, moment = lax.fori_loop(0, count, sweep, start)
    return final.astype(jnp.bfloat16)

def one_block(items):
    patch, cotangent, counts = items
    order = patch.shape[1]
    grad = jnp.dot(patch.T, cotangent, preferred_element_type=jnp.float32) / jnp.sqrt(jnp.float32(PIX * B))
    eye = jnp.eye(order, dtype=jnp.float32)
    left = jnp.dot(grad, grad.T, precision=lax.Precision.HIGHEST) + 0.1 * eye
    right = jnp.dot(grad.T, grad, precision=lax.Precision.HIGHEST) + 0.1 * eye
    left_root = newton_root(left, counts[0])
    right_root = newton_root(right, counts[1])
    partial_value = jnp.dot(left_root, grad.astype(jnp.bfloat16), preferred_element_type=jnp.float32).astype(jnp.bfloat16)
    return jnp.dot(partial_value, right_root, preferred_element_type=jnp.float32).astype(jnp.bfloat16)

def reference(patches, cotangents, newton_counts):
    return lax.map(one_block, (patches, cotangents, newton_counts))
```

```python
import functools

import jax
import jax.numpy as jnp
from jax import lax
from jax.experimental import pallas as pl
from jax.experimental.pallas import tpu as pltpu
from jax.sharding import PartitionSpec as P

F32 = jnp.float32
BF16 = jnp.bfloat16
VMEM = pl.BlockSpec(memory_space=pltpu.VMEM)
SMEM = pl.BlockSpec(memory_space=pltpu.SMEM)
ROWS_IN_COLS = (((0,), (0,)), ((), ()))
COLS_IN_COLS = (((1,), (1,)), ((), ()))


def params(limit):
    return pltpu.CompilerParams(vmem_limit_bytes=limit << 20)


def gram_kernel(scale, where_ref, patch_ref, cot_ref, out_ref):
    terms = lax.dot_general(patch_ref[0], cot_ref[0], ROWS_IN_COLS, preferred_element_type=F32)
    out_ref[0] = (terms * scale).astype(out_ref.dtype)


def gram(where, patches, cotangents, scale, dtype):
    count = where.shape[0]
    _, pix, width = patches.shape
    half = width // 2
    return pl.pallas_call(
        functools.partial(gram_kernel, scale),
        out_shape=jax.ShapeDtypeStruct((count, half, width), dtype),
        grid_spec=pltpu.PrefetchScalarGridSpec(
            num_scalar_prefetch=1,
            grid=(count,),
            in_specs=[
                pl.BlockSpec((1, pix, half), lambda m, where: (where[m, 0], 0, where[m, 1])),
                pl.BlockSpec((1, pix, width), lambda m, where: (where[m, 0], 0, 0)),
            ],
            out_specs=pl.BlockSpec((1, half, width), lambda m, where: (m, 0, 0)),
        ),
        compiler_params=params(16),
        cost_estimate=pl.CostEstimate(
            flops=2 * count * pix * half * width,
            bytes_accessed=2 * count * pix * (half + width),
            transcendentals=0,
        ),
    )(where, patches, cotangents)


def split_kernel(place_ref, kept_ref, came_ref, own_ref, *piece_refs):
    rows = own_ref.shape[0]
    place = place_ref[0]

    def piece(offset):
        where = pl.ds(pl.multiple_of((place ^ offset) * rows, rows), rows)
        return kept_ref[where, :] + came_ref[where, :].astype(F32)

    own_ref[...] = piece(0)
    for index, ref in enumerate(piece_refs):
        ref[...] = piece(index + 1).astype(BF16)


def split(place, kept, came, line):
    rows, width = kept.shape
    part = rows // line
    return pl.pallas_call(
        split_kernel,
        out_shape=[jax.ShapeDtypeStruct((part, width), F32)]
        + [jax.ShapeDtypeStruct((part, width), BF16)] * (line - 1),
        in_specs=[SMEM, VMEM, VMEM],
        out_specs=[VMEM] * line,
        compiler_params=params(16),
    )(place, kept, came)


def root_kernel(count_pieces, scalar_ref, *refs):
    pieces = refs[:count_pieces]
    out_ref, grad, q_left, q_right, m_left, m_right, x_left, x_right = refs[count_pieces:]
    part = pieces[0].shape[0]
    width = grad.shape[0]
    for index, ref in enumerate(pieces):
        grad[part * index : part * (index + 1), :] = ref[...]
    diagonal = lax.broadcasted_iota(jnp.int32, (width, width), 0) == lax.broadcasted_iota(
        jnp.int32, (width, width), 1
    )

    def dot(a, b):
        return jnp.dot(a, b, preferred_element_type=F32)

    def factor(moment):
        return (jnp.where(diagonal, 1.25, 0.0) - 0.25 * moment).astype(BF16)

    def begin(dims):
        stats = lax.dot_general(grad[...], grad[...], dims, preferred_element_type=F32)
        stats = stats + jnp.where(diagonal, 0.1, 0.0)
        scale = 2.5 / jnp.sqrt(jnp.sum(stats * stats, keepdims=True))
        first = jnp.sqrt(jnp.sqrt(scale)).astype(BF16).astype(F32)
        return scale * stats, first

    rows = pl.ds(pl.multiple_of(scalar_ref[2], part), part)
    moment, first = begin(COLS_IN_COLS)
    m_left[...] = moment.astype(BF16)
    q_left[...] = factor(moment)
    x_left[...] = (first * q_left[rows, :].astype(F32)).astype(BF16)
    moment, first = begin(ROWS_IN_COLS)
    m_right[...] = moment.astype(BF16)
    factor_value = factor(moment)
    q_right[...] = factor_value
    x_right[...] = (first * factor_value.astype(F32)).astype(BF16)

    count_left, count_right = scalar_ref[0], scalar_ref[1]

    def sweep(index, carry):
        second_left = dot(q_left[...], q_left[...]).astype(BF16)
        second_right = dot(q_right[...], q_right[...]).astype(BF16)
        fourth_left = dot(second_left, second_left).astype(BF16)
        fourth_right = dot(second_right, second_right).astype(BF16)
        moment_left = dot(fourth_left, m_left[...])
        moment_right = dot(fourth_right, m_right[...])
        m_left[...] = moment_left.astype(BF16)
        m_right[...] = moment_right.astype(BF16)
        factor_left = factor(moment_left)
        factor_right = factor(moment_right)
        q_left[...] = factor_left
        q_right[...] = factor_right

        @pl.when(index < count_left)
        def _():
            x_left[...] = dot(x_left[...], factor_left).astype(BF16)

        @pl.when(index < count_right)
        def _():
            x_right[...] = dot(x_right[...], factor_right).astype(BF16)

        return carry

    lax.fori_loop(1, jnp.maximum(count_left, count_right), sweep, 0)
    partial_value = dot(x_left[...], grad[...]).astype(BF16)
    out_ref[...] = dot(partial_value, x_right[...]).astype(BF16)


def root(scalars, pieces):
    part, width = pieces[0].shape
    square = pltpu.VMEM((width, width), BF16)
    return pl.pallas_call(
        functools.partial(root_kernel, len(pieces)),
        out_shape=jax.ShapeDtypeStruct((part, width), BF16),
        in_specs=[SMEM] + [VMEM] * len(pieces),
        out_specs=VMEM,
        scratch_shapes=[square] * 5 + [pltpu.VMEM((part, width), BF16), square],
        compiler_params=params(32),
    )(scalars, *pieces)


def shards(groups, patches, cotangents, newton_counts):
    blocks, pix, width = patches.shape
    devices = lax.axis_size("dp")
    line = devices // 4
    half = width // 2
    part = half // line
    rows = part // 2
    scale = 1.0 / float(pix * devices * width) ** 0.5
    mine = lax.axis_index("dp")
    core, column, place = mine % 2, mine // 2 % 2, mine // 4

    def swap(array, mask):
        return lax.ppermute(array, "dp", [(i, i ^ mask) for i in range(devices)])

    away = jnp.stack([jnp.stack([1 - column, 1 - core]), jnp.stack([column, 1 - core])])
    home = jnp.stack([jnp.stack([1 - column, core]), jnp.stack([column, core])])
    given = gram(away, patches, cotangents, scale, BF16)
    came_other = swap(given[0], 1)
    came_own = swap(given[1], 1)
    kept = gram(home, patches, cotangents, scale, F32)
    came_column = swap((kept[0] + came_other.astype(F32)).astype(BF16), 2)
    pair = kept[1] + came_own.astype(F32)
    own, *others = split(place[None], pair, came_column, line)
    for offset, piece in enumerate(others, 1):
        own = own + swap(piece, 4 * offset).astype(F32)
    own = own.astype(BF16)
    near = [own] + [swap(own, 4 * offset) for offset in range(1, line)]
    far = [swap(piece, 1) for piece in near]

    target = 2 * place + core
    start = ((target // line) ^ core) * half + ((target % line) ^ place) * part
    counts = lax.dynamic_index_in_dim(newton_counts, column, 0, keepdims=False)
    update = root(jnp.concatenate([counts, start[None]]), near + far)

    group = lax.axis_index("group")
    found = []
    for turn in range(groups):
        pair_found = []
        for flip in range(2):
            moves = []
            for index in range(devices):
                high, col, cor = index // 4, index // 2 % 2, index % 2
                to = 4 * high + 2 * cor + (col ^ flip)
                for g in range(groups):
                    moves.append((index * groups + g, to * groups + (g + turn) % groups))
            piece = lax.dynamic_slice_in_dim(update, (column ^ flip) * rows, rows, 0)
            pair_found.append(lax.ppermute(piece, ("dp", "group"), moves))
        found.append(
            jnp.stack(
                [
                    jnp.where(core == 0, pair_found[0], pair_found[1]),
                    jnp.where(core == 0, pair_found[1], pair_found[0]),
                ]
            )
        )
    ordered = jnp.stack(found[::-1])
    ordered = jnp.roll(ordered, group + 1, axis=0)
    return ordered.reshape(blocks * groups, rows, width)


def solution(mesh):
    placed = (P("group", "dp", None), P("group", "dp", None), P("group", None))
    return jax.shard_map(
        functools.partial(shards, mesh.shape["group"]),
        mesh=mesh,
        in_specs=placed,
        out_specs=P(None, "dp", None),
        check_vma=False,
    )
```

```python
import functools

import jax
import jax.numpy as jnp
from jax import lax
from jax.experimental import pallas as pl
from jax.experimental.pallas import tpu as pltpu
from jax.sharding import PartitionSpec as P

F32 = jnp.float32
BF16 = jnp.bfloat16
VMEM = pl.BlockSpec(memory_space=pltpu.VMEM)
SMEM = pl.BlockSpec(memory_space=pltpu.SMEM)
HBM = pl.BlockSpec(memory_space=pltpu.HBM)
ROWS_IN_COLS = (((0,), (0,)), ((), ()))
COLS_IN_COLS = (((1,), (1,)), ((), ()))


def params(limit):
    return pltpu.CompilerParams(vmem_limit_bytes=limit << 20)


def gram_kernel(scale, pieces, *refs):
    count = len(pieces)
    scalar_ref, patch_hbm, cot_hbm = refs[:3]
    outs = refs[3 : 3 + count]
    patch, cot, patch_sems, cot_sems = refs[3 + count :]
    half = patch.shape[2]
    distinct = sorted({block for block, _, _ in pieces}, key=[p[0] for p in pieces].index)
    copies = {}
    for index, (block, side, _) in enumerate(pieces):
        number = scalar_ref[block]
        if block not in copies:
            slot = distinct.index(block)
            copies[block] = pltpu.make_async_copy(
                cot_hbm.at[number], cot.at[slot], cot_sems.at[slot]
            )
            copies[block].start()
        columns = pl.ds(pl.multiple_of(scalar_ref[2 + side] * half, half), half)
        copies[index, None] = pltpu.make_async_copy(
            patch_hbm.at[number, :, columns], patch.at[index], patch_sems.at[index]
        )
        copies[index, None].start()
    waited = set()
    for index, (block, _, dtype) in enumerate(pieces):
        if block not in waited:
            copies[block].wait()
            waited.add(block)
        copies[index, None].wait()
        terms = lax.dot_general(
            patch[index], cot[distinct.index(block)], ROWS_IN_COLS, preferred_element_type=F32
        )
        outs[index][...] = (terms * scale).astype(dtype)


def gram(scalars, patches, cotangents, scale, pieces):
    _, pix, width = patches.shape
    half = width // 2
    count = len(pieces)
    blocks = len({block for block, _, _ in pieces})
    return pl.pallas_call(
        functools.partial(gram_kernel, scale, pieces),
        out_shape=[jax.ShapeDtypeStruct((half, width), dtype) for _, _, dtype in pieces],
        in_specs=[SMEM, HBM, HBM],
        out_specs=[VMEM] * count,
        scratch_shapes=[
            pltpu.VMEM((count, pix, half), BF16),
            pltpu.VMEM((blocks, pix, width), BF16),
            pltpu.SemaphoreType.DMA((count,)),
            pltpu.SemaphoreType.DMA((blocks,)),
        ],
        compiler_params=params(16),
        cost_estimate=pl.CostEstimate(
            flops=2 * count * pix * half * width,
            bytes_accessed=2 * (count * pix * half + blocks * pix * width),
            transcendentals=0,
        ),
    )(scalars, patches, cotangents)


def split_kernel(place_ref, kept_ref, came_ref, own_ref, *piece_refs):
    rows = own_ref.shape[0]
    place = place_ref[0]

    def piece(offset):
        where = pl.ds(pl.multiple_of((place ^ offset) * rows, rows), rows)
        return kept_ref[where, :] + came_ref[where, :].astype(F32)

    own_ref[...] = piece(0)
    for index, ref in enumerate(piece_refs):
        ref[...] = piece(index + 1).astype(BF16)


def split(place, kept, came, line):
    rows, width = kept.shape
    part = rows // line
    return pl.pallas_call(
        split_kernel,
        out_shape=[jax.ShapeDtypeStruct((part, width), F32)]
        + [jax.ShapeDtypeStruct((part, width), BF16)] * (line - 1),
        in_specs=[SMEM, VMEM, VMEM],
        out_specs=[VMEM] * line,
        compiler_params=params(16),
    )(place, kept, came)


def root_kernel(count_pieces, scalar_ref, *refs):
    pieces = refs[:count_pieces]
    out_ref, grad, q_left, q_right, m_left, m_right, x_left, x_right = refs[count_pieces:]
    part = pieces[0].shape[0]
    width = grad.shape[0]
    for index, ref in enumerate(pieces):
        grad[part * index : part * (index + 1), :] = ref[...]
    diagonal = lax.broadcasted_iota(jnp.int32, (width, width), 0) == lax.broadcasted_iota(
        jnp.int32, (width, width), 1
    )

    def dot(a, b):
        return jnp.dot(a, b, preferred_element_type=F32)

    def factor(moment):
        return (jnp.where(diagonal, 1.25, 0.0) - 0.25 * moment).astype(BF16)

    def begin(dims):
        stats = lax.dot_general(grad[...], grad[...], dims, preferred_element_type=F32)
        stats = stats + jnp.where(diagonal, 0.1, 0.0)
        scale = 2.5 / jnp.sqrt(jnp.sum(stats * stats, keepdims=True))
        first = jnp.sqrt(jnp.sqrt(scale)).astype(BF16).astype(F32)
        return scale * stats, first

    line = lax.broadcasted_iota(jnp.int32, (part, width), 0)
    spot = lax.broadcasted_iota(jnp.int32, (part, width), 1)
    wanted = jnp.where(line < part // 2, scalar_ref[2] + line, scalar_ref[3] + line - part // 2)
    pick = jnp.where(spot == wanted, 1.0, 0.0).astype(BF16)
    moment, first = begin(COLS_IN_COLS)
    m_left[...] = moment.astype(BF16)
    factor_value = factor(moment)
    q_left[...] = factor_value
    x_left[...] = (first * dot(pick, factor_value)).astype(BF16)
    moment, first = begin(ROWS_IN_COLS)
    m_right[...] = moment.astype(BF16)
    factor_value = factor(moment)
    q_right[...] = factor_value
    x_right[...] = (first * factor_value.astype(F32)).astype(BF16)

    count_left, count_right = scalar_ref[0], scalar_ref[1]

    def sweep(index, carry):
        second_left = dot(q_left[...], q_left[...]).astype(BF16)
        second_right = dot(q_right[...], q_right[...]).astype(BF16)
        fourth_left = dot(second_left, second_left).astype(BF16)
        fourth_right = dot(second_right, second_right).astype(BF16)
        moment_left = dot(fourth_left, m_left[...])
        moment_right = dot(fourth_right, m_right[...])
        m_left[...] = moment_left.astype(BF16)
        m_right[...] = moment_right.astype(BF16)
        factor_left = factor(moment_left)
        factor_right = factor(moment_right)
        q_left[...] = factor_left
        q_right[...] = factor_right

        @pl.when(index < count_left)
        def _():
            x_left[...] = dot(x_left[...], factor_left).astype(BF16)

        @pl.when(index < count_right)
        def _():
            x_right[...] = dot(x_right[...], factor_right).astype(BF16)

        return carry

    lax.fori_loop(1, jnp.maximum(count_left, count_right), sweep, 0)
    partial_value = dot(x_left[...], grad[...]).astype(BF16)
    update = dot(partial_value, x_right[...]).astype(BF16)
    for group in range(out_ref.shape[0]):
        out_ref[group] = update


def root(scalars, pieces, groups):
    part, width = pieces[0].shape
    square = pltpu.VMEM((width, width), BF16)
    return pl.pallas_call(
        functools.partial(root_kernel, len(pieces)),
        out_shape=jax.ShapeDtypeStruct((groups, part, width), BF16),
        in_specs=[SMEM] + [VMEM] * len(pieces),
        out_specs=VMEM,
        scratch_shapes=[square] * 5 + [pltpu.VMEM((part, width), BF16), square],
        compiler_params=params(32),
    )(scalars, *pieces)


def shards(line, groups, patches, cotangents, newton_counts):
    blocks, pix, width = patches.shape
    half = width // 2
    part = half // line
    rows = part // 2
    scale = 1.0 / float(pix * 4 * line * width) ** 0.5
    place, column, core = (lax.axis_index(name) for name in ("z", "x", "core"))

    def swap(array, axis, mask=1):
        return lax.ppermute(array, axis, [(i, i ^ mask) for i in range(lax.axis_size(axis))])

    where = jnp.stack([1 - column, column, 1 - core, core])
    (given,) = gram(where, patches, cotangents, scale, ((0, 0, BF16),))
    came = swap(given, "core")
    kept_other, given, kept = gram(
        where, patches, cotangents, scale, ((0, 1, F32), (1, 0, BF16), (1, 1, F32))
    )
    came_column = swap((kept_other + came.astype(F32)).astype(BF16), "x")
    pair = kept + swap(given, "core").astype(F32)
    own, *others = split(place[None], pair, came_column, line)
    for offset, piece in enumerate(others, 1):
        own = own + swap(piece, "z", offset).astype(F32)
    own = own.astype(BF16)
    near = [own] + [swap(own, "z", offset) for offset in range(1, line)]
    far = [swap(piece, "core") for piece in near]

    starts = []
    for index in range(2):
        target = 2 * place + index
        starts.append(
            ((target // line) ^ core) * half + ((target % line) ^ place) * part + core * rows
        )
    counts = lax.dynamic_index_in_dim(newton_counts, column, 0, keepdims=False)
    update = root(jnp.concatenate([counts, jnp.stack(starts)]), near + far, groups)
    update = update.reshape(groups * 2, rows, width)
    return lax.all_to_all(update, ("group", "x"), 0, 0, tiled=True)


def solution(mesh):
    devices, groups = mesh.shape["dp"], mesh.shape["group"]
    line = devices // 4
    cut = jax.sharding.Mesh(
        mesh.devices.reshape(line, 2, 2, groups), ("z", "x", "core", "group")
    )
    dp = ("z", "x", "core")
    placed = (P("group", dp, None), P("group", dp, None), P("group", None))
    return jax.shard_map(
        functools.partial(shards, line, groups),
        mesh=cut,
        in_specs=placed,
        out_specs=P(None, dp, None),
        check_vma=False,
    )
```

```python
import functools

import jax
import jax.numpy as jnp
from jax import lax
from jax.experimental import pallas as pl
from jax.experimental.pallas import tpu as pltpu
from jax.sharding import PartitionSpec as P

F32 = jnp.float32
BF16 = jnp.bfloat16
VMEM = pl.BlockSpec(memory_space=pltpu.VMEM)
SMEM = pl.BlockSpec(memory_space=pltpu.SMEM)
HBM = pl.BlockSpec(memory_space=pltpu.HBM)
ROWS_IN_COLS = (((0,), (0,)), ((), ()))
COLS_IN_COLS = (((1,), (1,)), ((), ()))


def params(limit):
    return pltpu.CompilerParams(vmem_limit_bytes=limit << 20)


def gram_kernel(scale, outputs, patch_hbm, cot_hbm, *refs):
    *outs, patch, cot, patch_sems, cot_sems = refs[-4 - len(outputs) :]
    half = cot.shape[2]
    column, core, parity = lax.axis_index("x"), lax.axis_index("core"), lax.axis_index("z") % 2
    pieces = [piece for _, group in outputs for piece in group]
    slots = {}
    copies = []
    for index, (block, columns, core_flip, parity_flip) in enumerate(pieces):
        number = column ^ block
        if (block, columns) not in slots:
            slot = len(slots)
            slots[block, columns] = slot
            copies.append(
                pltpu.make_async_copy(
                    cot_hbm.at[number, :, columns * half : (columns + 1) * half],
                    cot.at[slot],
                    cot_sems.at[slot],
                )
            )
            copies[-1].start()
        first = (core ^ core_flip) * half
        width = half
        if parity_flip is not None:
            width = half // 2
            first = first + (parity ^ parity_flip) * width
        copies.append(
            pltpu.make_async_copy(
                patch_hbm.at[number, :, pl.ds(pl.multiple_of(first, width), width)],
                patch.at[index, :, :width],
                patch_sems.at[index],
            )
        )
        copies[-1].start()
    index = 0
    waiting = iter(copies)
    ready = set()
    for (dtype, group), out in zip(outputs, outs):
        row = 0
        for block, columns, _, parity_flip in group:
            if (block, columns) not in ready:
                next(waiting).wait()
                ready.add((block, columns))
            next(waiting).wait()
            width = half if parity_flip is None else half // 2
            terms = lax.dot_general(
                patch[index, :, :width],
                cot[slots[block, columns]],
                ROWS_IN_COLS,
                preferred_element_type=F32,
            )
            out[row : row + width, :] = (terms * scale).astype(dtype)
            row += width
            index += 1


def gram(patches, cotangents, after, scale, *outputs):
    _, pix, width = patches.shape
    half = width // 2
    pieces = [piece for _, group in outputs for piece in group]
    sides = len({piece[:2] for piece in pieces})
    return pl.pallas_call(
        functools.partial(gram_kernel, scale, outputs),
        out_shape=[jax.ShapeDtypeStruct((2 * half, half), dtype) for dtype, _ in outputs],
        in_specs=[HBM, HBM] + [pl.BlockSpec(memory_space=pl.ANY)] * len(after),
        out_specs=[VMEM] * len(outputs),
        scratch_shapes=[
            pltpu.VMEM((len(pieces), pix, half), BF16),
            pltpu.VMEM((sides, pix, half), BF16),
            pltpu.SemaphoreType.DMA((len(pieces),)),
            pltpu.SemaphoreType.DMA((sides,)),
        ],
        compiler_params=params(16),
        cost_estimate=pl.CostEstimate(
            flops=4 * len(outputs) * pix * half * half,
            bytes_accessed=2 * (len(pieces) + sides) * pix * half,
            transcendentals=0,
        ),
    )(
        pltpu.with_memory_space_constraint(patches, pltpu.HBM),
        pltpu.with_memory_space_constraint(cotangents, pltpu.HBM),
        *after,
    )


def leave_kernel(kept_ref, came_ref, column_ref, line_ref):
    half = column_ref.shape[0]
    column_ref[...] = (kept_ref[:half, :] + came_ref[:half, :].astype(F32)).astype(BF16)
    line_ref[...] = (kept_ref[half:, :] + came_ref[half:, :].astype(F32)).astype(BF16)


def leave(kept, came):
    half = kept.shape[1]
    return pl.pallas_call(
        leave_kernel,
        out_shape=[jax.ShapeDtypeStruct((half, half), BF16)] * 2,
        in_specs=[VMEM] * 2,
        out_specs=[VMEM] * 2,
        compiler_params=params(16),
    )(kept, came)


def middle_kernel(kept_ref, given_ref, first_ref, second_ref, own_ref, line_ref, column_ref):
    rows, half = line_ref.shape
    parity = lax.axis_index("z") % 2

    def cut(flip):
        where = pl.ds(pl.multiple_of((parity ^ flip) * rows, rows), rows)
        total = kept_ref[where, :] + given_ref[where, :].astype(F32)
        return total + first_ref[where, :].astype(F32)

    def tail(block):
        where = slice((2 + block) * rows, (3 + block) * rows)
        total = kept_ref[where, :] + given_ref[where, :].astype(F32)
        return total + second_ref[block * rows : (block + 1) * rows, :].astype(F32)

    line_ref[...] = cut(1).astype(BF16)
    column_ref[...] = tail(0).astype(BF16)
    own_ref[:, :half] = cut(0)
    own_ref[:, half:] = tail(1)


def middle(kept, given, first, second):
    half = kept.shape[1]
    rows = half // 2
    return pl.pallas_call(
        middle_kernel,
        out_shape=[
            jax.ShapeDtypeStruct((rows, 2 * half), F32),
            jax.ShapeDtypeStruct((rows, half), BF16),
            jax.ShapeDtypeStruct((rows, half), BF16),
        ],
        in_specs=[VMEM] * 4,
        out_specs=[VMEM] * 3,
        compiler_params=params(16),
    )(kept, given, first, second)


def root_kernel(counts_ref, *refs):
    pieces = refs[:4]
    keep_ref, send_ref, grad, q_left, q_right, m_left, m_right, x_left, x_right = refs[4:]
    width = grad.shape[0]
    quarter = width // 4
    rows = keep_ref.shape[0]
    place, column, core = (lax.axis_index(name) for name in ("z", "x", "core"))
    for index, ref in enumerate(pieces):
        grad[quarter * index : quarter * (index + 1), :] = ref[...]
    diagonal = lax.broadcasted_iota(jnp.int32, (width, width), 0) == lax.broadcasted_iota(
        jnp.int32, (width, width), 1
    )

    def dot(a, b):
        return jnp.dot(a, b, preferred_element_type=F32)

    def factor(moment):
        return (jnp.where(diagonal, 1.25, 0.0) - 0.25 * moment).astype(BF16)

    def begin(dims):
        stats = lax.dot_general(grad[...], grad[...], dims, preferred_element_type=F32)
        stats = stats + jnp.where(diagonal, 0.1, 0.0)
        scale = 2.5 / jnp.sqrt(jnp.sum(stats * stats, keepdims=True))
        first = jnp.sqrt(jnp.sqrt(scale)).astype(BF16).astype(F32)
        return scale * stats, first

    def spot(flip):
        row = (4 * place + 2 * (column ^ flip) + core) * rows
        part = row // quarter
        return ((part // 2 ^ core) * 2 + (part % 2 ^ place % 2)) * quarter + row % quarter

    line = lax.broadcasted_iota(jnp.int32, (2 * rows, width), 0)
    wanted = jnp.where(line < rows, spot(0) + line, spot(1) + line - rows)
    pick = lax.broadcasted_iota(jnp.int32, (2 * rows, width), 1) == wanted
    pick = jnp.where(pick, 1.0, 0.0).astype(BF16)
    moment, first = begin(COLS_IN_COLS)
    m_left[...] = moment.astype(BF16)
    factor_value = factor(moment)
    q_left[...] = factor_value
    x_left[...] = (first * dot(pick, factor_value)).astype(BF16)
    moment, first = begin(ROWS_IN_COLS)
    m_right[...] = moment.astype(BF16)
    factor_value = factor(moment)
    q_right[...] = factor_value
    x_right[...] = (first * factor_value.astype(F32)).astype(BF16)

    count_left, count_right = counts_ref[column, 0], counts_ref[column, 1]

    def sweep(index, carry):
        second_left = dot(q_left[...], q_left[...]).astype(BF16)
        second_right = dot(q_right[...], q_right[...]).astype(BF16)
        fourth_left = dot(second_left, second_left).astype(BF16)
        fourth_right = dot(second_right, second_right).astype(BF16)
        moment_left = dot(fourth_left, m_left[...])
        moment_right = dot(fourth_right, m_right[...])
        m_left[...] = moment_left.astype(BF16)
        m_right[...] = moment_right.astype(BF16)
        factor_left = factor(moment_left)
        factor_right = factor(moment_right)
        q_left[...] = factor_left
        q_right[...] = factor_right
        next_left = dot(x_left[...], factor_left).astype(BF16)
        next_right = dot(x_right[...], factor_right).astype(BF16)
        x_left[...] = jnp.where(index < count_left, next_left, x_left[...])
        x_right[...] = jnp.where(index < count_right, next_right, x_right[...])
        return carry

    lax.fori_loop(1, jnp.maximum(count_left, count_right), sweep, 0)
    partial_value = dot(x_left[...], grad[...]).astype(BF16)
    update = dot(partial_value, x_right[...])
    keep_ref[...] = update[:rows, :].astype(BF16)
    send_ref[...] = update[rows:, :].astype(BF16)


def root(counts, pieces, rows):
    width = pieces[0].shape[1]
    square = pltpu.VMEM((width, width), BF16)
    out = jax.ShapeDtypeStruct((rows, width), BF16)
    return pl.pallas_call(
        root_kernel,
        out_shape=[out, out],
        in_specs=[SMEM] + [VMEM] * 4,
        out_specs=[VMEM] * 2,
        scratch_shapes=[square] * 5 + [pltpu.VMEM((2 * rows, width), BF16), square],
        compiler_params=params(32),
    )(counts, *pieces)


def shards(line, groups, patches, cotangents, newton_counts):
    blocks, pix, width = patches.shape
    half = width // 2
    rows = half // (2 * line)
    scale = 1.0 / float(pix * 4 * line * width) ** 0.5
    column, group = lax.axis_index("x"), lax.axis_index("group")

    def swap(array, axis, mask=1):
        return lax.ppermute(array, axis, [(i, i ^ mask) for i in range(lax.axis_size(axis))])

    def pieces(core_flip, leaves):
        if leaves:
            return ((1, 0, core_flip, None), (1, 1, core_flip, 1), (0, 1, core_flip, 1))
        return ((0, 0, core_flip, None), (1, 1, core_flip, 0), (0, 1, core_flip, 0))

    (given,) = gram(patches, cotangents, (), scale, (BF16, pieces(1, True)))
    came = swap(given, "core")
    kept, given_on = gram(
        patches, cotangents, (given,), scale, (F32, pieces(0, True)), (BF16, pieces(1, False))
    )
    came_on = swap(given_on, "core")
    to_column, to_line = leave(kept, came)
    came_first = swap(to_column, "x")
    came_second = swap(to_line, "z")
    (kept_on,) = gram(patches, cotangents, (to_column,), scale, (F32, pieces(0, False)))
    own, to_line, to_column = middle(kept_on, came_on, came_first, came_second)
    from_line = swap(to_line, "z")
    from_column = swap(to_column, "x")
    own = own + jnp.concatenate([from_line, from_column], 1).astype(F32)
    mask = 2
    while mask < line:
        own = own + swap(own.astype(BF16), "z", mask).astype(F32)
        mask *= 2
    own = own.astype(BF16)
    other = swap(own, "z")
    near = jnp.concatenate([own, other], 0)
    far = swap(near, "core")
    quarter = width // 4
    keep, send = root(newton_counts, [own, other, far[:quarter], far[quarter:]], rows)

    found = []
    for turn in range(groups):
        pair = []
        for flip in range(2):
            moves = [
                (c * groups + g, (c ^ flip) * groups + (g ^ turn))
                for c in range(2)
                for g in range(groups)
            ]
            piece = send if flip else keep
            pair.append(lax.ppermute(piece, ("x", "group"), moves) if turn or flip else piece)
        found.append(jnp.stack(pair))
    found = jnp.stack(found)
    found = jnp.where(column == 0, found, found[:, ::-1])
    bit = 1
    while bit < groups:
        shape = (groups // (2 * bit), 2, bit) + found.shape[1:]
        flipped = found.reshape(shape)[:, ::-1].reshape(found.shape)
        found = jnp.where(group & bit == 0, found, flipped)
        bit *= 2
    return found.reshape(blocks * groups, rows, width)


def solution(mesh):
    devices, groups = mesh.shape["dp"], mesh.shape["group"]
    line = devices // 4
    cut = jax.sharding.Mesh(
        mesh.devices.reshape(line, 2, 2, groups), ("z", "x", "core", "group")
    )
    dp = ("z", "x", "core")
    placed = (P("group", dp, None), P("group", dp, None), P("group", None))
    return jax.shard_map(
        functools.partial(shards, line, groups),
        mesh=cut,
        in_specs=placed,
        out_specs=P(None, dp, None),
        check_vma=False,
    )
```

```python
import functools

import jax
import jax.numpy as jnp
from jax import lax
from jax.experimental import pallas as pl
from jax.experimental.pallas import tpu as pltpu
from jax.sharding import PartitionSpec as P

F32 = jnp.float32
BF16 = jnp.bfloat16
VMEM = pl.BlockSpec(memory_space=pltpu.VMEM)
SMEM = pl.BlockSpec(memory_space=pltpu.SMEM)
HBM = pl.BlockSpec(memory_space=pltpu.HBM)
ROWS_IN_COLS = (((0,), (0,)), ((), ()))
COLS_IN_COLS = (((1,), (1,)), ((), ()))


def params(limit):
    return pltpu.CompilerParams(vmem_limit_bytes=limit << 20)


def piece_sum(patch, cot, scale, piece):
    block, columns, side, quarter = piece
    half = patch.shape[3]
    rows = slice(None) if quarter is None else slice(quarter * half // 2, (quarter + 1) * half // 2)
    terms = lax.dot_general(
        patch[block, side, :, rows],
        cot[block, :, columns * half : (columns + 1) * half],
        ROWS_IN_COLS,
        preferred_element_type=F32,
    )
    return terms * scale


def write_pieces(patch, cot, scale, pieces, out):
    row = 0
    for piece in pieces:
        value = piece_sum(patch, cot, scale, piece)
        out[row : row + value.shape[0], :] = value.astype(out.dtype)
        row += value.shape[0]


def load_kernel(scale, pieces, patch_hbm, cot_hbm, out, patch, cot, sems):
    half = patch.shape[3]
    width = half // 2
    column, core, parity = lax.axis_index("x"), lax.axis_index("core"), lax.axis_index("z") % 2
    copies = []

    def fetch(source, target):
        copies.append(pltpu.make_async_copy(source, target, sems.at[len(copies)]))
        copies[-1].start()

    def fetch_patch(block, side):
        for quarter in range(2):
            first = (core ^ side) * half + (parity ^ quarter) * width
            fetch(
                patch_hbm.at[column ^ block, :, pl.ds(pl.multiple_of(first, width), width)],
                patch.at[block, side, :, quarter * width : (quarter + 1) * width],
            )

    for block in (1, 0):
        fetch(cot_hbm.at[column ^ block], cot.at[block])
        fetch_patch(block, 1)
    needed = len(copies)
    for block in (1, 0):
        fetch_patch(block, 0)
    for copy in copies[:needed]:
        copy.wait()
    write_pieces(patch, cot, scale, pieces, out)
    for copy in copies[needed:]:
        copy.wait()


def load(patches, cotangents, scale, pieces):
    blocks, pix, width = patches.shape
    half = width // 2
    return pl.pallas_call(
        functools.partial(load_kernel, scale, pieces),
        out_shape=[
            jax.ShapeDtypeStruct((2 * half, half), BF16),
            jax.ShapeDtypeStruct((blocks, 2, pix, half), BF16),
            jax.ShapeDtypeStruct((blocks, pix, width), BF16),
        ],
        in_specs=[HBM, HBM],
        out_specs=[VMEM] * 3,
        scratch_shapes=[pltpu.SemaphoreType.DMA((10,))],
        compiler_params=params(16),
    )(
        pltpu.with_memory_space_constraint(patches, pltpu.HBM),
        pltpu.with_memory_space_constraint(cotangents, pltpu.HBM),
    )


def gram_kernel(scale, outputs, patch, cot, *refs):
    for (_, pieces), out in zip(outputs, refs[-len(outputs) :]):
        write_pieces(patch, cot, scale, pieces, out)


def gram(patch, cot, after, scale, *outputs):
    pix, half = patch.shape[2:]
    return pl.pallas_call(
        functools.partial(gram_kernel, scale, outputs),
        out_shape=[jax.ShapeDtypeStruct((2 * half, half), dtype) for dtype, _ in outputs],
        in_specs=[VMEM, VMEM] + [pl.BlockSpec(memory_space=pl.ANY)] * len(after),
        out_specs=[VMEM] * len(outputs),
        compiler_params=params(16),
        cost_estimate=pl.CostEstimate(
            flops=4 * len(outputs) * pix * half * half,
            bytes_accessed=2 * (patch.size + cot.size),
            transcendentals=0,
        ),
    )(patch, cot, *after)


def add(*values):
    total = values[0]
    for value in values[1:]:
        total = total + value.astype(F32)
    return total


def root_kernel(counts_hbm, *refs):
    pieces = refs[:6]
    keep_ref, send_ref, grad, q_left, q_right, m_left, m_right, x_left, x_right, counts, sem = refs[6:]
    counts_copy = pltpu.make_async_copy(counts_hbm, counts, sem)
    counts_copy.start()
    width = grad.shape[0]
    half, quarter = width // 2, width // 4
    rows = keep_ref.shape[0]
    place, column, core = (lax.axis_index(name) for name in ("z", "x", "core"))
    for index in range(2):
        own, other, far = pieces[3 * index : 3 * index + 3]
        columns = slice(half * index, half * (index + 1))
        grad[:quarter, columns] = own[...]
        grad[quarter:half, columns] = other[...]
        grad[half:, columns] = far[...]
    diagonal = lax.broadcasted_iota(jnp.int32, (width, width), 0) == lax.broadcasted_iota(
        jnp.int32, (width, width), 1
    )

    def dot(a, b):
        return jnp.dot(a, b, preferred_element_type=F32)

    def factor(moment):
        return (jnp.where(diagonal, 1.25, 0.0) - 0.25 * moment).astype(BF16)

    def begin(dims):
        stats = lax.dot_general(grad[...], grad[...], dims, preferred_element_type=F32)
        stats = stats + jnp.where(diagonal, 0.1, 0.0)
        scale = 2.5 / jnp.sqrt(jnp.sum(stats * stats, keepdims=True))
        first = jnp.sqrt(jnp.sqrt(scale)).astype(BF16).astype(F32)
        return scale * stats, first

    def spot(flip):
        row = (4 * place + 2 * (column ^ flip) + core) * rows
        part = row // quarter
        return ((part // 2 ^ core) * 2 + (part % 2 ^ place % 2)) * quarter + row % quarter

    line = lax.broadcasted_iota(jnp.int32, (2 * rows, width), 0)
    wanted = jnp.where(line < rows, spot(0) + line, spot(1) + line - rows)
    pick = lax.broadcasted_iota(jnp.int32, (2 * rows, width), 1) == wanted
    pick = jnp.where(pick, 1.0, 0.0).astype(BF16)
    moment, first = begin(COLS_IN_COLS)
    m_left[...] = moment.astype(BF16)
    factor_value = factor(moment)
    q_left[...] = factor_value
    x_left[...] = (first * dot(pick, factor_value)).astype(BF16)
    moment, first = begin(ROWS_IN_COLS)
    m_right[...] = moment.astype(BF16)
    factor_value = factor(moment)
    q_right[...] = factor_value
    x_right[...] = (first * factor_value.astype(F32)).astype(BF16)

    counts_copy.wait()
    count_left, count_right = counts[column, 0], counts[column, 1]

    def sweep(index, carry):
        second_left = dot(q_left[...], q_left[...]).astype(BF16)
        second_right = dot(q_right[...], q_right[...]).astype(BF16)
        fourth_left = dot(second_left, second_left).astype(BF16)
        fourth_right = dot(second_right, second_right).astype(BF16)
        moment_left = dot(fourth_left, m_left[...])
        moment_right = dot(fourth_right, m_right[...])
        m_left[...] = moment_left.astype(BF16)
        m_right[...] = moment_right.astype(BF16)
        factor_left = factor(moment_left)
        factor_right = factor(moment_right)
        q_left[...] = factor_left
        q_right[...] = factor_right
        next_left = dot(x_left[...], factor_left).astype(BF16)
        next_right = dot(x_right[...], factor_right).astype(BF16)
        x_left[...] = jnp.where(index < count_left, next_left, x_left[...])
        x_right[...] = jnp.where(index < count_right, next_right, x_right[...])
        return carry

    lax.fori_loop(1, jnp.maximum(count_left, count_right), sweep, 0)
    partial_value = dot(x_left[...], grad[...]).astype(BF16)
    update = dot(partial_value, x_right[...])
    keep_ref[...] = update[:rows, :].astype(BF16)
    send_ref[...] = update[rows:, :].astype(BF16)


def root(counts, pieces, rows):
    width = 4 * pieces[0].shape[0]
    square = pltpu.VMEM((width, width), BF16)
    out = jax.ShapeDtypeStruct((rows, width), BF16)
    return pl.pallas_call(
        root_kernel,
        out_shape=[out, out],
        in_specs=[HBM] + [VMEM] * 6,
        out_specs=[VMEM] * 2,
        scratch_shapes=[square] * 5
        + [
            pltpu.VMEM((2 * rows, width), BF16),
            square,
            pltpu.SMEM(counts.shape, jnp.int32),
            pltpu.SemaphoreType.DMA(()),
        ],
        compiler_params=params(32),
    )(pltpu.with_memory_space_constraint(counts, pltpu.HBM), *pieces)


def shards(line, groups, patches, cotangents, newton_counts):
    blocks, pix, width = patches.shape
    half, quarter = width // 2, width // 4
    rows = half // (2 * line)
    scale = 1.0 / float(pix * 4 * line * width) ** 0.5
    column, group = lax.axis_index("x"), lax.axis_index("group")

    def swap(array, axis, mask=1):
        return lax.ppermute(array, axis, [(i, i ^ mask) for i in range(lax.axis_size(axis))])

    def leaving(side):
        return ((1, 0, side, None), (1, 1, side, 1), (0, 1, side, 1))

    def staying(side):
        return ((0, 0, side, None), (1, 1, side, 0), (0, 1, side, 0))

    given, patch, cot = load(patches, cotangents, scale, leaving(1))
    came = swap(given, "core")
    kept, given_on = gram(patch, cot, (), scale, (F32, leaving(0)), (BF16, staying(1)))
    came_on = swap(given_on, "core")
    to_column = add(kept[:half], came[:half]).astype(BF16)
    to_line = add(kept[half:], came[half:]).astype(BF16)
    from_column = swap(to_column, "x")
    from_line = swap(to_line, "z")
    (kept_on,) = gram(patch, cot, (to_column,), scale, (F32, staying(0)))
    left = add(kept_on[:half], came_on[:half], from_column)
    from_line_left = swap(left[quarter:].astype(BF16), "z")
    right = add(kept_on[half:], came_on[half:], from_line)
    from_column_right = swap(right[:quarter].astype(BF16), "x")
    streams = [add(left[:quarter], from_line_left), add(right[quarter:], from_column_right)]
    mask = 2
    while mask < line:
        streams = [add(own, swap(own.astype(BF16), "z", mask)) for own in streams]
        mask *= 2
    pieces = []
    for own in streams:
        own = own.astype(BF16)
        other = swap(own, "z")
        pieces += [own, other, swap(jnp.concatenate([own, other], 0), "core")]
    keep, send = root(newton_counts, pieces, rows)

    found = []
    for turn in range(groups):
        pair = []
        for flip in range(2):
            moves = [
                (c * groups + g, (c ^ flip) * groups + (g ^ turn))
                for c in range(2)
                for g in range(groups)
            ]
            piece = send if flip else keep
            pair.append(lax.ppermute(piece, ("x", "group"), moves) if turn or flip else piece)
        found.append(jnp.stack(pair))
    found = jnp.stack(found)
    found = jnp.where(column == 0, found, found[:, ::-1])
    bit = 1
    while bit < groups:
        shape = (groups // (2 * bit), 2, bit) + found.shape[1:]
        flipped = found.reshape(shape)[:, ::-1].reshape(found.shape)
        found = jnp.where(group & bit == 0, found, flipped)
        bit *= 2
    return found.reshape(blocks * groups, rows, width)


def solution(mesh):
    devices, groups = mesh.shape["dp"], mesh.shape["group"]
    line = devices // 4
    cut = jax.sharding.Mesh(
        mesh.devices.reshape(line, 2, 2, groups), ("z", "x", "core", "group")
    )
    dp = ("z", "x", "core")
    placed = (P("group", dp, None), P("group", dp, None), P("group", None))
    return jax.shard_map(
        functools.partial(shards, line, groups),
        mesh=cut,
        in_specs=placed,
        out_specs=P(None, dp, None),
        check_vma=False,
    )
```

```python
import functools

import jax
import jax.numpy as jnp
from jax import lax
from jax.experimental import pallas as pl
from jax.experimental.pallas import tpu as pltpu
from jax.sharding import PartitionSpec as P

F32 = jnp.float32
BF16 = jnp.bfloat16
VMEM = pl.BlockSpec(memory_space=pltpu.VMEM)
SMEM = pl.BlockSpec(memory_space=pltpu.SMEM)
HBM = pl.BlockSpec(memory_space=pltpu.HBM)
ROWS_IN_COLS = (((0,), (0,)), ((), ()))
COLS_IN_COLS = (((1,), (1,)), ((), ()))


def params(limit):
    return pltpu.CompilerParams(vmem_limit_bytes=limit << 20)


def piece_place(kind, stage, index):
    early = 1 - stage
    block = jnp.where(kind == 0, early, index)
    rows = jnp.where(kind == 0, index, early)
    return block, rows


def write_pieces(patch, cot, scale, kind, columns, stage, out):
    half = patch.shape[3]
    for index in range(2):
        block, rows = piece_place(kind, stage, index)
        terms = lax.dot_general(
            patch[block, rows], cot[block, columns], ROWS_IN_COLS, preferred_element_type=F32
        )
        out[index * half : (index + 1) * half, :] = (terms * scale).astype(out.dtype)


def load_kernel(scale, patch_hbm, cot_hbm, out, patch, cot, sems):
    half = patch.shape[3]
    column, core, parity = lax.axis_index("x"), lax.axis_index("core"), lax.axis_index("z") % 2
    copies = []

    def fetch(source, target):
        copies.append(pltpu.make_async_copy(source, target, sems.at[len(copies)]))
        copies[-1].start()

    def part(array, block, number):
        first = pl.multiple_of(number * half, half)
        return array.at[column ^ block, :, pl.ds(first, half)]

    def fetch_patch(stage):
        for index in range(2):
            block, rows = piece_place(1 - core, stage, index)
            fetch(part(patch_hbm, block, parity ^ rows), patch.at[block, rows])

    def fetch_cot(columns):
        for block in (1, 0):
            fetch(part(cot_hbm, block, core ^ columns), cot.at[block, columns])

    fetch_patch(0)
    fetch_cot(1)
    needed = len(copies)
    fetch_patch(1)
    fetch_cot(0)
    for copy in copies[:needed]:
        copy.wait()
    write_pieces(patch, cot, scale, 1 - core, 1, 0, out)
    for copy in copies[needed:]:
        copy.wait()


def load(patches, cotangents, scale):
    blocks, pix, width = patches.shape
    half = width // 2
    return pl.pallas_call(
        functools.partial(load_kernel, scale),
        out_shape=[
            jax.ShapeDtypeStruct((width, half), BF16),
            jax.ShapeDtypeStruct((blocks, 2, pix, half), BF16),
            jax.ShapeDtypeStruct((blocks, 2, pix, half), BF16),
        ],
        in_specs=[HBM, HBM],
        out_specs=[VMEM] * 3,
        scratch_shapes=[pltpu.SemaphoreType.DMA((8,))],
        compiler_params=params(16),
    )(
        pltpu.with_memory_space_constraint(patches, pltpu.HBM),
        pltpu.with_memory_space_constraint(cotangents, pltpu.HBM),
    )


def gram_kernel(scale, outputs, patch, cot, *refs):
    core = lax.axis_index("core")
    for (_, columns, stage), out in zip(outputs, refs[-len(outputs) :]):
        write_pieces(patch, cot, scale, core ^ columns, columns, stage, out)


def gram(patch, cot, after, scale, *outputs):
    pix, half = patch.shape[2:]
    return pl.pallas_call(
        functools.partial(gram_kernel, scale, outputs),
        out_shape=[jax.ShapeDtypeStruct((2 * half, half), dtype) for dtype, _, _ in outputs],
        in_specs=[VMEM, VMEM] + [pl.BlockSpec(memory_space=pl.ANY)] * len(after),
        out_specs=[VMEM] * len(outputs),
        compiler_params=params(16),
        cost_estimate=pl.CostEstimate(
            flops=4 * len(outputs) * pix * half * half,
            bytes_accessed=2 * (patch.size + cot.size),
            transcendentals=0,
        ),
    )(patch, cot, *after)


def add(*values):
    total = values[0]
    for value in values[1:]:
        total = total + value.astype(F32)
    return total


def root_kernel(counts_hbm, own, other, far, out, grad, *refs):
    q_left, q_right, m_left, m_right, x_left, x_right, counts, sem = refs
    counts_copy = pltpu.make_async_copy(counts_hbm, counts, sem)
    counts_copy.start()
    width = grad.shape[0]
    half = width // 2
    rows = out.shape[0] // 2
    place, column, core = (lax.axis_index(name) for name in ("z", "x", "core"))
    for index, ref in enumerate((own, other)):
        where = slice(half * index, half * (index + 1))
        grad[where, :half] = jnp.where(core == 0, ref[...], far[where, :])
        grad[where, half:] = jnp.where(core == 0, far[where, :], ref[...])
    diagonal = lax.broadcasted_iota(jnp.int32, (width, width), 0) == lax.broadcasted_iota(
        jnp.int32, (width, width), 1
    )

    def dot(a, b):
        return jnp.dot(a, b, preferred_element_type=F32)

    def factor(moment):
        return (jnp.where(diagonal, 1.25, 0.0) - 0.25 * moment).astype(BF16)

    def begin(dims):
        stats = lax.dot_general(grad[...], grad[...], dims, preferred_element_type=F32)
        stats = stats + jnp.where(diagonal, 0.1, 0.0)
        scale = 2.5 / jnp.sqrt(jnp.sum(stats * stats, keepdims=True))
        first = jnp.sqrt(jnp.sqrt(scale)).astype(BF16).astype(F32)
        return scale * stats, first

    def spot(flip):
        row = (4 * place + 2 * (column ^ flip) + core) * rows
        return (row // half ^ place % 2) * half + row % half

    line = lax.broadcasted_iota(jnp.int32, (2 * rows, width), 0)
    wanted = jnp.where(line < rows, spot(1) + line, spot(0) + line - rows)
    pick = lax.broadcasted_iota(jnp.int32, (2 * rows, width), 1) == wanted
    pick = jnp.where(pick, 1.0, 0.0).astype(BF16)
    moment, first = begin(COLS_IN_COLS)
    m_left[...] = moment.astype(BF16)
    factor_value = factor(moment)
    q_left[...] = factor_value
    x_left[...] = (first * dot(pick, factor_value)).astype(BF16)
    moment, first = begin(ROWS_IN_COLS)
    m_right[...] = moment.astype(BF16)
    factor_value = factor(moment)
    q_right[...] = factor_value
    x_right[...] = (first * factor_value.astype(F32)).astype(BF16)

    counts_copy.wait()
    count_left, count_right = counts[column, 0], counts[column, 1]

    def sweep(index, carry):
        second_left = dot(q_left[...], q_left[...]).astype(BF16)
        second_right = dot(q_right[...], q_right[...]).astype(BF16)
        fourth_left = dot(second_left, second_left).astype(BF16)
        fourth_right = dot(second_right, second_right).astype(BF16)
        moment_left = dot(fourth_left, m_left[...])
        moment_right = dot(fourth_right, m_right[...])
        m_left[...] = moment_left.astype(BF16)
        m_right[...] = moment_right.astype(BF16)
        factor_left = factor(moment_left)
        factor_right = factor(moment_right)
        q_left[...] = factor_left
        q_right[...] = factor_right
        next_left = dot(x_left[...], factor_left).astype(BF16)
        next_right = dot(x_right[...], factor_right).astype(BF16)
        x_left[...] = jnp.where(index < count_left, next_left, x_left[...])
        x_right[...] = jnp.where(index < count_right, next_right, x_right[...])
        return carry

    lax.fori_loop(1, jnp.maximum(count_left, count_right), sweep, 0)
    partial_value = dot(x_left[...], grad[...]).astype(BF16)
    out[...] = dot(partial_value, x_right[...]).astype(BF16)


def root(counts, own, other, far, rows):
    width = far.shape[0]
    square = pltpu.VMEM((width, width), BF16)
    return pl.pallas_call(
        root_kernel,
        out_shape=jax.ShapeDtypeStruct((2 * rows, width), BF16),
        in_specs=[HBM] + [VMEM] * 3,
        out_specs=VMEM,
        scratch_shapes=[square] * 5
        + [
            pltpu.VMEM((2 * rows, width), BF16),
            square,
            pltpu.SMEM(counts.shape, jnp.int32),
            pltpu.SemaphoreType.DMA(()),
        ],
        compiler_params=params(32),
    )(pltpu.with_memory_space_constraint(counts, pltpu.HBM), own, other, far)


def spread_rows(groups, both):
    rows = both.shape[0] // 2
    send, keep = both[:rows], both[rows:]
    core = lax.axis_index("core")
    if groups == 2:
        moves = []
        for kinds in ((0, 1), (1, 0)):
            kind_moves = []
            for c in range(2):
                for k in range(2):
                    for g in range(2):
                        to = (c ^ 1, k, g) if kinds[k] == 0 else (c, k, g ^ 1)
                        kind_moves.append((4 * c + 2 * k + g, 4 * to[0] + 2 * to[1] + to[2]))
            moves.append(kind_moves)
        axes = ("x", "core", "group")
        first = lax.ppermute(both, axes, moves[0])
        passed = jnp.concatenate([jnp.where(core == 0, keep, send), first[:rows]], 0)
        second = lax.ppermute(passed, axes, moves[1])
        beside = jnp.where(core == 0, first[:rows], second[:rows])
        across = jnp.where(core == 0, second[:rows], first[rows:])
        return jnp.stack([jnp.stack([keep, beside]), jnp.stack([across, second[rows:]])])
    found = []
    for turn in range(groups):
        pair = []
        for flip in range(2):
            moves = [
                (c * groups + g, (c ^ flip) * groups + (g ^ turn))
                for c in range(2)
                for g in range(groups)
            ]
            piece = send if flip else keep
            pair.append(lax.ppermute(piece, ("x", "group"), moves) if turn or flip else piece)
        found.append(jnp.stack(pair))
    return jnp.stack(found)


def shards(line, groups, patches, cotangents, newton_counts):
    blocks, pix, width = patches.shape
    half = width // 2
    rows = half // (2 * line)
    scale = 1.0 / float(pix * 4 * line * width) ** 0.5
    column, group = lax.axis_index("x"), lax.axis_index("group")

    def swap(array, axis, mask=1):
        return lax.ppermute(array, axis, [(i, i ^ mask) for i in range(lax.axis_size(axis))])

    def cross(array, over_x):
        moves = []
        for z in range(line):
            for x in range(2):
                for core in range(2):
                    to = (z, x ^ 1) if core == over_x else (z ^ 1, x)
                    moves.append((4 * z + 2 * x + core, 4 * to[0] + 2 * to[1] + core))
        return lax.ppermute(array, ("z", "x", "core"), moves)

    given, patch, cot = load(patches, cotangents, scale)
    came = swap(given, "core")
    kept, given_on = gram(patch, cot, (), scale, (F32, 0, 0), (BF16, 1, 1))
    came_on = swap(given_on, "core")
    leaving = add(kept, came).astype(BF16)
    crossed = cross(leaving, 0)
    (kept_on,) = gram(patch, cot, (leaving,), scale, (F32, 0, 1))
    own = add(kept_on, came_on, crossed)
    own = add(own[:half], cross(own[half:].astype(BF16), 1))
    mask = 2
    while mask < line:
        own = add(own, swap(own.astype(BF16), "z", mask))
        mask *= 2
    own = own.astype(BF16)
    other = swap(own, "z")
    far = swap(jnp.concatenate([own, other], 0), "core")
    both = root(newton_counts, own, other, far, rows)

    found = spread_rows(groups, both)
    found = jnp.where(column == 0, found, found[:, ::-1])
    bit = 1
    while bit < groups:
        shape = (groups // (2 * bit), 2, bit) + found.shape[1:]
        flipped = found.reshape(shape)[:, ::-1].reshape(found.shape)
        found = jnp.where(group & bit == 0, found, flipped)
        bit *= 2
    return found.reshape(blocks * groups, rows, width)


def solution(mesh):
    devices, groups = mesh.shape["dp"], mesh.shape["group"]
    line = devices // 4
    cut = jax.sharding.Mesh(
        mesh.devices.reshape(line, 2, 2, groups), ("z", "x", "core", "group")
    )
    dp = ("z", "x", "core")
    placed = (P("group", dp, None), P("group", dp, None), P("group", None))
    return jax.shard_map(
        functools.partial(shards, line, groups),
        mesh=cut,
        in_specs=placed,
        out_specs=P(None, dp, None),
        check_vma=False,
    )
```

```python
import functools

import jax
import jax.numpy as jnp
from jax import lax
from jax.experimental import pallas as pl
from jax.experimental.pallas import tpu as pltpu
from jax.sharding import PartitionSpec as P

F32 = jnp.float32
BF16 = jnp.bfloat16
VMEM = pl.BlockSpec(memory_space=pltpu.VMEM)
SMEM = pl.BlockSpec(memory_space=pltpu.SMEM)
HBM = pl.BlockSpec(memory_space=pltpu.HBM)
ROWS_IN_COLS = (((0,), (0,)), ((), ()))
COLS_IN_COLS = (((1,), (1,)), ((), ()))


def params(limit):
    return pltpu.CompilerParams(vmem_limit_bytes=limit << 20)


def piece_sum(patch, cot, scale, piece):
    block, columns, side, quarter = piece
    half = patch.shape[3]
    rows = slice(None) if quarter is None else slice(quarter * half // 2, (quarter + 1) * half // 2)
    terms = lax.dot_general(
        patch[block, side, :, rows],
        cot[block, :, columns * half : (columns + 1) * half],
        ROWS_IN_COLS,
        preferred_element_type=F32,
    )
    return terms * scale


def write_pieces(patch, cot, scale, pieces, out):
    row = 0
    for piece in pieces:
        value = piece_sum(patch, cot, scale, piece)
        out[row : row + value.shape[0], :] = value.astype(out.dtype)
        row += value.shape[0]


def load_kernel(scale, pieces, patch_hbm, cot_hbm, out, patch, cot, sems):
    half = patch.shape[3]
    width = half // 2
    column, core, parity = lax.axis_index("x"), lax.axis_index("core"), lax.axis_index("z") % 2
    copies = []

    def fetch(source, target):
        copies.append(pltpu.make_async_copy(source, target, sems.at[len(copies)]))
        copies[-1].start()

    def fetch_patch(block, side):
        for quarter in range(2):
            first = (core ^ side) * half + (parity ^ quarter) * width
            fetch(
                patch_hbm.at[column ^ block, :, pl.ds(pl.multiple_of(first, width), width)],
                patch.at[block, side, :, quarter * width : (quarter + 1) * width],
            )

    for block in (1, 0):
        fetch(cot_hbm.at[column ^ block], cot.at[block])
        fetch_patch(block, 1)
    needed = len(copies)
    for block in (1, 0):
        fetch_patch(block, 0)
    for copy in copies[:needed]:
        copy.wait()
    write_pieces(patch, cot, scale, pieces, out)
    for copy in copies[needed:]:
        copy.wait()


def load(patches, cotangents, scale, pieces):
    blocks, pix, width = patches.shape
    half = width // 2
    return pl.pallas_call(
        functools.partial(load_kernel, scale, pieces),
        out_shape=[
            jax.ShapeDtypeStruct((2 * half, half), BF16),
            jax.ShapeDtypeStruct((blocks, 2, pix, half), BF16),
            jax.ShapeDtypeStruct((blocks, pix, width), BF16),
        ],
        in_specs=[HBM, HBM],
        out_specs=[VMEM] * 3,
        scratch_shapes=[pltpu.SemaphoreType.DMA((10,))],
        compiler_params=params(16),
    )(
        pltpu.with_memory_space_constraint(patches, pltpu.HBM),
        pltpu.with_memory_space_constraint(cotangents, pltpu.HBM),
    )


def gram_kernel(scale, outputs, patch, cot, *refs):
    for (_, pieces), out in zip(outputs, refs[-len(outputs) :]):
        write_pieces(patch, cot, scale, pieces, out)


def gram(patch, cot, after, scale, *outputs):
    pix, half = patch.shape[2:]
    return pl.pallas_call(
        functools.partial(gram_kernel, scale, outputs),
        out_shape=[jax.ShapeDtypeStruct((2 * half, half), dtype) for dtype, _ in outputs],
        in_specs=[VMEM, VMEM] + [pl.BlockSpec(memory_space=pl.ANY)] * len(after),
        out_specs=[VMEM] * len(outputs),
        compiler_params=params(16),
        cost_estimate=pl.CostEstimate(
            flops=4 * len(outputs) * pix * half * half,
            bytes_accessed=2 * (patch.size + cot.size),
            transcendentals=0,
        ),
    )(patch, cot, *after)


def add(*values):
    total = values[0]
    for value in values[1:]:
        total = total + value.astype(F32)
    return total


def root_kernel(most, counts_hbm, *refs):
    pieces = refs[:6]
    keep_ref, send_ref, grad, left, right, m_left, m_right, counts, sem = refs[6:]
    counts_copy = pltpu.make_async_copy(counts_hbm, counts, sem)
    counts_copy.start()
    width = grad.shape[0]
    half, quarter = width // 2, width // 4
    rows = keep_ref.shape[0]
    place, column, core = (lax.axis_index(name) for name in ("z", "x", "core"))
    for index in range(2):
        own, other, far = pieces[3 * index : 3 * index + 3]
        columns = slice(half * index, half * (index + 1))
        grad[:quarter, columns] = own[...]
        grad[quarter:half, columns] = other[...]
        grad[half:, columns] = far[...]
    diagonal = lax.broadcasted_iota(jnp.int32, (width, width), 0) == lax.broadcasted_iota(
        jnp.int32, (width, width), 1
    )

    def dot(a, b):
        return jnp.dot(a, b, preferred_element_type=F32)

    def factor(moment):
        return (jnp.where(diagonal, 1.25, 0.0) - 0.25 * moment).astype(BF16)

    def begin(dims):
        stats = lax.dot_general(grad[...], grad[...], dims, preferred_element_type=F32)
        stats = stats + jnp.where(diagonal, 0.1, 0.0)
        scale = 2.5 / jnp.sqrt(jnp.sum(stats * stats, keepdims=True))
        first = jnp.sqrt(jnp.sqrt(scale)).astype(BF16).astype(F32)
        return scale * stats, first

    def spot(flip):
        row = (4 * place + 2 * (column ^ flip) + core) * rows
        part = row // quarter
        return ((part // 2 ^ core) * 2 + (part % 2 ^ place % 2)) * quarter + row % quarter

    line = lax.broadcasted_iota(jnp.int32, (2 * rows, width), 0)
    wanted = jnp.where(line < rows, spot(0) + line, spot(1) + line - rows)
    pick = lax.broadcasted_iota(jnp.int32, (2 * rows, width), 1) == wanted
    pick = jnp.where(pick, 1.0, 0.0).astype(BF16)
    moment, first = begin(COLS_IN_COLS)
    m_left[...] = moment.astype(BF16)
    factor_value = factor(moment)
    left[2 * rows :, :] = factor_value
    left[: 2 * rows, :] = (first * dot(pick, factor_value)).astype(BF16)
    moment, first = begin(ROWS_IN_COLS)
    m_right[...] = moment.astype(BF16)
    factor_value = factor(moment)
    right[width:, :] = factor_value
    right[:width, :] = (first * factor_value.astype(F32)).astype(BF16)

    counts_copy.wait()
    sides = (
        (left, m_left, 2 * rows, counts[column, 0]),
        (right, m_right, width, counts[column, 1]),
    )
    for index in range(1, most):
        seconds = []
        for stacked, _, size, count in sides:
            if index == 1:
                factor_value = stacked[size:, :]
                seconds.append(dot(factor_value, factor_value).astype(BF16))
            else:
                product = dot(stacked[...], stacked[size:, :]).astype(BF16)
                if index > 2:
                    stacked[:size, :] = jnp.where(index <= count, product[:size], stacked[:size, :])
                else:
                    stacked[:size, :] = product[:size]
                seconds.append(product[size:])
        fourths = [dot(second, second).astype(BF16) for second in seconds]
        for (stacked, moment_ref, size, _), fourth in zip(sides, fourths):
            moment = dot(fourth, moment_ref[...])
            if index < most - 1:
                moment_ref[...] = moment.astype(BF16)
            stacked[size:, :] = factor(moment)
    finals = []
    for stacked, _, size, count in sides:
        product = dot(stacked[:size, :], stacked[size:, :]).astype(BF16)
        finals.append(jnp.where(most <= count, product, stacked[:size, :]))
    partial_value = dot(finals[0], grad[...]).astype(BF16)
    update = dot(partial_value, finals[1])
    keep_ref[...] = update[:rows, :].astype(BF16)
    send_ref[...] = update[rows:, :].astype(BF16)


def root(counts, pieces, rows, most=4):
    width = 4 * pieces[0].shape[0]
    square = pltpu.VMEM((width, width), BF16)
    out = jax.ShapeDtypeStruct((rows, width), BF16)
    return pl.pallas_call(
        functools.partial(root_kernel, most),
        out_shape=[out, out],
        in_specs=[HBM] + [VMEM] * 6,
        out_specs=[VMEM] * 2,
        scratch_shapes=[
            square,
            pltpu.VMEM((2 * rows + width, width), BF16),
            pltpu.VMEM((2 * width, width), BF16),
            square,
            square,
            pltpu.SMEM(counts.shape, jnp.int32),
            pltpu.SemaphoreType.DMA(()),
        ],
        compiler_params=params(40),
    )(pltpu.with_memory_space_constraint(counts, pltpu.HBM), *pieces)


def shards(line, groups, patches, cotangents, newton_counts):
    blocks, pix, width = patches.shape
    half, quarter = width // 2, width // 4
    rows = half // (2 * line)
    scale = 1.0 / float(pix * 4 * line * width) ** 0.5
    column, group = lax.axis_index("x"), lax.axis_index("group")

    def swap(array, axis, mask=1):
        return lax.ppermute(array, axis, [(i, i ^ mask) for i in range(lax.axis_size(axis))])

    def leaving(side):
        return ((1, 0, side, None), (1, 1, side, 1), (0, 1, side, 1))

    def staying(side):
        return ((0, 0, side, None), (1, 1, side, 0), (0, 1, side, 0))

    given, patch, cot = load(patches, cotangents, scale, leaving(1))
    came = swap(given, "core")
    kept, given_on = gram(patch, cot, (), scale, (F32, leaving(0)), (BF16, staying(1)))
    came_on = swap(given_on, "core")
    to_column = add(kept[:half], came[:half]).astype(BF16)
    to_line = add(kept[half:], came[half:]).astype(BF16)
    from_column = swap(to_column, "x")
    from_line = swap(to_line, "z")
    (kept_on,) = gram(patch, cot, (to_column,), scale, (F32, staying(0)))
    left = add(kept_on[:half], came_on[:half], from_column)
    from_line_left = swap(left[quarter:].astype(BF16), "z")
    right = add(kept_on[half:], came_on[half:], from_line)
    from_column_right = swap(right[:quarter].astype(BF16), "x")
    streams = [add(left[:quarter], from_line_left), add(right[quarter:], from_column_right)]
    mask = 2
    while mask < line:
        streams = [add(own, swap(own.astype(BF16), "z", mask)) for own in streams]
        mask *= 2
    pieces = []
    for own in streams:
        own = own.astype(BF16)
        other = swap(own, "z")
        pieces += [own, other, swap(jnp.concatenate([own, other], 0), "core")]
    keep, send = root(newton_counts, pieces, rows)

    found = []
    for turn in range(groups):
        pair = []
        for flip in range(2):
            moves = [
                (c * groups + g, (c ^ flip) * groups + (g ^ turn))
                for c in range(2)
                for g in range(groups)
            ]
            piece = send if flip else keep
            pair.append(lax.ppermute(piece, ("x", "group"), moves) if turn or flip else piece)
        found.append(jnp.stack(pair))
    found = jnp.stack(found)
    found = jnp.where(column == 0, found, found[:, ::-1])
    bit = 1
    while bit < groups:
        shape = (groups // (2 * bit), 2, bit) + found.shape[1:]
        flipped = found.reshape(shape)[:, ::-1].reshape(found.shape)
        found = jnp.where(group & bit == 0, found, flipped)
        bit *= 2
    return found.reshape(blocks * groups, rows, width)


def solution(mesh):
    devices, groups = mesh.shape["dp"], mesh.shape["group"]
    line = devices // 4
    cut = jax.sharding.Mesh(
        mesh.devices.reshape(line, 2, 2, groups), ("z", "x", "core", "group")
    )
    dp = ("z", "x", "core")
    placed = (P("group", dp, None), P("group", dp, None), P("group", None))
    return jax.shard_map(
        functools.partial(shards, line, groups),
        mesh=cut,
        in_specs=placed,
        out_specs=P(None, dp, None),
        check_vma=False,
    )
```

```python
import functools

import jax
import jax.numpy as jnp
from jax import lax
from jax.experimental import pallas as pl
from jax.experimental.pallas import tpu as pltpu
from jax.sharding import PartitionSpec as P

F32 = jnp.float32
BF16 = jnp.bfloat16
VMEM = pl.BlockSpec(memory_space=pltpu.VMEM)
SMEM = pl.BlockSpec(memory_space=pltpu.SMEM)
HBM = pl.BlockSpec(memory_space=pltpu.HBM)
ROWS_IN_COLS = (((0,), (0,)), ((), ()))
COLS_IN_COLS = (((1,), (1,)), ((), ()))


def params(limit):
    return pltpu.CompilerParams(vmem_limit_bytes=limit << 20)


def fetch_block(block, side_order, hbm, buffers, sems):
    patch_hbm, cot_hbm = hbm
    patch, cot = buffers
    half = patch.shape[2]
    width = half // 2
    column, core, parity = lax.axis_index("x"), lax.axis_index("core"), lax.axis_index("z") % 2
    copies = [pltpu.make_async_copy(cot_hbm.at[column ^ block], cot, sems.at[0])]
    for side in side_order:
        for quarter in range(2):
            first = (core ^ side) * half + (parity ^ quarter) * width
            copies.append(
                pltpu.make_async_copy(
                    patch_hbm.at[column ^ block, :, pl.ds(pl.multiple_of(first, width), width)],
                    patch.at[side, :, quarter * width : (quarter + 1) * width],
                    sems.at[len(copies)],
                )
            )
    for copy in copies:
        copy.start()
    return copies


def half_sum(patch, cot, side, scale):
    terms = lax.dot_general(patch[side], cot[...], ROWS_IN_COLS, preferred_element_type=F32)
    return terms * scale


def first_kernel(scale, patch_hbm, cot_hbm, given, patch, cot, sems):
    copies = fetch_block(1, (1, 0), (patch_hbm, cot_hbm), (patch, cot), sems)
    for copy in copies[:3]:
        copy.wait()
    given[...] = half_sum(patch, cot, 1, scale).astype(BF16)
    for copy in copies[3:]:
        copy.wait()


def second_kernel(scale, patch_hbm, cot_hbm, other_patch, other_cot, kept, given, patch, cot, sems):
    copies = fetch_block(0, (1, 0), (patch_hbm, cot_hbm), (patch, cot), sems)
    kept[...] = half_sum(other_patch, other_cot, 0, scale)
    for copy in copies[:3]:
        copy.wait()
    given[...] = half_sum(patch, cot, 1, scale).astype(BF16)
    for copy in copies[3:]:
        copy.wait()


def third_kernel(scale, patch, cot, _, kept):
    kept[...] = half_sum(patch, cot, 0, scale)


def pixel_sums(kernel, scale, shape, sums, loads, *operands):
    pix, width = shape
    half = width // 2
    out_shape = [jax.ShapeDtypeStruct((half, width), dtype) for dtype in sums]
    if loads:
        out_shape.append(jax.ShapeDtypeStruct((2, pix, half), BF16))
        out_shape.append(jax.ShapeDtypeStruct((pix, width), BF16))
    return pl.pallas_call(
        functools.partial(kernel, scale),
        out_shape=out_shape,
        in_specs=[HBM if loads and index < 2 else VMEM for index in range(len(operands))],
        out_specs=[VMEM] * len(out_shape),
        scratch_shapes=[pltpu.SemaphoreType.DMA((5,))] if loads else [],
        compiler_params=params(16),
        cost_estimate=pl.CostEstimate(
            flops=2 * len(sums) * pix * half * width,
            bytes_accessed=4 * pix * width,
            transcendentals=0,
        ),
    )(*operands)


def collect_kernel(own, *refs):
    *came, keep_left, keep_right, send_left, send_right = refs
    half = keep_left.shape[1]
    for columns, keep, send in (
        (slice(0, half), keep_left, send_left),
        (slice(half, 2 * half), keep_right, send_right),
    ):
        total = own[: keep.shape[0], columns]
        for ref in came:
            total = total + ref[:, columns].astype(F32)
        keep[...] = total
        send[...] = total.astype(BF16)


def collect(own, *came):
    rows, width = came[0].shape
    shape = (rows, width // 2)
    return pl.pallas_call(
        collect_kernel,
        out_shape=[jax.ShapeDtypeStruct(shape, F32)] * 2 + [jax.ShapeDtypeStruct(shape, BF16)] * 2,
        in_specs=[VMEM] * (1 + len(came)),
        out_specs=[VMEM] * 4,
        compiler_params=params(16),
    )(own, *came)


def add(*values):
    total = values[0]
    for value in values[1:]:
        total = total + value.astype(F32)
    return total


def root_kernel(most, counts_hbm, *refs):
    pieces = refs[:6]
    keep_ref, send_ref, grad, left, right, m_left, m_right, counts, sem = refs[6:]
    counts_copy = pltpu.make_async_copy(counts_hbm, counts, sem)
    counts_copy.start()
    width = grad.shape[0]
    half, quarter = width // 2, width // 4
    rows = keep_ref.shape[0]
    place, column, core = (lax.axis_index(name) for name in ("z", "x", "core"))
    for index in range(2):
        own, other, far = pieces[3 * index : 3 * index + 3]
        columns = slice(half * index, half * (index + 1))
        grad[:quarter, columns] = own[...]
        grad[quarter:half, columns] = other[...]
        grad[half:, columns] = far[...]
    diagonal = lax.broadcasted_iota(jnp.int32, (width, width), 0) == lax.broadcasted_iota(
        jnp.int32, (width, width), 1
    )

    def dot(a, b):
        return jnp.dot(a, b, preferred_element_type=F32)

    def factor(moment):
        return (jnp.where(diagonal, 1.25, 0.0) - 0.25 * moment).astype(BF16)

    def begin(dims):
        stats = lax.dot_general(grad[...], grad[...], dims, preferred_element_type=F32)
        stats = stats + jnp.where(diagonal, 0.1, 0.0)
        scale = 2.5 / jnp.sqrt(jnp.sum(stats * stats, keepdims=True))
        first = jnp.sqrt(jnp.sqrt(scale)).astype(BF16).astype(F32)
        return scale * stats, first

    def spot(flip):
        row = (4 * place + 2 * (column ^ flip) + core) * rows
        part = row // quarter
        return ((part // 2 ^ core) * 2 + (part % 2 ^ place % 2)) * quarter + row % quarter

    line = lax.broadcasted_iota(jnp.int32, (2 * rows, width), 0)
    wanted = jnp.where(line < rows, spot(0) + line, spot(1) + line - rows)
    pick = lax.broadcasted_iota(jnp.int32, (2 * rows, width), 1) == wanted
    pick = jnp.where(pick, 1.0, 0.0).astype(BF16)
    moment, first = begin(COLS_IN_COLS)
    m_left[...] = moment.astype(BF16)
    factor_value = factor(moment)
    left[2 * rows :, :] = factor_value
    left[: 2 * rows, :] = (first * dot(pick, factor_value)).astype(BF16)
    moment, first = begin(ROWS_IN_COLS)
    m_right[...] = moment.astype(BF16)
    factor_value = factor(moment)
    right[width:, :] = factor_value
    right[:width, :] = (first * factor_value.astype(F32)).astype(BF16)

    counts_copy.wait()
    sides = (
        (left, m_left, 2 * rows, counts[column, 0]),
        (right, m_right, width, counts[column, 1]),
    )
    for index in range(1, most):
        seconds = []
        for stacked, _, size, count in sides:
            if index == 1:
                factor_value = stacked[size:, :]
                seconds.append(dot(factor_value, factor_value).astype(BF16))
            else:
                product = dot(stacked[...], stacked[size:, :]).astype(BF16)
                if index > 2:
                    stacked[:size, :] = jnp.where(index <= count, product[:size], stacked[:size, :])
                else:
                    stacked[:size, :] = product[:size]
                seconds.append(product[size:])
        fourths = [dot(second, second).astype(BF16) for second in seconds]
        for (stacked, moment_ref, size, _), fourth in zip(sides, fourths):
            moment = dot(fourth, moment_ref[...])
            if index < most - 1:
                moment_ref[...] = moment.astype(BF16)
            stacked[size:, :] = factor(moment)
    finals = []
    for stacked, _, size, count in sides:
        product = dot(stacked[:size, :], stacked[size:, :]).astype(BF16)
        finals.append(jnp.where(most <= count, product, stacked[:size, :]))
    partial_value = dot(finals[0], grad[...]).astype(BF16)
    update = dot(partial_value, finals[1])
    keep_ref[...] = update[:rows, :].astype(BF16)
    send_ref[...] = update[rows:, :].astype(BF16)


def root(counts, pieces, rows, most=4):
    width = 4 * pieces[0].shape[0]
    square = pltpu.VMEM((width, width), BF16)
    out = jax.ShapeDtypeStruct((rows, width), BF16)
    return pl.pallas_call(
        functools.partial(root_kernel, most),
        out_shape=[out, out],
        in_specs=[HBM] + [VMEM] * 6,
        out_specs=[VMEM] * 2,
        scratch_shapes=[
            square,
            pltpu.VMEM((2 * rows + width, width), BF16),
            pltpu.VMEM((2 * width, width), BF16),
            square,
            square,
            pltpu.SMEM(counts.shape, jnp.int32),
            pltpu.SemaphoreType.DMA(()),
        ],
        compiler_params=params(40),
    )(pltpu.with_memory_space_constraint(counts, pltpu.HBM), *pieces)


def shards(line, groups, patches, cotangents, newton_counts):
    blocks, pix, width = patches.shape
    half, quarter = width // 2, width // 4
    rows = half // (2 * line)
    scale = 1.0 / float(pix * 4 * line * width) ** 0.5
    column, group = lax.axis_index("x"), lax.axis_index("group")

    def swap(array, axis, mask=1):
        return lax.ppermute(array, axis, [(i, i ^ mask) for i in range(lax.axis_size(axis))])

    def swap_diagonal(array):
        moves = [(2 * z + x, 2 * (z ^ 1) + (x ^ 1)) for z in range(line) for x in range(2)]
        return lax.ppermute(array, ("z", "x"), moves)

    patches = pltpu.with_memory_space_constraint(patches, pltpu.HBM)
    cotangents = pltpu.with_memory_space_constraint(cotangents, pltpu.HBM)
    shape = (pix, width)
    given, *loaded = pixel_sums(first_kernel, scale, shape, (BF16,), True, patches, cotangents)
    came = swap(given, "core")
    kept, given_on, *loaded = pixel_sums(
        second_kernel, scale, shape, (F32, BF16), True, patches, cotangents, *loaded
    )
    came_on = swap(given_on, "core")
    leaving = add(kept, came).astype(BF16)
    to_diagonal, to_column = leaving[quarter:], leaving[:quarter]
    from_diagonal = swap_diagonal(to_diagonal)
    from_column = swap(to_column, "x")
    (kept_on,) = pixel_sums(third_kernel, scale, shape, (F32,), False, *loaded, to_diagonal)
    own = add(kept_on, came_on)
    from_line = swap(own[quarter:].astype(BF16), "z")
    left, right, send_left, send_right = collect(own, from_diagonal, from_column, from_line)
    pieces = []
    for own, send in ((left, send_left), (right, send_right)):
        mask = 2
        while mask < line:
            own = add(own, swap(send, "z", mask))
            send = own.astype(BF16)
            mask *= 2
        own = send
        other = swap(own, "z")
        pieces += [own, other, swap(jnp.concatenate([own, other], 0), "core")]
    keep, send = root(newton_counts, pieces, rows)

    found = []
    for turn in range(groups):
        pair = []
        for flip in range(2):
            moves = [
                (c * groups + g, (c ^ flip) * groups + (g ^ turn))
                for c in range(2)
                for g in range(groups)
            ]
            piece = send if flip else keep
            pair.append(lax.ppermute(piece, ("x", "group"), moves) if turn or flip else piece)
        found.append(jnp.stack(pair))
    found = jnp.stack(found)
    found = jnp.where(column == 0, found, found[:, ::-1])
    bit = 1
    while bit < groups:
        shape = (groups // (2 * bit), 2, bit) + found.shape[1:]
        flipped = found.reshape(shape)[:, ::-1].reshape(found.shape)
        found = jnp.where(group & bit == 0, found, flipped)
        bit *= 2
    return found.reshape(blocks * groups, rows, width)


def solution(mesh):
    devices, groups = mesh.shape["dp"], mesh.shape["group"]
    line = devices // 4
    cut = jax.sharding.Mesh(
        mesh.devices.reshape(line, 2, 2, groups), ("z", "x", "core", "group")
    )
    dp = ("z", "x", "core")
    placed = (P("group", dp, None), P("group", dp, None), P("group", None))
    return jax.shard_map(
        functools.partial(shards, line, groups),
        mesh=cut,
        in_specs=placed,
        out_specs=P(None, dp, None),
        check_vma=False,
    )
```

```python
import functools

import jax
import jax.numpy as jnp
from jax import lax
from jax.experimental import pallas as pl
from jax.experimental.pallas import tpu as pltpu
from jax.sharding import PartitionSpec as P

F32 = jnp.float32
BF16 = jnp.bfloat16
VMEM = pl.BlockSpec(memory_space=pltpu.VMEM)
SMEM = pl.BlockSpec(memory_space=pltpu.SMEM)
HBM = pl.BlockSpec(memory_space=pltpu.HBM)
ROWS_IN_COLS = (((0,), (0,)), ((), ()))
COLS_IN_COLS = (((1,), (1,)), ((), ()))


def params(limit):
    return pltpu.CompilerParams(vmem_limit_bytes=limit << 20)


def fetch_block(block, side_order, hbm, buffers, sems):
    patch_hbm, cot_hbm = hbm
    patch, cot = buffers
    half = patch.shape[2]
    width = half // 2
    column, core, parity = lax.axis_index("x"), lax.axis_index("core"), lax.axis_index("z") % 2
    copies = [pltpu.make_async_copy(cot_hbm.at[column ^ block], cot, sems.at[0])]
    for side in side_order:
        for quarter in range(2):
            first = (core ^ side) * half + (parity ^ quarter) * width
            copies.append(
                pltpu.make_async_copy(
                    patch_hbm.at[column ^ block, :, pl.ds(pl.multiple_of(first, width), width)],
                    patch.at[side, :, quarter * width : (quarter + 1) * width],
                    sems.at[len(copies)],
                )
            )
    for copy in copies:
        copy.start()
    return copies


def half_sum(patch, cot, side, scale):
    terms = lax.dot_general(patch[side], cot[...], ROWS_IN_COLS, preferred_element_type=F32)
    return terms * scale


def first_kernel(scale, patch_hbm, cot_hbm, given, patch, cot, sems):
    copies = fetch_block(1, (1, 0), (patch_hbm, cot_hbm), (patch, cot), sems)
    for copy in copies[:3]:
        copy.wait()
    given[...] = half_sum(patch, cot, 1, scale).astype(BF16)
    for copy in copies[3:]:
        copy.wait()


def second_kernel(scale, patch_hbm, cot_hbm, other_patch, other_cot, kept, given, patch, cot, sems):
    copies = fetch_block(0, (1, 0), (patch_hbm, cot_hbm), (patch, cot), sems)
    kept[...] = half_sum(other_patch, other_cot, 0, scale)
    for copy in copies[:3]:
        copy.wait()
    given[...] = half_sum(patch, cot, 1, scale).astype(BF16)
    for copy in copies[3:]:
        copy.wait()


def third_kernel(scale, patch, cot, _, kept):
    kept[...] = half_sum(patch, cot, 0, scale)


def pixel_sums(kernel, scale, shape, sums, loads, *operands):
    pix, width = shape
    half = width // 2
    out_shape = [jax.ShapeDtypeStruct((half, width), dtype) for dtype in sums]
    if loads:
        out_shape.append(jax.ShapeDtypeStruct((2, pix, half), BF16))
        out_shape.append(jax.ShapeDtypeStruct((pix, width), BF16))
    return pl.pallas_call(
        functools.partial(kernel, scale),
        out_shape=out_shape,
        in_specs=[HBM if loads and index < 2 else VMEM for index in range(len(operands))],
        out_specs=[VMEM] * len(out_shape),
        scratch_shapes=[pltpu.SemaphoreType.DMA((5,))] if loads else [],
        compiler_params=params(16),
        cost_estimate=pl.CostEstimate(
            flops=2 * len(sums) * pix * half * width,
            bytes_accessed=4 * pix * width,
            transcendentals=0,
        ),
    )(*operands)


def collect_kernel(own, *refs):
    *came, keep_left, keep_right, send_left, send_right = refs
    half = keep_left.shape[1]
    for columns, keep, send in (
        (slice(0, half), keep_left, send_left),
        (slice(half, 2 * half), keep_right, send_right),
    ):
        total = own[: keep.shape[0], columns]
        for ref in came:
            total = total + ref[:, columns].astype(F32)
        keep[...] = total
        send[...] = total.astype(BF16)


def collect(own, *came):
    rows, width = came[0].shape
    shape = (rows, width // 2)
    return pl.pallas_call(
        collect_kernel,
        out_shape=[jax.ShapeDtypeStruct(shape, F32)] * 2 + [jax.ShapeDtypeStruct(shape, BF16)] * 2,
        in_specs=[VMEM] * (1 + len(came)),
        out_specs=[VMEM] * 4,
        compiler_params=params(16),
    )(own, *came)


def add(*values):
    total = values[0]
    for value in values[1:]:
        total = total + value.astype(F32)
    return total


def root_kernel(most, counts_hbm, *refs):
    pieces = refs[:6]
    keep_ref, send_ref, grad, left, right, m_left, m_right, s_left, s_right, counts, sem = refs[6:]
    counts_copy = pltpu.make_async_copy(counts_hbm, counts, sem)
    counts_copy.start()
    width = grad.shape[0]
    half, quarter = width // 2, width // 4
    rows = keep_ref.shape[0]
    low, high = slice(0, half), slice(half, width)
    place, column, core = (lax.axis_index(name) for name in ("z", "x", "core"))
    for index in range(2):
        own, other, far = pieces[3 * index : 3 * index + 3]
        columns = slice(half * index, half * (index + 1))
        grad[:quarter, columns] = own[...]
        grad[quarter:half, columns] = other[...]
        grad[half:, columns] = far[...]
    diagonal = lax.broadcasted_iota(jnp.int32, (half, half), 0) == lax.broadcasted_iota(
        jnp.int32, (half, half), 1
    )

    def dot(a, b):
        return jnp.dot(a, b, preferred_element_type=F32)

    def fill(ref, start, tiles):
        upper_left, upper_right, lower_right = (tile.astype(BF16) for tile in tiles)
        ref[start : start + half, low] = upper_left
        ref[start : start + half, high] = upper_right
        ref[start + half : start + width, low] = upper_right.T
        ref[start + half : start + width, high] = lower_right

    def factor(tiles):
        upper_left, upper_right, lower_right = tiles
        five = jnp.where(diagonal, 1.25, 0.0)
        return five - 0.25 * upper_left, -0.25 * upper_right, five - 0.25 * lower_right

    def begin(dims, upper, lower):
        tenth = jnp.where(diagonal, 0.1, 0.0)
        tiles = [
            lax.dot_general(a, b, dims, preferred_element_type=F32)
            for a, b in ((upper, upper), (upper, lower), (lower, lower))
        ]
        tiles = [tiles[0] + tenth, tiles[1], tiles[2] + tenth]
        squares = tiles[0] * tiles[0] + 2.0 * (tiles[1] * tiles[1]) + tiles[2] * tiles[2]
        scale = 2.5 / jnp.sqrt(jnp.sum(squares, keepdims=True))
        first = jnp.sqrt(jnp.sqrt(scale)).astype(BF16).astype(F32)
        return [scale * tile for tile in tiles], first

    def spot(flip):
        row = (4 * place + 2 * (column ^ flip) + core) * rows
        part = row // quarter
        return ((part // 2 ^ core) * 2 + (part % 2 ^ place % 2)) * quarter + row % quarter

    line = lax.broadcasted_iota(jnp.int32, (2 * rows, width), 0)
    wanted = jnp.where(line < rows, spot(0) + line, spot(1) + line - rows)
    pick = lax.broadcasted_iota(jnp.int32, (2 * rows, width), 1) == wanted
    pick = jnp.where(pick, 1.0, 0.0).astype(BF16)
    picked = 2 * rows
    tiles, first = begin(COLS_IN_COLS, grad[low, :], grad[high, :])
    fill(m_left, 0, tiles)
    fill(left, picked, factor(tiles))
    left[:picked, :] = (first * dot(pick, left[picked:, :])).astype(BF16)
    tiles, first = begin(ROWS_IN_COLS, grad[:, low], grad[:, high])
    fill(m_right, 0, tiles)
    tiles = [tile.astype(BF16) for tile in factor(tiles)]
    fill(right, width, tiles)
    tiles = [(first * tile.astype(F32)).astype(BF16) for tile in tiles]
    right[half:width, low] = tiles[0]
    right[half:width, high] = tiles[1]
    right[:half, low] = tiles[1].T
    right[:half, high] = tiles[2]

    def square(ref):
        by_high = dot(ref[...], ref[:, high])
        return dot(ref[low, :], ref[:, low]), by_high[low], by_high[high]

    counts_copy.wait()
    count_left, count_right = counts[column, 0], counts[column, 1]
    for index in range(1, most):
        q_left, q_right = left.at[picked:, :], right.at[width:, :]
        if index == 1:
            fill(s_left, 0, square(q_left))
            fill(s_right, 0, square(q_right))
        else:
            by_high = dot(left[...], q_left[:, high])
            by_low = dot(left[: picked + half, :], q_left[:, low])
            right_by_high = dot(right[...], q_right[:, high])
            right_by_low = dot(right[half : width + half, :], q_right[:, low])
            fill(s_left, 0, (by_low[picked:], by_high[picked : picked + half], by_high[picked + half :]))
            fill(
                s_right,
                0,
                (right_by_low[half:], right_by_high[width : width + half], right_by_high[width + half :]),
            )

            def keep_if(ref, value, goes_on):
                value = value.astype(BF16)
                return value if index == 2 else jnp.where(goes_on, value, ref)

            left[:picked, low] = keep_if(left[:picked, low], by_low[:picked], index <= count_left)
            left[:picked, high] = keep_if(left[:picked, high], by_high[:picked], index <= count_left)
            goes_on = index <= count_right
            upper_right = keep_if(right[half:width, high], right_by_high[half:width], goes_on)
            right[half:width, low] = keep_if(right[half:width, low], right_by_low[:half], goes_on)
            right[half:width, high] = upper_right
            right[:half, low] = upper_right.T
            right[:half, high] = keep_if(right[:half, high], right_by_high[:half], goes_on)
        fourths = square(s_left), square(s_right)
        fill(s_left, 0, fourths[0])
        fill(s_right, 0, fourths[1])
        for fourth, moment_ref, ref, start in (
            (s_left, m_left, left, picked),
            (s_right, m_right, right, width),
        ):
            by_high = dot(fourth[...], moment_ref[:, high])
            tiles = (dot(fourth[low, :], moment_ref[:, low]), by_high[low], by_high[high])
            if index < most - 1:
                fill(moment_ref, 0, tiles)
            fill(ref, start, factor(tiles))
    final_left = dot(left[:picked, :], left[picked:, :]).astype(BF16)
    final_left = jnp.where(most <= count_left, final_left, left[:picked, :])
    by_high = dot(right[:width, :], right[width:, high])
    by_low = dot(right[half:width, :], right[width:, low])
    goes_on = most <= count_right
    upper_right = jnp.where(goes_on, by_high[half:].astype(BF16), right[half:width, high])
    right[half:width, low] = jnp.where(goes_on, by_low.astype(BF16), right[half:width, low])
    right[half:width, high] = upper_right
    right[:half, low] = upper_right.T
    right[:half, high] = jnp.where(goes_on, by_high[:half].astype(BF16), right[:half, high])
    partial_value = dot(final_left, grad[...]).astype(BF16)
    update = dot(partial_value[:, low], right[half:width, :]) + dot(
        partial_value[:, high], right[:half, :]
    )
    keep_ref[...] = update[:rows, :].astype(BF16)
    send_ref[...] = update[rows:, :].astype(BF16)


def root(counts, pieces, rows, most=4):
    width = 4 * pieces[0].shape[0]
    square = pltpu.VMEM((width, width), BF16)
    out = jax.ShapeDtypeStruct((rows, width), BF16)
    return pl.pallas_call(
        functools.partial(root_kernel, most),
        out_shape=[out, out],
        in_specs=[HBM] + [VMEM] * 6,
        out_specs=[VMEM] * 2,
        scratch_shapes=[
            square,
            pltpu.VMEM((2 * rows + width, width), BF16),
            pltpu.VMEM((2 * width, width), BF16),
            square,
            square,
            square,
            square,
            pltpu.SMEM(counts.shape, jnp.int32),
            pltpu.SemaphoreType.DMA(()),
        ],
        compiler_params=params(40),
    )(pltpu.with_memory_space_constraint(counts, pltpu.HBM), *pieces)


def shards(line, groups, patches, cotangents, newton_counts):
    blocks, pix, width = patches.shape
    half, quarter = width // 2, width // 4
    rows = half // (2 * line)
    scale = 1.0 / float(pix * 4 * line * width) ** 0.5
    column, group = lax.axis_index("x"), lax.axis_index("group")

    def swap(array, axis, mask=1):
        return lax.ppermute(array, axis, [(i, i ^ mask) for i in range(lax.axis_size(axis))])

    def swap_diagonal(array):
        moves = [(2 * z + x, 2 * (z ^ 1) + (x ^ 1)) for z in range(line) for x in range(2)]
        return lax.ppermute(array, ("z", "x"), moves)

    patches = pltpu.with_memory_space_constraint(patches, pltpu.HBM)
    cotangents = pltpu.with_memory_space_constraint(cotangents, pltpu.HBM)
    shape = (pix, width)
    given, *loaded = pixel_sums(first_kernel, scale, shape, (BF16,), True, patches, cotangents)
    came = swap(given, "core")
    kept, given_on, *loaded = pixel_sums(
        second_kernel, scale, shape, (F32, BF16), True, patches, cotangents, *loaded
    )
    came_on = swap(given_on, "core")
    leaving = add(kept, came).astype(BF16)
    to_diagonal, to_column = leaving[quarter:], leaving[:quarter]
    from_diagonal = swap_diagonal(to_diagonal)
    from_column = swap(to_column, "x")
    (kept_on,) = pixel_sums(third_kernel, scale, shape, (F32,), False, *loaded, to_diagonal)
    own = add(kept_on, came_on)
    from_line = swap(own[quarter:].astype(BF16), "z")
    left, right, send_left, send_right = collect(own, from_diagonal, from_column, from_line)
    pieces = []
    for own, send in ((left, send_left), (right, send_right)):
        mask = 2
        while mask < line:
            own = add(own, swap(send, "z", mask))
            send = own.astype(BF16)
            mask *= 2
        own = send
        other = swap(own, "z")
        pieces += [own, other, swap(jnp.concatenate([own, other], 0), "core")]
    keep, send = root(newton_counts, pieces, rows)

    found = []
    for turn in range(groups):
        pair = []
        for flip in range(2):
            moves = [
                (c * groups + g, (c ^ flip) * groups + (g ^ turn))
                for c in range(2)
                for g in range(groups)
            ]
            piece = send if flip else keep
            pair.append(lax.ppermute(piece, ("x", "group"), moves) if turn or flip else piece)
        found.append(jnp.stack(pair))
    found = jnp.stack(found)
    found = jnp.where(column == 0, found, found[:, ::-1])
    bit = 1
    while bit < groups:
        shape = (groups // (2 * bit), 2, bit) + found.shape[1:]
        flipped = found.reshape(shape)[:, ::-1].reshape(found.shape)
        found = jnp.where(group & bit == 0, found, flipped)
        bit *= 2
    return found.reshape(blocks * groups, rows, width)


def solution(mesh):
    devices, groups = mesh.shape["dp"], mesh.shape["group"]
    line = devices // 4
    cut = jax.sharding.Mesh(
        mesh.devices.reshape(line, 2, 2, groups), ("z", "x", "core", "group")
    )
    dp = ("z", "x", "core")
    placed = (P("group", dp, None), P("group", dp, None), P("group", None))
    return jax.shard_map(
        functools.partial(shards, line, groups),
        mesh=cut,
        in_specs=placed,
        out_specs=P(None, dp, None),
        check_vma=False,
    )
```

```python
import functools

import jax
import jax.numpy as jnp
from jax import lax
from jax.experimental import pallas as pl
from jax.experimental.pallas import tpu as pltpu
from jax.sharding import PartitionSpec as P

F32 = jnp.float32
BF16 = jnp.bfloat16
VMEM = pl.BlockSpec(memory_space=pltpu.VMEM)
SMEM = pl.BlockSpec(memory_space=pltpu.SMEM)
HBM = pl.BlockSpec(memory_space=pltpu.HBM)
ROWS_IN_COLS = (((0,), (0,)), ((), ()))
COLS_IN_COLS = (((1,), (1,)), ((), ()))
QUICK = pl.CostEstimate(flops=1, bytes_accessed=1, transcendentals=0)


def params(limit):
    return pltpu.CompilerParams(vmem_limit_bytes=limit << 20)


def fetch_block(block, side_order, hbm, buffers, sems):
    patch_hbm, cot_hbm = hbm
    patch, cot = buffers
    half = patch.shape[2]
    width = half // 2
    column, core, parity = lax.axis_index("x"), lax.axis_index("core"), lax.axis_index("z") % 2
    copies = [pltpu.make_async_copy(cot_hbm.at[column ^ block], cot, sems.at[0])]
    for side in side_order:
        for quarter in range(2):
            first = (core ^ side) * half + (parity ^ quarter) * width
            copies.append(
                pltpu.make_async_copy(
                    patch_hbm.at[column ^ block, :, pl.ds(pl.multiple_of(first, width), width)],
                    patch.at[side, :, quarter * width : (quarter + 1) * width],
                    sems.at[len(copies)],
                )
            )
    for copy in copies:
        copy.start()
    return copies


def half_sum(patch, cot, side, scale):
    terms = lax.dot_general(patch[side], cot[...], ROWS_IN_COLS, preferred_element_type=F32)
    return terms * scale


def first_kernel(scale, patch_hbm, cot_hbm, given, patch, cot, sems):
    copies = fetch_block(1, (1, 0), (patch_hbm, cot_hbm), (patch, cot), sems)
    for copy in copies[:3]:
        copy.wait()
    given[...] = half_sum(patch, cot, 1, scale).astype(BF16)
    for copy in copies[3:]:
        copy.wait()


def second_kernel(scale, patch_hbm, cot_hbm, other_patch, other_cot, kept, given, patch, cot, sems):
    copies = fetch_block(0, (1, 0), (patch_hbm, cot_hbm), (patch, cot), sems)
    kept[...] = half_sum(other_patch, other_cot, 0, scale)
    for copy in copies[:3]:
        copy.wait()
    given[...] = half_sum(patch, cot, 1, scale).astype(BF16)
    for copy in copies[3:]:
        copy.wait()


def third_kernel(scale, patch, cot, _, kept):
    kept[...] = half_sum(patch, cot, 0, scale)


def pixel_sums(kernel, scale, shape, sums, loads, *operands):
    pix, width = shape
    half = width // 2
    out_shape = [jax.ShapeDtypeStruct((half, width), dtype) for dtype in sums]
    if loads:
        out_shape.append(jax.ShapeDtypeStruct((2, pix, half), BF16))
        out_shape.append(jax.ShapeDtypeStruct((pix, width), BF16))
    return pl.pallas_call(
        functools.partial(kernel, scale),
        out_shape=out_shape,
        in_specs=[HBM if loads and index < 2 else VMEM for index in range(len(operands))],
        out_specs=[VMEM] * len(out_shape),
        scratch_shapes=[pltpu.SemaphoreType.DMA((5,))] if loads else [],
        compiler_params=params(16),
        cost_estimate=QUICK,
    )(*operands)


def cut_kernel(columns, dtypes, mine, theirs, *refs):
    half = mine.shape[1] // 2
    where = slice(columns * half, (columns + 1) * half)
    outs = refs[-2:]
    rows = outs[0].shape[0]
    for index, out in enumerate(outs):
        lines = slice(index * rows, (index + 1) * rows)
        total = mine[lines, where] + theirs[lines, where].astype(F32)
        out[...] = total.astype(out.dtype)


def cut(mine, theirs, columns, dtypes, after=()):
    rows, width = mine.shape
    return pl.pallas_call(
        functools.partial(cut_kernel, columns, dtypes),
        out_shape=[jax.ShapeDtypeStruct((rows // 2, width // 2), dtype) for dtype in dtypes],
        in_specs=[VMEM] * 2 + [pl.BlockSpec(memory_space=pl.ANY)] * len(after),
        out_specs=[VMEM] * 2,
        compiler_params=params(16),
        cost_estimate=QUICK,
    )(mine, theirs, *after)


def add(*values):
    total = values[0]
    for value in values[1:]:
        total = total + value.astype(F32)
    return total


def root_kernel(most, counts_hbm, *refs):
    pieces = refs[:6]
    keep_ref, send_ref, grad, left, right, m_left, m_right, s_left, s_right, counts, sem = refs[6:]
    counts_copy = pltpu.make_async_copy(counts_hbm, counts, sem)
    counts_copy.start()
    width = grad.shape[0]
    half, quarter = width // 2, width // 4
    rows = keep_ref.shape[0]
    low, high = slice(0, half), slice(half, width)
    place, column, core = (lax.axis_index(name) for name in ("z", "x", "core"))
    for index in range(2):
        own, other, far = pieces[3 * index : 3 * index + 3]
        columns = slice(half * index, half * (index + 1))
        grad[:quarter, columns] = own[...]
        grad[quarter:half, columns] = other[...]
        grad[half:, columns] = far[...]
    diagonal = lax.broadcasted_iota(jnp.int32, (half, half), 0) == lax.broadcasted_iota(
        jnp.int32, (half, half), 1
    )

    def dot(a, b):
        return jnp.dot(a, b, preferred_element_type=F32)

    def fill(ref, start, tiles):
        upper_left, upper_right, lower_right = (tile.astype(BF16) for tile in tiles)
        ref[start : start + half, low] = upper_left
        ref[start : start + half, high] = upper_right
        ref[start + half : start + width, low] = upper_right.T
        ref[start + half : start + width, high] = lower_right

    def factor(tiles):
        upper_left, upper_right, lower_right = tiles
        five = jnp.where(diagonal, 1.25, 0.0)
        return five - 0.25 * upper_left, -0.25 * upper_right, five - 0.25 * lower_right

    def begin(dims, upper, lower):
        tenth = jnp.where(diagonal, 0.1, 0.0)
        tiles = [
            lax.dot_general(a, b, dims, preferred_element_type=F32)
            for a, b in ((upper, upper), (upper, lower), (lower, lower))
        ]
        tiles = [tiles[0] + tenth, tiles[1], tiles[2] + tenth]
        squares = tiles[0] * tiles[0] + 2.0 * (tiles[1] * tiles[1]) + tiles[2] * tiles[2]
        scale = 2.5 / jnp.sqrt(jnp.sum(squares, keepdims=True))
        first = jnp.sqrt(jnp.sqrt(scale)).astype(BF16).astype(F32)
        return [scale * tile for tile in tiles], first

    def spot(flip):
        row = (4 * place + 2 * (column ^ flip) + core) * rows
        part = row // quarter
        return ((part // 2 ^ core) * 2 + (part % 2 ^ place % 2)) * quarter + row % quarter

    line = lax.broadcasted_iota(jnp.int32, (2 * rows, width), 0)
    wanted = jnp.where(line < rows, spot(0) + line, spot(1) + line - rows)
    pick = lax.broadcasted_iota(jnp.int32, (2 * rows, width), 1) == wanted
    pick = jnp.where(pick, 1.0, 0.0).astype(BF16)
    picked = 2 * rows
    tiles, first = begin(COLS_IN_COLS, grad[low, :], grad[high, :])
    fill(m_left, 0, tiles)
    fill(left, picked, factor(tiles))
    left[:picked, :] = (first * dot(pick, left[picked:, :])).astype(BF16)
    tiles, first = begin(ROWS_IN_COLS, grad[:, low], grad[:, high])
    fill(m_right, 0, tiles)
    tiles = [tile.astype(BF16) for tile in factor(tiles)]
    fill(right, width, tiles)
    tiles = [(first * tile.astype(F32)).astype(BF16) for tile in tiles]
    right[half:width, low] = tiles[0]
    right[half:width, high] = tiles[1]
    right[:half, low] = tiles[1].T
    right[:half, high] = tiles[2]

    def square(ref):
        by_high = dot(ref[...], ref[:, high])
        return dot(ref[low, :], ref[:, low]), by_high[low], by_high[high]

    counts_copy.wait()
    count_left, count_right = counts[column, 0], counts[column, 1]
    for index in range(1, most):
        q_left, q_right = left.at[picked:, :], right.at[width:, :]
        if index == 1:
            fill(s_left, 0, square(q_left))
            fill(s_right, 0, square(q_right))
        else:
            by_high = dot(left[...], q_left[:, high])
            by_low = dot(left[: picked + half, :], q_left[:, low])
            right_by_high = dot(right[...], q_right[:, high])
            right_by_low = dot(right[half : width + half, :], q_right[:, low])
            fill(s_left, 0, (by_low[picked:], by_high[picked : picked + half], by_high[picked + half :]))
            fill(
                s_right,
                0,
                (right_by_low[half:], right_by_high[width : width + half], right_by_high[width + half :]),
            )

            def keep_if(ref, value, goes_on):
                value = value.astype(BF16)
                return value if index == 2 else jnp.where(goes_on, value, ref)

            left[:picked, low] = keep_if(left[:picked, low], by_low[:picked], index <= count_left)
            left[:picked, high] = keep_if(left[:picked, high], by_high[:picked], index <= count_left)
            goes_on = index <= count_right
            upper_right = keep_if(right[half:width, high], right_by_high[half:width], goes_on)
            right[half:width, low] = keep_if(right[half:width, low], right_by_low[:half], goes_on)
            right[half:width, high] = upper_right
            right[:half, low] = upper_right.T
            right[:half, high] = keep_if(right[:half, high], right_by_high[:half], goes_on)
        fourths = square(s_left), square(s_right)
        fill(s_left, 0, fourths[0])
        fill(s_right, 0, fourths[1])
        for fourth, moment_ref, ref, start in (
            (s_left, m_left, left, picked),
            (s_right, m_right, right, width),
        ):
            by_high = dot(fourth[...], moment_ref[:, high])
            tiles = (dot(fourth[low, :], moment_ref[:, low]), by_high[low], by_high[high])
            if index < most - 1:
                fill(moment_ref, 0, tiles)
            fill(ref, start, factor(tiles))
    final_left = dot(left[:picked, :], left[picked:, :]).astype(BF16)
    final_left = jnp.where(most <= count_left, final_left, left[:picked, :])
    by_high = dot(right[:width, :], right[width:, high])
    by_low = dot(right[half:width, :], right[width:, low])
    goes_on = most <= count_right
    upper_right = jnp.where(goes_on, by_high[half:].astype(BF16), right[half:width, high])
    right[half:width, low] = jnp.where(goes_on, by_low.astype(BF16), right[half:width, low])
    right[half:width, high] = upper_right
    right[:half, low] = upper_right.T
    right[:half, high] = jnp.where(goes_on, by_high[:half].astype(BF16), right[:half, high])
    partial_value = dot(final_left, grad[...]).astype(BF16)
    update = dot(partial_value[:, low], right[half:width, :]) + dot(
        partial_value[:, high], right[:half, :]
    )
    keep_ref[...] = update[:rows, :].astype(BF16)
    send_ref[...] = update[rows:, :].astype(BF16)


def root(counts, pieces, rows, most=4):
    width = 4 * pieces[0].shape[0]
    square = pltpu.VMEM((width, width), BF16)
    out = jax.ShapeDtypeStruct((rows, width), BF16)
    return pl.pallas_call(
        functools.partial(root_kernel, most),
        out_shape=[out, out],
        in_specs=[HBM] + [VMEM] * 6,
        out_specs=[VMEM] * 2,
        scratch_shapes=[
            square,
            pltpu.VMEM((2 * rows + width, width), BF16),
            pltpu.VMEM((2 * width, width), BF16),
            square,
            square,
            square,
            square,
            pltpu.SMEM(counts.shape, jnp.int32),
            pltpu.SemaphoreType.DMA(()),
        ],
        compiler_params=params(40),
    )(pltpu.with_memory_space_constraint(counts, pltpu.HBM), *pieces)


def shards(line, groups, patches, cotangents, newton_counts):
    blocks, pix, width = patches.shape
    half = width // 2
    rows = half // (2 * line)
    scale = 1.0 / float(pix * 4 * line * width) ** 0.5
    column, group = lax.axis_index("x"), lax.axis_index("group")

    def swap(array, axis, mask=1):
        return lax.ppermute(array, axis, [(i, i ^ mask) for i in range(lax.axis_size(axis))])

    def swap_diagonal(array):
        moves = [(2 * z + x, 2 * (z ^ 1) + (x ^ 1)) for z in range(line) for x in range(2)]
        return lax.ppermute(array, ("z", "x"), moves)

    patches = pltpu.with_memory_space_constraint(patches, pltpu.HBM)
    cotangents = pltpu.with_memory_space_constraint(cotangents, pltpu.HBM)
    shape = (pix, width)
    given, *loaded = pixel_sums(first_kernel, scale, shape, (BF16,), True, patches, cotangents)
    came = swap(given, "core")
    kept, given_on, *loaded = pixel_sums(
        second_kernel, scale, shape, (F32, BF16), True, patches, cotangents, *loaded
    )
    came_on = swap(given_on, "core")
    to_column, to_diagonal = cut(kept, came, 0, (BF16, BF16))
    from_diagonal = swap_diagonal(to_diagonal)
    from_column = swap(to_column, "x")
    (kept_on,) = pixel_sums(third_kernel, scale, shape, (F32,), False, *loaded, to_diagonal)
    left, to_line = cut(kept_on, came_on, 0, (F32, BF16))
    left = add(left, from_diagonal, from_column, swap(to_line, "z"))
    to_column, to_diagonal = cut(kept, came, 1, (BF16, BF16), (from_diagonal,))
    right, to_line = cut(kept_on, came_on, 1, (F32, BF16), (to_diagonal,))
    from_diagonal = swap_diagonal(to_diagonal)
    right = add(right, from_diagonal, swap(to_column, "x"), swap(to_line, "z"))
    pieces = []
    for own in (left, right):
        mask = 2
        while mask < line:
            own = add(own, swap(own.astype(BF16), "z", mask))
            mask *= 2
        own = own.astype(BF16)
        other = swap(own, "z")
        pieces += [own, other, swap(jnp.concatenate([own, other], 0), "core")]
    keep, send = root(newton_counts, pieces, rows)

    found = []
    for turn in range(groups):
        pair = []
        for flip in range(2):
            moves = [
                (c * groups + g, (c ^ flip) * groups + (g ^ turn))
                for c in range(2)
                for g in range(groups)
            ]
            piece = send if flip else keep
            pair.append(lax.ppermute(piece, ("x", "group"), moves) if turn or flip else piece)
        found.append(jnp.stack(pair))
    found = jnp.stack(found)
    found = jnp.where(column == 0, found, found[:, ::-1])
    bit = 1
    while bit < groups:
        shape = (groups // (2 * bit), 2, bit) + found.shape[1:]
        flipped = found.reshape(shape)[:, ::-1].reshape(found.shape)
        found = jnp.where(group & bit == 0, found, flipped)
        bit *= 2
    return found.reshape(blocks * groups, rows, width)


def solution(mesh):
    devices, groups = mesh.shape["dp"], mesh.shape["group"]
    line = devices // 4
    cut = jax.sharding.Mesh(
        mesh.devices.reshape(line, 2, 2, groups), ("z", "x", "core", "group")
    )
    dp = ("z", "x", "core")
    placed = (P("group", dp, None), P("group", dp, None), P("group", None))
    return jax.shard_map(
        functools.partial(shards, line, groups),
        mesh=cut,
        in_specs=placed,
        out_specs=P(None, dp, None),
        check_vma=False,
    )
```

```python
import functools

import jax
import jax.numpy as jnp
from jax import lax
from jax.experimental import pallas as pl
from jax.experimental.pallas import tpu as pltpu
from jax.sharding import PartitionSpec as P

F32 = jnp.float32
BF16 = jnp.bfloat16
VMEM = pl.BlockSpec(memory_space=pltpu.VMEM)
SMEM = pl.BlockSpec(memory_space=pltpu.SMEM)
HBM = pl.BlockSpec(memory_space=pltpu.HBM)
ROWS_IN_COLS = (((0,), (0,)), ((), ()))
COLS_IN_COLS = (((1,), (1,)), ((), ()))


def params(limit):
    return pltpu.CompilerParams(vmem_limit_bytes=limit << 20)


def fetch_block(block, side_order, hbm, buffers, sems):
    patch_hbm, cot_hbm = hbm
    patch, cot = buffers
    half = patch.shape[2]
    width = half // 2
    column, core, parity = lax.axis_index("x"), lax.axis_index("core"), lax.axis_index("z") % 2
    copies = [pltpu.make_async_copy(cot_hbm.at[column ^ block], cot, sems.at[0])]
    for side in side_order:
        for quarter in range(2):
            first = (core ^ side) * half + (parity ^ quarter) * width
            copies.append(
                pltpu.make_async_copy(
                    patch_hbm.at[column ^ block, :, pl.ds(pl.multiple_of(first, width), width)],
                    patch.at[side, :, quarter * width : (quarter + 1) * width],
                    sems.at[len(copies)],
                )
            )
    for copy in copies:
        copy.start()
    return copies


def half_sum(patch, cot, side, scale):
    terms = lax.dot_general(patch[side], cot[...], ROWS_IN_COLS, preferred_element_type=F32)
    return terms * scale


def first_kernel(scale, patch_hbm, cot_hbm, given, patch, cot, sems):
    copies = fetch_block(1, (1, 0), (patch_hbm, cot_hbm), (patch, cot), sems)
    for copy in copies[:3]:
        copy.wait()
    given[...] = half_sum(patch, cot, 1, scale).astype(BF16)
    for copy in copies[3:]:
        copy.wait()


def second_kernel(scale, patch_hbm, cot_hbm, other_patch, other_cot, kept, given, patch, cot, sems):
    copies = fetch_block(0, (1, 0), (patch_hbm, cot_hbm), (patch, cot), sems)
    kept[...] = half_sum(other_patch, other_cot, 0, scale)
    for copy in copies[:3]:
        copy.wait()
    given[...] = half_sum(patch, cot, 1, scale).astype(BF16)
    for copy in copies[3:]:
        copy.wait()


def third_kernel(scale, patch, cot, _, kept):
    kept[...] = half_sum(patch, cot, 0, scale)


def pixel_sums(kernel, scale, shape, sums, loads, *operands):
    pix, width = shape
    half = width // 2
    out_shape = [jax.ShapeDtypeStruct((half, width), dtype) for dtype in sums]
    if loads:
        out_shape.append(jax.ShapeDtypeStruct((2, pix, half), BF16))
        out_shape.append(jax.ShapeDtypeStruct((pix, width), BF16))
    return pl.pallas_call(
        functools.partial(kernel, scale),
        out_shape=out_shape,
        in_specs=[HBM if loads and index < 2 else VMEM for index in range(len(operands))],
        out_specs=[VMEM] * len(out_shape),
        scratch_shapes=[pltpu.SemaphoreType.DMA((5,))] if loads else [],
        compiler_params=params(16),
        cost_estimate=pl.CostEstimate(
            flops=2 * len(sums) * pix * half * width,
            bytes_accessed=4 * pix * width,
            transcendentals=0,
        ),
    )(*operands)


def add(*values):
    total = values[0]
    for value in values[1:]:
        total = total + value.astype(F32)
    return total


def root_kernel(most, counts_hbm, near, far, keep_ref, send_ref, *refs):
    grad, left, right, m_left, m_right, s_left, s_right, counts, sem = refs
    counts_copy = pltpu.make_async_copy(counts_hbm, counts, sem)
    counts_copy.start()
    width = grad.shape[0]
    half, quarter = width // 2, width // 4
    rows = keep_ref.shape[0]
    low, high = slice(0, half), slice(half, width)
    place, column, core = (lax.axis_index(name) for name in ("z", "x", "core"))
    grad[low, :] = near[...]
    grad[high, :] = far[...]
    diagonal = lax.broadcasted_iota(jnp.int32, (half, half), 0) == lax.broadcasted_iota(
        jnp.int32, (half, half), 1
    )

    def dot(a, b):
        return jnp.dot(a, b, preferred_element_type=F32)

    def fill(ref, start, tiles):
        upper_left, upper_right, lower_right = (tile.astype(BF16) for tile in tiles)
        ref[start : start + half, low] = upper_left
        ref[start : start + half, high] = upper_right
        ref[start + half : start + width, low] = upper_right.T
        ref[start + half : start + width, high] = lower_right

    def factor(tiles):
        upper_left, upper_right, lower_right = tiles
        five = jnp.where(diagonal, 1.25, 0.0)
        return five - 0.25 * upper_left, -0.25 * upper_right, five - 0.25 * lower_right

    def begin(dims, upper, lower):
        tenth = jnp.where(diagonal, 0.1, 0.0)
        tiles = [
            lax.dot_general(a, b, dims, preferred_element_type=F32)
            for a, b in ((upper, upper), (upper, lower), (lower, lower))
        ]
        tiles = [tiles[0] + tenth, tiles[1], tiles[2] + tenth]
        squares = tiles[0] * tiles[0] + 2.0 * (tiles[1] * tiles[1]) + tiles[2] * tiles[2]
        scale = 2.5 / jnp.sqrt(jnp.sum(squares, keepdims=True))
        first = jnp.sqrt(jnp.sqrt(scale)).astype(BF16).astype(F32)
        return [scale * tile for tile in tiles], first

    def spot(flip):
        row = (4 * place + 2 * (column ^ flip) + core) * rows
        part = row // quarter
        return ((part // 2 ^ core) * 2 + (part % 2 ^ place % 2)) * quarter + row % quarter

    line = lax.broadcasted_iota(jnp.int32, (2 * rows, width), 0)
    wanted = jnp.where(line < rows, spot(0) + line, spot(1) + line - rows)
    pick = lax.broadcasted_iota(jnp.int32, (2 * rows, width), 1) == wanted
    pick = jnp.where(pick, 1.0, 0.0).astype(BF16)
    picked = 2 * rows
    counts_copy.wait()
    count_left, count_right = counts[column, 0], counts[column, 1]

    def square(ref):
        by_high = dot(ref[...], ref[:, high])
        return dot(ref[low, :], ref[:, low]), by_high[low], by_high[high]

    def keep_if(old, value, goes_on):
        return jnp.where(goes_on, value.astype(BF16), old)

    def end_sweep(index, second, moment_ref, ref, start):
        fill(second, 0, square(second))
        yield
        by_high = dot(second[...], moment_ref[:, high])
        tiles = (dot(second[low, :], moment_ref[:, low]), by_high[low], by_high[high])
        if index < most - 1:
            fill(moment_ref, 0, tiles)
        fill(ref, start, factor(tiles))
        yield

    def left_steps():
        tiles, first = begin(COLS_IN_COLS, grad[low, :], grad[high, :])
        fill(m_left, 0, tiles)
        fill(left, picked, factor(tiles))
        left[:picked, :] = (first * dot(pick, left[picked:, :])).astype(BF16)
        yield
        factor_ref = left.at[picked:, :]
        for index in range(1, most):
            if index == 1:
                fill(s_left, 0, square(factor_ref))
            else:
                goes_on = index <= count_left
                by_high = dot(left[...], factor_ref[:, high])
                by_low = dot(left[: picked + half, :], factor_ref[:, low])
                second = by_high[picked:]
                fill(s_left, 0, (by_low[picked:], second[low], second[high]))
                left[:picked, low] = keep_if(left[:picked, low], by_low[:picked], goes_on)
                left[:picked, high] = keep_if(left[:picked, high], by_high[:picked], goes_on)
            yield
            yield from end_sweep(index, s_left, m_left, left, picked)
        product = dot(left[:picked, :], factor_ref[...])
        left[:picked, :] = keep_if(left[:picked, :], product, most <= count_left)
        yield
        left[:picked, :] = dot(left[:picked, :], grad[...]).astype(BF16)
        yield

    def right_steps():
        def keep_x(by_low, by_high, goes_on):
            upper_right = keep_if(right[half:width, high], by_high[high], goes_on)
            right[half:width, low] = keep_if(right[half:width, low], by_low, goes_on)
            right[half:width, high] = upper_right
            right[:half, low] = upper_right.T
            right[:half, high] = keep_if(right[:half, high], by_high[low], goes_on)

        tiles, first = begin(ROWS_IN_COLS, grad[:, low], grad[:, high])
        fill(m_right, 0, tiles)
        tiles = [tile.astype(BF16) for tile in factor(tiles)]
        fill(right, width, tiles)
        tiles = [(first * tile.astype(F32)).astype(BF16) for tile in tiles]
        right[half:width, low] = tiles[0]
        right[half:width, high] = tiles[1]
        right[:half, low] = tiles[1].T
        right[:half, high] = tiles[2]
        yield
        factor_ref = right.at[width:, :]
        for index in range(1, most):
            if index == 1:
                fill(s_right, 0, square(factor_ref))
            else:
                by_high = dot(right[...], factor_ref[:, high])
                by_low = dot(right[half : width + half, :], factor_ref[:, low])
                second = by_high[width:]
                fill(s_right, 0, (by_low[half:], second[low], second[high]))
                keep_x(by_low[:half], by_high[:width], index <= count_right)
            yield
            yield from end_sweep(index, s_right, m_right, right, width)
        by_high = dot(right[:width, :], factor_ref[:, high])
        keep_x(dot(right[half:width, :], factor_ref[:, low]), by_high, most <= count_right)
        yield

    lefts, rights = left_steps(), right_steps()
    next(lefts)
    going = True
    while going:
        going = next(lefts, True) is None
        going = (next(rights, True) is None) or going
    partial_value = left[:picked, :]
    update = dot(partial_value[:, low], right[half:width, :]) + dot(
        partial_value[:, high], right[:half, :]
    )
    keep_ref[...] = update[:rows, :].astype(BF16)
    send_ref[...] = update[rows:, :].astype(BF16)


def root(counts, near, far, rows, most=4):
    width = near.shape[1]
    square = pltpu.VMEM((width, width), BF16)
    out = jax.ShapeDtypeStruct((rows, width), BF16)
    return pl.pallas_call(
        functools.partial(root_kernel, most),
        out_shape=[out, out],
        in_specs=[HBM] + [VMEM] * 2,
        out_specs=[VMEM] * 2,
        scratch_shapes=[
            square,
            pltpu.VMEM((2 * rows + width, width), BF16),
            pltpu.VMEM((2 * width, width), BF16),
            square,
            square,
            square,
            square,
            pltpu.SMEM(counts.shape, jnp.int32),
            pltpu.SemaphoreType.DMA(()),
        ],
        compiler_params=params(40),
    )(pltpu.with_memory_space_constraint(counts, pltpu.HBM), near, far)


def shards(line, groups, patches, cotangents, newton_counts):
    blocks, pix, width = patches.shape
    half, quarter = width // 2, width // 4
    rows = half // (2 * line)
    scale = 1.0 / float(pix * 4 * line * width) ** 0.5
    column, group = lax.axis_index("x"), lax.axis_index("group")

    def swap(array, axis, mask=1):
        return lax.ppermute(array, axis, [(i, i ^ mask) for i in range(lax.axis_size(axis))])

    def swap_diagonal(array):
        moves = [(2 * z + x, 2 * (z ^ 1) + (x ^ 1)) for z in range(line) for x in range(2)]
        return lax.ppermute(array, ("z", "x"), moves)

    patches = pltpu.with_memory_space_constraint(patches, pltpu.HBM)
    cotangents = pltpu.with_memory_space_constraint(cotangents, pltpu.HBM)
    shape = (pix, width)
    given, *loaded = pixel_sums(first_kernel, scale, shape, (BF16,), True, patches, cotangents)
    came = swap(given, "core")
    kept, given_on, *loaded = pixel_sums(
        second_kernel, scale, shape, (F32, BF16), True, patches, cotangents, *loaded
    )
    came_on = swap(given_on, "core")
    leaving = add(kept, came).astype(BF16)
    to_diagonal, to_column = leaving[quarter:], leaving[:quarter]
    from_diagonal = swap_diagonal(to_diagonal)
    from_column = swap(to_column, "x")
    (kept_on,) = pixel_sums(third_kernel, scale, shape, (F32,), False, *loaded, to_diagonal)
    own = add(kept_on, came_on)
    from_line = swap(own[quarter:].astype(BF16), "z")
    own = add(own[:quarter], from_diagonal, from_column, from_line)
    mask = 2
    while mask < line:
        own = add(own, swap(own.astype(BF16), "z", mask))
        mask *= 2
    own = own.astype(BF16)
    near = jnp.concatenate([own, swap(own, "z")], 0)
    keep, send = root(newton_counts, near, swap(near, "core"), rows)

    found = []
    for turn in range(groups):
        pair = []
        for flip in range(2):
            moves = [
                (c * groups + g, (c ^ flip) * groups + (g ^ turn))
                for c in range(2)
                for g in range(groups)
            ]
            piece = send if flip else keep
            pair.append(lax.ppermute(piece, ("x", "group"), moves) if turn or flip else piece)
        found.append(jnp.stack(pair))
    found = jnp.stack(found)
    found = jnp.where(column == 0, found, found[:, ::-1])
    bit = 1
    while bit < groups:
        shape = (groups // (2 * bit), 2, bit) + found.shape[1:]
        flipped = found.reshape(shape)[:, ::-1].reshape(found.shape)
        found = jnp.where(group & bit == 0, found, flipped)
        bit *= 2
    return found.reshape(blocks * groups, rows, width)


def solution(mesh):
    devices, groups = mesh.shape["dp"], mesh.shape["group"]
    line = devices // 4
    cut = jax.sharding.Mesh(
        mesh.devices.reshape(line, 2, 2, groups), ("z", "x", "core", "group")
    )
    dp = ("z", "x", "core")
    placed = (P("group", dp, None), P("group", dp, None), P("group", None))
    return jax.shard_map(
        functools.partial(shards, line, groups),
        mesh=cut,
        in_specs=placed,
        out_specs=P(None, dp, None),
        check_vma=False,
    )
```

```python
import functools

import jax
import jax.numpy as jnp
from jax import lax
from jax.experimental import pallas as pl
from jax.experimental.pallas import tpu as pltpu
from jax.sharding import PartitionSpec as P

F32 = jnp.float32
BF16 = jnp.bfloat16
VMEM = pl.BlockSpec(memory_space=pltpu.VMEM)
SMEM = pl.BlockSpec(memory_space=pltpu.SMEM)
HBM = pl.BlockSpec(memory_space=pltpu.HBM)
ROWS_IN_COLS = (((0,), (0,)), ((), ()))
COLS_IN_COLS = (((1,), (1,)), ((), ()))


def params(limit):
    return pltpu.CompilerParams(vmem_limit_bytes=limit << 20)


def half_sum(patch, cot, block, side, scale):
    terms = lax.dot_general(
        patch[block, side], cot[block], ROWS_IN_COLS, preferred_element_type=F32
    )
    return terms * scale


def load_kernel(scale, patch_hbm, cot_hbm, given, patch, cot, sems):
    half = patch.shape[3]
    width = half // 2
    column, core, parity = lax.axis_index("x"), lax.axis_index("core"), lax.axis_index("z") % 2
    copies = []

    def fetch(source, target):
        copies.append(pltpu.make_async_copy(source, target, sems.at[len(copies)]))
        copies[-1].start()

    def fetch_patch(block, side):
        for quarter in range(2):
            first = (core ^ side) * half + (parity ^ quarter) * width
            fetch(
                patch_hbm.at[column ^ block, :, pl.ds(pl.multiple_of(first, width), width)],
                patch.at[block, side, :, quarter * width : (quarter + 1) * width],
            )

    fetch(cot_hbm.at[column ^ 1], cot.at[1])
    fetch_patch(1, 1)
    needed = len(copies)
    fetch_patch(1, 0)
    fetch(cot_hbm.at[column], cot.at[0])
    fetch_patch(0, 1)
    fetch_patch(0, 0)
    for copy in copies[:needed]:
        copy.wait()
    given[...] = half_sum(patch, cot, 1, 1, scale).astype(BF16)
    for copy in copies[needed:]:
        copy.wait()


def load(scale, patches, cotangents):
    blocks, pix, width = patches.shape
    half = width // 2
    return pl.pallas_call(
        functools.partial(load_kernel, scale),
        out_shape=[
            jax.ShapeDtypeStruct((half, width), BF16),
            jax.ShapeDtypeStruct((blocks, 2, pix, half), BF16),
            jax.ShapeDtypeStruct((blocks, pix, width), BF16),
        ],
        in_specs=[HBM] * 2,
        out_specs=[VMEM] * 3,
        scratch_shapes=[pltpu.SemaphoreType.DMA((10,))],
        compiler_params=params(16),
    )(
        pltpu.with_memory_space_constraint(patches, pltpu.HBM),
        pltpu.with_memory_space_constraint(cotangents, pltpu.HBM),
    )


def sums_kernel(scale, wanted, patch, cot, *refs):
    for (block, side, dtype), out in zip(wanted, refs[-len(wanted) :]):
        out[...] = half_sum(patch, cot, block, side, scale).astype(dtype)


def sums(scale, patch, cot, after, *wanted):
    pix, half = patch.shape[2:]
    return pl.pallas_call(
        functools.partial(sums_kernel, scale, wanted),
        out_shape=[jax.ShapeDtypeStruct((half, 2 * half), dtype) for _, _, dtype in wanted],
        in_specs=[VMEM] * 2 + [pl.BlockSpec(memory_space=pl.ANY)] * len(after),
        out_specs=[VMEM] * len(wanted),
        compiler_params=params(16),
        cost_estimate=pl.CostEstimate(
            flops=4 * len(wanted) * pix * half * half,
            bytes_accessed=8 * pix * half,
            transcendentals=0,
        ),
    )(patch, cot, *after)


def collect_kernel(own, *refs):
    *came, keep_left, keep_right, send_left, send_right = refs
    half = keep_left.shape[1]
    for columns, keep, send in (
        (slice(0, half), keep_left, send_left),
        (slice(half, 2 * half), keep_right, send_right),
    ):
        total = own[: keep.shape[0], columns]
        for ref in came:
            total = total + ref[:, columns].astype(F32)
        keep[...] = total
        send[...] = total.astype(BF16)


def collect(own, *came):
    rows, width = came[0].shape
    shape = (rows, width // 2)
    return pl.pallas_call(
        collect_kernel,
        out_shape=[jax.ShapeDtypeStruct(shape, F32)] * 2 + [jax.ShapeDtypeStruct(shape, BF16)] * 2,
        in_specs=[VMEM] * (1 + len(came)),
        out_specs=[VMEM] * 4,
        compiler_params=params(16),
    )(own, *came)


def add(*values):
    total = values[0]
    for value in values[1:]:
        total = total + value.astype(F32)
    return total


def root_kernel(most, counts_hbm, *refs):
    pieces = refs[:6]
    keep_ref, send_ref, grad, left, right, m_left, m_right, s_left, s_right, counts, sem = refs[6:]
    counts_copy = pltpu.make_async_copy(counts_hbm, counts, sem)
    counts_copy.start()
    width = grad.shape[0]
    half, quarter = width // 2, width // 4
    rows = keep_ref.shape[0]
    low, high = slice(0, half), slice(half, width)
    place, column, core = (lax.axis_index(name) for name in ("z", "x", "core"))
    for index in range(2):
        own, other, far = pieces[3 * index : 3 * index + 3]
        columns = slice(half * index, half * (index + 1))
        grad[:quarter, columns] = own[...]
        grad[quarter:half, columns] = other[...]
        grad[half:, columns] = far[...]
    diagonal = lax.broadcasted_iota(jnp.int32, (half, half), 0) == lax.broadcasted_iota(
        jnp.int32, (half, half), 1
    )

    def dot(a, b):
        return jnp.dot(a, b, preferred_element_type=F32)

    def fill(ref, start, tiles):
        upper_left, upper_right, lower_right = (tile.astype(BF16) for tile in tiles)
        ref[start : start + half, low] = upper_left
        ref[start : start + half, high] = upper_right
        ref[start + half : start + width, low] = upper_right.T
        ref[start + half : start + width, high] = lower_right

    def factor(tiles):
        upper_left, upper_right, lower_right = tiles
        five = jnp.where(diagonal, 1.25, 0.0)
        return five - 0.25 * upper_left, -0.25 * upper_right, five - 0.25 * lower_right

    def statistics(dims, upper, lower):
        tiles = [
            lax.dot_general(a, b, dims, preferred_element_type=F32)
            for a, b in ((upper, upper), (upper, lower), (lower, lower))
        ]
        tenth = jnp.where(diagonal, 0.1, 0.0)
        return tiles[0] + tenth, tiles[1], tiles[2] + tenth

    def spot(flip):
        row = (4 * place + 2 * (column ^ flip) + core) * rows
        part = row // quarter
        return ((part // 2 ^ core) * 2 + (part % 2 ^ place % 2)) * quarter + row % quarter

    line = lax.broadcasted_iota(jnp.int32, (2 * rows, width), 0)
    wanted = jnp.where(line < rows, spot(0) + line, spot(1) + line - rows)
    pick = lax.broadcasted_iota(jnp.int32, (2 * rows, width), 1) == wanted
    pick = jnp.where(pick, 1.0, 0.0).astype(BF16)
    picked = 2 * rows
    stats_left = statistics(COLS_IN_COLS, grad[low, :], grad[high, :])
    stats_right = statistics(ROWS_IN_COLS, grad[:, low], grad[:, high])
    squares = [tile * tile for tile in stats_left]
    norm = jnp.sqrt(jnp.sum(squares[0] + 2.0 * squares[1] + squares[2], keepdims=True))
    scale = 2.5 / norm
    first = jnp.sqrt(jnp.sqrt(scale)).astype(BF16).astype(F32)
    tiles = [scale * tile for tile in stats_left]
    fill(m_left, 0, tiles)
    fill(left, picked, factor(tiles))
    left[:picked, :] = (first * dot(pick, left[picked:, :])).astype(BF16)
    tiles = [scale * tile for tile in stats_right]
    fill(m_right, 0, tiles)
    tiles = [tile.astype(BF16) for tile in factor(tiles)]
    fill(right, width, tiles)
    tiles = [(first * tile.astype(F32)).astype(BF16) for tile in tiles]
    right[half:width, low] = tiles[0]
    right[half:width, high] = tiles[1]
    right[:half, low] = tiles[1].T
    right[:half, high] = tiles[2]

    def square(ref):
        by_high = dot(ref[...], ref[:, high])
        return dot(ref[low, :], ref[:, low]), by_high[low], by_high[high]

    counts_copy.wait()
    count_left, count_right = counts[column, 0], counts[column, 1]
    for index in range(1, most):
        q_left, q_right = left.at[picked:, :], right.at[width:, :]
        if index == 1:
            fill(s_left, 0, square(q_left))
            fill(s_right, 0, square(q_right))
        else:
            by_high = dot(left[...], q_left[:, high])
            by_low = dot(left[: picked + half, :], q_left[:, low])
            right_by_high = dot(right[...], q_right[:, high])
            right_by_low = dot(right[half : width + half, :], q_right[:, low])
            fill(s_left, 0, (by_low[picked:], by_high[picked : picked + half], by_high[picked + half :]))
            fill(
                s_right,
                0,
                (right_by_low[half:], right_by_high[width : width + half], right_by_high[width + half :]),
            )

            def keep_if(ref, value, goes_on):
                value = value.astype(BF16)
                return value if index == 2 else jnp.where(goes_on, value, ref)

            left[:picked, low] = keep_if(left[:picked, low], by_low[:picked], index <= count_left)
            left[:picked, high] = keep_if(left[:picked, high], by_high[:picked], index <= count_left)
            goes_on = index <= count_right
            upper_right = keep_if(right[half:width, high], right_by_high[half:width], goes_on)
            right[half:width, low] = keep_if(right[half:width, low], right_by_low[:half], goes_on)
            right[half:width, high] = upper_right
            right[:half, low] = upper_right.T
            right[:half, high] = keep_if(right[:half, high], right_by_high[:half], goes_on)
        fourths = square(s_left), square(s_right)
        fill(s_left, 0, fourths[0])
        fill(s_right, 0, fourths[1])
        for fourth, moment_ref, ref, start in (
            (s_left, m_left, left, picked),
            (s_right, m_right, right, width),
        ):
            by_high = dot(fourth[...], moment_ref[:, high])
            tiles = (dot(fourth[low, :], moment_ref[:, low]), by_high[low], by_high[high])
            if index < most - 1:
                fill(moment_ref, 0, tiles)
            fill(ref, start, factor(tiles))
    final_left = dot(left[:picked, :], left[picked:, :]).astype(BF16)
    final_left = jnp.where(most <= count_left, final_left, left[:picked, :])
    by_high = dot(right[:width, :], right[width:, high])
    by_low = dot(right[half:width, :], right[width:, low])
    goes_on = most <= count_right
    upper_right = jnp.where(goes_on, by_high[half:].astype(BF16), right[half:width, high])
    right[half:width, low] = jnp.where(goes_on, by_low.astype(BF16), right[half:width, low])
    right[half:width, high] = upper_right
    right[:half, low] = upper_right.T
    right[:half, high] = jnp.where(goes_on, by_high[:half].astype(BF16), right[:half, high])
    partial_value = dot(final_left, grad[...]).astype(BF16)
    update = dot(partial_value[:, low], right[half:width, :]) + dot(
        partial_value[:, high], right[:half, :]
    )
    keep_ref[...] = update[:rows, :].astype(BF16)
    send_ref[...] = update[rows:, :].astype(BF16)


def root(counts, pieces, rows, most=4):
    width = 4 * pieces[0].shape[0]
    square = pltpu.VMEM((width, width), BF16)
    out = jax.ShapeDtypeStruct((rows, width), BF16)
    return pl.pallas_call(
        functools.partial(root_kernel, most),
        out_shape=[out, out],
        in_specs=[HBM] + [VMEM] * 6,
        out_specs=[VMEM] * 2,
        scratch_shapes=[
            square,
            pltpu.VMEM((2 * rows + width, width), BF16),
            pltpu.VMEM((2 * width, width), BF16),
            square,
            square,
            square,
            square,
            pltpu.SMEM(counts.shape, jnp.int32),
            pltpu.SemaphoreType.DMA(()),
        ],
        compiler_params=params(40),
    )(pltpu.with_memory_space_constraint(counts, pltpu.HBM), *pieces)


def place_kernel(*refs):
    *pieces, out, sems = refs
    column, group = lax.axis_index("x"), lax.axis_index("group")
    copies = []
    for index, piece in enumerate(pieces):
        number = 2 * (group ^ (index // 2)) + (column ^ (index % 2))
        copies.append(pltpu.make_async_copy(piece, out.at[number], sems.at[index]))
        copies[-1].start()
    for copy in copies:
        copy.wait()


def place(pieces):
    rows, width = pieces[0].shape
    return pl.pallas_call(
        place_kernel,
        out_shape=jax.ShapeDtypeStruct((len(pieces), rows, width), BF16),
        in_specs=[VMEM] * len(pieces),
        out_specs=HBM,
        scratch_shapes=[pltpu.SemaphoreType.DMA((len(pieces),))],
        compiler_params=params(16),
    )(*pieces)


def shards(line, groups, patches, cotangents, newton_counts):
    blocks, pix, width = patches.shape
    half, quarter = width // 2, width // 4
    rows = half // (2 * line)
    scale = 1.0 / float(pix * 4 * line * width) ** 0.5

    def swap(array, axis, mask=1):
        return lax.ppermute(array, axis, [(i, i ^ mask) for i in range(lax.axis_size(axis))])

    def swap_diagonal(array):
        moves = [(2 * z + x, 2 * (z ^ 1) + (x ^ 1)) for z in range(line) for x in range(2)]
        return lax.ppermute(array, ("z", "x"), moves)

    given, patch, cot = load(scale, patches, cotangents)
    came = swap(given, "core")
    kept, given_on = sums(scale, patch, cot, (), (1, 0, F32), (0, 1, BF16))
    came_on = swap(given_on, "core")
    leaving = add(kept, came).astype(BF16)
    to_diagonal, to_column = leaving[quarter:], leaving[:quarter]
    from_diagonal = swap_diagonal(to_diagonal)
    from_column = swap(to_column, "x")
    (kept_on,) = sums(scale, patch, cot, (to_diagonal,), (0, 0, F32))
    own = add(kept_on, came_on)
    from_line = swap(own[quarter:].astype(BF16), "z")
    left, right, send_left, send_right = collect(own, from_diagonal, from_column, from_line)
    pieces = []
    for own, send in ((left, send_left), (right, send_right)):
        mask = 2
        while mask < line:
            own = add(own, swap(send, "z", mask))
            send = own.astype(BF16)
            mask *= 2
        own = send
        other = swap(own, "z")
        pieces += [own, other, swap(jnp.concatenate([own, other], 0), "core")]
    keep, send = root(newton_counts, pieces, rows)

    pieces = []
    for turn in range(groups):
        for flip in range(2):
            moves = [
                (c * groups + g, (c ^ flip) * groups + (g ^ turn))
                for c in range(2)
                for g in range(groups)
            ]
            piece = send if flip else keep
            pieces.append(lax.ppermute(piece, ("x", "group"), moves) if turn or flip else piece)
    return place(pieces)


def solution(mesh):
    devices, groups = mesh.shape["dp"], mesh.shape["group"]
    line = devices // 4
    cut = jax.sharding.Mesh(
        mesh.devices.reshape(line, 2, 2, groups), ("z", "x", "core", "group")
    )
    dp = ("z", "x", "core")
    placed = (P("group", dp, None), P("group", dp, None), P("group", None))
    return jax.shard_map(
        functools.partial(shards, line, groups),
        mesh=cut,
        in_specs=placed,
        out_specs=P(None, dp, None),
        check_vma=False,
    )
```

```python
import functools

import jax
import jax.numpy as jnp
from jax import lax
from jax.experimental import pallas as pl
from jax.experimental.pallas import tpu as pltpu
from jax.sharding import PartitionSpec as P

F32 = jnp.float32
BF16 = jnp.bfloat16
VMEM = pl.BlockSpec(memory_space=pltpu.VMEM)
SMEM = pl.BlockSpec(memory_space=pltpu.SMEM)
HBM = pl.BlockSpec(memory_space=pltpu.HBM)
ROWS_IN_COLS = (((0,), (0,)), ((), ()))
COLS_IN_COLS = (((1,), (1,)), ((), ()))


def params(limit):
    return pltpu.CompilerParams(vmem_limit_bytes=limit << 20)


def half_sum(patch, cot, block, side, scale):
    terms = lax.dot_general(
        patch[block, side], cot[block], ROWS_IN_COLS, preferred_element_type=F32
    )
    return terms * scale


def load_kernel(scale, patch_hbm, cot_hbm, given, patch, cot, sems):
    half = patch.shape[3]
    width = half // 2
    column, core, parity = lax.axis_index("x"), lax.axis_index("core"), lax.axis_index("z") % 2
    copies = []

    def fetch(source, target):
        copies.append(pltpu.make_async_copy(source, target, sems.at[len(copies)]))
        copies[-1].start()

    def fetch_patch(block, side):
        for quarter in range(2):
            first = (column ^ side) * half + (parity ^ quarter) * width
            fetch(
                patch_hbm.at[core ^ block, :, pl.ds(pl.multiple_of(first, width), width)],
                patch.at[block, side, :, quarter * width : (quarter + 1) * width],
            )

    fetch(cot_hbm.at[core ^ 1], cot.at[1])
    fetch_patch(1, 1)
    needed = len(copies)
    fetch(cot_hbm.at[core], cot.at[0])
    fetch_patch(0, 1)
    fetch_patch(1, 0)
    fetch_patch(0, 0)
    for copy in copies[:needed]:
        copy.wait()
    given[...] = half_sum(patch, cot, 1, 1, scale).astype(BF16)
    for copy in copies[needed:]:
        copy.wait()


def load(scale, patches, cotangents):
    blocks, pix, width = patches.shape
    half = width // 2
    return pl.pallas_call(
        functools.partial(load_kernel, scale),
        out_shape=[
            jax.ShapeDtypeStruct((half, width), BF16),
            jax.ShapeDtypeStruct((blocks, 2, pix, half), BF16),
            jax.ShapeDtypeStruct((blocks, pix, width), BF16),
        ],
        in_specs=[HBM] * 2,
        out_specs=[VMEM] * 3,
        scratch_shapes=[pltpu.SemaphoreType.DMA((10,))],
        compiler_params=params(16),
    )(
        pltpu.with_memory_space_constraint(patches, pltpu.HBM),
        pltpu.with_memory_space_constraint(cotangents, pltpu.HBM),
    )


def sums_kernel(scale, wanted, patch, cot, *refs):
    for (block, side, dtype), out in zip(wanted, refs[-len(wanted) :]):
        out[...] = half_sum(patch, cot, block, side, scale).astype(dtype)


def sums(scale, patch, cot, after, *wanted):
    pix, half = patch.shape[2:]
    return pl.pallas_call(
        functools.partial(sums_kernel, scale, wanted),
        out_shape=[jax.ShapeDtypeStruct((half, 2 * half), dtype) for _, _, dtype in wanted],
        in_specs=[VMEM] * 2 + [pl.BlockSpec(memory_space=pl.ANY)] * len(after),
        out_specs=[VMEM] * len(wanted),
        compiler_params=params(16),
        cost_estimate=pl.CostEstimate(
            flops=4 * len(wanted) * pix * half * half,
            bytes_accessed=8 * pix * half,
            transcendentals=0,
        ),
    )(patch, cot, *after)


def collect_kernel(own, *refs):
    *came, keep_left, keep_right, send_left, send_right = refs
    half = keep_left.shape[1]
    for columns, keep, send in (
        (slice(0, half), keep_left, send_left),
        (slice(half, 2 * half), keep_right, send_right),
    ):
        total = own[: keep.shape[0], columns]
        for ref in came:
            total = total + ref[:, columns].astype(F32)
        keep[...] = total
        send[...] = total.astype(BF16)


def collect(own, *came):
    rows, width = came[0].shape
    shape = (rows, width // 2)
    return pl.pallas_call(
        collect_kernel,
        out_shape=[jax.ShapeDtypeStruct(shape, F32)] * 2 + [jax.ShapeDtypeStruct(shape, BF16)] * 2,
        in_specs=[VMEM] * (1 + len(came)),
        out_specs=[VMEM] * 4,
        compiler_params=params(16),
    )(own, *came)


def add(*values):
    total = values[0]
    for value in values[1:]:
        total = total + value.astype(F32)
    return total


def root_kernel(most, counts_hbm, *refs):
    pieces = refs[:8]
    keep_ref, send_ref, grad, left, right, m_left, m_right, s_left, s_right, counts, sem = refs[8:]
    counts_copy = pltpu.make_async_copy(counts_hbm, counts, sem)
    counts_copy.start()
    width = grad.shape[0]
    half, quarter = width // 2, width // 4
    rows = keep_ref.shape[0]
    low, high = slice(0, half), slice(half, width)
    place, column, core = (lax.axis_index(name) for name in ("z", "x", "core"))
    for index, piece in enumerate(pieces):
        column_half, part = index // 4, index % 4
        columns = slice(half * column_half, half * (column_half + 1))
        grad[quarter * part : quarter * (part + 1), columns] = piece[...]
    diagonal = lax.broadcasted_iota(jnp.int32, (half, half), 0) == lax.broadcasted_iota(
        jnp.int32, (half, half), 1
    )

    def dot(a, b):
        return jnp.dot(a, b, preferred_element_type=F32)

    def fill(ref, start, tiles):
        upper_left, upper_right, lower_right = (tile.astype(BF16) for tile in tiles)
        ref[start : start + half, low] = upper_left
        ref[start : start + half, high] = upper_right
        ref[start + half : start + width, low] = upper_right.T
        ref[start + half : start + width, high] = lower_right

    def factor(tiles):
        upper_left, upper_right, lower_right = tiles
        five = jnp.where(diagonal, 1.25, 0.0)
        return five - 0.25 * upper_left, -0.25 * upper_right, five - 0.25 * lower_right

    def statistics(dims, upper, lower):
        tiles = [
            lax.dot_general(a, b, dims, preferred_element_type=F32)
            for a, b in ((upper, upper), (upper, lower), (lower, lower))
        ]
        tenth = jnp.where(diagonal, 0.1, 0.0)
        return tiles[0] + tenth, tiles[1], tiles[2] + tenth

    def spot(flip):
        row = (4 * place + 2 * column + (core ^ flip)) * rows
        part = row // quarter
        return ((part // 2 ^ column) * 2 + (part % 2 ^ place % 2)) * quarter + row % quarter

    line = lax.broadcasted_iota(jnp.int32, (2 * rows, width), 0)
    wanted = jnp.where(line < rows, spot(0) + line, spot(1) + line - rows)
    pick = lax.broadcasted_iota(jnp.int32, (2 * rows, width), 1) == wanted
    pick = jnp.where(pick, 1.0, 0.0).astype(BF16)
    picked = 2 * rows
    stats_left = statistics(COLS_IN_COLS, grad[low, :], grad[high, :])
    stats_right = statistics(ROWS_IN_COLS, grad[:, low], grad[:, high])
    squares = [tile * tile for tile in stats_left]
    norm = jnp.sqrt(jnp.sum(squares[0] + 2.0 * squares[1] + squares[2], keepdims=True))
    scale = 2.5 / norm
    first = jnp.sqrt(jnp.sqrt(scale)).astype(BF16).astype(F32)
    tiles = [scale * tile for tile in stats_left]
    fill(m_left, 0, tiles)
    fill(left, picked, factor(tiles))
    left[:picked, :] = (first * dot(pick, left[picked:, :])).astype(BF16)
    tiles = [scale * tile for tile in stats_right]
    fill(m_right, 0, tiles)
    tiles = [tile.astype(BF16) for tile in factor(tiles)]
    fill(right, width, tiles)
    tiles = [(first * tile.astype(F32)).astype(BF16) for tile in tiles]
    right[half:width, low] = tiles[0]
    right[half:width, high] = tiles[1]
    right[:half, low] = tiles[1].T
    right[:half, high] = tiles[2]

    def square(ref):
        by_high = dot(ref[...], ref[:, high])
        return dot(ref[low, :], ref[:, low]), by_high[low], by_high[high]

    counts_copy.wait()
    count_left, count_right = counts[core, 0], counts[core, 1]
    for index in range(1, most):
        q_left, q_right = left.at[picked:, :], right.at[width:, :]
        if index == 1:
            fill(s_left, 0, square(q_left))
            fill(s_right, 0, square(q_right))
        else:
            by_high = dot(left[...], q_left[:, high])
            by_low = dot(left[: picked + half, :], q_left[:, low])
            right_by_high = dot(right[...], q_right[:, high])
            right_by_low = dot(right[half : width + half, :], q_right[:, low])
            fill(s_left, 0, (by_low[picked:], by_high[picked : picked + half], by_high[picked + half :]))
            fill(
                s_right,
                0,
                (right_by_low[half:], right_by_high[width : width + half], right_by_high[width + half :]),
            )

            def keep_if(ref, value, goes_on):
                value = value.astype(BF16)
                return value if index == 2 else jnp.where(goes_on, value, ref)

            left[:picked, low] = keep_if(left[:picked, low], by_low[:picked], index <= count_left)
            left[:picked, high] = keep_if(left[:picked, high], by_high[:picked], index <= count_left)
            goes_on = index <= count_right
            upper_right = keep_if(right[half:width, high], right_by_high[half:width], goes_on)
            right[half:width, low] = keep_if(right[half:width, low], right_by_low[:half], goes_on)
            right[half:width, high] = upper_right
            right[:half, low] = upper_right.T
            right[:half, high] = keep_if(right[:half, high], right_by_high[:half], goes_on)
        fourths = square(s_left), square(s_right)
        fill(s_left, 0, fourths[0])
        fill(s_right, 0, fourths[1])
        for fourth, moment_ref, ref, start in (
            (s_left, m_left, left, picked),
            (s_right, m_right, right, width),
        ):
            by_high = dot(fourth[...], moment_ref[:, high])
            tiles = (dot(fourth[low, :], moment_ref[:, low]), by_high[low], by_high[high])
            if index < most - 1:
                fill(moment_ref, 0, tiles)
            fill(ref, start, factor(tiles))
    final_left = dot(left[:picked, :], left[picked:, :]).astype(BF16)
    final_left = jnp.where(most <= count_left, final_left, left[:picked, :])
    by_high = dot(right[:width, :], right[width:, high])
    by_low = dot(right[half:width, :], right[width:, low])
    goes_on = most <= count_right
    upper_right = jnp.where(goes_on, by_high[half:].astype(BF16), right[half:width, high])
    right[half:width, low] = jnp.where(goes_on, by_low.astype(BF16), right[half:width, low])
    right[half:width, high] = upper_right
    right[:half, low] = upper_right.T
    right[:half, high] = jnp.where(goes_on, by_high[:half].astype(BF16), right[:half, high])
    partial_value = dot(final_left, grad[...]).astype(BF16)
    update = dot(partial_value[:, low], right[half:width, :]) + dot(
        partial_value[:, high], right[:half, :]
    )
    keep_ref[...] = update[:rows, :].astype(BF16)
    send_ref[...] = update[rows:, :].astype(BF16)


def root(counts, pieces, rows, most=4):
    width = 4 * pieces[0].shape[0]
    square = pltpu.VMEM((width, width), BF16)
    out = jax.ShapeDtypeStruct((rows, width), BF16)
    return pl.pallas_call(
        functools.partial(root_kernel, most),
        out_shape=[out, out],
        in_specs=[HBM] + [VMEM] * 8,
        out_specs=[VMEM] * 2,
        scratch_shapes=[
            square,
            pltpu.VMEM((2 * rows + width, width), BF16),
            pltpu.VMEM((2 * width, width), BF16),
            square,
            square,
            square,
            square,
            pltpu.SMEM(counts.shape, jnp.int32),
            pltpu.SemaphoreType.DMA(()),
        ],
        compiler_params=params(40),
    )(pltpu.with_memory_space_constraint(counts, pltpu.HBM), *pieces)


def place_kernel(*refs):
    *pieces, out, sems = refs
    core, group = lax.axis_index("core"), lax.axis_index("group")
    copies = []
    for index, piece in enumerate(pieces):
        number = 2 * (group ^ (index // 2)) + (core ^ (index % 2))
        copies.append(pltpu.make_async_copy(piece, out.at[number], sems.at[index]))
        copies[-1].start()
    for copy in copies:
        copy.wait()


def place(pieces):
    rows, width = pieces[0].shape
    return pl.pallas_call(
        place_kernel,
        out_shape=jax.ShapeDtypeStruct((len(pieces), rows, width), BF16),
        in_specs=[VMEM] * len(pieces),
        out_specs=HBM,
        scratch_shapes=[pltpu.SemaphoreType.DMA((len(pieces),))],
        compiler_params=params(16),
    )(*pieces)


def shards(line, groups, patches, cotangents, newton_counts):
    blocks, pix, width = patches.shape
    half, quarter = width // 2, width // 4
    rows = half // (2 * line)
    scale = 1.0 / float(pix * 4 * line * width) ** 0.5

    def swap(array, axis, mask=1):
        return lax.ppermute(array, axis, [(i, i ^ mask) for i in range(lax.axis_size(axis))])

    def swap_diagonal(array):
        moves = [(2 * z + x, 2 * (z ^ 1) + (x ^ 1)) for z in range(line) for x in range(2)]
        return lax.ppermute(array, ("z", "x"), moves)

    given, patch, cot = load(scale, patches, cotangents)
    came = swap(given, "core")
    kept, given_on = sums(scale, patch, cot, (), (0, 1, F32), (1, 0, BF16))
    came_on = swap(given_on, "core")
    leaving = add(kept, came).astype(BF16)
    to_diagonal, to_column = leaving[quarter:], leaving[:quarter]
    from_diagonal = swap_diagonal(to_diagonal)
    from_column = swap(to_column, "x")
    (kept_on,) = sums(scale, patch, cot, (to_diagonal,), (0, 0, F32))
    own = add(kept_on, came_on)
    from_line = swap(own[quarter:].astype(BF16), "z")
    left, right, send_left, send_right = collect(own, from_diagonal, from_column, from_line)
    pieces = []
    for own, send in ((left, send_left), (right, send_right)):
        mask = 2
        while mask < line:
            own = add(own, swap(send, "z", mask))
            send = own.astype(BF16)
            mask *= 2
        pieces += [send, swap(send, "z"), swap(send, "x"), swap_diagonal(send)]
    keep, send = root(newton_counts, pieces, rows)

    pieces = []
    for turn in range(groups):
        for flip in range(2):
            moves = [
                (c * groups + g, (c ^ flip) * groups + (g ^ turn))
                for c in range(2)
                for g in range(groups)
            ]
            piece = send if flip else keep
            pieces.append(lax.ppermute(piece, ("core", "group"), moves) if turn or flip else piece)
    return place(pieces)


def solution(mesh):
    devices, groups = mesh.shape["dp"], mesh.shape["group"]
    line = devices // 4
    cut = jax.sharding.Mesh(
        mesh.devices.reshape(line, 2, 2, groups), ("z", "x", "core", "group")
    )
    dp = ("z", "x", "core")
    placed = (P("group", dp, None), P("group", dp, None), P("group", None))
    return jax.shard_map(
        functools.partial(shards, line, groups),
        mesh=cut,
        in_specs=placed,
        out_specs=P(None, dp, None),
        check_vma=False,
    )
```

```python
import functools

import jax
import jax.numpy as jnp
from jax import lax
from jax.experimental import pallas as pl
from jax.experimental.pallas import tpu as pltpu
from jax.sharding import PartitionSpec as P

F32 = jnp.float32
BF16 = jnp.bfloat16
VMEM = pl.BlockSpec(memory_space=pltpu.VMEM)
SMEM = pl.BlockSpec(memory_space=pltpu.SMEM)
HBM = pl.BlockSpec(memory_space=pltpu.HBM)
ROWS_IN_COLS = (((0,), (0,)), ((), ()))


def params(limit):
    return pltpu.CompilerParams(vmem_limit_bytes=limit << 20)


def half_sum(patch, cot, block, side, scale):
    terms = lax.dot_general(
        patch[block, side], cot[block], ROWS_IN_COLS, preferred_element_type=F32
    )
    return terms * scale


def load_kernel(scale, patch_hbm, cot_hbm, given, patch, cot, sems):
    half = patch.shape[3]
    width = half // 2
    column, core, parity = lax.axis_index("x"), lax.axis_index("core"), lax.axis_index("z") % 2
    copies = []

    def fetch(source, target):
        copies.append(pltpu.make_async_copy(source, target, sems.at[len(copies)]))
        copies[-1].start()

    def fetch_patch(block, side):
        for quarter in range(2):
            first = (core ^ side) * half + (parity ^ quarter) * width
            fetch(
                patch_hbm.at[column ^ block, :, pl.ds(pl.multiple_of(first, width), width)],
                patch.at[block, side, :, quarter * width : (quarter + 1) * width],
            )

    fetch(cot_hbm.at[column ^ 1], cot.at[1])
    fetch_patch(1, 1)
    needed = len(copies)
    fetch_patch(1, 0)
    fetch(cot_hbm.at[column], cot.at[0])
    fetch_patch(0, 1)
    fetch_patch(0, 0)
    for copy in copies[:needed]:
        copy.wait()
    given[...] = half_sum(patch, cot, 1, 1, scale).astype(BF16)
    for copy in copies[needed:]:
        copy.wait()


def load(scale, patches, cotangents):
    blocks, pix, width = patches.shape
    half = width // 2
    return pl.pallas_call(
        functools.partial(load_kernel, scale),
        out_shape=[
            jax.ShapeDtypeStruct((half, width), BF16),
            jax.ShapeDtypeStruct((blocks, 2, pix, half), BF16),
            jax.ShapeDtypeStruct((blocks, pix, width), BF16),
        ],
        in_specs=[HBM] * 2,
        out_specs=[VMEM] * 3,
        scratch_shapes=[pltpu.SemaphoreType.DMA((10,))],
        compiler_params=params(16),
    )(
        pltpu.with_memory_space_constraint(patches, pltpu.HBM),
        pltpu.with_memory_space_constraint(cotangents, pltpu.HBM),
    )


def sums_kernel(scale, wanted, patch, cot, *refs):
    for (block, side, dtype), out in zip(wanted, refs[-len(wanted) :]):
        out[...] = half_sum(patch, cot, block, side, scale).astype(dtype)


def sums(scale, patch, cot, after, *wanted):
    pix, half = patch.shape[2:]
    return pl.pallas_call(
        functools.partial(sums_kernel, scale, wanted),
        out_shape=[jax.ShapeDtypeStruct((half, 2 * half), dtype) for _, _, dtype in wanted],
        in_specs=[VMEM] * 2 + [pl.BlockSpec(memory_space=pl.ANY)] * len(after),
        out_specs=[VMEM] * len(wanted),
        compiler_params=params(16),
        cost_estimate=pl.CostEstimate(
            flops=4 * len(wanted) * pix * half * half,
            bytes_accessed=8 * pix * half,
            transcendentals=0,
        ),
    )(patch, cot, *after)


def collect_kernel(own, *refs):
    *came, keep_left, keep_right, send_left, send_right = refs
    split = keep_left.shape[1]
    for columns, keep, send in (
        (slice(0, split), keep_left, send_left),
        (slice(split, own.shape[1]), keep_right, send_right),
    ):
        total = own[: keep.shape[0], columns]
        for ref in came:
            total = total + ref[:, columns].astype(F32)
        keep[...] = total
        send[...] = total.astype(BF16)


def collect(split, own, *came):
    rows, width = came[0].shape
    shapes = [(rows, split), (rows, width - split)]
    return pl.pallas_call(
        collect_kernel,
        out_shape=[jax.ShapeDtypeStruct(shape, F32) for shape in shapes]
        + [jax.ShapeDtypeStruct(shape, BF16) for shape in shapes],
        in_specs=[VMEM] * (1 + len(came)),
        out_specs=[VMEM] * 4,
        compiler_params=params(16),
    )(own, *came)


def add(*values):
    total = values[0]
    for value in values[1:]:
        total = total + value.astype(F32)
    return total


def root_kernel(most, counts_hbm, *refs):
    pieces = refs[:6]
    keep_ref, send_ref, grad, turned, left, right, m_left, m_right, s_left, s_right, counts, sem = refs[6:]
    counts_copy = pltpu.make_async_copy(counts_hbm, counts, sem)
    counts_copy.start()
    width = grad.shape[0]
    half, quarter = width // 2, width // 4
    rows = keep_ref.shape[0]
    low, high = slice(0, half), slice(half, width)
    place, column, core = (lax.axis_index(name) for name in ("z", "x", "core"))
    column_start = 0
    for index in range(2):
        own, other, far = pieces[3 * index : 3 * index + 3]
        columns = slice(column_start, column_start + own.shape[1])
        column_start += own.shape[1]
        grad[:quarter, columns] = own[...]
        grad[quarter:half, columns] = other[...]
        grad[half:, columns] = far[...]
    turned[...] = grad[...].T
    diagonal = lax.broadcasted_iota(jnp.int32, (half, half), 0) == lax.broadcasted_iota(
        jnp.int32, (half, half), 1
    )

    def dot(a, b):
        return jnp.dot(a, b, preferred_element_type=F32)

    def fill(ref, start, tiles):
        upper_left, upper_right, lower_right = (tile.astype(BF16) for tile in tiles)
        ref[start : start + half, low] = upper_left
        ref[start : start + half, high] = upper_right
        ref[start + half : start + width, low] = upper_right.T
        ref[start + half : start + width, high] = lower_right

    def factor(tiles):
        upper_left, upper_right, lower_right = tiles
        five = jnp.where(diagonal, 1.25, 0.0)
        return five - 0.25 * upper_left, -0.25 * upper_right, five - 0.25 * lower_right

    def statistics(first, second):
        tiles = [
            dot(first[a, :], second[:, b]) for a, b in ((low, low), (low, high), (high, high))
        ]
        tenth = jnp.where(diagonal, 0.1, 0.0)
        return tiles[0] + tenth, tiles[1], tiles[2] + tenth

    def spot(flip):
        row = (4 * place + 2 * (column ^ flip) + core) * rows
        part = row // quarter
        return ((part // 2 ^ core) * 2 + (part % 2 ^ place % 2)) * quarter + row % quarter

    line = lax.broadcasted_iota(jnp.int32, (2 * rows, width), 0)
    wanted = jnp.where(line < rows, spot(0) + line, spot(1) + line - rows)
    pick = lax.broadcasted_iota(jnp.int32, (2 * rows, width), 1) == wanted
    pick = jnp.where(pick, 1.0, 0.0).astype(BF16)
    picked = 2 * rows
    stats_left = statistics(grad, turned)
    stats_right = statistics(turned, grad)
    squares = [tile * tile for tile in stats_left]
    norm = jnp.sqrt(jnp.sum(squares[0] + 2.0 * squares[1] + squares[2], keepdims=True))
    scale = 2.5 / norm
    first = jnp.sqrt(jnp.sqrt(scale)).astype(BF16).astype(F32)
    tiles = [scale * tile for tile in stats_left]
    fill(m_left, 0, tiles)
    fill(left, picked, factor(tiles))
    left[:picked, :] = (first * dot(pick, left[picked:, :])).astype(BF16)
    tiles = [scale * tile for tile in stats_right]
    fill(m_right, 0, tiles)
    tiles = [tile.astype(BF16) for tile in factor(tiles)]
    fill(right, width, tiles)
    tiles = [(first * tile.astype(F32)).astype(BF16) for tile in tiles]
    right[half:width, low] = tiles[0]
    right[half:width, high] = tiles[1]
    right[:half, low] = tiles[1].T
    right[:half, high] = tiles[2]

    def square(ref):
        by_high = dot(ref[...], ref[:, high])
        return dot(ref[low, :], ref[:, low]), by_high[low], by_high[high]

    counts_copy.wait()
    count_left, count_right = counts[column, 0], counts[column, 1]
    for index in range(1, most):
        q_left, q_right = left.at[picked:, :], right.at[width:, :]
        if index == 1:
            fill(s_left, 0, square(q_left))
            fill(s_right, 0, square(q_right))
        else:
            by_high = dot(left[...], q_left[:, high])
            by_low = dot(left[: picked + half, :], q_left[:, low])
            right_by_high = dot(right[...], q_right[:, high])
            right_by_low = dot(right[half : width + half, :], q_right[:, low])
            fill(s_left, 0, (by_low[picked:], by_high[picked : picked + half], by_high[picked + half :]))
            fill(
                s_right,
                0,
                (right_by_low[half:], right_by_high[width : width + half], right_by_high[width + half :]),
            )

            def keep_if(ref, value, goes_on):
                value = value.astype(BF16)
                return value if index == 2 else jnp.where(goes_on, value, ref)

            left[:picked, low] = keep_if(left[:picked, low], by_low[:picked], index <= count_left)
            left[:picked, high] = keep_if(left[:picked, high], by_high[:picked], index <= count_left)
            goes_on = index <= count_right
            upper_right = keep_if(right[half:width, high], right_by_high[half:width], goes_on)
            right[half:width, low] = keep_if(right[half:width, low], right_by_low[:half], goes_on)
            right[half:width, high] = upper_right
            right[:half, low] = upper_right.T
            right[:half, high] = keep_if(right[:half, high], right_by_high[:half], goes_on)
        fourths = square(s_left), square(s_right)
        fill(s_left, 0, fourths[0])
        fill(s_right, 0, fourths[1])
        for fourth, moment_ref, ref, start in (
            (s_left, m_left, left, picked),
            (s_right, m_right, right, width),
        ):
            by_high = dot(fourth[...], moment_ref[:, high])
            tiles = (dot(fourth[low, :], moment_ref[:, low]), by_high[low], by_high[high])
            if index < most - 1:
                fill(moment_ref, 0, tiles)
            fill(ref, start, factor(tiles))
    final_left = dot(left[:picked, :], left[picked:, :]).astype(BF16)
    final_left = jnp.where(most <= count_left, final_left, left[:picked, :])
    by_high = dot(right[:width, :], right[width:, high])
    by_low = dot(right[half:width, :], right[width:, low])
    goes_on = most <= count_right
    upper_right = jnp.where(goes_on, by_high[half:].astype(BF16), right[half:width, high])
    right[half:width, low] = jnp.where(goes_on, by_low.astype(BF16), right[half:width, low])
    right[half:width, high] = upper_right
    right[:half, low] = upper_right.T
    right[:half, high] = jnp.where(goes_on, by_high[:half].astype(BF16), right[:half, high])
    partial_value = dot(final_left, grad[...]).astype(BF16)
    update = dot(partial_value[:, low], right[half:width, :]) + dot(
        partial_value[:, high], right[:half, :]
    )
    keep_ref[...] = update[:rows, :].astype(BF16)
    send_ref[...] = update[rows:, :].astype(BF16)


def root(counts, pieces, rows, most=4):
    width = 4 * pieces[0].shape[0]
    square = pltpu.VMEM((width, width), BF16)
    out = jax.ShapeDtypeStruct((rows, width), BF16)
    return pl.pallas_call(
        functools.partial(root_kernel, most),
        out_shape=[out, out],
        in_specs=[HBM] + [VMEM] * 6,
        out_specs=[VMEM] * 2,
        scratch_shapes=[
            square,
            square,
            pltpu.VMEM((2 * rows + width, width), BF16),
            pltpu.VMEM((2 * width, width), BF16),
            square,
            square,
            square,
            square,
            pltpu.SMEM(counts.shape, jnp.int32),
            pltpu.SemaphoreType.DMA(()),
        ],
        compiler_params=params(40),
    )(pltpu.with_memory_space_constraint(counts, pltpu.HBM), *pieces)


def place_kernel(*refs):
    *pieces, out, sems = refs
    column, group = lax.axis_index("x"), lax.axis_index("group")
    copies = []
    for index, piece in enumerate(pieces):
        number = 2 * (group ^ (index // 2)) + (column ^ (index % 2))
        copies.append(pltpu.make_async_copy(piece, out.at[number], sems.at[index]))
        copies[-1].start()
    for copy in copies:
        copy.wait()


def place(pieces):
    rows, width = pieces[0].shape
    return pl.pallas_call(
        place_kernel,
        out_shape=jax.ShapeDtypeStruct((len(pieces), rows, width), BF16),
        in_specs=[VMEM] * len(pieces),
        out_specs=HBM,
        scratch_shapes=[pltpu.SemaphoreType.DMA((len(pieces),))],
        compiler_params=params(16),
    )(*pieces)


def shards(line, groups, patches, cotangents, newton_counts):
    blocks, pix, width = patches.shape
    half, quarter = width // 2, width // 4
    rows = half // (2 * line)
    scale = 1.0 / float(pix * 4 * line * width) ** 0.5

    def swap(array, axis, mask=1):
        return lax.ppermute(array, axis, [(i, i ^ mask) for i in range(lax.axis_size(axis))])

    def swap_diagonal(array):
        moves = [(2 * z + x, 2 * (z ^ 1) + (x ^ 1)) for z in range(line) for x in range(2)]
        return lax.ppermute(array, ("z", "x"), moves)

    given, patch, cot = load(scale, patches, cotangents)
    came = swap(given, "core")
    kept, given_on = sums(scale, patch, cot, (), (1, 0, F32), (0, 1, BF16))
    came_on = swap(given_on, "core")
    leaving = add(kept, came).astype(BF16)
    to_diagonal, to_column = leaving[quarter:], leaving[:quarter]
    from_diagonal = swap_diagonal(to_diagonal)
    from_column = swap(to_column, "x")
    (kept_on,) = sums(scale, patch, cot, (to_diagonal,), (0, 0, F32))
    own = add(kept_on, came_on)
    from_line = swap(own[quarter:].astype(BF16), "z")
    left, right, send_left, send_right = collect(
        width * 3 // 4, own, from_diagonal, from_column, from_line
    )
    pieces = []
    for own, send in ((left, send_left), (right, send_right)):
        mask = 2
        while mask < line:
            own = add(own, swap(send, "z", mask))
            send = own.astype(BF16)
            mask *= 2
        own = send
        other = swap(own, "z")
        pieces += [own, other, swap(jnp.concatenate([own, other], 0), "core")]
    keep, send = root(newton_counts, pieces, rows)

    pieces = []
    for turn in range(groups):
        for flip in range(2):
            moves = [
                (c * groups + g, (c ^ flip) * groups + (g ^ turn))
                for c in range(2)
                for g in range(groups)
            ]
            piece = send if flip else keep
            pieces.append(lax.ppermute(piece, ("x", "group"), moves) if turn or flip else piece)
    return place(pieces)


def solution(mesh):
    devices, groups = mesh.shape["dp"], mesh.shape["group"]
    line = devices // 4
    cut = jax.sharding.Mesh(
        mesh.devices.reshape(line, 2, 2, groups), ("z", "x", "core", "group")
    )
    dp = ("z", "x", "core")
    placed = (P("group", dp, None), P("group", dp, None), P("group", None))
    return jax.shard_map(
        functools.partial(shards, line, groups),
        mesh=cut,
        in_specs=placed,
        out_specs=P(None, dp, None),
        check_vma=False,
    )
```

```python
import functools

import jax
import jax.numpy as jnp
from jax import lax
from jax.experimental import pallas as pl
from jax.experimental.pallas import tpu as pltpu
from jax.sharding import PartitionSpec as P

F32 = jnp.float32
BF16 = jnp.bfloat16
VMEM = pl.BlockSpec(memory_space=pltpu.VMEM)
SMEM = pl.BlockSpec(memory_space=pltpu.SMEM)
HBM = pl.BlockSpec(memory_space=pltpu.HBM)
ROWS_IN_COLS = (((0,), (0,)), ((), ()))


def params(limit):
    return pltpu.CompilerParams(vmem_limit_bytes=limit << 20)


def half_sum(patch, cot, block, side, scale):
    terms = lax.dot_general(
        patch[block, side], cot[block], ROWS_IN_COLS, preferred_element_type=F32
    )
    return terms * scale


def load_kernel(scale, patch_hbm, cot_hbm, given, patch, cot, sems):
    half = patch.shape[3]
    width = half // 2
    column, core, parity = lax.axis_index("x"), lax.axis_index("core"), lax.axis_index("z") % 2
    copies = []

    def fetch(source, target):
        copies.append(pltpu.make_async_copy(source, target, sems.at[len(copies)]))
        copies[-1].start()

    def fetch_patch(block, side):
        for quarter in range(2):
            first = (core ^ side) * half + (parity ^ quarter) * width
            fetch(
                patch_hbm.at[column ^ block, :, pl.ds(pl.multiple_of(first, width), width)],
                patch.at[block, side, :, quarter * width : (quarter + 1) * width],
            )

    fetch(cot_hbm.at[column ^ 1], cot.at[1])
    fetch_patch(1, 1)
    needed = len(copies)
    fetch_patch(1, 0)
    fetch(cot_hbm.at[column], cot.at[0])
    fetch_patch(0, 1)
    fetch_patch(0, 0)
    for copy in copies[:needed]:
        copy.wait()
    given[...] = half_sum(patch, cot, 1, 1, scale).astype(BF16)
    for copy in copies[needed:]:
        copy.wait()


def load(scale, patches, cotangents):
    blocks, pix, width = patches.shape
    half = width // 2
    return pl.pallas_call(
        functools.partial(load_kernel, scale),
        out_shape=[
            jax.ShapeDtypeStruct((half, width), BF16),
            jax.ShapeDtypeStruct((blocks, 2, pix, half), BF16),
            jax.ShapeDtypeStruct((blocks, pix, width), BF16),
        ],
        in_specs=[HBM] * 2,
        out_specs=[VMEM] * 3,
        scratch_shapes=[pltpu.SemaphoreType.DMA((10,))],
        compiler_params=params(16),
    )(
        pltpu.with_memory_space_constraint(patches, pltpu.HBM),
        pltpu.with_memory_space_constraint(cotangents, pltpu.HBM),
    )


def sums_kernel(scale, wanted, patch, cot, *refs):
    for (block, side, dtype), out in zip(wanted, refs[-len(wanted) :]):
        out[...] = half_sum(patch, cot, block, side, scale).astype(dtype)


def sums(scale, patch, cot, after, *wanted):
    pix, half = patch.shape[2:]
    return pl.pallas_call(
        functools.partial(sums_kernel, scale, wanted),
        out_shape=[jax.ShapeDtypeStruct((half, 2 * half), dtype) for _, _, dtype in wanted],
        in_specs=[VMEM] * 2 + [pl.BlockSpec(memory_space=pl.ANY)] * len(after),
        out_specs=[VMEM] * len(wanted),
        compiler_params=params(16),
        cost_estimate=pl.CostEstimate(
            flops=4 * len(wanted) * pix * half * half,
            bytes_accessed=8 * pix * half,
            transcendentals=0,
        ),
    )(patch, cot, *after)


def collect_kernel(own, *refs):
    *came, keep_left, keep_right, send_left, send_right = refs
    split = keep_left.shape[1]
    for columns, keep, send in (
        (slice(0, split), keep_left, send_left),
        (slice(split, own.shape[1]), keep_right, send_right),
    ):
        total = own[: keep.shape[0], columns]
        for ref in came:
            total = total + ref[:, columns].astype(F32)
        keep[...] = total
        send[...] = total.astype(BF16)


def collect(split, own, *came):
    rows, width = came[0].shape
    shapes = [(rows, split), (rows, width - split)]
    return pl.pallas_call(
        collect_kernel,
        out_shape=[jax.ShapeDtypeStruct(shape, F32) for shape in shapes]
        + [jax.ShapeDtypeStruct(shape, BF16) for shape in shapes],
        in_specs=[VMEM] * (1 + len(came)),
        out_specs=[VMEM] * 4,
        compiler_params=params(16),
    )(own, *came)


def add(*values):
    total = values[0]
    for value in values[1:]:
        total = total + value.astype(F32)
    return total


def root_kernel(most, counts_hbm, *refs):
    pieces = refs[:6]
    keep_ref, send_ref, grad, turned, left, right, m_left, m_right, s_left, s_right, counts, sem = refs[6:]
    counts_copy = pltpu.make_async_copy(counts_hbm, counts, sem)
    counts_copy.start()
    width = grad.shape[0]
    half, quarter = width // 2, width // 4
    rows = keep_ref.shape[0]
    low, high = slice(0, half), slice(half, width)
    place, column, core = (lax.axis_index(name) for name in ("z", "x", "core"))
    column_start = 0
    for index in range(2):
        own, other, far = pieces[3 * index : 3 * index + 3]
        columns = slice(column_start, column_start + own.shape[1])
        column_start += own.shape[1]
        grad[:quarter, columns] = own[...]
        grad[quarter:half, columns] = other[...]
        grad[half:, columns] = far[...]
    turned[...] = grad[...].T
    diagonal = lax.broadcasted_iota(jnp.int32, (half, half), 0) == lax.broadcasted_iota(
        jnp.int32, (half, half), 1
    )

    def dot(a, b):
        return jnp.dot(a, b, preferred_element_type=F32)

    def fill(ref, start, tiles):
        upper_left, upper_right, lower_right = (tile.astype(BF16) for tile in tiles)
        ref[start : start + half, low] = upper_left
        ref[start : start + half, high] = upper_right
        ref[start + half : start + width, low] = upper_right.T
        ref[start + half : start + width, high] = lower_right

    def factor(tiles):
        upper_left, upper_right, lower_right = tiles
        five = jnp.where(diagonal, 1.25, 0.0)
        return five - 0.25 * upper_left, -0.25 * upper_right, five - 0.25 * lower_right

    def statistics(first, second):
        tiles = [
            dot(first[a, :], second[:, b]) for a, b in ((low, low), (low, high), (high, high))
        ]
        tenth = jnp.where(diagonal, 0.1, 0.0)
        return tiles[0] + tenth, tiles[1], tiles[2] + tenth

    def spot(flip):
        row = (4 * place + 2 * (column ^ flip) + core) * rows
        part = row // quarter
        return ((part // 2 ^ core) * 2 + (part % 2 ^ place % 2)) * quarter + row % quarter

    line = lax.broadcasted_iota(jnp.int32, (2 * rows, width), 0)
    wanted = jnp.where(line < rows, spot(0) + line, spot(1) + line - rows)
    pick = lax.broadcasted_iota(jnp.int32, (2 * rows, width), 1) == wanted
    pick = jnp.where(pick, 1.0, 0.0).astype(BF16)
    picked = 2 * rows
    counts_copy.wait()
    count_left, count_right = counts[column, 0], counts[column, 1]

    def by_tiles(first, second):
        by_high = dot(first[...], second[:, high])
        return dot(first[low, :], second[:, low]), by_high[low], by_high[high]

    def keep_if(old, value, goes_on):
        return jnp.where(goes_on, value.astype(BF16), old)

    def steps(stats, shared, stacked, second, moment_ref, start, first_x, next_x):
        tiles = statistics(*stats)
        yield
        if not shared:
            squares = [tile * tile for tile in tiles]
            total = jnp.sum(squares[0] + 2.0 * squares[1] + squares[2], keepdims=True)
            scale = 2.5 / jnp.sqrt(total)
            shared += [scale, jnp.sqrt(jnp.sqrt(scale)).astype(BF16).astype(F32)]
        scale, first = shared
        tiles = [scale * tile for tile in tiles]
        fill(moment_ref, 0, tiles)
        tiles = [tile.astype(BF16) for tile in factor(tiles)]
        fill(stacked, start, tiles)
        factor_ref = stacked.at[start : start + width, :]
        tiles_x = first_x(first, tiles, factor_ref)
        products = by_tiles(factor_ref, factor_ref)
        yield
        tiles_x()
        for index in range(1, most):
            if index > 1:
                products = next_x(products, index)
            fill(second, 0, products)
            products = by_tiles(second, second)
            yield
            fill(second, 0, products)
            products = by_tiles(second, moment_ref)
            yield
            if index < most - 1:
                fill(moment_ref, 0, products)
            fill(stacked, start, factor(products))
            if index < most - 1:
                products = dot(stacked[...], factor_ref[:, high]), dot(
                    stacked[max(start - half, 0) : start + half, :], factor_ref[:, low]
                )
                yield

    def first_left(first, tiles, factor_ref):
        product = first * dot(pick, factor_ref[...])

        def store():
            left[:picked, :] = product.astype(BF16)

        return store

    def next_left(products, index):
        by_high, by_low = products
        goes_on = index <= count_left
        left[:picked, low] = keep_if(left[:picked, low], by_low[:picked], goes_on)
        left[:picked, high] = keep_if(left[:picked, high], by_high[:picked], goes_on)
        return by_low[picked:], by_high[picked : picked + half], by_high[picked + half :]

    def first_right(first, tiles, factor_ref):
        def store():
            values = [(first * tile.astype(F32)).astype(BF16) for tile in tiles]
            right[half:width, low] = values[0]
            right[half:width, high] = values[1]
            right[:half, low] = values[1].T
            right[:half, high] = values[2]

        return store

    def keep_right(by_low, by_high, goes_on):
        upper_right = keep_if(right[half:width, high], by_high[half:width], goes_on)
        right[half:width, low] = keep_if(right[half:width, low], by_low[:half], goes_on)
        right[half:width, high] = upper_right
        right[:half, low] = upper_right.T
        right[:half, high] = keep_if(right[:half, high], by_high[:half], goes_on)

    def next_right(products, index):
        by_high, by_low = products
        keep_right(by_low, by_high, index <= count_right)
        return by_low[half:], by_high[width : width + half], by_high[width + half :]

    def left_steps(shared):
        yield from steps((grad, turned), shared, left, s_left, m_left, picked, first_left, next_left)
        product = dot(left[:picked, :], left[picked:, :])
        yield
        left[:picked, :] = keep_if(left[:picked, :], product, most <= count_left)
        product = dot(left[:picked, :], grad[...])
        yield
        left[:picked, :] = product.astype(BF16)

    def right_steps(shared):
        yield from steps(
            (turned, grad), shared, right, s_right, m_right, width, first_right, next_right
        )
        by_high = dot(right[:width, :], right[width:, high])
        by_low = dot(right[half:width, :], right[width:, low])
        yield
        keep_right(by_low, by_high, most <= count_right)

    shared = []
    sides = [left_steps(shared), right_steps(shared)]
    while sides:
        sides = [side for side in sides if next(side, True) is None]
    partial_value = left[:picked, :]
    update = dot(partial_value[:, low], right[half:width, :]) + dot(
        partial_value[:, high], right[:half, :]
    )
    keep_ref[...] = update[:rows, :].astype(BF16)
    send_ref[...] = update[rows:, :].astype(BF16)


def root(counts, pieces, rows, most=4):
    width = 4 * pieces[0].shape[0]
    square = pltpu.VMEM((width, width), BF16)
    out = jax.ShapeDtypeStruct((rows, width), BF16)
    return pl.pallas_call(
        functools.partial(root_kernel, most),
        out_shape=[out, out],
        in_specs=[HBM] + [VMEM] * 6,
        out_specs=[VMEM] * 2,
        scratch_shapes=[
            square,
            square,
            pltpu.VMEM((2 * rows + width, width), BF16),
            pltpu.VMEM((2 * width, width), BF16),
            square,
            square,
            square,
            square,
            pltpu.SMEM(counts.shape, jnp.int32),
            pltpu.SemaphoreType.DMA(()),
        ],
        compiler_params=params(40),
    )(pltpu.with_memory_space_constraint(counts, pltpu.HBM), *pieces)


def place_kernel(*refs):
    *pieces, out, sems = refs
    column, group = lax.axis_index("x"), lax.axis_index("group")
    copies = []
    for index, piece in enumerate(pieces):
        number = 2 * (group ^ (index // 2)) + (column ^ (index % 2))
        copies.append(pltpu.make_async_copy(piece, out.at[number], sems.at[index]))
        copies[-1].start()
    for copy in copies:
        copy.wait()


def place(pieces):
    rows, width = pieces[0].shape
    return pl.pallas_call(
        place_kernel,
        out_shape=jax.ShapeDtypeStruct((len(pieces), rows, width), BF16),
        in_specs=[VMEM] * len(pieces),
        out_specs=HBM,
        scratch_shapes=[pltpu.SemaphoreType.DMA((len(pieces),))],
        compiler_params=params(16),
    )(*pieces)


def shards(line, groups, patches, cotangents, newton_counts):
    blocks, pix, width = patches.shape
    half, quarter = width // 2, width // 4
    rows = half // (2 * line)
    scale = 1.0 / float(pix * 4 * line * width) ** 0.5

    def swap(array, axis, mask=1):
        return lax.ppermute(array, axis, [(i, i ^ mask) for i in range(lax.axis_size(axis))])

    def swap_diagonal(array):
        moves = [(2 * z + x, 2 * (z ^ 1) + (x ^ 1)) for z in range(line) for x in range(2)]
        return lax.ppermute(array, ("z", "x"), moves)

    given, patch, cot = load(scale, patches, cotangents)
    came = swap(given, "core")
    kept, given_on = sums(scale, patch, cot, (), (1, 0, F32), (0, 1, BF16))
    came_on = swap(given_on, "core")
    leaving = add(kept, came).astype(BF16)
    to_diagonal, to_column = leaving[quarter:], leaving[:quarter]
    from_diagonal = swap_diagonal(to_diagonal)
    from_column = swap(to_column, "x")
    (kept_on,) = sums(scale, patch, cot, (to_diagonal,), (0, 0, F32))
    own = add(kept_on, came_on)
    from_line = swap(own[quarter:].astype(BF16), "z")
    left, right, send_left, send_right = collect(
        width * 3 // 4, own, from_diagonal, from_column, from_line
    )
    pieces = []
    for own, send in ((left, send_left), (right, send_right)):
        mask = 2
        while mask < line:
            own = add(own, swap(send, "z", mask))
            send = own.astype(BF16)
            mask *= 2
        own = send
        other = swap(own, "z")
        pieces += [own, other, swap(jnp.concatenate([own, other], 0), "core")]
    keep, send = root(newton_counts, pieces, rows)

    pieces = []
    for turn in range(groups):
        for flip in range(2):
            moves = [
                (c * groups + g, (c ^ flip) * groups + (g ^ turn))
                for c in range(2)
                for g in range(groups)
            ]
            piece = send if flip else keep
            pieces.append(lax.ppermute(piece, ("x", "group"), moves) if turn or flip else piece)
    return place(pieces)


def solution(mesh):
    devices, groups = mesh.shape["dp"], mesh.shape["group"]
    line = devices // 4
    cut = jax.sharding.Mesh(
        mesh.devices.reshape(line, 2, 2, groups), ("z", "x", "core", "group")
    )
    dp = ("z", "x", "core")
    placed = (P("group", dp, None), P("group", dp, None), P("group", None))
    return jax.shard_map(
        functools.partial(shards, line, groups),
        mesh=cut,
        in_specs=placed,
        out_specs=P(None, dp, None),
        check_vma=False,
    )
```

```python
import functools

import jax
import jax.numpy as jnp
from jax import lax
from jax.experimental import pallas as pl
from jax.experimental.pallas import tpu as pltpu
from jax.sharding import PartitionSpec as P

F32 = jnp.float32
BF16 = jnp.bfloat16
VMEM = pl.BlockSpec(memory_space=pltpu.VMEM)
SMEM = pl.BlockSpec(memory_space=pltpu.SMEM)
HBM = pl.BlockSpec(memory_space=pltpu.HBM)
ROWS_IN_COLS = (((0,), (0,)), ((), ()))


def params(limit):
    return pltpu.CompilerParams(vmem_limit_bytes=limit << 20)


def half_sum(patch, cot, block, side, scale):
    terms = lax.dot_general(
        patch[block, side], cot[block], ROWS_IN_COLS, preferred_element_type=F32
    )
    return terms * scale


def load_kernel(scale, patch_hbm, cot_hbm, given, patch, cot, sems):
    half = patch.shape[3]
    width = half // 2
    column, core, parity = lax.axis_index("x"), lax.axis_index("core"), lax.axis_index("z") % 2
    copies = []

    def fetch(source, target):
        copies.append(pltpu.make_async_copy(source, target, sems.at[len(copies)]))
        copies[-1].start()

    def fetch_patch(block, side):
        for quarter in range(2):
            first = (core ^ side) * half + (parity ^ quarter) * width
            fetch(
                patch_hbm.at[column ^ block, :, pl.ds(pl.multiple_of(first, width), width)],
                patch.at[block, side, :, quarter * width : (quarter + 1) * width],
            )

    fetch(cot_hbm.at[column ^ 1], cot.at[1])
    fetch_patch(1, 1)
    needed = len(copies)
    fetch_patch(1, 0)
    fetch(cot_hbm.at[column], cot.at[0])
    fetch_patch(0, 1)
    fetch_patch(0, 0)
    for copy in copies[:needed]:
        copy.wait()
    given[...] = half_sum(patch, cot, 1, 1, scale).astype(BF16)
    for copy in copies[needed:]:
        copy.wait()


def load(scale, patches, cotangents):
    blocks, pix, width = patches.shape
    half = width // 2
    return pl.pallas_call(
        functools.partial(load_kernel, scale),
        out_shape=[
            jax.ShapeDtypeStruct((half, width), BF16),
            jax.ShapeDtypeStruct((blocks, 2, pix, half), BF16),
            jax.ShapeDtypeStruct((blocks, pix, width), BF16),
        ],
        in_specs=[HBM] * 2,
        out_specs=[VMEM] * 3,
        scratch_shapes=[pltpu.SemaphoreType.DMA((10,))],
        compiler_params=params(16),
    )(
        pltpu.with_memory_space_constraint(patches, pltpu.HBM),
        pltpu.with_memory_space_constraint(cotangents, pltpu.HBM),
    )


def sums_kernel(scale, wanted, patch, cot, *refs):
    for (block, side, dtype), out in zip(wanted, refs[-len(wanted) :]):
        out[...] = half_sum(patch, cot, block, side, scale).astype(dtype)


def sums(scale, patch, cot, after, *wanted):
    pix, half = patch.shape[2:]
    return pl.pallas_call(
        functools.partial(sums_kernel, scale, wanted),
        out_shape=[jax.ShapeDtypeStruct((half, 2 * half), dtype) for _, _, dtype in wanted],
        in_specs=[VMEM] * 2 + [pl.BlockSpec(memory_space=pl.ANY)] * len(after),
        out_specs=[VMEM] * len(wanted),
        compiler_params=params(16),
        cost_estimate=pl.CostEstimate(
            flops=4 * len(wanted) * pix * half * half,
            bytes_accessed=8 * pix * half,
            transcendentals=0,
        ),
    )(patch, cot, *after)


def collect_kernel(own, *refs):
    *came, keep_left, keep_right, send_left, send_right = refs
    split = keep_left.shape[1]
    for columns, keep, send in (
        (slice(0, split), keep_left, send_left),
        (slice(split, own.shape[1]), keep_right, send_right),
    ):
        total = own[: keep.shape[0], columns]
        for ref in came:
            total = total + ref[:, columns].astype(F32)
        keep[...] = total
        send[...] = total.astype(BF16)


def collect(split, own, *came):
    rows, width = came[0].shape
    shapes = [(rows, split), (rows, width - split)]
    return pl.pallas_call(
        collect_kernel,
        out_shape=[jax.ShapeDtypeStruct(shape, F32) for shape in shapes]
        + [jax.ShapeDtypeStruct(shape, BF16) for shape in shapes],
        in_specs=[VMEM] * (1 + len(came)),
        out_specs=[VMEM] * 4,
        compiler_params=params(16),
    )(own, *came)


def add(*values):
    total = values[0]
    for value in values[1:]:
        total = total + value.astype(F32)
    return total


def near_kernel(left_own, left_other, right_own, right_other, near, turned, *tiles):
    quarter, split = left_own.shape
    for first, columns in ((left_own, slice(0, split)), (right_own, slice(split, None))):
        near[:quarter, columns] = first[...]
    for second, columns in ((left_other, slice(0, split)), (right_other, slice(split, None))):
        near[quarter:, columns] = second[...]
    turned[...] = near[...].T
    *inner, outer = tiles
    half = near.shape[0]
    low, high = slice(0, half), slice(half, 2 * half)
    for (a, b), tile in zip(((low, low), (low, high), (high, high)), inner):
        tile[...] = jnp.dot(turned[a, :], near[:, b], preferred_element_type=F32)
    outer[...] = jnp.dot(near[...], turned[...], preferred_element_type=F32)


def near_part(*pieces):
    half = 2 * pieces[0].shape[0]
    tile = jax.ShapeDtypeStruct((half, half), F32)
    return pl.pallas_call(
        near_kernel,
        out_shape=[
            jax.ShapeDtypeStruct((half, 2 * half), BF16),
            jax.ShapeDtypeStruct((2 * half, half), BF16),
        ]
        + [tile] * 4,
        in_specs=[VMEM] * 4,
        out_specs=[VMEM] * 6,
        compiler_params=params(16),
        cost_estimate=pl.CostEstimate(
            flops=10 * half**3, bytes_accessed=16 * half**2, transcendentals=0
        ),
    )(*pieces)


def root_kernel(most, counts_hbm, *refs):
    near, near_turned, *near_tiles, near_outer, left_far, right_far, keep_ref, send_ref = refs[:10]
    far, far_turned, left, right, m_left, m_right, s_left, s_right, counts, sem = refs[10:]
    counts_copy = pltpu.make_async_copy(counts_hbm, counts, sem)
    counts_copy.start()
    width = far.shape[1]
    half = width // 2
    rows = keep_ref.shape[0]
    low, high = slice(0, half), slice(half, width)
    place, column, core = (lax.axis_index(name) for name in ("z", "x", "core"))
    split = left_far.shape[1]
    far[:, :split] = left_far[...]
    far[:, split:] = right_far[...]
    far_turned[...] = far[...].T
    diagonal = lax.broadcasted_iota(jnp.int32, (half, half), 0) == lax.broadcasted_iota(
        jnp.int32, (half, half), 1
    )

    def dot(a, b):
        return jnp.dot(a, b, preferred_element_type=F32)

    def fill(ref, start, tiles):
        upper_left, upper_right, lower_right = (tile.astype(BF16) for tile in tiles)
        ref[start : start + half, low] = upper_left
        ref[start : start + half, high] = upper_right
        ref[start + half : start + width, low] = upper_right.T
        ref[start + half : start + width, high] = lower_right

    def factor(tiles):
        upper_left, upper_right, lower_right = tiles
        five = jnp.where(diagonal, 1.25, 0.0)
        return five - 0.25 * upper_left, -0.25 * upper_right, five - 0.25 * lower_right

    def damped(tiles):
        tenth = jnp.where(diagonal, 0.1, 0.0)
        return tiles[0] + tenth, tiles[1], tiles[2] + tenth

    def spot(flip):
        row = (4 * place + 2 * (column ^ flip) + core) * rows
        part = row // (half // 2)
        start = ((part // 2 ^ core) * 2 + (part % 2 ^ place % 2)) * (half // 2)
        return start + row % (half // 2)

    line = lax.broadcasted_iota(jnp.int32, (2 * rows, width), 0)
    wanted = jnp.where(line < rows, spot(0) + line, spot(1) + line - rows)
    pick = lax.broadcasted_iota(jnp.int32, (2 * rows, width), 1) == wanted
    pick = jnp.where(pick, 1.0, 0.0).astype(BF16)
    picked = 2 * rows
    stats_left = damped(
        (near_outer[...], dot(near[...], far_turned[...]), dot(far[...], far_turned[...]))
    )
    stats_right = damped(
        [
            tile[...] + dot(far_turned[a, :], far[:, b])
            for (a, b), tile in zip(((low, low), (low, high), (high, high)), near_tiles)
        ]
    )
    squares = [tile * tile for tile in stats_left]
    norm = jnp.sqrt(jnp.sum(squares[0] + 2.0 * squares[1] + squares[2], keepdims=True))
    scale = 2.5 / norm
    first = jnp.sqrt(jnp.sqrt(scale)).astype(BF16).astype(F32)
    tiles = [scale * tile for tile in stats_left]
    fill(m_left, 0, tiles)
    fill(left, picked, factor(tiles))
    left[:picked, :] = (first * dot(pick, left[picked:, :])).astype(BF16)
    tiles = [scale * tile for tile in stats_right]
    fill(m_right, 0, tiles)
    tiles = [tile.astype(BF16) for tile in factor(tiles)]
    fill(right, width, tiles)
    tiles = [(first * tile.astype(F32)).astype(BF16) for tile in tiles]
    right[half:width, low] = tiles[0]
    right[half:width, high] = tiles[1]
    right[:half, low] = tiles[1].T
    right[:half, high] = tiles[2]

    def square(ref):
        by_high = dot(ref[...], ref[:, high])
        return dot(ref[low, :], ref[:, low]), by_high[low], by_high[high]

    counts_copy.wait()
    count_left, count_right = counts[column, 0], counts[column, 1]
    for index in range(1, most):
        q_left, q_right = left.at[picked:, :], right.at[width:, :]
        if index == 1:
            fill(s_left, 0, square(q_left))
            fill(s_right, 0, square(q_right))
        else:
            by_high = dot(left[...], q_left[:, high])
            by_low = dot(left[: picked + half, :], q_left[:, low])
            right_by_high = dot(right[...], q_right[:, high])
            right_by_low = dot(right[half : width + half, :], q_right[:, low])
            fill(s_left, 0, (by_low[picked:], by_high[picked : picked + half], by_high[picked + half :]))
            fill(
                s_right,
                0,
                (right_by_low[half:], right_by_high[width : width + half], right_by_high[width + half :]),
            )

            def keep_if(ref, value, goes_on):
                value = value.astype(BF16)
                return value if index == 2 else jnp.where(goes_on, value, ref)

            left[:picked, low] = keep_if(left[:picked, low], by_low[:picked], index <= count_left)
            left[:picked, high] = keep_if(left[:picked, high], by_high[:picked], index <= count_left)
            goes_on = index <= count_right
            upper_right = keep_if(right[half:width, high], right_by_high[half:width], goes_on)
            right[half:width, low] = keep_if(right[half:width, low], right_by_low[:half], goes_on)
            right[half:width, high] = upper_right
            right[:half, low] = upper_right.T
            right[:half, high] = keep_if(right[:half, high], right_by_high[:half], goes_on)
        fourths = square(s_left), square(s_right)
        fill(s_left, 0, fourths[0])
        fill(s_right, 0, fourths[1])
        for fourth, moment_ref, ref, start in (
            (s_left, m_left, left, picked),
            (s_right, m_right, right, width),
        ):
            by_high = dot(fourth[...], moment_ref[:, high])
            tiles = (dot(fourth[low, :], moment_ref[:, low]), by_high[low], by_high[high])
            if index < most - 1:
                fill(moment_ref, 0, tiles)
            fill(ref, start, factor(tiles))
    final_left = dot(left[:picked, :], left[picked:, :]).astype(BF16)
    final_left = jnp.where(most <= count_left, final_left, left[:picked, :])
    by_high = dot(right[:width, :], right[width:, high])
    by_low = dot(right[half:width, :], right[width:, low])
    goes_on = most <= count_right
    upper_right = jnp.where(goes_on, by_high[half:].astype(BF16), right[half:width, high])
    right[half:width, low] = jnp.where(goes_on, by_low.astype(BF16), right[half:width, low])
    right[half:width, high] = upper_right
    right[:half, low] = upper_right.T
    right[:half, high] = jnp.where(goes_on, by_high[:half].astype(BF16), right[:half, high])
    partial_value = dot(final_left[:, low], near[...]) + dot(final_left[:, high], far[...])
    partial_value = partial_value.astype(BF16)
    update = dot(partial_value[:, low], right[half:width, :]) + dot(
        partial_value[:, high], right[:half, :]
    )
    keep_ref[...] = update[:rows, :].astype(BF16)
    send_ref[...] = update[rows:, :].astype(BF16)


def root(counts, early, fars, rows, most=4):
    width = early[0].shape[1]
    square = pltpu.VMEM((width, width), BF16)
    out = jax.ShapeDtypeStruct((rows, width), BF16)
    return pl.pallas_call(
        functools.partial(root_kernel, most),
        out_shape=[out, out],
        in_specs=[HBM] + [VMEM] * 8,
        out_specs=[VMEM] * 2,
        scratch_shapes=[
            pltpu.VMEM((width // 2, width), BF16),
            pltpu.VMEM((width, width // 2), BF16),
            pltpu.VMEM((2 * rows + width, width), BF16),
            pltpu.VMEM((2 * width, width), BF16),
            square,
            square,
            square,
            square,
            pltpu.SMEM(counts.shape, jnp.int32),
            pltpu.SemaphoreType.DMA(()),
        ],
        compiler_params=params(40),
    )(pltpu.with_memory_space_constraint(counts, pltpu.HBM), *early, *fars)


def place_kernel(*refs):
    *pieces, out, sems = refs
    column, group = lax.axis_index("x"), lax.axis_index("group")
    copies = []
    for index, piece in enumerate(pieces):
        number = 2 * (group ^ (index // 2)) + (column ^ (index % 2))
        copies.append(pltpu.make_async_copy(piece, out.at[number], sems.at[index]))
        copies[-1].start()
    for copy in copies:
        copy.wait()


def place(pieces):
    rows, width = pieces[0].shape
    return pl.pallas_call(
        place_kernel,
        out_shape=jax.ShapeDtypeStruct((len(pieces), rows, width), BF16),
        in_specs=[VMEM] * len(pieces),
        out_specs=HBM,
        scratch_shapes=[pltpu.SemaphoreType.DMA((len(pieces),))],
        compiler_params=params(16),
    )(*pieces)


def shards(line, groups, patches, cotangents, newton_counts):
    blocks, pix, width = patches.shape
    half, quarter = width // 2, width // 4
    rows = half // (2 * line)
    scale = 1.0 / float(pix * 4 * line * width) ** 0.5

    def swap(array, axis, mask=1):
        return lax.ppermute(array, axis, [(i, i ^ mask) for i in range(lax.axis_size(axis))])

    def swap_diagonal(array):
        moves = [(2 * z + x, 2 * (z ^ 1) + (x ^ 1)) for z in range(line) for x in range(2)]
        return lax.ppermute(array, ("z", "x"), moves)

    given, patch, cot = load(scale, patches, cotangents)
    came = swap(given, "core")
    kept, given_on = sums(scale, patch, cot, (), (1, 0, F32), (0, 1, BF16))
    came_on = swap(given_on, "core")
    leaving = add(kept, came).astype(BF16)
    to_diagonal, to_column = leaving[quarter:], leaving[:quarter]
    from_diagonal = swap_diagonal(to_diagonal)
    from_column = swap(to_column, "x")
    (kept_on,) = sums(scale, patch, cot, (to_diagonal,), (0, 0, F32))
    own = add(kept_on, came_on)
    from_line = swap(own[quarter:].astype(BF16), "z")
    left, right, send_left, send_right = collect(
        width * 3 // 4, own, from_diagonal, from_column, from_line
    )
    pieces, fars = [], []
    for own, send in ((left, send_left), (right, send_right)):
        mask = 2
        while mask < line:
            own = add(own, swap(send, "z", mask))
            send = own.astype(BF16)
            mask *= 2
        own = send
        other = swap(own, "z")
        pieces += [own, other]
        fars.append(swap(jnp.concatenate([own, other], 0), "core"))
    keep, send = root(newton_counts, near_part(*pieces), fars, rows)

    pieces = []
    for turn in range(groups):
        for flip in range(2):
            moves = [
                (c * groups + g, (c ^ flip) * groups + (g ^ turn))
                for c in range(2)
                for g in range(groups)
            ]
            piece = send if flip else keep
            pieces.append(lax.ppermute(piece, ("x", "group"), moves) if turn or flip else piece)
    return place(pieces)


def solution(mesh):
    devices, groups = mesh.shape["dp"], mesh.shape["group"]
    line = devices // 4
    cut = jax.sharding.Mesh(
        mesh.devices.reshape(line, 2, 2, groups), ("z", "x", "core", "group")
    )
    dp = ("z", "x", "core")
    placed = (P("group", dp, None), P("group", dp, None), P("group", None))
    return jax.shard_map(
        functools.partial(shards, line, groups),
        mesh=cut,
        in_specs=placed,
        out_specs=P(None, dp, None),
        check_vma=False,
    )
```

```python
import functools

import jax
import jax.numpy as jnp
from jax import lax
from jax.experimental import pallas as pl
from jax.experimental.pallas import tpu as pltpu
from jax.sharding import PartitionSpec as P

F32 = jnp.float32
BF16 = jnp.bfloat16
VMEM = pl.BlockSpec(memory_space=pltpu.VMEM)
SMEM = pl.BlockSpec(memory_space=pltpu.SMEM)
HBM = pl.BlockSpec(memory_space=pltpu.HBM)
ROWS_IN_COLS = (((0,), (0,)), ((), ()))


def params(limit):
    return pltpu.CompilerParams(vmem_limit_bytes=limit << 20)


def half_sum(patch, cot, block, side, scale):
    terms = lax.dot_general(
        patch[block, side], cot[block], ROWS_IN_COLS, preferred_element_type=F32
    )
    return terms * scale


def load_kernel(scale, patch_hbm, cot_hbm, given, patch, cot, sems):
    half = patch.shape[3]
    width = half // 2
    column, core, parity = lax.axis_index("x"), lax.axis_index("core"), lax.axis_index("z") % 2
    copies = []

    def fetch(source, target):
        copies.append(pltpu.make_async_copy(source, target, sems.at[len(copies)]))
        copies[-1].start()

    def fetch_patch(block, side):
        for quarter in range(2):
            first = (core ^ side) * half + (parity ^ quarter) * width
            fetch(
                patch_hbm.at[column ^ block, :, pl.ds(pl.multiple_of(first, width), width)],
                patch.at[block, side, :, quarter * width : (quarter + 1) * width],
            )

    fetch(cot_hbm.at[column ^ 1], cot.at[1])
    fetch_patch(1, 1)
    needed = len(copies)
    fetch_patch(1, 0)
    fetch(cot_hbm.at[column], cot.at[0])
    fetch_patch(0, 1)
    fetch_patch(0, 0)
    for copy in copies[:needed]:
        copy.wait()
    given[...] = half_sum(patch, cot, 1, 1, scale).astype(BF16)
    for copy in copies[needed:]:
        copy.wait()


def load(scale, patches, cotangents):
    blocks, pix, width = patches.shape
    half = width // 2
    return pl.pallas_call(
        functools.partial(load_kernel, scale),
        out_shape=[
            jax.ShapeDtypeStruct((half, width), BF16),
            jax.ShapeDtypeStruct((blocks, 2, pix, half), BF16),
            jax.ShapeDtypeStruct((blocks, pix, width), BF16),
        ],
        in_specs=[HBM] * 2,
        out_specs=[VMEM] * 3,
        scratch_shapes=[pltpu.SemaphoreType.DMA((10,))],
        compiler_params=params(16),
    )(
        pltpu.with_memory_space_constraint(patches, pltpu.HBM),
        pltpu.with_memory_space_constraint(cotangents, pltpu.HBM),
    )


def sums_kernel(scale, wanted, patch, cot, *refs):
    for (block, side, dtype), out in zip(wanted, refs[-len(wanted) :]):
        out[...] = half_sum(patch, cot, block, side, scale).astype(dtype)


def sums(scale, patch, cot, after, *wanted):
    pix, half = patch.shape[2:]
    return pl.pallas_call(
        functools.partial(sums_kernel, scale, wanted),
        out_shape=[jax.ShapeDtypeStruct((half, 2 * half), dtype) for _, _, dtype in wanted],
        in_specs=[VMEM] * 2 + [pl.BlockSpec(memory_space=pl.ANY)] * len(after),
        out_specs=[VMEM] * len(wanted),
        compiler_params=params(16),
        cost_estimate=pl.CostEstimate(
            flops=4 * len(wanted) * pix * half * half,
            bytes_accessed=8 * pix * half,
            transcendentals=0,
        ),
    )(patch, cot, *after)


def collect_kernel(own, *refs):
    *came, keep_left, keep_right, send_left, send_right = refs
    split = keep_left.shape[1]
    for columns, keep, send in (
        (slice(0, split), keep_left, send_left),
        (slice(split, own.shape[1]), keep_right, send_right),
    ):
        total = own[: keep.shape[0], columns]
        for ref in came:
            total = total + ref[:, columns].astype(F32)
        keep[...] = total
        send[...] = total.astype(BF16)


def collect(split, own, *came):
    rows, width = came[0].shape
    shapes = [(rows, split), (rows, width - split)]
    return pl.pallas_call(
        collect_kernel,
        out_shape=[jax.ShapeDtypeStruct(shape, F32) for shape in shapes]
        + [jax.ShapeDtypeStruct(shape, BF16) for shape in shapes],
        in_specs=[VMEM] * (1 + len(came)),
        out_specs=[VMEM] * 4,
        compiler_params=params(16),
    )(own, *came)


def add(*values):
    total = values[0]
    for value in values[1:]:
        total = total + value.astype(F32)
    return total


def root_kernel(most, counts_hbm, *refs):
    pieces = refs[:6]
    keep_ref, send_ref, grad, turned, left, right, m_left, m_right, s_left, s_right, counts, sem = refs[6:]
    counts_copy = pltpu.make_async_copy(counts_hbm, counts, sem)
    counts_copy.start()
    width = grad.shape[0]
    half, quarter = width // 2, width // 4
    rows = keep_ref.shape[0]
    low, high = slice(0, half), slice(half, width)
    place, column, core = (lax.axis_index(name) for name in ("z", "x", "core"))
    column_start = 0
    for index in range(2):
        own, other, far = pieces[3 * index : 3 * index + 3]
        columns = slice(column_start, column_start + own.shape[1])
        column_start += own.shape[1]
        grad[:quarter, columns] = own[...]
        grad[quarter:half, columns] = other[...]
        grad[half:, columns] = far[...]
    turned[...] = grad[...].T
    diagonal = lax.broadcasted_iota(jnp.int32, (half, half), 0) == lax.broadcasted_iota(
        jnp.int32, (half, half), 1
    )

    def dot(a, b):
        return jnp.dot(a, b, preferred_element_type=F32)

    def fill(ref, start, tiles):
        upper_left, upper_right, lower_right = (tile.astype(BF16) for tile in tiles)
        ref[start : start + half, low] = upper_left
        ref[start : start + half, high] = upper_right
        ref[start + half : start + width, low] = upper_right.T
        ref[start + half : start + width, high] = lower_right

    def factor(tiles):
        upper_left, upper_right, lower_right = tiles
        five = jnp.where(diagonal, 1.25, 0.0)
        return five - 0.25 * upper_left, -0.25 * upper_right, five - 0.25 * lower_right

    def statistics(first, second):
        tiles = [
            dot(first[a, :], second[:, b]) for a, b in ((low, low), (low, high), (high, high))
        ]
        tenth = jnp.where(diagonal, 0.1, 0.0)
        return tiles[0] + tenth, tiles[1], tiles[2] + tenth

    def spot(flip):
        row = (4 * place + 2 * (column ^ flip) + core) * rows
        part = row // quarter
        return ((part // 2 ^ core) * 2 + (part % 2 ^ place % 2)) * quarter + row % quarter

    line = lax.broadcasted_iota(jnp.int32, (2 * rows, width), 0)
    wanted = jnp.where(line < rows, spot(0) + line, spot(1) + line - rows)
    pick = lax.broadcasted_iota(jnp.int32, (2 * rows, width), 1) == wanted
    pick = jnp.where(pick, 1.0, 0.0).astype(BF16)
    picked = 2 * rows
    stats_left = statistics(grad, turned)
    stats_right = statistics(turned, grad)
    squares = [tile * tile for tile in stats_left]
    norm = jnp.sqrt(jnp.sum(squares[0] + 2.0 * squares[1] + squares[2], keepdims=True))
    scale = 2.5 / norm
    first = jnp.sqrt(jnp.sqrt(scale)).astype(BF16).astype(F32)
    tiles = [scale * tile for tile in stats_left]
    fill(m_left, 0, tiles)
    fill(left, picked, factor(tiles))
    left[:picked, :] = (first * dot(pick, left[picked:, :])).astype(BF16)
    tiles = [scale * tile for tile in stats_right]
    fill(m_right, 0, tiles)
    tiles = [tile.astype(BF16) for tile in factor(tiles)]
    fill(right, width, tiles)
    tiles = [(first * tile.astype(F32)).astype(BF16) for tile in tiles]
    right[half:width, low] = tiles[0]
    right[half:width, high] = tiles[1]
    right[:half, low] = tiles[1].T
    right[:half, high] = tiles[2]

    def square(ref):
        by_high = dot(ref[...], ref[:, high])
        return dot(ref[low, :], ref[:, low]), by_high[low], by_high[high]

    counts_copy.wait()
    count_left, count_right = counts[column, 0], counts[column, 1]
    q_left, q_right = left.at[picked:, :], right.at[width:, :]

    def finish_sweep(last):
        fourths = square(s_left), square(s_right)
        fill(s_left, 0, fourths[0])
        fill(s_right, 0, fourths[1])
        for fourth, moment_ref, ref, start in (
            (s_left, m_left, left, picked),
            (s_right, m_right, right, width),
        ):
            by_high = dot(fourth[...], moment_ref[:, high])
            tiles = (dot(fourth[low, :], moment_ref[:, low]), by_high[low], by_high[high])
            if not last:
                fill(moment_ref, 0, tiles)
            fill(ref, start, factor(tiles))

    def keep_if(old, value, goes_on):
        return jnp.where(goes_on, value.astype(BF16), old)

    def sweep(index, carry):
        finish_sweep(False)
        by_high = dot(left[...], q_left[:, high])
        by_low = dot(left[: picked + half, :], q_left[:, low])
        right_by_high = dot(right[...], q_right[:, high])
        right_by_low = dot(right[half : width + half, :], q_right[:, low])
        fill(s_left, 0, (by_low[picked:], by_high[picked : picked + half], by_high[picked + half :]))
        fill(
            s_right,
            0,
            (right_by_low[half:], right_by_high[width : width + half], right_by_high[width + half :]),
        )
        goes_on = index <= count_left
        left[:picked, low] = keep_if(left[:picked, low], by_low[:picked], goes_on)
        left[:picked, high] = keep_if(left[:picked, high], by_high[:picked], goes_on)
        goes_on = index <= count_right
        upper_right = keep_if(right[half:width, high], right_by_high[half:width], goes_on)
        right[half:width, low] = keep_if(right[half:width, low], right_by_low[:half], goes_on)
        right[half:width, high] = upper_right
        right[:half, low] = upper_right.T
        right[:half, high] = keep_if(right[:half, high], right_by_high[:half], goes_on)
        return carry

    fill(s_left, 0, square(q_left))
    fill(s_right, 0, square(q_right))
    lax.fori_loop(2, most, sweep, 0)
    finish_sweep(True)
    final_left = dot(left[:picked, :], left[picked:, :]).astype(BF16)
    final_left = jnp.where(most <= count_left, final_left, left[:picked, :])
    by_high = dot(right[:width, :], right[width:, high])
    by_low = dot(right[half:width, :], right[width:, low])
    goes_on = most <= count_right
    upper_right = jnp.where(goes_on, by_high[half:].astype(BF16), right[half:width, high])
    right[half:width, low] = jnp.where(goes_on, by_low.astype(BF16), right[half:width, low])
    right[half:width, high] = upper_right
    right[:half, low] = upper_right.T
    right[:half, high] = jnp.where(goes_on, by_high[:half].astype(BF16), right[:half, high])
    partial_value = dot(final_left, grad[...]).astype(BF16)
    update = dot(partial_value[:, low], right[half:width, :]) + dot(
        partial_value[:, high], right[:half, :]
    )
    keep_ref[...] = update[:rows, :].astype(BF16)
    send_ref[...] = update[rows:, :].astype(BF16)


def root(counts, pieces, rows, most=4):
    width = 4 * pieces[0].shape[0]
    square = pltpu.VMEM((width, width), BF16)
    out = jax.ShapeDtypeStruct((rows, width), BF16)
    return pl.pallas_call(
        functools.partial(root_kernel, most),
        out_shape=[out, out],
        in_specs=[HBM] + [VMEM] * 6,
        out_specs=[VMEM] * 2,
        scratch_shapes=[
            square,
            square,
            pltpu.VMEM((2 * rows + width, width), BF16),
            pltpu.VMEM((2 * width, width), BF16),
            square,
            square,
            square,
            square,
            pltpu.SMEM(counts.shape, jnp.int32),
            pltpu.SemaphoreType.DMA(()),
        ],
        compiler_params=params(40),
    )(pltpu.with_memory_space_constraint(counts, pltpu.HBM), *pieces)


def place_kernel(*refs):
    *pieces, out, sems = refs
    column, group = lax.axis_index("x"), lax.axis_index("group")
    copies = []
    for index, piece in enumerate(pieces):
        number = 2 * (group ^ (index // 2)) + (column ^ (index % 2))
        copies.append(pltpu.make_async_copy(piece, out.at[number], sems.at[index]))
        copies[-1].start()
    for copy in copies:
        copy.wait()


def place(pieces):
    rows, width = pieces[0].shape
    return pl.pallas_call(
        place_kernel,
        out_shape=jax.ShapeDtypeStruct((len(pieces), rows, width), BF16),
        in_specs=[VMEM] * len(pieces),
        out_specs=HBM,
        scratch_shapes=[pltpu.SemaphoreType.DMA((len(pieces),))],
        compiler_params=params(16),
    )(*pieces)


def shards(line, groups, patches, cotangents, newton_counts):
    blocks, pix, width = patches.shape
    half, quarter = width // 2, width // 4
    rows = half // (2 * line)
    scale = 1.0 / float(pix * 4 * line * width) ** 0.5

    def swap(array, axis, mask=1):
        return lax.ppermute(array, axis, [(i, i ^ mask) for i in range(lax.axis_size(axis))])

    def swap_diagonal(array):
        moves = [(2 * z + x, 2 * (z ^ 1) + (x ^ 1)) for z in range(line) for x in range(2)]
        return lax.ppermute(array, ("z", "x"), moves)

    given, patch, cot = load(scale, patches, cotangents)
    came = swap(given, "core")
    kept, given_on = sums(scale, patch, cot, (), (1, 0, F32), (0, 1, BF16))
    came_on = swap(given_on, "core")
    leaving = add(kept, came).astype(BF16)
    to_diagonal, to_column = leaving[quarter:], leaving[:quarter]
    from_diagonal = swap_diagonal(to_diagonal)
    from_column = swap(to_column, "x")
    (kept_on,) = sums(scale, patch, cot, (to_diagonal,), (0, 0, F32))
    own = add(kept_on, came_on)
    from_line = swap(own[quarter:].astype(BF16), "z")
    left, right, send_left, send_right = collect(
        width * 3 // 4, own, from_diagonal, from_column, from_line
    )
    pieces = []
    for own, send in ((left, send_left), (right, send_right)):
        mask = 2
        while mask < line:
            own = add(own, swap(send, "z", mask))
            send = own.astype(BF16)
            mask *= 2
        own = send
        other = swap(own, "z")
        pieces += [own, other, swap(jnp.concatenate([own, other], 0), "core")]
    keep, send = root(newton_counts, pieces, rows)

    pieces = []
    for turn in range(groups):
        for flip in range(2):
            moves = [
                (c * groups + g, (c ^ flip) * groups + (g ^ turn))
                for c in range(2)
                for g in range(groups)
            ]
            piece = send if flip else keep
            pieces.append(lax.ppermute(piece, ("x", "group"), moves) if turn or flip else piece)
    return place(pieces)


def solution(mesh):
    devices, groups = mesh.shape["dp"], mesh.shape["group"]
    line = devices // 4
    cut = jax.sharding.Mesh(
        mesh.devices.reshape(line, 2, 2, groups), ("z", "x", "core", "group")
    )
    dp = ("z", "x", "core")
    placed = (P("group", dp, None), P("group", dp, None), P("group", None))
    return jax.shard_map(
        functools.partial(shards, line, groups),
        mesh=cut,
        in_specs=placed,
        out_specs=P(None, dp, None),
        check_vma=False,
    )
```

```python
import functools

import jax
import jax.numpy as jnp
from jax import lax
from jax.experimental import pallas as pl
from jax.experimental.pallas import tpu as pltpu
from jax.sharding import PartitionSpec as P

F32 = jnp.float32
BF16 = jnp.bfloat16
VMEM = pl.BlockSpec(memory_space=pltpu.VMEM)
SMEM = pl.BlockSpec(memory_space=pltpu.SMEM)
HBM = pl.BlockSpec(memory_space=pltpu.HBM)
ROWS_IN_COLS = (((0,), (0,)), ((), ()))


def params(limit):
    return pltpu.CompilerParams(vmem_limit_bytes=limit << 20)


def half_sum(patch, cot, block, side, scale, part=None):
    quarter = patch.shape[3] // 2
    rows = slice(None) if part is None else slice(part * quarter, (part + 1) * quarter)
    terms = lax.dot_general(
        patch[block, side, :, rows], cot[block], ROWS_IN_COLS, preferred_element_type=F32
    )
    return terms * scale


def load_kernel(scale, patch_hbm, cot_hbm, given_near, given_far, patch, cot, sems):
    half = patch.shape[3]
    width = half // 2
    column, core, parity = lax.axis_index("x"), lax.axis_index("core"), lax.axis_index("z") % 2
    copies = []
    quarter = given_near.shape[0]

    def fetch(source, target):
        copies.append(pltpu.make_async_copy(source, target, sems.at[len(copies)]))
        copies[-1].start()

    def fetch_patch(block, side):
        for quarter in range(2):
            first = (core ^ side) * half + (parity ^ quarter) * width
            fetch(
                patch_hbm.at[column ^ block, :, pl.ds(pl.multiple_of(first, width), width)],
                patch.at[block, side, :, quarter * width : (quarter + 1) * width],
            )

    fetch(cot_hbm.at[column ^ 1], cot.at[1])
    fetch_patch(1, 1)
    needed = len(copies)
    fetch_patch(1, 0)
    fetch(cot_hbm.at[column], cot.at[0])
    fetch_patch(0, 1)
    fetch_patch(0, 0)
    for copy in copies[:needed]:
        copy.wait()
    terms = half_sum(patch, cot, 1, 1, scale).astype(BF16)
    given_near[...] = terms[:quarter]
    given_far[...] = terms[quarter:]
    for copy in copies[needed:]:
        copy.wait()


def load(scale, patches, cotangents):
    blocks, pix, width = patches.shape
    half = width // 2
    return pl.pallas_call(
        functools.partial(load_kernel, scale),
        out_shape=[
            jax.ShapeDtypeStruct((half // 2, width), BF16),
            jax.ShapeDtypeStruct((half // 2, width), BF16),
            jax.ShapeDtypeStruct((blocks, 2, pix, half), BF16),
            jax.ShapeDtypeStruct((blocks, pix, width), BF16),
        ],
        in_specs=[HBM] * 2,
        out_specs=[VMEM] * 4,
        scratch_shapes=[pltpu.SemaphoreType.DMA((10,))],
        compiler_params=params(16),
    )(
        pltpu.with_memory_space_constraint(patches, pltpu.HBM),
        pltpu.with_memory_space_constraint(cotangents, pltpu.HBM),
    )


def sums_kernel(scale, wanted, patch, cot, *refs):
    for (block, side, part, dtype), out in zip(wanted, refs[-len(wanted) :]):
        out[...] = half_sum(patch, cot, block, side, scale, part).astype(dtype)


def sums(scale, patch, cot, after, *wanted):
    pix, half = patch.shape[2:]
    return pl.pallas_call(
        functools.partial(sums_kernel, scale, wanted),
        out_shape=[
            jax.ShapeDtypeStruct((half if part is None else half // 2, 2 * half), dtype)
            for _, _, part, dtype in wanted
        ],
        in_specs=[VMEM] * 2 + [pl.BlockSpec(memory_space=pl.ANY)] * len(after),
        out_specs=[VMEM] * len(wanted),
        compiler_params=params(16),
        cost_estimate=pl.CostEstimate(
            flops=4 * len(wanted) * pix * half * half,
            bytes_accessed=8 * pix * half,
            transcendentals=0,
        ),
    )(patch, cot, *after)


def collect_kernel(own, *refs):
    *came, keep_left, keep_right, send_left, send_right = refs
    split = keep_left.shape[1]
    for columns, keep, send in (
        (slice(0, split), keep_left, send_left),
        (slice(split, own.shape[1]), keep_right, send_right),
    ):
        total = own[: keep.shape[0], columns]
        for ref in came:
            total = total + ref[:, columns].astype(F32)
        keep[...] = total
        send[...] = total.astype(BF16)


def collect(split, own, *came):
    rows, width = came[0].shape
    shapes = [(rows, split), (rows, width - split)]
    return pl.pallas_call(
        collect_kernel,
        out_shape=[jax.ShapeDtypeStruct(shape, F32) for shape in shapes]
        + [jax.ShapeDtypeStruct(shape, BF16) for shape in shapes],
        in_specs=[VMEM] * (1 + len(came)),
        out_specs=[VMEM] * 4,
        compiler_params=params(16),
    )(own, *came)


def add(*values):
    total = values[0]
    for value in values[1:]:
        total = total + value.astype(F32)
    return total


def root_kernel(most, counts_hbm, *refs):
    pieces = refs[:6]
    keep_ref, send_ref, grad, turned, left, right, m_left, m_right, s_left, s_right, counts, sem = refs[6:]
    counts_copy = pltpu.make_async_copy(counts_hbm, counts, sem)
    counts_copy.start()
    width = grad.shape[0]
    half, quarter = width // 2, width // 4
    rows = keep_ref.shape[0]
    low, high = slice(0, half), slice(half, width)
    place, column, core = (lax.axis_index(name) for name in ("z", "x", "core"))
    column_start = 0
    for index in range(2):
        own, other, far = pieces[3 * index : 3 * index + 3]
        columns = slice(column_start, column_start + own.shape[1])
        column_start += own.shape[1]
        grad[:quarter, columns] = own[...]
        grad[quarter:half, columns] = other[...]
        grad[half:, columns] = far[...]
    turned[...] = grad[...].T
    diagonal = lax.broadcasted_iota(jnp.int32, (half, half), 0) == lax.broadcasted_iota(
        jnp.int32, (half, half), 1
    )

    def dot(a, b):
        return jnp.dot(a, b, preferred_element_type=F32)

    def fill(ref, start, tiles):
        upper_left, upper_right, lower_right = (tile.astype(BF16) for tile in tiles)
        ref[start : start + half, low] = upper_left
        ref[start : start + half, high] = upper_right
        ref[start + half : start + width, low] = upper_right.T
        ref[start + half : start + width, high] = lower_right

    def factor(tiles):
        upper_left, upper_right, lower_right = tiles
        five = jnp.where(diagonal, 1.25, 0.0)
        return five - 0.25 * upper_left, -0.25 * upper_right, five - 0.25 * lower_right

    def statistics(first, second):
        tiles = [
            dot(first[a, :], second[:, b]) for a, b in ((low, low), (low, high), (high, high))
        ]
        tenth = jnp.where(diagonal, 0.1, 0.0)
        return tiles[0] + tenth, tiles[1], tiles[2] + tenth

    def spot(flip):
        row = (4 * place + 2 * (column ^ flip) + core) * rows
        part = row // quarter
        return ((part // 2 ^ core) * 2 + (part % 2 ^ place % 2)) * quarter + row % quarter

    line = lax.broadcasted_iota(jnp.int32, (2 * rows, width), 0)
    wanted = jnp.where(line < rows, spot(0) + line, spot(1) + line - rows)
    pick = lax.broadcasted_iota(jnp.int32, (2 * rows, width), 1) == wanted
    pick = jnp.where(pick, 1.0, 0.0).astype(BF16)
    picked = 2 * rows
    stats_left = statistics(grad, turned)
    stats_right = statistics(turned, grad)
    squares = [tile * tile for tile in stats_left]
    norm = jnp.sqrt(jnp.sum(squares[0] + 2.0 * squares[1] + squares[2], keepdims=True))
    scale = 2.5 / norm
    first = jnp.sqrt(jnp.sqrt(scale)).astype(BF16).astype(F32)
    tiles = [scale * tile for tile in stats_left]
    fill(m_left, 0, tiles)
    fill(left, picked, factor(tiles))
    left[:picked, :] = (first * dot(pick, left[picked:, :])).astype(BF16)
    tiles = [scale * tile for tile in stats_right]
    fill(m_right, 0, tiles)
    tiles = [tile.astype(BF16) for tile in factor(tiles)]
    fill(right, width, tiles)
    tiles = [(first * tile.astype(F32)).astype(BF16) for tile in tiles]
    right[half:width, low] = tiles[0]
    right[half:width, high] = tiles[1]
    right[:half, low] = tiles[1].T
    right[:half, high] = tiles[2]

    def square(ref):
        by_high = dot(ref[...], ref[:, high])
        return dot(ref[low, :], ref[:, low]), by_high[low], by_high[high]

    counts_copy.wait()
    count_left, count_right = counts[column, 0], counts[column, 1]
    for index in range(1, most):
        q_left, q_right = left.at[picked:, :], right.at[width:, :]
        if index == 1:
            fill(s_left, 0, square(q_left))
            fill(s_right, 0, square(q_right))
        else:
            by_high = dot(left[...], q_left[:, high])
            by_low = dot(left[: picked + half, :], q_left[:, low])
            right_by_high = dot(right[...], q_right[:, high])
            right_by_low = dot(right[half : width + half, :], q_right[:, low])
            fill(s_left, 0, (by_low[picked:], by_high[picked : picked + half], by_high[picked + half :]))
            fill(
                s_right,
                0,
                (right_by_low[half:], right_by_high[width : width + half], right_by_high[width + half :]),
            )

            def keep_if(ref, value, goes_on):
                value = value.astype(BF16)
                return value if index == 2 else jnp.where(goes_on, value, ref)

            left[:picked, low] = keep_if(left[:picked, low], by_low[:picked], index <= count_left)
            left[:picked, high] = keep_if(left[:picked, high], by_high[:picked], index <= count_left)
            goes_on = index <= count_right
            upper_right = keep_if(right[half:width, high], right_by_high[half:width], goes_on)
            right[half:width, low] = keep_if(right[half:width, low], right_by_low[:half], goes_on)
            right[half:width, high] = upper_right
            right[:half, low] = upper_right.T
            right[:half, high] = keep_if(right[:half, high], right_by_high[:half], goes_on)
        fourths = square(s_left), square(s_right)
        fill(s_left, 0, fourths[0])
        fill(s_right, 0, fourths[1])
        for fourth, moment_ref, ref, start in (
            (s_left, m_left, left, picked),
            (s_right, m_right, right, width),
        ):
            by_high = dot(fourth[...], moment_ref[:, high])
            tiles = (dot(fourth[low, :], moment_ref[:, low]), by_high[low], by_high[high])
            if index < most - 1:
                fill(moment_ref, 0, tiles)
            fill(ref, start, factor(tiles))
    final_left = dot(left[:picked, :], left[picked:, :]).astype(BF16)
    final_left = jnp.where(most <= count_left, final_left, left[:picked, :])
    by_high = dot(right[:width, :], right[width:, high])
    by_low = dot(right[half:width, :], right[width:, low])
    goes_on = most <= count_right
    upper_right = jnp.where(goes_on, by_high[half:].astype(BF16), right[half:width, high])
    right[half:width, low] = jnp.where(goes_on, by_low.astype(BF16), right[half:width, low])
    right[half:width, high] = upper_right
    right[:half, low] = upper_right.T
    right[:half, high] = jnp.where(goes_on, by_high[:half].astype(BF16), right[:half, high])
    partial_value = dot(final_left, grad[...]).astype(BF16)
    update = dot(partial_value[:, low], right[half:width, :]) + dot(
        partial_value[:, high], right[:half, :]
    )
    keep_ref[...] = update[:rows, :].astype(BF16)
    send_ref[...] = update[rows:, :].astype(BF16)


def root(counts, pieces, rows, most=4):
    width = 4 * pieces[0].shape[0]
    square = pltpu.VMEM((width, width), BF16)
    out = jax.ShapeDtypeStruct((rows, width), BF16)
    return pl.pallas_call(
        functools.partial(root_kernel, most),
        out_shape=[out, out],
        in_specs=[HBM] + [VMEM] * 6,
        out_specs=[VMEM] * 2,
        scratch_shapes=[
            square,
            square,
            pltpu.VMEM((2 * rows + width, width), BF16),
            pltpu.VMEM((2 * width, width), BF16),
            square,
            square,
            square,
            square,
            pltpu.SMEM(counts.shape, jnp.int32),
            pltpu.SemaphoreType.DMA(()),
        ],
        compiler_params=params(40),
    )(pltpu.with_memory_space_constraint(counts, pltpu.HBM), *pieces)


def place_kernel(origins, *refs):
    *pieces, out, sems = refs
    column, group = lax.axis_index("x"), lax.axis_index("group")
    copies = []
    for index, (piece, (turn, flip)) in enumerate(zip(pieces, origins)):
        number = 2 * (group ^ turn) + (column ^ flip)
        copies.append(pltpu.make_async_copy(piece, out.at[number], sems.at[index]))
        copies[-1].start()
    for copy in copies:
        copy.wait()


def place(found):
    origins, pieces = zip(*found.items())
    rows, width = pieces[0].shape
    return pl.pallas_call(
        functools.partial(place_kernel, origins),
        out_shape=jax.ShapeDtypeStruct((len(pieces), rows, width), BF16),
        in_specs=[VMEM] * len(pieces),
        out_specs=HBM,
        scratch_shapes=[pltpu.SemaphoreType.DMA((len(pieces),))],
        compiler_params=params(16),
    )(*pieces)


def shards(line, groups, patches, cotangents, newton_counts):
    blocks, pix, width = patches.shape
    half, quarter = width // 2, width // 4
    rows = half // (2 * line)
    scale = 1.0 / float(pix * 4 * line * width) ** 0.5

    def swap(array, axis, mask=1):
        return lax.ppermute(array, axis, [(i, i ^ mask) for i in range(lax.axis_size(axis))])

    def swap_diagonal(array):
        moves = [(2 * z + x, 2 * (z ^ 1) + (x ^ 1)) for z in range(line) for x in range(2)]
        return lax.ppermute(array, ("z", "x"), moves)

    given_near, given_far, patch, cot = load(scale, patches, cotangents)
    came_near, came_far = swap(given_near, "core"), swap(given_far, "core")
    kept_near, kept_far, given_on = sums(
        scale, patch, cot, (), (1, 0, 0, F32), (1, 0, 1, F32), (0, 1, None, BF16)
    )
    came_on = swap(given_on, "core")
    to_column = add(kept_near, came_near).astype(BF16)
    to_diagonal = add(kept_far, came_far).astype(BF16)
    from_diagonal = swap_diagonal(to_diagonal)
    from_column = swap(to_column, "x")
    (kept_on,) = sums(scale, patch, cot, (to_diagonal,), (0, 0, None, F32))
    own = add(kept_on, came_on)
    from_line = swap(own[quarter:].astype(BF16), "z")
    left, right, send_left, send_right = collect(
        width * 3 // 4, own, from_diagonal, from_column, from_line
    )
    pieces = []
    for own, send in ((left, send_left), (right, send_right)):
        mask = 2
        while mask < line:
            own = add(own, swap(send, "z", mask))
            send = own.astype(BF16)
            mask *= 2
        own = send
        other = swap(own, "z")
        pieces += [own, other, swap(jnp.concatenate([own, other], 0), "core")]
    keep, send = root(newton_counts, pieces, rows)

    def pass_on(turn, flip):
        moves = [
            (c * groups + g, (c ^ flip) * groups + (g ^ turn))
            for c in range(2)
            for g in range(groups)
        ]
        return lax.ppermute(send if flip else keep, ("x", "group"), moves)

    others = [(turn, flip) for turn in range(groups) for flip in range(2) if turn or flip]
    found = {(turn, flip): pass_on(turn, flip) for turn, flip in others}
    found[0, 0] = keep
    return place(found)


def solution(mesh):
    devices, groups = mesh.shape["dp"], mesh.shape["group"]
    line = devices // 4
    cut = jax.sharding.Mesh(
        mesh.devices.reshape(line, 2, 2, groups), ("z", "x", "core", "group")
    )
    dp = ("z", "x", "core")
    placed = (P("group", dp, None), P("group", dp, None), P("group", None))
    return jax.shard_map(
        functools.partial(shards, line, groups),
        mesh=cut,
        in_specs=placed,
        out_specs=P(None, dp, None),
        check_vma=False,
    )
```

```python
import functools

import jax
import jax.numpy as jnp
from jax import lax
from jax.experimental import pallas as pl
from jax.experimental.pallas import tpu as pltpu
from jax.sharding import PartitionSpec as P

F32 = jnp.float32
BF16 = jnp.bfloat16
VMEM = pl.BlockSpec(memory_space=pltpu.VMEM)
SMEM = pl.BlockSpec(memory_space=pltpu.SMEM)
HBM = pl.BlockSpec(memory_space=pltpu.HBM)
ROWS_IN_COLS = (((0,), (0,)), ((), ()))


def params(limit):
    return pltpu.CompilerParams(vmem_limit_bytes=limit << 20)


def half_sum(patch, cot, block, side, scale, part=None):
    quarter = patch.shape[3] // 2
    rows = slice(None) if part is None else slice(part * quarter, (part + 1) * quarter)
    terms = lax.dot_general(
        patch[block, side, :, rows], cot[block], ROWS_IN_COLS, preferred_element_type=F32
    )
    return terms * scale


def load_kernel(scale, patch_hbm, cot_hbm, given_near, given_far, patch, cot, sems):
    half = patch.shape[3]
    width = half // 2
    column, core, parity = lax.axis_index("x"), lax.axis_index("core"), lax.axis_index("z") % 2
    copies = []
    quarter = given_near.shape[0]

    def fetch(source, target):
        copies.append(pltpu.make_async_copy(source, target, sems.at[len(copies)]))
        copies[-1].start()

    def fetch_patch(block, side):
        for quarter in range(2):
            first = (core ^ side) * half + (parity ^ quarter) * width
            fetch(
                patch_hbm.at[column ^ block, :, pl.ds(pl.multiple_of(first, width), width)],
                patch.at[block, side, :, quarter * width : (quarter + 1) * width],
            )

    fetch(cot_hbm.at[column ^ 1], cot.at[1])
    fetch_patch(1, 1)
    needed = len(copies)
    fetch_patch(1, 0)
    fetch(cot_hbm.at[column], cot.at[0])
    fetch_patch(0, 1)
    fetch_patch(0, 0)
    for copy in copies[:needed]:
        copy.wait()
    terms = half_sum(patch, cot, 1, 1, scale).astype(BF16)
    given_near[...] = terms[:quarter]
    given_far[...] = terms[quarter:]
    for copy in copies[needed:]:
        copy.wait()


def load(scale, patches, cotangents):
    blocks, pix, width = patches.shape
    half = width // 2
    return pl.pallas_call(
        functools.partial(load_kernel, scale),
        out_shape=[
            jax.ShapeDtypeStruct((half // 2, width), BF16),
            jax.ShapeDtypeStruct((half // 2, width), BF16),
            jax.ShapeDtypeStruct((blocks, 2, pix, half), BF16),
            jax.ShapeDtypeStruct((blocks, pix, width), BF16),
        ],
        in_specs=[HBM] * 2,
        out_specs=[VMEM] * 4,
        scratch_shapes=[pltpu.SemaphoreType.DMA((10,))],
        compiler_params=params(16),
    )(
        pltpu.with_memory_space_constraint(patches, pltpu.HBM),
        pltpu.with_memory_space_constraint(cotangents, pltpu.HBM),
    )


def sums_kernel(scale, wanted, patch, cot, *refs):
    for (block, side, part, dtype), out in zip(wanted, refs[-len(wanted) :]):
        out[...] = half_sum(patch, cot, block, side, scale, part).astype(dtype)


def sums(scale, patch, cot, after, *wanted):
    pix, half = patch.shape[2:]
    return pl.pallas_call(
        functools.partial(sums_kernel, scale, wanted),
        out_shape=[
            jax.ShapeDtypeStruct((half if part is None else half // 2, 2 * half), dtype)
            for _, _, part, dtype in wanted
        ],
        in_specs=[VMEM] * 2 + [pl.BlockSpec(memory_space=pl.ANY)] * len(after),
        out_specs=[VMEM] * len(wanted),
        compiler_params=params(16),
        cost_estimate=pl.CostEstimate(
            flops=4 * len(wanted) * pix * half * half,
            bytes_accessed=8 * pix * half,
            transcendentals=0,
        ),
    )(patch, cot, *after)


def collect_kernel(own, *refs):
    *came, keep_left, keep_right, send_left, send_right = refs
    split = keep_left.shape[1]
    for columns, keep, send in (
        (slice(0, split), keep_left, send_left),
        (slice(split, own.shape[1]), keep_right, send_right),
    ):
        total = own[: keep.shape[0], columns]
        for ref in came:
            total = total + ref[:, columns].astype(F32)
        keep[...] = total
        send[...] = total.astype(BF16)


def collect(split, own, *came):
    rows, width = came[0].shape
    shapes = [(rows, split), (rows, width - split)]
    return pl.pallas_call(
        collect_kernel,
        out_shape=[jax.ShapeDtypeStruct(shape, F32) for shape in shapes]
        + [jax.ShapeDtypeStruct(shape, BF16) for shape in shapes],
        in_specs=[VMEM] * (1 + len(came)),
        out_specs=[VMEM] * 4,
        compiler_params=params(16),
    )(own, *came)


def add(*values):
    total = values[0]
    for value in values[1:]:
        total = total + value.astype(F32)
    return total


def root_kernel(most, counts_hbm, *refs):
    pieces = refs[:6]
    keep_ref, send_ref, grad, turned, left, right, m_left, m_right, s_left, s_right, counts, sem = refs[6:]
    counts_copy = pltpu.make_async_copy(counts_hbm, counts, sem)
    counts_copy.start()
    width = grad.shape[0]
    half, quarter = width // 2, width // 4
    rows = keep_ref.shape[0]
    low, high = slice(0, half), slice(half, width)
    place, column, core = (lax.axis_index(name) for name in ("z", "x", "core"))
    column_start = 0
    for index in range(2):
        own, other, far = pieces[3 * index : 3 * index + 3]
        columns = slice(column_start, column_start + own.shape[1])
        column_start += own.shape[1]
        grad[:quarter, columns] = own[...]
        grad[quarter:half, columns] = other[...]
        grad[half:, columns] = far[...]
    turned[...] = grad[...].T
    diagonal = lax.broadcasted_iota(jnp.int32, (half, half), 0) == lax.broadcasted_iota(
        jnp.int32, (half, half), 1
    )

    def dot(a, b):
        return jnp.dot(a, b, preferred_element_type=F32)

    def fill(ref, start, tiles):
        upper_left, upper_right, lower_right = (tile.astype(BF16) for tile in tiles)
        ref[start : start + half, low] = upper_left
        ref[start : start + half, high] = upper_right
        ref[start + half : start + width, low] = upper_right.T
        ref[start + half : start + width, high] = lower_right

    def factor(tiles):
        upper_left, upper_right, lower_right = tiles
        five = jnp.where(diagonal, 1.25, 0.0)
        return five - 0.25 * upper_left, -0.25 * upper_right, five - 0.25 * lower_right

    def statistics(first, second):
        tiles = [
            dot(first[a, :], second[:, b]) for a, b in ((low, low), (low, high), (high, high))
        ]
        tenth = jnp.where(diagonal, 0.1, 0.0)
        return tiles[0] + tenth, tiles[1], tiles[2] + tenth

    def spot(flip):
        row = (4 * place + 2 * (column ^ flip) + core) * rows
        part = row // quarter
        return ((part // 2 ^ core) * 2 + (part % 2 ^ place % 2)) * quarter + row % quarter

    line = lax.broadcasted_iota(jnp.int32, (2 * rows, width), 0)
    wanted = jnp.where(line < rows, spot(0) + line, spot(1) + line - rows)
    pick = lax.broadcasted_iota(jnp.int32, (2 * rows, width), 1) == wanted
    pick = jnp.where(pick, 1.0, 0.0).astype(BF16)
    picked = 2 * rows
    stats_left = statistics(grad, turned)
    stats_right = statistics(turned, grad)
    squares = [tile * tile for tile in stats_left]
    norm = jnp.sqrt(jnp.sum(squares[0] + 2.0 * squares[1] + squares[2], keepdims=True))
    scale = 2.5 / norm
    first = jnp.sqrt(jnp.sqrt(scale)).astype(BF16).astype(F32)
    tiles = [scale * tile for tile in stats_left]
    fill(m_left, 0, tiles)
    fill(left, picked, factor(tiles))
    left[:picked, :] = (first * dot(pick, left[picked:, :])).astype(BF16)
    tiles = [scale * tile for tile in stats_right]
    fill(m_right, 0, tiles)
    tiles = [tile.astype(BF16) for tile in factor(tiles)]
    fill(right, width, tiles)
    tiles = [(first * tile.astype(F32)).astype(BF16) for tile in tiles]
    right[half:width, low] = tiles[0]
    right[half:width, high] = tiles[1]
    right[:half, low] = tiles[1].T
    right[:half, high] = tiles[2]

    def square(ref):
        by_high = dot(ref[...], ref[:, high])
        return dot(ref[low, :], ref[:, low]), by_high[low], by_high[high]

    counts_copy.wait()
    count_left, count_right = counts[column, 0], counts[column, 1]
    for index in range(1, most):
        q_left, q_right = left.at[picked:, :], right.at[width:, :]
        if index == 1:
            fill(s_left, 0, square(q_left))
            fill(s_right, 0, square(q_right))
        else:
            by_high = dot(left[...], q_left[:, high])
            by_low = dot(left[: picked + half, :], q_left[:, low])
            right_by_high = dot(right[...], q_right[:, high])
            right_by_low = dot(right[half : width + half, :], q_right[:, low])
            fill(s_left, 0, (by_low[picked:], by_high[picked : picked + half], by_high[picked + half :]))
            fill(
                s_right,
                0,
                (right_by_low[half:], right_by_high[width : width + half], right_by_high[width + half :]),
            )

            def keep_if(ref, value, goes_on):
                value = value.astype(BF16)
                return value if index == 2 else jnp.where(goes_on, value, ref)

            left[:picked, low] = keep_if(left[:picked, low], by_low[:picked], index <= count_left)
            left[:picked, high] = keep_if(left[:picked, high], by_high[:picked], index <= count_left)
            goes_on = index <= count_right
            upper_right = keep_if(right[half:width, high], right_by_high[half:width], goes_on)
            right[half:width, low] = keep_if(right[half:width, low], right_by_low[:half], goes_on)
            right[half:width, high] = upper_right
            right[:half, low] = upper_right.T
            right[:half, high] = keep_if(right[:half, high], right_by_high[:half], goes_on)
        fourths = square(s_left), square(s_right)
        fill(s_left, 0, fourths[0])
        fill(s_right, 0, fourths[1])
        for fourth, moment_ref, ref, start in (
            (s_left, m_left, left, picked),
            (s_right, m_right, right, width),
        ):
            by_high = dot(fourth[...], moment_ref[:, high])
            tiles = (dot(fourth[low, :], moment_ref[:, low]), by_high[low], by_high[high])
            if index < most - 1:
                fill(moment_ref, 0, tiles)
            fill(ref, start, factor(tiles))
    final_left = dot(left[:picked, :], left[picked:, :]).astype(BF16)
    final_left = jnp.where(most <= count_left, final_left, left[:picked, :])
    by_high = dot(right[:width, :], right[width:, high])
    by_low = dot(right[half:width, :], right[width:, low])
    goes_on = most <= count_right
    upper_right = jnp.where(goes_on, by_high[half:].astype(BF16), right[half:width, high])
    right[half:width, low] = jnp.where(goes_on, by_low.astype(BF16), right[half:width, low])
    right[half:width, high] = upper_right
    right[:half, low] = upper_right.T
    right[:half, high] = jnp.where(goes_on, by_high[:half].astype(BF16), right[:half, high])
    partial_value = dot(final_left, grad[...]).astype(BF16)
    update = dot(partial_value[:, low], right[half:width, :]) + dot(
        partial_value[:, high], right[:half, :]
    )
    keep_ref[...] = update[:rows, :].astype(BF16)
    send_ref[...] = update[rows:, :].astype(BF16)


def root(counts, pieces, rows, most=4):
    width = 4 * pieces[0].shape[0]
    square = pltpu.VMEM((width, width), BF16)
    out = jax.ShapeDtypeStruct((rows, width), BF16)
    return pl.pallas_call(
        functools.partial(root_kernel, most),
        out_shape=[out, out],
        in_specs=[HBM] + [VMEM] * 6,
        out_specs=[VMEM] * 2,
        scratch_shapes=[
            square,
            square,
            pltpu.VMEM((2 * rows + width, width), BF16),
            pltpu.VMEM((2 * width, width), BF16),
            square,
            square,
            square,
            square,
            pltpu.SMEM(counts.shape, jnp.int32),
            pltpu.SemaphoreType.DMA(()),
        ],
        compiler_params=params(40),
    )(pltpu.with_memory_space_constraint(counts, pltpu.HBM), *pieces)


def place_kernel(origins, *refs):
    *pieces, out, sems = refs
    column, group = lax.axis_index("x"), lax.axis_index("group")
    copies = []
    for index, (piece, (turn, flip)) in enumerate(zip(pieces, origins)):
        number = 2 * (group ^ turn) + (column ^ flip)
        copies.append(pltpu.make_async_copy(piece, out.at[number], sems.at[index]))
        copies[-1].start()
    for copy in copies:
        copy.wait()


def place(found):
    origins, pieces = zip(*found.items())
    rows, width = pieces[0].shape
    return pl.pallas_call(
        functools.partial(place_kernel, origins),
        out_shape=jax.ShapeDtypeStruct((len(pieces), rows, width), BF16),
        in_specs=[VMEM] * len(pieces),
        out_specs=HBM,
        scratch_shapes=[pltpu.SemaphoreType.DMA((len(pieces),))],
        compiler_params=params(16),
    )(*pieces)


def shards(line, groups, patches, cotangents, newton_counts):
    blocks, pix, width = patches.shape
    half, quarter = width // 2, width // 4
    rows = half // (2 * line)
    scale = 1.0 / float(pix * 4 * line * width) ** 0.5

    def swap(array, axis, mask=1):
        return lax.ppermute(array, axis, [(i, i ^ mask) for i in range(lax.axis_size(axis))])

    def swap_diagonal(array):
        moves = [(2 * z + x, 2 * (z ^ 1) + (x ^ 1)) for z in range(line) for x in range(2)]
        return lax.ppermute(array, ("z", "x"), moves)

    given_near, given_far, patch, cot = load(scale, patches, cotangents)
    came_near, came_far = swap(given_near, "core"), swap(given_far, "core")
    kept_near, kept_far, given_on = sums(
        scale, patch, cot, (), (1, 0, 0, F32), (1, 0, 1, F32), (0, 1, None, BF16)
    )
    came_on = swap(given_on, "core")
    to_column = add(kept_near, came_near).astype(BF16)
    to_diagonal = add(kept_far, came_far).astype(BF16)
    from_diagonal = swap_diagonal(to_diagonal)
    from_column = swap(to_column, "x")
    (kept_on,) = sums(scale, patch, cot, (to_column,), (0, 0, None, F32))
    own = add(kept_on, came_on)
    from_line = swap(own[quarter:].astype(BF16), "z")
    left, right, send_left, send_right = collect(
        width * 3 // 4, own, from_diagonal, from_column, from_line
    )
    pieces = []
    for own, send in ((left, send_left), (right, send_right)):
        mask = 2
        while mask < line:
            own = add(own, swap(send, "z", mask))
            send = own.astype(BF16)
            mask *= 2
        own = send
        other = swap(own, "z")
        pieces += [own, other, swap(jnp.concatenate([own, other], 0), "core")]
    keep, send = root(newton_counts, pieces, rows)

    def pass_on(turn, flip):
        moves = [
            (c * groups + g, (c ^ flip) * groups + (g ^ turn))
            for c in range(2)
            for g in range(groups)
        ]
        return lax.ppermute(send if flip else keep, ("x", "group"), moves)

    others = [(turn, flip) for flip in (0, 1) for turn in range(groups) if turn or flip]
    found = {(turn, flip): pass_on(turn, flip) for turn, flip in others}
    found[0, 0] = keep
    return place(found)


def solution(mesh):
    devices, groups = mesh.shape["dp"], mesh.shape["group"]
    line = devices // 4
    cut = jax.sharding.Mesh(
        mesh.devices.reshape(line, 2, 2, groups), ("z", "x", "core", "group")
    )
    dp = ("z", "x", "core")
    placed = (P("group", dp, None), P("group", dp, None), P("group", None))
    return jax.shard_map(
        functools.partial(shards, line, groups),
        mesh=cut,
        in_specs=placed,
        out_specs=P(None, dp, None),
        check_vma=False,
    )
```

```python
import functools

import jax
import jax.numpy as jnp
from jax import lax
from jax.experimental import pallas as pl
from jax.experimental.pallas import tpu as pltpu
from jax.sharding import PartitionSpec as P

F32 = jnp.float32
BF16 = jnp.bfloat16
VMEM = pl.BlockSpec(memory_space=pltpu.VMEM)
SMEM = pl.BlockSpec(memory_space=pltpu.SMEM)
HBM = pl.BlockSpec(memory_space=pltpu.HBM)
ROWS_IN_COLS = (((0,), (0,)), ((), ()))


def params(limit):
    return pltpu.CompilerParams(vmem_limit_bytes=limit << 20)


def piece_sum(patch, cot, scale, block, side, part):
    quarter = patch.shape[3] // 2
    rows = slice(part * quarter, (part + 1) * quarter)
    terms = lax.dot_general(
        patch[block, side, :, rows], cot[block], ROWS_IN_COLS, preferred_element_type=F32
    )
    return terms * scale


def load_kernel(scale, patch_hbm, cot_hbm, given_column, given_line, patch, cot, sems):
    half = patch.shape[3]
    width = half // 2
    column, core, parity = lax.axis_index("x"), lax.axis_index("core"), lax.axis_index("z") % 2
    copies = []

    def fetch(source, target):
        copies.append(pltpu.make_async_copy(source, target, sems.at[len(copies)]))
        copies[-1].start()

    def fetch_patch(block, side, part):
        first = (core ^ side) * half + (parity ^ part) * width
        fetch(
            patch_hbm.at[column ^ block, :, pl.ds(pl.multiple_of(first, width), width)],
            patch.at[block, side, :, part * width : (part + 1) * width],
        )

    fetch(cot_hbm.at[column ^ 1], cot.at[1])
    fetch_patch(1, 1, 0)
    fetch(cot_hbm.at[column], cot.at[0])
    fetch_patch(0, 1, 1)
    needed = len(copies)
    for side in range(2):
        for block, part in ((1, 0), (0, 1), (1, 1), (0, 0)):
            if side == 0 or block == part:
                fetch_patch(block, side, part)
    for copy in copies[:2]:
        copy.wait()
    given_column[...] = piece_sum(patch, cot, scale, 1, 1, 0).astype(BF16)
    for copy in copies[2:needed]:
        copy.wait()
    given_line[...] = piece_sum(patch, cot, scale, 0, 1, 1).astype(BF16)
    for copy in copies[needed:]:
        copy.wait()


def load(scale, patches, cotangents):
    blocks, pix, width = patches.shape
    half = width // 2
    return pl.pallas_call(
        functools.partial(load_kernel, scale),
        out_shape=[
            jax.ShapeDtypeStruct((half // 2, width), BF16),
            jax.ShapeDtypeStruct((half // 2, width), BF16),
            jax.ShapeDtypeStruct((blocks, 2, pix, half), BF16),
            jax.ShapeDtypeStruct((blocks, pix, width), BF16),
        ],
        in_specs=[HBM] * 2,
        out_specs=[VMEM] * 4,
        scratch_shapes=[pltpu.SemaphoreType.DMA((10,))],
        compiler_params=params(16),
    )(
        pltpu.with_memory_space_constraint(patches, pltpu.HBM),
        pltpu.with_memory_space_constraint(cotangents, pltpu.HBM),
    )


def sums_kernel(scale, wanted, patch, cot, *refs):
    for (dtype, pieces), out in zip(wanted, refs[-len(wanted) :]):
        rows = out.shape[0] // len(pieces)
        for index, piece in enumerate(pieces):
            value = piece_sum(patch, cot, scale, *piece).astype(dtype)
            out[index * rows : (index + 1) * rows, :] = value


def sums(scale, patch, cot, after, *wanted):
    pix, half = patch.shape[2:]
    return pl.pallas_call(
        functools.partial(sums_kernel, scale, wanted),
        out_shape=[
            jax.ShapeDtypeStruct((len(pieces) * half // 2, 2 * half), dtype)
            for dtype, pieces in wanted
        ],
        in_specs=[VMEM] * 2 + [pl.BlockSpec(memory_space=pl.ANY)] * len(after),
        out_specs=[VMEM] * len(wanted),
        compiler_params=params(16),
        cost_estimate=pl.CostEstimate(
            flops=4 * len(wanted) * pix * half * half,
            bytes_accessed=8 * pix * half,
            transcendentals=0,
        ),
    )(patch, cot, *after)


def collect_kernel(own, *refs):
    *came, keep_left, keep_right, send_left, send_right = refs
    split = keep_left.shape[1]
    for columns, keep, send in (
        (slice(0, split), keep_left, send_left),
        (slice(split, own.shape[1]), keep_right, send_right),
    ):
        total = own[: keep.shape[0], columns]
        for ref in came:
            total = total + ref[:, columns].astype(F32)
        keep[...] = total
        send[...] = total.astype(BF16)


def collect(split, own, *came):
    rows, width = came[0].shape
    shapes = [(rows, split), (rows, width - split)]
    return pl.pallas_call(
        collect_kernel,
        out_shape=[jax.ShapeDtypeStruct(shape, F32) for shape in shapes]
        + [jax.ShapeDtypeStruct(shape, BF16) for shape in shapes],
        in_specs=[VMEM] * (1 + len(came)),
        out_specs=[VMEM] * 4,
        compiler_params=params(16),
    )(own, *came)


def add(*values):
    total = values[0]
    for value in values[1:]:
        total = total + value.astype(F32)
    return total


def root_kernel(most, counts_hbm, *refs):
    pieces = refs[:6]
    keep_ref, send_ref, grad, turned, left, right, m_left, m_right, s_left, s_right, counts, sem = refs[6:]
    counts_copy = pltpu.make_async_copy(counts_hbm, counts, sem)
    counts_copy.start()
    width = grad.shape[0]
    half, quarter = width // 2, width // 4
    rows = keep_ref.shape[0]
    low, high = slice(0, half), slice(half, width)
    place, column, core = (lax.axis_index(name) for name in ("z", "x", "core"))
    column_start = 0
    for index in range(2):
        own, other, far = pieces[3 * index : 3 * index + 3]
        columns = slice(column_start, column_start + own.shape[1])
        column_start += own.shape[1]
        grad[:quarter, columns] = own[...]
        grad[quarter:half, columns] = other[...]
        grad[half:, columns] = far[...]
    turned[...] = grad[...].T
    diagonal = lax.broadcasted_iota(jnp.int32, (half, half), 0) == lax.broadcasted_iota(
        jnp.int32, (half, half), 1
    )

    def dot(a, b):
        return jnp.dot(a, b, preferred_element_type=F32)

    def fill(ref, start, tiles):
        upper_left, upper_right, lower_right = (tile.astype(BF16) for tile in tiles)
        ref[start : start + half, low] = upper_left
        ref[start : start + half, high] = upper_right
        ref[start + half : start + width, low] = upper_right.T
        ref[start + half : start + width, high] = lower_right

    def factor(tiles):
        upper_left, upper_right, lower_right = tiles
        five = jnp.where(diagonal, 1.25, 0.0)
        return five - 0.25 * upper_left, -0.25 * upper_right, five - 0.25 * lower_right

    def statistics(first, second):
        tiles = [
            dot(first[a, :], second[:, b]) for a, b in ((low, low), (low, high), (high, high))
        ]
        tenth = jnp.where(diagonal, 0.1, 0.0)
        return tiles[0] + tenth, tiles[1], tiles[2] + tenth

    def spot(flip):
        row = (4 * place + 2 * (column ^ flip) + core) * rows
        part = row // quarter
        return ((part // 2 ^ core) * 2 + (part % 2 ^ place % 2)) * quarter + row % quarter

    line = lax.broadcasted_iota(jnp.int32, (2 * rows, width), 0)
    wanted = jnp.where(line < rows, spot(0) + line, spot(1) + line - rows)
    pick = lax.broadcasted_iota(jnp.int32, (2 * rows, width), 1) == wanted
    pick = jnp.where(pick, 1.0, 0.0).astype(BF16)
    picked = 2 * rows
    stats_left = statistics(grad, turned)
    stats_right = statistics(turned, grad)
    squares = [tile * tile for tile in stats_left]
    norm = jnp.sqrt(jnp.sum(squares[0] + 2.0 * squares[1] + squares[2], keepdims=True))
    scale = 2.5 / norm
    first = jnp.sqrt(jnp.sqrt(scale)).astype(BF16).astype(F32)
    tiles = [scale * tile for tile in stats_left]
    fill(m_left, 0, tiles)
    fill(left, picked, factor(tiles))
    left[:picked, :] = (first * dot(pick, left[picked:, :])).astype(BF16)
    tiles = [scale * tile for tile in stats_right]
    fill(m_right, 0, tiles)
    tiles = [tile.astype(BF16) for tile in factor(tiles)]
    fill(right, width, tiles)
    tiles = [(first * tile.astype(F32)).astype(BF16) for tile in tiles]
    right[half:width, low] = tiles[0]
    right[half:width, high] = tiles[1]
    right[:half, low] = tiles[1].T
    right[:half, high] = tiles[2]

    def square(ref):
        by_high = dot(ref[...], ref[:, high])
        return dot(ref[low, :], ref[:, low]), by_high[low], by_high[high]

    counts_copy.wait()
    count_left, count_right = counts[column, 0], counts[column, 1]
    for index in range(1, most):
        q_left, q_right = left.at[picked:, :], right.at[width:, :]
        if index == 1:
            fill(s_left, 0, square(q_left))
            fill(s_right, 0, square(q_right))
        else:
            by_high = dot(left[...], q_left[:, high])
            by_low = dot(left[: picked + half, :], q_left[:, low])
            right_by_high = dot(right[...], q_right[:, high])
            right_by_low = dot(right[half : width + half, :], q_right[:, low])
            fill(s_left, 0, (by_low[picked:], by_high[picked : picked + half], by_high[picked + half :]))
            fill(
                s_right,
                0,
                (right_by_low[half:], right_by_high[width : width + half], right_by_high[width + half :]),
            )

            def keep_if(ref, value, goes_on):
                value = value.astype(BF16)
                return value if index == 2 else jnp.where(goes_on, value, ref)

            left[:picked, low] = keep_if(left[:picked, low], by_low[:picked], index <= count_left)
            left[:picked, high] = keep_if(left[:picked, high], by_high[:picked], index <= count_left)
            goes_on = index <= count_right
            upper_right = keep_if(right[half:width, high], right_by_high[half:width], goes_on)
            right[half:width, low] = keep_if(right[half:width, low], right_by_low[:half], goes_on)
            right[half:width, high] = upper_right
            right[:half, low] = upper_right.T
            right[:half, high] = keep_if(right[:half, high], right_by_high[:half], goes_on)
        fourths = square(s_left), square(s_right)
        fill(s_left, 0, fourths[0])
        fill(s_right, 0, fourths[1])
        for fourth, moment_ref, ref, start in (
            (s_left, m_left, left, picked),
            (s_right, m_right, right, width),
        ):
            by_high = dot(fourth[...], moment_ref[:, high])
            tiles = (dot(fourth[low, :], moment_ref[:, low]), by_high[low], by_high[high])
            if index < most - 1:
                fill(moment_ref, 0, tiles)
            fill(ref, start, factor(tiles))
    final_left = dot(left[:picked, :], left[picked:, :]).astype(BF16)
    final_left = jnp.where(most <= count_left, final_left, left[:picked, :])
    by_high = dot(right[:width, :], right[width:, high])
    by_low = dot(right[half:width, :], right[width:, low])
    goes_on = most <= count_right
    upper_right = jnp.where(goes_on, by_high[half:].astype(BF16), right[half:width, high])
    right[half:width, low] = jnp.where(goes_on, by_low.astype(BF16), right[half:width, low])
    right[half:width, high] = upper_right
    right[:half, low] = upper_right.T
    right[:half, high] = jnp.where(goes_on, by_high[:half].astype(BF16), right[:half, high])
    partial_value = dot(final_left, grad[...]).astype(BF16)
    update = dot(partial_value[:, low], right[half:width, :]) + dot(
        partial_value[:, high], right[:half, :]
    )
    keep_ref[...] = update[:rows, :].astype(BF16)
    send_ref[...] = update[rows:, :].astype(BF16)


def root(counts, pieces, rows, most=4):
    width = 4 * pieces[0].shape[0]
    square = pltpu.VMEM((width, width), BF16)
    out = jax.ShapeDtypeStruct((rows, width), BF16)
    return pl.pallas_call(
        functools.partial(root_kernel, most),
        out_shape=[out, out],
        in_specs=[HBM] + [VMEM] * 6,
        out_specs=[VMEM] * 2,
        scratch_shapes=[
            square,
            square,
            pltpu.VMEM((2 * rows + width, width), BF16),
            pltpu.VMEM((2 * width, width), BF16),
            square,
            square,
            square,
            square,
            pltpu.SMEM(counts.shape, jnp.int32),
            pltpu.SemaphoreType.DMA(()),
        ],
        compiler_params=params(40),
    )(pltpu.with_memory_space_constraint(counts, pltpu.HBM), *pieces)


def place_kernel(origins, *refs):
    *pieces, out, sems = refs
    column, group = lax.axis_index("x"), lax.axis_index("group")
    copies = []
    for index, (piece, (turn, flip)) in enumerate(zip(pieces, origins)):
        number = 2 * (group ^ turn) + (column ^ flip)
        copies.append(pltpu.make_async_copy(piece, out.at[number], sems.at[index]))
        copies[-1].start()
    for copy in copies:
        copy.wait()


def place(found):
    origins, pieces = zip(*found.items())
    rows, width = pieces[0].shape
    return pl.pallas_call(
        functools.partial(place_kernel, origins),
        out_shape=jax.ShapeDtypeStruct((len(pieces), rows, width), BF16),
        in_specs=[VMEM] * len(pieces),
        out_specs=HBM,
        scratch_shapes=[pltpu.SemaphoreType.DMA((len(pieces),))],
        compiler_params=params(16),
    )(*pieces)


def shards(line, groups, patches, cotangents, newton_counts):
    blocks, pix, width = patches.shape
    half = width // 2
    rows = half // (2 * line)
    scale = 1.0 / float(pix * 4 * line * width) ** 0.5

    def swap(array, axis, mask=1):
        return lax.ppermute(array, axis, [(i, i ^ mask) for i in range(lax.axis_size(axis))])

    def swap_diagonal(array):
        moves = [(2 * z + x, 2 * (z ^ 1) + (x ^ 1)) for z in range(line) for x in range(2)]
        return lax.ppermute(array, ("z", "x"), moves)

    given_column, given_line, patch, cot = load(scale, patches, cotangents)
    came_column, came_line = swap(given_column, "core"), swap(given_line, "core")
    kept_column, kept_line, given_rest = sums(
        scale,
        patch,
        cot,
        (),
        (F32, ((1, 0, 0),)),
        (F32, ((0, 0, 1),)),
        (BF16, ((1, 1, 1), (0, 1, 0))),
    )
    came_rest = swap(given_rest, "core")
    to_column = add(kept_column, came_column).astype(BF16)
    from_column = swap(to_column, "x")
    to_line = add(kept_line, came_line).astype(BF16)
    from_line = swap(to_line, "z")
    kept_diagonal, own = sums(
        scale, patch, cot, (to_line,), (F32, ((1, 0, 1),)), (F32, ((0, 0, 0),))
    )
    quarter = own.shape[0]
    to_diagonal = add(kept_diagonal, came_rest[:quarter]).astype(BF16)
    own = add(own, came_rest[quarter:])
    from_diagonal = swap_diagonal(to_diagonal)
    left, right, send_left, send_right = collect(
        width * 3 // 4, own, from_diagonal, from_column, from_line
    )
    pieces = []
    for own, send in ((left, send_left), (right, send_right)):
        mask = 2
        while mask < line:
            own = add(own, swap(send, "z", mask))
            send = own.astype(BF16)
            mask *= 2
        own = send
        other = swap(own, "z")
        pieces += [own, other, swap(jnp.concatenate([own, other], 0), "core")]
    keep, send = root(newton_counts, pieces, rows)

    def pass_on(turn, flip):
        moves = [
            (c * groups + g, (c ^ flip) * groups + (g ^ turn))
            for c in range(2)
            for g in range(groups)
        ]
        return lax.ppermute(send if flip else keep, ("x", "group"), moves)

    others = [(turn, flip) for flip in (0, 1) for turn in range(groups) if turn or flip]
    found = {(turn, flip): pass_on(turn, flip) for turn, flip in others}
    found[0, 0] = keep
    return place(found)


def solution(mesh):
    devices, groups = mesh.shape["dp"], mesh.shape["group"]
    line = devices // 4
    cut = jax.sharding.Mesh(
        mesh.devices.reshape(line, 2, 2, groups), ("z", "x", "core", "group")
    )
    dp = ("z", "x", "core")
    placed = (P("group", dp, None), P("group", dp, None), P("group", None))
    return jax.shard_map(
        functools.partial(shards, line, groups),
        mesh=cut,
        in_specs=placed,
        out_specs=P(None, dp, None),
        check_vma=False,
    )
```

```python
import functools

import jax
import jax.numpy as jnp
from jax import lax
from jax.experimental import pallas as pl
from jax.experimental.pallas import tpu as pltpu
from jax.sharding import PartitionSpec as P

F32 = jnp.float32
BF16 = jnp.bfloat16
VMEM = pl.BlockSpec(memory_space=pltpu.VMEM)
SMEM = pl.BlockSpec(memory_space=pltpu.SMEM)
HBM = pl.BlockSpec(memory_space=pltpu.HBM)
ROWS_IN_COLS = (((0,), (0,)), ((), ()))


def params(limit):
    return pltpu.CompilerParams(vmem_limit_bytes=limit << 20)


def piece_sum(patch, cot, scale, block, side, part):
    quarter = patch.shape[3] // 2
    rows = slice(part * quarter, (part + 1) * quarter)
    terms = lax.dot_general(
        patch[block, side, :, rows], cot[block], ROWS_IN_COLS, preferred_element_type=F32
    )
    return terms * scale


def load_kernel(scale, patch_hbm, cot_hbm, given_column, given_line, patch, cot, sems):
    half = patch.shape[3]
    width = half // 2
    column, core, parity = lax.axis_index("x"), lax.axis_index("core"), lax.axis_index("z") % 2
    copies = []

    def fetch(source, target):
        copies.append(pltpu.make_async_copy(source, target, sems.at[len(copies)]))
        copies[-1].start()

    def fetch_patch(block, side, part):
        first = (core ^ side) * half + (parity ^ part) * width
        fetch(
            patch_hbm.at[column ^ block, :, pl.ds(pl.multiple_of(first, width), width)],
            patch.at[block, side, :, part * width : (part + 1) * width],
        )

    fetch(cot_hbm.at[column ^ 1], cot.at[1])
    fetch_patch(1, 1, 0)
    fetch(cot_hbm.at[column], cot.at[0])
    fetch_patch(0, 1, 1)
    needed = len(copies)
    for side in range(2):
        for block, part in ((1, 0), (0, 1), (1, 1), (0, 0)):
            if side == 0 or block == part:
                fetch_patch(block, side, part)
    for copy in copies[:2]:
        copy.wait()
    given_column[...] = piece_sum(patch, cot, scale, 1, 1, 0).astype(BF16)
    for copy in copies[2:needed]:
        copy.wait()
    given_line[...] = piece_sum(patch, cot, scale, 0, 1, 1).astype(BF16)
    for copy in copies[needed:]:
        copy.wait()


def load(scale, patches, cotangents):
    blocks, pix, width = patches.shape
    half = width // 2
    return pl.pallas_call(
        functools.partial(load_kernel, scale),
        out_shape=[
            jax.ShapeDtypeStruct((half // 2, width), BF16),
            jax.ShapeDtypeStruct((half // 2, width), BF16),
            jax.ShapeDtypeStruct((blocks, 2, pix, half), BF16),
            jax.ShapeDtypeStruct((blocks, pix, width), BF16),
        ],
        in_specs=[HBM] * 2,
        out_specs=[VMEM] * 4,
        scratch_shapes=[pltpu.SemaphoreType.DMA((10,))],
        compiler_params=params(16),
    )(
        pltpu.with_memory_space_constraint(patches, pltpu.HBM),
        pltpu.with_memory_space_constraint(cotangents, pltpu.HBM),
    )


def sums_kernel(scale, wanted, patch, cot, *refs):
    for (dtype, pieces), out in zip(wanted, refs[-len(wanted) :]):
        rows = out.shape[0] // len(pieces)
        for index, piece in enumerate(pieces):
            value = piece_sum(patch, cot, scale, *piece).astype(dtype)
            out[index * rows : (index + 1) * rows, :] = value


def sums(scale, patch, cot, after, *wanted):
    pix, half = patch.shape[2:]
    return pl.pallas_call(
        functools.partial(sums_kernel, scale, wanted),
        out_shape=[
            jax.ShapeDtypeStruct((len(pieces) * half // 2, 2 * half), dtype)
            for dtype, pieces in wanted
        ],
        in_specs=[VMEM] * 2 + [pl.BlockSpec(memory_space=pl.ANY)] * len(after),
        out_specs=[VMEM] * len(wanted),
        compiler_params=params(16),
        cost_estimate=pl.CostEstimate(
            flops=4 * len(wanted) * pix * half * half,
            bytes_accessed=8 * pix * half,
            transcendentals=0,
        ),
    )(patch, cot, *after)


def collect_kernel(own, *refs):
    *came, keep_left, keep_right, send_left, send_right = refs
    split = keep_left.shape[1]
    for columns, keep, send in (
        (slice(0, split), keep_left, send_left),
        (slice(split, own.shape[1]), keep_right, send_right),
    ):
        total = own[: keep.shape[0], columns]
        for ref in came:
            total = total + ref[:, columns].astype(F32)
        keep[...] = total
        send[...] = total.astype(BF16)


def collect(split, own, *came):
    rows, width = came[0].shape
    shapes = [(rows, split), (rows, width - split)]
    return pl.pallas_call(
        collect_kernel,
        out_shape=[jax.ShapeDtypeStruct(shape, F32) for shape in shapes]
        + [jax.ShapeDtypeStruct(shape, BF16) for shape in shapes],
        in_specs=[VMEM] * (1 + len(came)),
        out_specs=[VMEM] * 4,
        compiler_params=params(16),
    )(own, *came)


def add(*values):
    total = values[0]
    for value in values[1:]:
        total = total + value.astype(F32)
    return total


def root_kernel(most, counts_hbm, *refs):
    pieces = refs[:6]
    keep_ref, send_ref, grad, turned, left, right, m_left, m_right, s_left, s_right, counts, sem = refs[6:]
    counts_copy = pltpu.make_async_copy(counts_hbm, counts, sem)
    counts_copy.start()
    width = grad.shape[0]
    half, quarter = width // 2, width // 4
    rows = keep_ref.shape[0]
    low, high = slice(0, half), slice(half, width)
    place, column, core = (lax.axis_index(name) for name in ("z", "x", "core"))
    column_start = 0
    for index in range(2):
        own, other, far = pieces[3 * index : 3 * index + 3]
        columns = slice(column_start, column_start + own.shape[1])
        column_start += own.shape[1]
        grad[:quarter, columns] = own[...]
        grad[quarter:half, columns] = other[...]
        grad[half:, columns] = far[...]
    turned[...] = grad[...].T
    diagonal = lax.broadcasted_iota(jnp.int32, (half, half), 0) == lax.broadcasted_iota(
        jnp.int32, (half, half), 1
    )

    def dot(a, b):
        return jnp.dot(a, b, preferred_element_type=F32)

    def fill(ref, start, tiles):
        upper_left, upper_right, lower_right = (tile.astype(BF16) for tile in tiles)
        ref[start : start + half, low] = upper_left
        ref[start : start + half, high] = upper_right
        ref[start + half : start + width, low] = upper_right.T
        ref[start + half : start + width, high] = lower_right

    def factor(tiles):
        upper_left, upper_right, lower_right = tiles
        five = jnp.where(diagonal, 1.25, 0.0)
        return five - 0.25 * upper_left, -0.25 * upper_right, five - 0.25 * lower_right

    def statistics(first, second):
        tiles = [
            dot(first[a, :], second[:, b]) for a, b in ((low, low), (low, high), (high, high))
        ]
        tenth = jnp.where(diagonal, 0.1, 0.0)
        return tiles[0] + tenth, tiles[1], tiles[2] + tenth

    def spot(flip):
        row = (4 * place + 2 * (column ^ flip) + core) * rows
        part = row // quarter
        return ((part // 2 ^ core) * 2 + (part % 2 ^ place % 2)) * quarter + row % quarter

    line = lax.broadcasted_iota(jnp.int32, (2 * rows, width), 0)
    wanted = jnp.where(line < rows, spot(0) + line, spot(1) + line - rows)
    pick = lax.broadcasted_iota(jnp.int32, (2 * rows, width), 1) == wanted
    pick = jnp.where(pick, 1.0, 0.0).astype(BF16)
    picked = 2 * rows
    stats_left = statistics(grad, turned)
    stats_right = statistics(turned, grad)
    squares = [tile * tile for tile in stats_left]
    norm = jnp.sqrt(jnp.sum(squares[0] + 2.0 * squares[1] + squares[2], keepdims=True))
    scale = 2.5 / norm
    first = jnp.sqrt(jnp.sqrt(scale)).astype(BF16).astype(F32)
    tiles = [scale * tile for tile in stats_left]
    fill(m_left, 0, tiles)
    fill(left, picked, factor(tiles))
    left[:picked, :] = (first * dot(pick, left[picked:, :])).astype(BF16)
    tiles = [scale * tile for tile in stats_right]
    fill(m_right, 0, tiles)
    tiles = [tile.astype(BF16) for tile in factor(tiles)]
    fill(right, width, tiles)
    tiles = [(first * tile.astype(F32)).astype(BF16) for tile in tiles]
    right[half:width, low] = tiles[0]
    right[half:width, high] = tiles[1]
    right[:half, low] = tiles[1].T
    right[:half, high] = tiles[2]

    def square(ref):
        by_high = dot(ref[...], ref[:, high])
        return dot(ref[low, :], ref[:, low]), by_high[low], by_high[high]

    counts_copy.wait()
    count_left, count_right = counts[column, 0], counts[column, 1]
    for index in range(1, most):
        q_left, q_right = left.at[picked:, :], right.at[width:, :]
        if index == 1:
            fill(s_left, 0, square(q_left))
            fill(s_right, 0, square(q_right))
        else:
            by_high = dot(left[...], q_left[:, high])
            by_low = dot(left[: picked + half, :], q_left[:, low])
            right_by_high = dot(right[...], q_right[:, high])
            right_by_low = dot(right[half : width + half, :], q_right[:, low])
            fill(s_left, 0, (by_low[picked:], by_high[picked : picked + half], by_high[picked + half :]))
            fill(
                s_right,
                0,
                (right_by_low[half:], right_by_high[width : width + half], right_by_high[width + half :]),
            )

            def keep_if(ref, value, goes_on):
                value = value.astype(BF16)
                return value if index == 2 else jnp.where(goes_on, value, ref)

            left[:picked, low] = keep_if(left[:picked, low], by_low[:picked], index <= count_left)
            left[:picked, high] = keep_if(left[:picked, high], by_high[:picked], index <= count_left)
            goes_on = index <= count_right
            upper_right = keep_if(right[half:width, high], right_by_high[half:width], goes_on)
            right[half:width, low] = keep_if(right[half:width, low], right_by_low[:half], goes_on)
            right[half:width, high] = upper_right
            right[:half, low] = upper_right.T
            right[:half, high] = keep_if(right[:half, high], right_by_high[:half], goes_on)
        fourths = square(s_left), square(s_right)
        fill(s_left, 0, fourths[0])
        fill(s_right, 0, fourths[1])
        for fourth, moment_ref, ref, start in (
            (s_left, m_left, left, picked),
            (s_right, m_right, right, width),
        ):
            by_high = dot(fourth[...], moment_ref[:, high])
            tiles = (dot(fourth[low, :], moment_ref[:, low]), by_high[low], by_high[high])
            if index < most - 1:
                fill(moment_ref, 0, tiles)
            fill(ref, start, factor(tiles))
    final_left = dot(left[:picked, :], left[picked:, :]).astype(BF16)
    final_left = jnp.where(most <= count_left, final_left, left[:picked, :])
    by_high = dot(right[:width, :], right[width:, high])
    by_low = dot(right[half:width, :], right[width:, low])
    goes_on = most <= count_right
    upper_right = jnp.where(goes_on, by_high[half:].astype(BF16), right[half:width, high])
    right[half:width, low] = jnp.where(goes_on, by_low.astype(BF16), right[half:width, low])
    right[half:width, high] = upper_right
    right[:half, low] = upper_right.T
    right[:half, high] = jnp.where(goes_on, by_high[:half].astype(BF16), right[:half, high])
    partial_value = dot(final_left, grad[...]).astype(BF16)
    update = dot(partial_value[:, low], right[half:width, :]) + dot(
        partial_value[:, high], right[:half, :]
    )
    keep_ref[...] = update[:rows, :].astype(BF16)
    send_ref[...] = update[rows:, :].astype(BF16)


def root(counts, pieces, rows, most=4):
    width = 4 * pieces[0].shape[0]
    square = pltpu.VMEM((width, width), BF16)
    out = jax.ShapeDtypeStruct((rows, width), BF16)
    return pl.pallas_call(
        functools.partial(root_kernel, most),
        out_shape=[out, out],
        in_specs=[HBM] + [VMEM] * 6,
        out_specs=[VMEM] * 2,
        scratch_shapes=[
            square,
            square,
            pltpu.VMEM((2 * rows + width, width), BF16),
            pltpu.VMEM((2 * width, width), BF16),
            square,
            square,
            square,
            square,
            pltpu.SMEM(counts.shape, jnp.int32),
            pltpu.SemaphoreType.DMA(()),
        ],
        compiler_params=params(40),
    )(pltpu.with_memory_space_constraint(counts, pltpu.HBM), *pieces)


def place_kernel(origins, *refs):
    *pieces, out, sems = refs
    column, group = lax.axis_index("x"), lax.axis_index("group")
    copies = []
    for index, (piece, (turn, flip)) in enumerate(zip(pieces, origins)):
        number = 2 * (group ^ turn) + (column ^ flip)
        copies.append(pltpu.make_async_copy(piece, out.at[number], sems.at[index]))
        copies[-1].start()
    for copy in copies:
        copy.wait()


def place(found):
    origins, pieces = zip(*found.items())
    rows, width = pieces[0].shape
    return pl.pallas_call(
        functools.partial(place_kernel, origins),
        out_shape=jax.ShapeDtypeStruct((len(pieces), rows, width), BF16),
        in_specs=[VMEM] * len(pieces),
        out_specs=HBM,
        scratch_shapes=[pltpu.SemaphoreType.DMA((len(pieces),))],
        compiler_params=params(16),
    )(*pieces)


def shards(line, groups, patches, cotangents, newton_counts):
    blocks, pix, width = patches.shape
    half = width // 2
    rows = half // (2 * line)
    scale = 1.0 / float(pix * 4 * line * width) ** 0.5

    def swap(array, axis, mask=1):
        return lax.ppermute(array, axis, [(i, i ^ mask) for i in range(lax.axis_size(axis))])

    def swap_diagonal(array):
        moves = [(2 * z + x, 2 * (z ^ 1) + (x ^ 1)) for z in range(line) for x in range(2)]
        return lax.ppermute(array, ("z", "x"), moves)

    given_column, given_line, patch, cot = load(scale, patches, cotangents)
    came_column, came_line = swap(given_column, "core"), swap(given_line, "core")
    kept_column, kept_line, given_rest = sums(
        scale,
        patch,
        cot,
        (),
        (F32, ((1, 0, 0),)),
        (F32, ((0, 0, 1),)),
        (BF16, ((1, 1, 1), (0, 1, 0))),
    )
    came_rest = swap(given_rest, "core")
    to_column = add(kept_column, came_column).astype(BF16)
    from_column = swap(to_column, "x")
    to_line = add(kept_line, came_line).astype(BF16)
    from_line = swap(to_line, "z")
    kept_diagonal, own = sums(
        scale, patch, cot, (to_line,), (F32, ((1, 0, 1),)), (F32, ((0, 0, 0),))
    )
    quarter = own.shape[0]
    to_diagonal = add(kept_diagonal, came_rest[:quarter]).astype(BF16)
    own = add(own, came_rest[quarter:])
    from_diagonal = swap_diagonal(to_diagonal)
    left, right, send_left, send_right = collect(
        width * 3 // 4, own, from_diagonal, from_column, from_line
    )
    pieces = []
    for own, send in ((left, send_left), (right, send_right)):
        mask = 2
        while mask < line:
            own = add(own, swap(send, "z", mask))
            send = own.astype(BF16)
            mask *= 2
        own = send
        other = swap(own, "z")
        pieces += [own, other, swap(jnp.concatenate([own, other], 0), "core")]
    keep, send = root(newton_counts, pieces, rows)

    def pass_on(turn, flip):
        moves = [
            (c * groups + g, (c ^ flip) * groups + (g ^ turn))
            for c in range(2)
            for g in range(groups)
        ]
        return lax.ppermute(send if flip else keep, ("x", "group"), moves)

    others = [(turn, flip) for turn in range(groups) for flip in range(2) if turn or flip]
    found = {(turn, flip): pass_on(turn, flip) for turn, flip in others}
    found[0, 0] = keep
    return place(found)


def solution(mesh):
    devices, groups = mesh.shape["dp"], mesh.shape["group"]
    line = devices // 4
    cut = jax.sharding.Mesh(
        mesh.devices.reshape(line, 2, 2, groups), ("z", "x", "core", "group")
    )
    dp = ("z", "x", "core")
    placed = (P("group", dp, None), P("group", dp, None), P("group", None))
    return jax.shard_map(
        functools.partial(shards, line, groups),
        mesh=cut,
        in_specs=placed,
        out_specs=P(None, dp, None),
        check_vma=False,
    )
```

```python
import functools

import jax
import jax.numpy as jnp
from jax import lax
from jax.experimental import pallas as pl
from jax.experimental.pallas import tpu as pltpu
from jax.sharding import PartitionSpec as P

F32 = jnp.float32
BF16 = jnp.bfloat16
VMEM = pl.BlockSpec(memory_space=pltpu.VMEM)
SMEM = pl.BlockSpec(memory_space=pltpu.SMEM)
HBM = pl.BlockSpec(memory_space=pltpu.HBM)
ROWS_IN_COLS = (((0,), (0,)), ((), ()))


def params(limit):
    return pltpu.CompilerParams(vmem_limit_bytes=limit << 20)


def piece_sum(patch, cot, scale, block, side, part):
    quarter = patch.shape[3] // 2
    rows = slice(part * quarter, (part + 1) * quarter)
    terms = lax.dot_general(
        patch[block, side, :, rows], cot[block], ROWS_IN_COLS, preferred_element_type=F32
    )
    return terms * scale


def load_kernel(scale, patch_hbm, cot_hbm, given_column, given_line, patch, cot, sems):
    half = patch.shape[3]
    width = half // 2
    column, core, parity = lax.axis_index("x"), lax.axis_index("core"), lax.axis_index("z") % 2
    copies = []

    def fetch(source, target):
        copies.append(pltpu.make_async_copy(source, target, sems.at[len(copies)]))
        copies[-1].start()

    def fetch_patch(block, side, part):
        first = (core ^ side) * half + (parity ^ part) * width
        fetch(
            patch_hbm.at[column ^ block, :, pl.ds(pl.multiple_of(first, width), width)],
            patch.at[block, side, :, part * width : (part + 1) * width],
        )

    fetch(cot_hbm.at[column ^ 1], cot.at[1])
    fetch_patch(1, 1, 0)
    fetch(cot_hbm.at[column], cot.at[0])
    fetch_patch(0, 1, 1)
    needed = len(copies)
    for side in range(2):
        for block, part in ((1, 0), (0, 1), (1, 1), (0, 0)):
            if side == 0 or block == part:
                fetch_patch(block, side, part)
    for copy in copies[:2]:
        copy.wait()
    given_column[...] = piece_sum(patch, cot, scale, 1, 1, 0).astype(BF16)
    for copy in copies[2:needed]:
        copy.wait()
    given_line[...] = piece_sum(patch, cot, scale, 0, 1, 1).astype(BF16)
    for copy in copies[needed:]:
        copy.wait()


def load(scale, patches, cotangents):
    blocks, pix, width = patches.shape
    half = width // 2
    return pl.pallas_call(
        functools.partial(load_kernel, scale),
        out_shape=[
            jax.ShapeDtypeStruct((half // 2, width), BF16),
            jax.ShapeDtypeStruct((half // 2, width), BF16),
            jax.ShapeDtypeStruct((blocks, 2, pix, half), BF16),
            jax.ShapeDtypeStruct((blocks, pix, width), BF16),
        ],
        in_specs=[HBM] * 2,
        out_specs=[VMEM] * 4,
        scratch_shapes=[pltpu.SemaphoreType.DMA((10,))],
        compiler_params=params(16),
    )(
        pltpu.with_memory_space_constraint(patches, pltpu.HBM),
        pltpu.with_memory_space_constraint(cotangents, pltpu.HBM),
    )


def sums_kernel(scale, wanted, patch, cot, *refs):
    for (dtype, pieces), out in zip(wanted, refs[-len(wanted) :]):
        rows = out.shape[0] // len(pieces)
        for index, piece in enumerate(pieces):
            value = piece_sum(patch, cot, scale, *piece).astype(dtype)
            out[index * rows : (index + 1) * rows, :] = value


def sums(scale, patch, cot, after, *wanted):
    pix, half = patch.shape[2:]
    return pl.pallas_call(
        functools.partial(sums_kernel, scale, wanted),
        out_shape=[
            jax.ShapeDtypeStruct((len(pieces) * half // 2, 2 * half), dtype)
            for dtype, pieces in wanted
        ],
        in_specs=[VMEM] * 2 + [pl.BlockSpec(memory_space=pl.ANY)] * len(after),
        out_specs=[VMEM] * len(wanted),
        compiler_params=params(16),
        cost_estimate=pl.CostEstimate(
            flops=4 * len(wanted) * pix * half * half,
            bytes_accessed=8 * pix * half,
            transcendentals=0,
        ),
    )(patch, cot, *after)


def collect_kernel(own, *refs):
    *came, keep_left, keep_right, send_left, send_right = refs
    split = keep_left.shape[1]
    for columns, keep, send in (
        (slice(0, split), keep_left, send_left),
        (slice(split, own.shape[1]), keep_right, send_right),
    ):
        total = own[: keep.shape[0], columns]
        for ref in came:
            total = total + ref[:, columns].astype(F32)
        keep[...] = total
        send[...] = total.astype(BF16)


def collect(split, own, *came):
    rows, width = came[0].shape
    shapes = [(rows, split), (rows, width - split)]
    return pl.pallas_call(
        collect_kernel,
        out_shape=[jax.ShapeDtypeStruct(shape, F32) for shape in shapes]
        + [jax.ShapeDtypeStruct(shape, BF16) for shape in shapes],
        in_specs=[VMEM] * (1 + len(came)),
        out_specs=[VMEM] * 4,
        compiler_params=params(16),
    )(own, *came)


def add(*values):
    total = values[0]
    for value in values[1:]:
        total = total + value.astype(F32)
    return total


def root_kernel(most, counts_hbm, *refs):
    pieces = refs[:6]
    keep_ref, send_ref, grad, turned, left, right, m_left, m_right, s_left, s_right, counts, sem = refs[6:]
    counts_copy = pltpu.make_async_copy(counts_hbm, counts, sem)
    counts_copy.start()
    width = grad.shape[0]
    half, quarter = width // 2, width // 4
    rows = keep_ref.shape[0]
    low, high = slice(0, half), slice(half, width)
    place, column, core = (lax.axis_index(name) for name in ("z", "x", "core"))
    column_start = 0
    for index in range(2):
        own, other, far = pieces[3 * index : 3 * index + 3]
        columns = slice(column_start, column_start + own.shape[1])
        column_start += own.shape[1]
        grad[:quarter, columns] = own[...]
        grad[quarter:half, columns] = other[...]
        grad[half:, columns] = far[...]
    turned[...] = grad[...].T
    diagonal = lax.broadcasted_iota(jnp.int32, (half, half), 0) == lax.broadcasted_iota(
        jnp.int32, (half, half), 1
    )

    def dot(a, b):
        return jnp.dot(a, b, preferred_element_type=F32)

    def fill(ref, start, tiles):
        upper_left, upper_right, lower_right = (tile.astype(BF16) for tile in tiles)
        ref[start : start + half, low] = upper_left
        ref[start : start + half, high] = upper_right
        ref[start + half : start + width, low] = upper_right.T
        ref[start + half : start + width, high] = lower_right

    def factor(tiles):
        upper_left, upper_right, lower_right = tiles
        five = jnp.where(diagonal, 1.25, 0.0)
        return five - 0.25 * upper_left, -0.25 * upper_right, five - 0.25 * lower_right

    def statistics(first, second):
        tiles = [
            dot(first[a, :], second[:, b]) for a, b in ((low, low), (low, high), (high, high))
        ]
        tenth = jnp.where(diagonal, 0.1, 0.0)
        return tiles[0] + tenth, tiles[1], tiles[2] + tenth

    def spot(flip):
        row = (4 * place + 2 * (column ^ flip) + core) * rows
        part = row // quarter
        return ((part // 2 ^ core) * 2 + (part % 2 ^ place % 2)) * quarter + row % quarter

    line = lax.broadcasted_iota(jnp.int32, (2 * rows, width), 0)
    wanted = jnp.where(line < rows, spot(0) + line, spot(1) + line - rows)
    pick = lax.broadcasted_iota(jnp.int32, (2 * rows, width), 1) == wanted
    pick = jnp.where(pick, 1.0, 0.0).astype(BF16)
    picked = 2 * rows
    stats_left = statistics(grad, turned)
    stats_right = statistics(turned, grad)
    squares = [tile * tile for tile in stats_left]
    norm = jnp.sqrt(jnp.sum(squares[0] + 2.0 * squares[1] + squares[2], keepdims=True))
    scale = 2.5 / norm
    first = jnp.sqrt(jnp.sqrt(scale)).astype(BF16).astype(F32)
    tiles = [scale * tile for tile in stats_left]
    fill(m_left, 0, tiles)
    fill(left, picked, factor(tiles))
    left[:picked, :] = (first * dot(pick, left[picked:, :])).astype(BF16)
    tiles = [scale * tile for tile in stats_right]
    fill(m_right, 0, tiles)
    tiles = [tile.astype(BF16) for tile in factor(tiles)]
    fill(right, width, tiles)
    tiles = [(first * tile.astype(F32)).astype(BF16) for tile in tiles]
    right[half:width, low] = tiles[0]
    right[half:width, high] = tiles[1]
    right[:half, low] = tiles[1].T
    right[:half, high] = tiles[2]

    def square(ref):
        by_high = dot(ref[...], ref[:, high])
        return dot(ref[low, :], ref[:, low]), by_high[low], by_high[high]

    counts_copy.wait()
    count_left, count_right = counts[column, 0], counts[column, 1]
    for index in range(1, most):
        q_left, q_right = left.at[picked:, :], right.at[width:, :]
        if index == 1:
            fill(s_left, 0, square(q_left))
            fill(s_right, 0, square(q_right))
        else:
            by_high = dot(left[...], q_left[:, high])
            by_low = dot(left[: picked + half, :], q_left[:, low])
            right_by_high = dot(right[...], q_right[:, high])
            right_by_low = dot(right[half : width + half, :], q_right[:, low])
            fill(s_left, 0, (by_low[picked:], by_high[picked : picked + half], by_high[picked + half :]))
            fill(
                s_right,
                0,
                (right_by_low[half:], right_by_high[width : width + half], right_by_high[width + half :]),
            )

            def keep_if(ref, value, goes_on):
                value = value.astype(BF16)
                return value if index == 2 else jnp.where(goes_on, value, ref)

            left[:picked, low] = keep_if(left[:picked, low], by_low[:picked], index <= count_left)
            left[:picked, high] = keep_if(left[:picked, high], by_high[:picked], index <= count_left)
            goes_on = index <= count_right
            upper_right = keep_if(right[half:width, high], right_by_high[half:width], goes_on)
            right[half:width, low] = keep_if(right[half:width, low], right_by_low[:half], goes_on)
            right[half:width, high] = upper_right
            right[:half, low] = upper_right.T
            right[:half, high] = keep_if(right[:half, high], right_by_high[:half], goes_on)
        fourths = square(s_left), square(s_right)
        fill(s_left, 0, fourths[0])
        fill(s_right, 0, fourths[1])
        for fourth, moment_ref, ref, start in (
            (s_left, m_left, left, picked),
            (s_right, m_right, right, width),
        ):
            by_high = dot(fourth[...], moment_ref[:, high])
            tiles = (dot(fourth[low, :], moment_ref[:, low]), by_high[low], by_high[high])
            if index < most - 1:
                fill(moment_ref, 0, tiles)
            fill(ref, start, factor(tiles))
    final_left = dot(left[:picked, :], left[picked:, :]).astype(BF16)
    final_left = jnp.where(most <= count_left, final_left, left[:picked, :])
    by_high = dot(right[:width, :], right[width:, high])
    by_low = dot(right[half:width, :], right[width:, low])
    goes_on = most <= count_right
    upper_right = jnp.where(goes_on, by_high[half:].astype(BF16), right[half:width, high])
    right[half:width, low] = jnp.where(goes_on, by_low.astype(BF16), right[half:width, low])
    right[half:width, high] = upper_right
    right[:half, low] = upper_right.T
    right[:half, high] = jnp.where(goes_on, by_high[:half].astype(BF16), right[:half, high])
    partial_value = dot(final_left, grad[...]).astype(BF16)
    update = dot(partial_value[:, low], right[half:width, :]) + dot(
        partial_value[:, high], right[:half, :]
    )
    keep_ref[...] = update[:rows, :].astype(BF16)
    send_ref[...] = update[rows:, :].astype(BF16)


def root(counts, pieces, rows, most=4):
    width = 4 * pieces[0].shape[0]
    square = pltpu.VMEM((width, width), BF16)
    out = jax.ShapeDtypeStruct((rows, width), BF16)
    return pl.pallas_call(
        functools.partial(root_kernel, most),
        out_shape=[out, out],
        in_specs=[HBM] + [VMEM] * 6,
        out_specs=[VMEM] * 2,
        scratch_shapes=[
            square,
            square,
            pltpu.VMEM((2 * rows + width, width), BF16),
            pltpu.VMEM((2 * width, width), BF16),
            square,
            square,
            square,
            square,
            pltpu.SMEM(counts.shape, jnp.int32),
            pltpu.SemaphoreType.DMA(()),
        ],
        compiler_params=params(40),
    )(pltpu.with_memory_space_constraint(counts, pltpu.HBM), *pieces)


def place_kernel(origins, *refs):
    *pieces, out, sems = refs
    column, group = lax.axis_index("x"), lax.axis_index("group")
    copies = []
    for index, (piece, (turn, flip)) in enumerate(zip(pieces, origins)):
        number = 2 * (group ^ turn) + (column ^ flip)
        copies.append(pltpu.make_async_copy(piece, out.at[number], sems.at[index]))
        copies[-1].start()
    for copy in copies:
        copy.wait()


def place(found):
    origins, pieces = zip(*found.items())
    rows, width = pieces[0].shape
    return pl.pallas_call(
        functools.partial(place_kernel, origins),
        out_shape=jax.ShapeDtypeStruct((len(pieces), rows, width), BF16),
        in_specs=[VMEM] * len(pieces),
        out_specs=HBM,
        scratch_shapes=[pltpu.SemaphoreType.DMA((len(pieces),))],
        compiler_params=params(16),
    )(*pieces)


def shards(line, groups, patches, cotangents, newton_counts):
    blocks, pix, width = patches.shape
    half = width // 2
    rows = half // (2 * line)
    scale = 1.0 / float(pix * 4 * line * width) ** 0.5

    def swap(array, axis, mask=1):
        return lax.ppermute(array, axis, [(i, i ^ mask) for i in range(lax.axis_size(axis))])

    def swap_diagonal(array):
        moves = [(2 * z + x, 2 * (z ^ 1) + (x ^ 1)) for z in range(line) for x in range(2)]
        return lax.ppermute(array, ("z", "x"), moves)

    given_column, given_line, patch, cot = load(scale, patches, cotangents)
    came_column, came_line = swap(given_column, "core"), swap(given_line, "core")
    kept_column, kept_line, given_rest = sums(
        scale,
        patch,
        cot,
        (),
        (F32, ((1, 0, 0),)),
        (F32, ((0, 0, 1),)),
        (BF16, ((1, 1, 1), (0, 1, 0))),
    )
    came_rest = swap(given_rest, "core")
    to_column = add(kept_column, came_column).astype(BF16)
    from_column = swap(to_column, "x")
    to_line = add(kept_line, came_line).astype(BF16)
    from_line = swap(to_line, "z")
    kept_diagonal, own = sums(
        scale, patch, cot, (to_column,), (F32, ((1, 0, 1),)), (F32, ((0, 0, 0),))
    )
    quarter = own.shape[0]
    to_diagonal = add(kept_diagonal, came_rest[:quarter]).astype(BF16)
    own = add(own, came_rest[quarter:])
    from_diagonal = swap_diagonal(to_diagonal)
    left, right, send_left, send_right = collect(
        width * 3 // 4, own, from_diagonal, from_column, from_line
    )
    pieces = []
    for own, send in ((left, send_left), (right, send_right)):
        mask = 2
        while mask < line:
            own = add(own, swap(send, "z", mask))
            send = own.astype(BF16)
            mask *= 2
        own = send
        other = swap(own, "z")
        pieces += [own, other, swap(jnp.concatenate([own, other], 0), "core")]
    keep, send = root(newton_counts, pieces, rows)

    def pass_on(turn, flip):
        moves = [
            (c * groups + g, (c ^ flip) * groups + (g ^ turn))
            for c in range(2)
            for g in range(groups)
        ]
        return lax.ppermute(send if flip else keep, ("x", "group"), moves)

    others = [(turn, flip) for turn in range(groups) for flip in range(2) if turn or flip]
    found = {(turn, flip): pass_on(turn, flip) for turn, flip in others}
    found[0, 0] = keep
    return place(found)


def solution(mesh):
    devices, groups = mesh.shape["dp"], mesh.shape["group"]
    line = devices // 4
    cut = jax.sharding.Mesh(
        mesh.devices.reshape(line, 2, 2, groups), ("z", "x", "core", "group")
    )
    dp = ("z", "x", "core")
    placed = (P("group", dp, None), P("group", dp, None), P("group", None))
    return jax.shard_map(
        functools.partial(shards, line, groups),
        mesh=cut,
        in_specs=placed,
        out_specs=P(None, dp, None),
        check_vma=False,
    )
```

```python
import functools

import jax
import jax.numpy as jnp
from jax import lax
from jax.experimental import pallas as pl
from jax.experimental.pallas import tpu as pltpu
from jax.sharding import PartitionSpec as P

F32 = jnp.float32
BF16 = jnp.bfloat16
VMEM = pl.BlockSpec(memory_space=pltpu.VMEM)
SMEM = pl.BlockSpec(memory_space=pltpu.SMEM)
HBM = pl.BlockSpec(memory_space=pltpu.HBM)
ROWS_IN_COLS = (((0,), (0,)), ((), ()))


def params(limit):
    return pltpu.CompilerParams(vmem_limit_bytes=limit << 20)


def piece_sum(patch, cot, scale, block, side, part):
    quarter = patch.shape[3] // 2
    rows = slice(part * quarter, (part + 1) * quarter)
    terms = lax.dot_general(
        patch[block, side, :, rows], cot[block], ROWS_IN_COLS, preferred_element_type=F32
    )
    return terms * scale


def load_kernel(scale, patch_hbm, cot_hbm, given_column, given_line, patch, cot, sems):
    half = patch.shape[3]
    width = half // 2
    column, core, parity = lax.axis_index("x"), lax.axis_index("core"), lax.axis_index("z") % 2
    copies = []

    def fetch(source, target):
        copies.append(pltpu.make_async_copy(source, target, sems.at[len(copies)]))
        copies[-1].start()

    def fetch_patch(block, side, part):
        first = (core ^ side) * half + (parity ^ part) * width
        fetch(
            patch_hbm.at[column ^ block, :, pl.ds(pl.multiple_of(first, width), width)],
            patch.at[block, side, :, part * width : (part + 1) * width],
        )

    fetch(cot_hbm.at[column ^ 1], cot.at[1])
    fetch_patch(1, 1, 0)
    fetch(cot_hbm.at[column], cot.at[0])
    fetch_patch(0, 1, 1)
    needed = len(copies)
    for side in range(2):
        for block, part in ((1, 0), (0, 1), (1, 1), (0, 0)):
            if side == 0 or block == part:
                fetch_patch(block, side, part)
    for copy in copies[:2]:
        copy.wait()
    given_column[...] = piece_sum(patch, cot, scale, 1, 1, 0).astype(BF16)
    for copy in copies[2:needed]:
        copy.wait()
    given_line[...] = piece_sum(patch, cot, scale, 0, 1, 1).astype(BF16)
    for copy in copies[needed:]:
        copy.wait()


def load(scale, patches, cotangents):
    blocks, pix, width = patches.shape
    half = width // 2
    return pl.pallas_call(
        functools.partial(load_kernel, scale),
        out_shape=[
            jax.ShapeDtypeStruct((half // 2, width), BF16),
            jax.ShapeDtypeStruct((half // 2, width), BF16),
            jax.ShapeDtypeStruct((blocks, 2, pix, half), BF16),
            jax.ShapeDtypeStruct((blocks, pix, width), BF16),
        ],
        in_specs=[HBM] * 2,
        out_specs=[VMEM] * 4,
        scratch_shapes=[pltpu.SemaphoreType.DMA((10,))],
        compiler_params=params(16),
    )(
        pltpu.with_memory_space_constraint(patches, pltpu.HBM),
        pltpu.with_memory_space_constraint(cotangents, pltpu.HBM),
    )


def sums_kernel(scale, wanted, patch, cot, *refs):
    for (dtype, pieces), out in zip(wanted, refs[-len(wanted) :]):
        rows = out.shape[0] // len(pieces)
        for index, piece in enumerate(pieces):
            value = piece_sum(patch, cot, scale, *piece).astype(dtype)
            out[index * rows : (index + 1) * rows, :] = value


def sums(scale, patch, cot, after, *wanted):
    pix, half = patch.shape[2:]
    return pl.pallas_call(
        functools.partial(sums_kernel, scale, wanted),
        out_shape=[
            jax.ShapeDtypeStruct((len(pieces) * half // 2, 2 * half), dtype)
            for dtype, pieces in wanted
        ],
        in_specs=[VMEM] * 2 + [pl.BlockSpec(memory_space=pl.ANY)] * len(after),
        out_specs=[VMEM] * len(wanted),
        compiler_params=params(16),
        cost_estimate=pl.CostEstimate(
            flops=4 * len(wanted) * pix * half * half,
            bytes_accessed=8 * pix * half,
            transcendentals=0,
        ),
    )(patch, cot, *after)


def collect_kernel(own, *refs):
    *came, keep_left, keep_right, send_left, send_right = refs
    split = keep_left.shape[1]
    for columns, keep, send in (
        (slice(0, split), keep_left, send_left),
        (slice(split, own.shape[1]), keep_right, send_right),
    ):
        total = own[: keep.shape[0], columns]
        for ref in came:
            total = total + ref[:, columns].astype(F32)
        keep[...] = total
        send[...] = total.astype(BF16)


def collect(split, own, *came):
    rows, width = came[0].shape
    shapes = [(rows, split), (rows, width - split)]
    return pl.pallas_call(
        collect_kernel,
        out_shape=[jax.ShapeDtypeStruct(shape, F32) for shape in shapes]
        + [jax.ShapeDtypeStruct(shape, BF16) for shape in shapes],
        in_specs=[VMEM] * (1 + len(came)),
        out_specs=[VMEM] * 4,
        compiler_params=params(16),
    )(own, *came)


def add(*values):
    total = values[0]
    for value in values[1:]:
        total = total + value.astype(F32)
    return total


def root_kernel(most, counts_hbm, *refs):
    pieces = refs[:6]
    keep_ref, send_ref, grad, turned, left, right, m_left, m_right, s_left, s_right, counts, sem = refs[6:]
    counts_copy = pltpu.make_async_copy(counts_hbm, counts, sem)
    counts_copy.start()
    width = grad.shape[0]
    half, quarter = width // 2, width // 4
    rows = keep_ref.shape[0]
    low, high = slice(0, half), slice(half, width)
    place, column, core = (lax.axis_index(name) for name in ("z", "x", "core"))
    column_start = 0
    for index in range(2):
        own, other, far = pieces[3 * index : 3 * index + 3]
        columns = slice(column_start, column_start + own.shape[1])
        column_start += own.shape[1]
        grad[:quarter, columns] = own[...]
        grad[quarter:half, columns] = other[...]
        grad[half:, columns] = far[...]
    turned[...] = grad[...].T
    diagonal = lax.broadcasted_iota(jnp.int32, (half, half), 0) == lax.broadcasted_iota(
        jnp.int32, (half, half), 1
    )

    def dot(a, b):
        return jnp.dot(a, b, preferred_element_type=F32)

    def fill(ref, start, tiles):
        upper_left, upper_right, lower_right = (tile.astype(BF16) for tile in tiles)
        ref[start : start + half, low] = upper_left
        ref[start : start + half, high] = upper_right
        ref[start + half : start + width, low] = upper_right.T
        ref[start + half : start + width, high] = lower_right

    def factor(tiles):
        upper_left, upper_right, lower_right = tiles
        five = jnp.where(diagonal, 1.25, 0.0)
        return five - 0.25 * upper_left, -0.25 * upper_right, five - 0.25 * lower_right

    def statistics(first, second):
        tiles = [
            dot(first[a, :], second[:, b]) for a, b in ((low, low), (low, high), (high, high))
        ]
        tenth = jnp.where(diagonal, 0.1, 0.0)
        return tiles[0] + tenth, tiles[1], tiles[2] + tenth

    def spot(flip):
        row = (4 * place + 2 * (column ^ flip) + core) * rows
        part = row // quarter
        return ((part // 2 ^ core) * 2 + (part % 2 ^ place % 2)) * quarter + row % quarter

    line = lax.broadcasted_iota(jnp.int32, (2 * rows, width), 0)
    wanted = jnp.where(line < rows, spot(0) + line, spot(1) + line - rows)
    pick = lax.broadcasted_iota(jnp.int32, (2 * rows, width), 1) == wanted
    pick = jnp.where(pick, 1.0, 0.0).astype(BF16)
    picked = 2 * rows
    stats_left = statistics(grad, turned)
    stats_right = statistics(turned, grad)
    squares = [tile * tile for tile in stats_left]
    norm = jnp.sqrt(jnp.sum(squares[0] + 2.0 * squares[1] + squares[2], keepdims=True))
    scale = 2.5 / norm
    first = jnp.sqrt(jnp.sqrt(scale)).astype(BF16).astype(F32)
    tiles = [scale * tile for tile in stats_left]
    fill(m_left, 0, tiles)
    fill(left, picked, factor(tiles))
    left[:picked, :] = (first * dot(pick, left[picked:, :])).astype(BF16)
    tiles = [scale * tile for tile in stats_right]
    fill(m_right, 0, tiles)
    tiles = [tile.astype(BF16) for tile in factor(tiles)]
    fill(right, width, tiles)
    tiles = [(first * tile.astype(F32)).astype(BF16) for tile in tiles]
    right[half:width, low] = tiles[0]
    right[half:width, high] = tiles[1]
    right[:half, low] = tiles[1].T
    right[:half, high] = tiles[2]

    def square(ref):
        by_high = dot(ref[...], ref[:, high])
        return dot(ref[low, :], ref[:, low]), by_high[low], by_high[high]

    counts_copy.wait()
    count_left, count_right = counts[column, 0], counts[column, 1]
    for index in range(1, most):
        q_left, q_right = left.at[picked:, :], right.at[width:, :]
        if index == 1:
            seconds = square(q_left), square(q_right)
            fill(s_left, 0, seconds[0])
            fill(s_right, 0, seconds[1])
        else:
            by_high = dot(left[...], q_left[:, high])
            by_low = dot(left[: picked + half, :], q_left[:, low])
            right_by_high = dot(right[...], q_right[:, high])
            right_by_low = dot(right[half : width + half, :], q_right[:, low])
            fill(s_left, 0, (by_low[picked:], by_high[picked : picked + half], by_high[picked + half :]))
            fill(
                s_right,
                0,
                (right_by_low[half:], right_by_high[width : width + half], right_by_high[width + half :]),
            )

            def keep_if(ref, value, goes_on):
                value = value.astype(BF16)
                return value if index == 2 else jnp.where(goes_on, value, ref)

            left[:picked, low] = keep_if(left[:picked, low], by_low[:picked], index <= count_left)
            left[:picked, high] = keep_if(left[:picked, high], by_high[:picked], index <= count_left)
            goes_on = index <= count_right
            upper_right = keep_if(right[half:width, high], right_by_high[half:width], goes_on)
            right[half:width, low] = keep_if(right[half:width, low], right_by_low[:half], goes_on)
            right[half:width, high] = upper_right
            right[:half, low] = upper_right.T
            right[:half, high] = keep_if(right[:half, high], right_by_high[:half], goes_on)
        fourths = square(s_left), square(s_right)
        fill(s_left, 0, fourths[0])
        fill(s_right, 0, fourths[1])
        moments = []
        for fourth, moment_ref in ((s_left, m_left), (s_right, m_right)):
            by_high = dot(fourth[...], moment_ref[:, high])
            by_low = dot(fourth[low, :], moment_ref[:, low])
            moments.append((by_low, by_high[low], by_high[high]))
        fill(left, picked, factor(moments[0]))
        fill(right, width, factor(moments[1]))
        if index < most - 1:
            fill(m_left, 0, moments[0])
            fill(m_right, 0, moments[1])
    final_left = dot(left[:picked, :], left[picked:, :]).astype(BF16)
    final_left = jnp.where(most <= count_left, final_left, left[:picked, :])
    by_high = dot(right[:width, :], right[width:, high])
    by_low = dot(right[half:width, :], right[width:, low])
    goes_on = most <= count_right
    upper_right = jnp.where(goes_on, by_high[half:].astype(BF16), right[half:width, high])
    right[half:width, low] = jnp.where(goes_on, by_low.astype(BF16), right[half:width, low])
    right[half:width, high] = upper_right
    right[:half, low] = upper_right.T
    right[:half, high] = jnp.where(goes_on, by_high[:half].astype(BF16), right[:half, high])
    partial_value = dot(final_left, grad[...]).astype(BF16)
    update = dot(partial_value[:, low], right[half:width, :]) + dot(
        partial_value[:, high], right[:half, :]
    )
    keep_ref[...] = update[:rows, :].astype(BF16)
    send_ref[...] = update[rows:, :].astype(BF16)


def root(counts, pieces, rows, most=4):
    width = 4 * pieces[0].shape[0]
    square = pltpu.VMEM((width, width), BF16)
    out = jax.ShapeDtypeStruct((rows, width), BF16)
    return pl.pallas_call(
        functools.partial(root_kernel, most),
        out_shape=[out, out],
        in_specs=[HBM] + [VMEM] * 6,
        out_specs=[VMEM] * 2,
        scratch_shapes=[
            square,
            square,
            pltpu.VMEM((2 * rows + width, width), BF16),
            pltpu.VMEM((2 * width, width), BF16),
            square,
            square,
            square,
            square,
            pltpu.SMEM(counts.shape, jnp.int32),
            pltpu.SemaphoreType.DMA(()),
        ],
        compiler_params=params(40),
    )(pltpu.with_memory_space_constraint(counts, pltpu.HBM), *pieces)


def place_kernel(origins, *refs):
    *pieces, out, sems = refs
    column, group = lax.axis_index("x"), lax.axis_index("group")
    copies = []
    for index, (piece, (turn, flip)) in enumerate(zip(pieces, origins)):
        number = 2 * (group ^ turn) + (column ^ flip)
        copies.append(pltpu.make_async_copy(piece, out.at[number], sems.at[index]))
        copies[-1].start()
    for copy in copies:
        copy.wait()


def place(found):
    origins, pieces = zip(*found.items())
    rows, width = pieces[0].shape
    return pl.pallas_call(
        functools.partial(place_kernel, origins),
        out_shape=jax.ShapeDtypeStruct((len(pieces), rows, width), BF16),
        in_specs=[VMEM] * len(pieces),
        out_specs=HBM,
        scratch_shapes=[pltpu.SemaphoreType.DMA((len(pieces),))],
        compiler_params=params(16),
    )(*pieces)


def shards(line, groups, patches, cotangents, newton_counts):
    blocks, pix, width = patches.shape
    half = width // 2
    rows = half // (2 * line)
    scale = 1.0 / float(pix * 4 * line * width) ** 0.5

    def swap(array, axis, mask=1):
        return lax.ppermute(array, axis, [(i, i ^ mask) for i in range(lax.axis_size(axis))])

    def swap_diagonal(array):
        moves = [(2 * z + x, 2 * (z ^ 1) + (x ^ 1)) for z in range(line) for x in range(2)]
        return lax.ppermute(array, ("z", "x"), moves)

    given_column, given_line, patch, cot = load(scale, patches, cotangents)
    came_column, came_line = swap(given_column, "core"), swap(given_line, "core")
    kept_column, kept_line, given_rest = sums(
        scale,
        patch,
        cot,
        (),
        (F32, ((1, 0, 0),)),
        (F32, ((0, 0, 1),)),
        (BF16, ((1, 1, 1), (0, 1, 0))),
    )
    came_rest = swap(given_rest, "core")
    to_column = add(kept_column, came_column).astype(BF16)
    from_column = swap(to_column, "x")
    to_line = add(kept_line, came_line).astype(BF16)
    from_line = swap(to_line, "z")
    kept_diagonal, own = sums(
        scale, patch, cot, (to_line,), (F32, ((1, 0, 1),)), (F32, ((0, 0, 0),))
    )
    quarter = own.shape[0]
    to_diagonal = add(kept_diagonal, came_rest[:quarter]).astype(BF16)
    own = add(own, came_rest[quarter:])
    from_diagonal = swap_diagonal(to_diagonal)
    left, right, send_left, send_right = collect(
        width * 3 // 4, own, from_diagonal, from_column, from_line
    )
    pieces = []
    for own, send in ((left, send_left), (right, send_right)):
        mask = 2
        while mask < line:
            own = add(own, swap(send, "z", mask))
            send = own.astype(BF16)
            mask *= 2
        own = send
        other = swap(own, "z")
        pieces += [own, other, swap(jnp.concatenate([own, other], 0), "core")]
    keep, send = root(newton_counts, pieces, rows)

    def pass_on(turn, flip):
        moves = [
            (c * groups + g, (c ^ flip) * groups + (g ^ turn))
            for c in range(2)
            for g in range(groups)
        ]
        return lax.ppermute(send if flip else keep, ("x", "group"), moves)

    others = [(turn, flip) for turn in range(groups) for flip in range(2) if turn or flip]
    found = {(turn, flip): pass_on(turn, flip) for turn, flip in others}
    found[0, 0] = keep
    return place(found)


def solution(mesh):
    devices, groups = mesh.shape["dp"], mesh.shape["group"]
    line = devices // 4
    cut = jax.sharding.Mesh(
        mesh.devices.reshape(line, 2, 2, groups), ("z", "x", "core", "group")
    )
    dp = ("z", "x", "core")
    placed = (P("group", dp, None), P("group", dp, None), P("group", None))
    return jax.shard_map(
        functools.partial(shards, line, groups),
        mesh=cut,
        in_specs=placed,
        out_specs=P(None, dp, None),
        check_vma=False,
    )
```

```python
import functools

import jax
import jax.numpy as jnp
from jax import lax
from jax.experimental import pallas as pl
from jax.experimental.pallas import tpu as pltpu
from jax.sharding import PartitionSpec as P

F32 = jnp.float32
BF16 = jnp.bfloat16
VMEM = pl.BlockSpec(memory_space=pltpu.VMEM)
SMEM = pl.BlockSpec(memory_space=pltpu.SMEM)
HBM = pl.BlockSpec(memory_space=pltpu.HBM)
ROWS_IN_COLS = (((0,), (0,)), ((), ()))


def params(limit):
    return pltpu.CompilerParams(vmem_limit_bytes=limit << 20)


def piece_sum(patch, cot, scale, block, side, part):
    quarter = patch.shape[3] // 2
    rows = slice(part * quarter, (part + 1) * quarter)
    terms = lax.dot_general(
        patch[block, side, :, rows], cot[block], ROWS_IN_COLS, preferred_element_type=F32
    )
    return terms * scale


def load_kernel(scale, patch_hbm, cot_hbm, given_column, given_line, patch, cot, sems):
    half = patch.shape[3]
    width = half // 2
    column, core, parity = lax.axis_index("x"), lax.axis_index("core"), lax.axis_index("z") % 2
    copies = []

    def fetch(source, target):
        copies.append(pltpu.make_async_copy(source, target, sems.at[len(copies)]))
        copies[-1].start()

    def fetch_patch(block, side, part):
        first = (core ^ side) * half + (parity ^ part) * width
        fetch(
            patch_hbm.at[column ^ block, :, pl.ds(pl.multiple_of(first, width), width)],
            patch.at[block, side, :, part * width : (part + 1) * width],
        )

    fetch(cot_hbm.at[column ^ 1], cot.at[1])
    fetch_patch(1, 1, 0)
    fetch(cot_hbm.at[column], cot.at[0])
    fetch_patch(0, 1, 1)
    needed = len(copies)
    for side in range(2):
        for block, part in ((1, 0), (0, 1), (1, 1), (0, 0)):
            if side == 0 or block == part:
                fetch_patch(block, side, part)
    for copy in copies[:2]:
        copy.wait()
    given_column[...] = piece_sum(patch, cot, scale, 1, 1, 0).astype(BF16)
    for copy in copies[2:needed]:
        copy.wait()
    given_line[...] = piece_sum(patch, cot, scale, 0, 1, 1).astype(BF16)
    for copy in copies[needed:]:
        copy.wait()


def load(scale, patches, cotangents):
    blocks, pix, width = patches.shape
    half = width // 2
    return pl.pallas_call(
        functools.partial(load_kernel, scale),
        out_shape=[
            jax.ShapeDtypeStruct((half // 2, width), BF16),
            jax.ShapeDtypeStruct((half // 2, width), BF16),
            jax.ShapeDtypeStruct((blocks, 2, pix, half), BF16),
            jax.ShapeDtypeStruct((blocks, pix, width), BF16),
        ],
        in_specs=[HBM] * 2,
        out_specs=[VMEM] * 4,
        scratch_shapes=[pltpu.SemaphoreType.DMA((10,))],
        compiler_params=params(16),
    )(
        pltpu.with_memory_space_constraint(patches, pltpu.HBM),
        pltpu.with_memory_space_constraint(cotangents, pltpu.HBM),
    )


def sums_kernel(scale, wanted, patch, cot, *refs):
    for (dtype, pieces), out in zip(wanted, refs[-len(wanted) :]):
        rows = out.shape[0] // len(pieces)
        for index, piece in enumerate(pieces):
            value = piece_sum(patch, cot, scale, *piece).astype(dtype)
            out[index * rows : (index + 1) * rows, :] = value


def sums(scale, patch, cot, after, *wanted):
    pix, half = patch.shape[2:]
    return pl.pallas_call(
        functools.partial(sums_kernel, scale, wanted),
        out_shape=[
            jax.ShapeDtypeStruct((len(pieces) * half // 2, 2 * half), dtype)
            for dtype, pieces in wanted
        ],
        in_specs=[VMEM] * 2 + [pl.BlockSpec(memory_space=pl.ANY)] * len(after),
        out_specs=[VMEM] * len(wanted),
        compiler_params=params(16),
        cost_estimate=pl.CostEstimate(
            flops=4 * len(wanted) * pix * half * half,
            bytes_accessed=8 * pix * half,
            transcendentals=0,
        ),
    )(patch, cot, *after)


def collect_kernel(own, *refs):
    *came, keep_left, keep_right, send_left, send_right = refs
    split = keep_left.shape[1]
    for columns, keep, send in (
        (slice(0, split), keep_left, send_left),
        (slice(split, own.shape[1]), keep_right, send_right),
    ):
        total = own[: keep.shape[0], columns]
        for ref in came:
            total = total + ref[:, columns].astype(F32)
        keep[...] = total
        send[...] = total.astype(BF16)


def collect(split, own, *came):
    rows, width = came[0].shape
    shapes = [(rows, split), (rows, width - split)]
    return pl.pallas_call(
        collect_kernel,
        out_shape=[jax.ShapeDtypeStruct(shape, F32) for shape in shapes]
        + [jax.ShapeDtypeStruct(shape, BF16) for shape in shapes],
        in_specs=[VMEM] * (1 + len(came)),
        out_specs=[VMEM] * 4,
        compiler_params=params(16),
    )(own, *came)


def add(*values):
    total = values[0]
    for value in values[1:]:
        total = total + value.astype(F32)
    return total


def root_kernel(most, counts_hbm, *refs):
    pieces = refs[:6]
    keep_ref, send_ref, grad, turned, left, right, m_left, m_right, s_left, s_right, counts, sem = refs[6:]
    counts_copy = pltpu.make_async_copy(counts_hbm, counts, sem)
    counts_copy.start()
    width = grad.shape[0]
    half, quarter = width // 2, width // 4
    rows = keep_ref.shape[0]
    low, high = slice(0, half), slice(half, width)
    place, column, core = (lax.axis_index(name) for name in ("z", "x", "core"))
    column_start = 0
    for index in range(2):
        own, other, far = pieces[3 * index : 3 * index + 3]
        columns = slice(column_start, column_start + own.shape[1])
        column_start += own.shape[1]
        grad[:quarter, columns] = own[...]
        grad[quarter:half, columns] = other[...]
        grad[half:, columns] = far[...]
    turned[...] = grad[...].T
    diagonal = lax.broadcasted_iota(jnp.int32, (half, half), 0) == lax.broadcasted_iota(
        jnp.int32, (half, half), 1
    )

    def dot(a, b):
        return jnp.dot(a, b, preferred_element_type=F32)

    def fill(ref, start, tiles):
        upper_left, upper_right, lower_right = (tile.astype(BF16) for tile in tiles)
        ref[start : start + half, low] = upper_left
        ref[start : start + half, high] = upper_right
        ref[start + half : start + width, low] = upper_right.T
        ref[start + half : start + width, high] = lower_right

    def factor(tiles):
        upper_left, upper_right, lower_right = tiles
        five = jnp.where(diagonal, 1.25, 0.0)
        return five - 0.25 * upper_left, -0.25 * upper_right, five - 0.25 * lower_right

    def statistics(first, second):
        tiles = [
            dot(first[a, :], second[:, b]) for a, b in ((low, low), (low, high), (high, high))
        ]
        tenth = jnp.where(diagonal, 0.1, 0.0)
        return tiles[0] + tenth, tiles[1], tiles[2] + tenth

    def spot(flip):
        row = (4 * place + 2 * (column ^ flip) + core) * rows
        part = row // quarter
        return ((part // 2 ^ core) * 2 + (part % 2 ^ place % 2)) * quarter + row % quarter

    line = lax.broadcasted_iota(jnp.int32, (2 * rows, width), 0)
    wanted = jnp.where(line < rows, spot(0) + line, spot(1) + line - rows)
    pick = lax.broadcasted_iota(jnp.int32, (2 * rows, width), 1) == wanted
    pick = jnp.where(pick, 1.0, 0.0).astype(BF16)
    picked = 2 * rows
    stats_left = statistics(grad, turned)
    stats_right = statistics(turned, grad)
    squares = [tile * tile for tile in stats_left]
    norm = jnp.sqrt(jnp.sum(squares[0] + 2.0 * squares[1] + squares[2], keepdims=True))
    scale = 2.5 / norm
    first = jnp.sqrt(jnp.sqrt(scale)).astype(BF16).astype(F32)
    tiles = [scale * tile for tile in stats_left]
    fill(m_left, 0, tiles)
    fill(left, picked, factor(tiles))
    left[:picked, :] = (first * dot(pick, left[picked:, :])).astype(BF16)
    tiles = [scale * tile for tile in stats_right]
    fill(m_right, 0, tiles)
    tiles = [tile.astype(BF16) for tile in factor(tiles)]
    fill(right, width, tiles)
    tiles = [(first * tile.astype(F32)).astype(BF16) for tile in tiles]
    right[half:width, low] = tiles[0]
    right[half:width, high] = tiles[1]
    right[:half, low] = tiles[1].T
    right[:half, high] = tiles[2]

    def square(ref):
        by_high = dot(ref[...], ref[:, high])
        return dot(ref[low, :], ref[:, low]), by_high[low], by_high[high]

    counts_copy.wait()
    count_left, count_right = counts[column, 0], counts[column, 1]
    for index in range(1, most):
        q_left, q_right = left.at[picked:, :], right.at[width:, :]
        if index == 1:
            seconds = square(q_left), square(q_right)
            fill(s_left, 0, seconds[0])
            fill(s_right, 0, seconds[1])
        else:
            by_high = dot(left[...], q_left[:, high])
            by_low = dot(left[: picked + half, :], q_left[:, low])
            right_by_high = dot(right[...], q_right[:, high])
            right_by_low = dot(right[half : width + half, :], q_right[:, low])
            fill(s_left, 0, (by_low[picked:], by_high[picked : picked + half], by_high[picked + half :]))
            fill(
                s_right,
                0,
                (right_by_low[half:], right_by_high[width : width + half], right_by_high[width + half :]),
            )

            def keep_if(ref, value, goes_on):
                value = value.astype(BF16)
                return value if index == 2 else jnp.where(goes_on, value, ref)

            left[:picked, low] = keep_if(left[:picked, low], by_low[:picked], index <= count_left)
            left[:picked, high] = keep_if(left[:picked, high], by_high[:picked], index <= count_left)
            goes_on = index <= count_right
            upper_right = keep_if(right[half:width, high], right_by_high[half:width], goes_on)
            right[half:width, low] = keep_if(right[half:width, low], right_by_low[:half], goes_on)
            right[half:width, high] = upper_right
            right[:half, low] = upper_right.T
            right[:half, high] = keep_if(right[:half, high], right_by_high[:half], goes_on)
        fourths = square(s_left), square(s_right)
        fill(s_left, 0, fourths[0])
        fill(s_right, 0, fourths[1])
        moments = []
        for fourth, moment_ref in ((s_left, m_left), (s_right, m_right)):
            by_high = dot(fourth[...], moment_ref[:, high])
            by_low = dot(fourth[low, :], moment_ref[:, low])
            moments.append((by_low, by_high[low], by_high[high]))
        fill(left, picked, factor(moments[0]))
        fill(right, width, factor(moments[1]))
        if index < most - 1:
            fill(m_left, 0, moments[0])
            fill(m_right, 0, moments[1])
    final_left = dot(left[:picked, :], left[picked:, :]).astype(BF16)
    final_left = jnp.where(most <= count_left, final_left, left[:picked, :])
    by_high = dot(right[:width, :], right[width:, high])
    by_low = dot(right[half:width, :], right[width:, low])
    goes_on = most <= count_right
    upper_right = jnp.where(goes_on, by_high[half:].astype(BF16), right[half:width, high])
    right[half:width, low] = jnp.where(goes_on, by_low.astype(BF16), right[half:width, low])
    right[half:width, high] = upper_right
    right[:half, low] = upper_right.T
    right[:half, high] = jnp.where(goes_on, by_high[:half].astype(BF16), right[:half, high])
    partial_value = dot(final_left, grad[...]).astype(BF16)
    update = dot(partial_value[:, low], right[half:width, :]) + dot(
        partial_value[:, high], right[:half, :]
    )
    keep_ref[...] = update[:rows, :].astype(BF16)
    send_ref[...] = update[rows:, :].astype(BF16)


def root(counts, pieces, rows, most=4):
    width = 4 * pieces[0].shape[0]
    square = pltpu.VMEM((width, width), BF16)
    out = jax.ShapeDtypeStruct((rows, width), BF16)
    return pl.pallas_call(
        functools.partial(root_kernel, most),
        out_shape=[out, out],
        in_specs=[HBM] + [VMEM] * 6,
        out_specs=[VMEM] * 2,
        scratch_shapes=[
            square,
            square,
            pltpu.VMEM((2 * rows + width, width), BF16),
            pltpu.VMEM((2 * width, width), BF16),
            square,
            square,
            square,
            square,
            pltpu.SMEM(counts.shape, jnp.int32),
            pltpu.SemaphoreType.DMA(()),
        ],
        compiler_params=params(40),
    )(pltpu.with_memory_space_constraint(counts, pltpu.HBM), *pieces)


def place_kernel(origins, *refs):
    *pieces, out, sems = refs
    column, group = lax.axis_index("x"), lax.axis_index("group")
    copies = []
    for index, (piece, (turn, flip)) in enumerate(zip(pieces, origins)):
        number = 2 * (group ^ turn) + (column ^ flip)
        copies.append(pltpu.make_async_copy(piece, out.at[number], sems.at[index]))
        copies[-1].start()
    for copy in copies:
        copy.wait()


def place(found):
    origins, pieces = zip(*found.items())
    rows, width = pieces[0].shape
    return pl.pallas_call(
        functools.partial(place_kernel, origins),
        out_shape=jax.ShapeDtypeStruct((len(pieces), rows, width), BF16),
        in_specs=[VMEM] * len(pieces),
        out_specs=HBM,
        scratch_shapes=[pltpu.SemaphoreType.DMA((len(pieces),))],
        compiler_params=params(16),
    )(*pieces)


def shards(line, groups, patches, cotangents, newton_counts):
    blocks, pix, width = patches.shape
    half = width // 2
    rows = half // (2 * line)
    scale = 1.0 / float(pix * 4 * line * width) ** 0.5

    def swap(array, axis, mask=1):
        return lax.ppermute(array, axis, [(i, i ^ mask) for i in range(lax.axis_size(axis))])

    def swap_diagonal(array):
        moves = [(2 * z + x, 2 * (z ^ 1) + (x ^ 1)) for z in range(line) for x in range(2)]
        return lax.ppermute(array, ("z", "x"), moves)

    given_column, given_line, patch, cot = load(scale, patches, cotangents)
    came_column, came_line = swap(given_column, "core"), swap(given_line, "core")
    kept_column, kept_line, given_rest = sums(
        scale,
        patch,
        cot,
        (),
        (F32, ((1, 0, 0),)),
        (F32, ((0, 0, 1),)),
        (BF16, ((1, 1, 1), (0, 1, 0))),
    )
    came_rest = swap(given_rest, "core")
    to_column = add(kept_column, came_column).astype(BF16)
    from_column = swap(to_column, "x")
    to_line = add(kept_line, came_line).astype(BF16)
    from_line = swap(to_line, "z")
    kept_diagonal, own = sums(
        scale, patch, cot, (to_line,), (F32, ((1, 0, 1),)), (F32, ((0, 0, 0),))
    )
    quarter = own.shape[0]
    to_diagonal = add(kept_diagonal, came_rest[:quarter]).astype(BF16)
    own = add(own, came_rest[quarter:])
    from_diagonal = swap_diagonal(to_diagonal)
    left, right, send_left, send_right = collect(
        width * 3 // 4, own, from_diagonal, from_column, from_line
    )
    pieces = []
    for own, send in ((left, send_left), (right, send_right)):
        mask = 2
        while mask < line:
            own = add(own, swap(send, "z", mask))
            send = own.astype(BF16)
            mask *= 2
        own = send
        other = swap(own, "z")
        pieces += [own, other, swap(jnp.concatenate([own, other], 0), "core")]
    keep, send = root(newton_counts, pieces, rows)

    def pass_on(turn, flip):
        moves = [
            (c * groups + g, (c ^ flip) * groups + (g ^ turn))
            for c in range(2)
            for g in range(groups)
        ]
        return lax.ppermute(send if flip else keep, ("x", "group"), moves)

    others = [(turn, flip) for flip in (1, 0) for turn in range(groups - 1, -1, -1) if turn or flip]
    found = {(turn, flip): pass_on(turn, flip) for turn, flip in others}
    found[0, 0] = keep
    return place(found)


def solution(mesh):
    devices, groups = mesh.shape["dp"], mesh.shape["group"]
    line = devices // 4
    cut = jax.sharding.Mesh(
        mesh.devices.reshape(line, 2, 2, groups), ("z", "x", "core", "group")
    )
    dp = ("z", "x", "core")
    placed = (P("group", dp, None), P("group", dp, None), P("group", None))
    return jax.shard_map(
        functools.partial(shards, line, groups),
        mesh=cut,
        in_specs=placed,
        out_specs=P(None, dp, None),
        check_vma=False,
    )
```

```python
import functools

import jax
import jax.numpy as jnp
from jax import lax
from jax.experimental import pallas as pl
from jax.experimental.pallas import tpu as pltpu
from jax.sharding import PartitionSpec as P

F32 = jnp.float32
BF16 = jnp.bfloat16
VMEM = pl.BlockSpec(memory_space=pltpu.VMEM)
SMEM = pl.BlockSpec(memory_space=pltpu.SMEM)
HBM = pl.BlockSpec(memory_space=pltpu.HBM)
ROWS_IN_COLS = (((0,), (0,)), ((), ()))


def params(limit):
    return pltpu.CompilerParams(vmem_limit_bytes=limit << 20)


def piece_sum(patch, cot, scale, block, side, part):
    quarter = patch.shape[3] // 2
    rows = slice(part * quarter, (part + 1) * quarter)
    terms = lax.dot_general(
        patch[block, side, :, rows], cot[block], ROWS_IN_COLS, preferred_element_type=F32
    )
    return terms * scale


def load_kernel(scale, patch_hbm, cot_hbm, given_column, given_line, patch, cot, sems):
    half = patch.shape[3]
    width = half // 2
    column, core, parity = lax.axis_index("x"), lax.axis_index("core"), lax.axis_index("z") % 2
    copies = []

    def fetch(source, target):
        copies.append(pltpu.make_async_copy(source, target, sems.at[len(copies)]))
        copies[-1].start()

    def fetch_patch(block, side, part):
        first = (core ^ side) * half + (parity ^ part) * width
        fetch(
            patch_hbm.at[column ^ block, :, pl.ds(pl.multiple_of(first, width), width)],
            patch.at[block, side, :, part * width : (part + 1) * width],
        )

    fetch(cot_hbm.at[column ^ 1], cot.at[1])
    fetch_patch(1, 1, 0)
    fetch(cot_hbm.at[column], cot.at[0])
    fetch_patch(0, 1, 1)
    needed = len(copies)
    for side in range(2):
        for block, part in ((1, 0), (0, 1), (1, 1), (0, 0)):
            if side == 0 or block == part:
                fetch_patch(block, side, part)
    for copy in copies[:2]:
        copy.wait()
    given_column[...] = piece_sum(patch, cot, scale, 1, 1, 0).astype(BF16)
    for copy in copies[2:needed]:
        copy.wait()
    given_line[...] = piece_sum(patch, cot, scale, 0, 1, 1).astype(BF16)
    for copy in copies[needed:]:
        copy.wait()


def load(scale, patches, cotangents):
    blocks, pix, width = patches.shape
    half = width // 2
    return pl.pallas_call(
        functools.partial(load_kernel, scale),
        out_shape=[
            jax.ShapeDtypeStruct((half // 2, width), BF16),
            jax.ShapeDtypeStruct((half // 2, width), BF16),
            jax.ShapeDtypeStruct((blocks, 2, pix, half), BF16),
            jax.ShapeDtypeStruct((blocks, pix, width), BF16),
        ],
        in_specs=[HBM] * 2,
        out_specs=[VMEM] * 4,
        scratch_shapes=[pltpu.SemaphoreType.DMA((10,))],
        compiler_params=params(16),
    )(
        pltpu.with_memory_space_constraint(patches, pltpu.HBM),
        pltpu.with_memory_space_constraint(cotangents, pltpu.HBM),
    )


def sums_kernel(scale, wanted, patch, cot, *refs):
    for (dtype, pieces), out in zip(wanted, refs[-len(wanted) :]):
        rows = out.shape[0] // len(pieces)
        for index, piece in enumerate(pieces):
            value = piece_sum(patch, cot, scale, *piece).astype(dtype)
            out[index * rows : (index + 1) * rows, :] = value


def sums(scale, patch, cot, after, *wanted):
    pix, half = patch.shape[2:]
    return pl.pallas_call(
        functools.partial(sums_kernel, scale, wanted),
        out_shape=[
            jax.ShapeDtypeStruct((len(pieces) * half // 2, 2 * half), dtype)
            for dtype, pieces in wanted
        ],
        in_specs=[VMEM] * 2 + [pl.BlockSpec(memory_space=pl.ANY)] * len(after),
        out_specs=[VMEM] * len(wanted),
        compiler_params=params(16),
        cost_estimate=pl.CostEstimate(
            flops=4 * len(wanted) * pix * half * half,
            bytes_accessed=8 * pix * half,
            transcendentals=0,
        ),
    )(patch, cot, *after)


def collect_kernel(own, *refs):
    *came, keep_left, keep_right, send_left, send_right = refs
    split = keep_left.shape[1]
    for columns, keep, send in (
        (slice(0, split), keep_left, send_left),
        (slice(split, own.shape[1]), keep_right, send_right),
    ):
        total = own[: keep.shape[0], columns]
        for ref in came:
            total = total + ref[:, columns].astype(F32)
        keep[...] = total
        send[...] = total.astype(BF16)


def collect(split, own, *came):
    rows, width = came[0].shape
    shapes = [(rows, split), (rows, width - split)]
    return pl.pallas_call(
        collect_kernel,
        out_shape=[jax.ShapeDtypeStruct(shape, F32) for shape in shapes]
        + [jax.ShapeDtypeStruct(shape, BF16) for shape in shapes],
        in_specs=[VMEM] * (1 + len(came)),
        out_specs=[VMEM] * 4,
        compiler_params=params(16),
    )(own, *came)


def add(*values):
    total = values[0]
    for value in values[1:]:
        total = total + value.astype(F32)
    return total


def root_kernel(most, counts_hbm, *refs):
    pieces = refs[:6]
    keep_ref, send_ref, grad, turned, left, right, m_left, m_right, s_left, s_right, counts, sem = refs[6:]
    counts_copy = pltpu.make_async_copy(counts_hbm, counts, sem)
    counts_copy.start()
    width = grad.shape[0]
    half, quarter = width // 2, width // 4
    rows = keep_ref.shape[0]
    low, high = slice(0, half), slice(half, width)
    place, column, core = (lax.axis_index(name) for name in ("z", "x", "core"))
    column_start = 0
    for index in range(2):
        own, other, far = pieces[3 * index : 3 * index + 3]
        columns = slice(column_start, column_start + own.shape[1])
        column_start += own.shape[1]
        grad[:quarter, columns] = own[...]
        grad[quarter:half, columns] = other[...]
        grad[half:, columns] = far[...]
    turned[...] = grad[...].T
    diagonal = lax.broadcasted_iota(jnp.int32, (half, half), 0) == lax.broadcasted_iota(
        jnp.int32, (half, half), 1
    )

    def dot(a, b):
        return jnp.dot(a, b, preferred_element_type=F32)

    def fill(ref, start, tiles):
        upper_left, upper_right, lower_right = (tile.astype(BF16) for tile in tiles)
        ref[start : start + half, low] = upper_left
        ref[start : start + half, high] = upper_right
        ref[start + half : start + width, low] = upper_right.T
        ref[start + half : start + width, high] = lower_right

    def factor(tiles):
        upper_left, upper_right, lower_right = tiles
        five = jnp.where(diagonal, 1.25, 0.0)
        return five - 0.25 * upper_left, -0.25 * upper_right, five - 0.25 * lower_right

    def statistics(first, second):
        tiles = [
            dot(first[a, :], second[:, b]) for a, b in ((low, low), (low, high), (high, high))
        ]
        tenth = jnp.where(diagonal, 0.1, 0.0)
        return tiles[0] + tenth, tiles[1], tiles[2] + tenth

    def spot(flip):
        row = (4 * place + 2 * (column ^ flip) + core) * rows
        part = row // quarter
        return ((part // 2 ^ core) * 2 + (part % 2 ^ place % 2)) * quarter + row % quarter

    line = lax.broadcasted_iota(jnp.int32, (2 * rows, width), 0)
    wanted = jnp.where(line < rows, spot(0) + line, spot(1) + line - rows)
    pick = lax.broadcasted_iota(jnp.int32, (2 * rows, width), 1) == wanted
    pick = jnp.where(pick, 1.0, 0.0).astype(BF16)
    picked = 2 * rows
    stats_left = statistics(grad, turned)
    stats_right = statistics(turned, grad)
    squares = [tile * tile for tile in stats_left]
    norm = jnp.sqrt(jnp.sum(squares[0] + 2.0 * squares[1] + squares[2], keepdims=True))
    scale = 2.5 / norm
    first = jnp.sqrt(jnp.sqrt(scale)).astype(BF16).astype(F32)
    tiles = [scale * tile for tile in stats_left]
    fill(m_left, 0, tiles)
    fill(left, picked, factor(tiles))
    left[:picked, :] = (first * dot(pick, left[picked:, :])).astype(BF16)
    tiles = [scale * tile for tile in stats_right]
    fill(m_right, 0, tiles)
    tiles = [tile.astype(BF16) for tile in factor(tiles)]
    fill(right, width, tiles)
    tiles = [(first * tile.astype(F32)).astype(BF16) for tile in tiles]
    right[half:width, low] = tiles[0]
    right[half:width, high] = tiles[1]
    right[:half, low] = tiles[1].T
    right[:half, high] = tiles[2]

    def square(ref):
        by_high = dot(ref[...], ref[:, high])
        return dot(ref[low, :], ref[:, low]), by_high[low], by_high[high]

    counts_copy.wait()
    count_left, count_right = counts[column, 0], counts[column, 1]
    for index in range(1, most):
        q_left, q_right = left.at[picked:, :], right.at[width:, :]
        if index == 1:
            seconds = square(q_left), square(q_right)
            fill(s_left, 0, seconds[0])
            fill(s_right, 0, seconds[1])
        else:
            by_high = dot(left[...], q_left[:, high])
            by_low = dot(left[: picked + half, :], q_left[:, low])
            right_by_high = dot(right[...], q_right[:, high])
            right_by_low = dot(right[half : width + half, :], q_right[:, low])
            fill(s_left, 0, (by_low[picked:], by_high[picked : picked + half], by_high[picked + half :]))
            fill(
                s_right,
                0,
                (right_by_low[half:], right_by_high[width : width + half], right_by_high[width + half :]),
            )

            def keep_if(ref, value, goes_on):
                value = value.astype(BF16)
                return value if index == 2 else jnp.where(goes_on, value, ref)

            left[:picked, low] = keep_if(left[:picked, low], by_low[:picked], index <= count_left)
            left[:picked, high] = keep_if(left[:picked, high], by_high[:picked], index <= count_left)
            goes_on = index <= count_right
            upper_right = keep_if(right[half:width, high], right_by_high[half:width], goes_on)
            right[half:width, low] = keep_if(right[half:width, low], right_by_low[:half], goes_on)
            right[half:width, high] = upper_right
            right[:half, low] = upper_right.T
            right[:half, high] = keep_if(right[:half, high], right_by_high[:half], goes_on)
        fourths = square(s_left), square(s_right)
        fill(s_left, 0, fourths[0])
        fill(s_right, 0, fourths[1])
        moments = []
        for fourth, moment_ref in ((s_left, m_left), (s_right, m_right)):
            by_high = dot(fourth[...], moment_ref[:, high])
            by_low = dot(fourth[low, :], moment_ref[:, low])
            moments.append((by_low, by_high[low], by_high[high]))
        fill(left, picked, factor(moments[0]))
        fill(right, width, factor(moments[1]))
        if index < most - 1:
            fill(m_left, 0, moments[0])
            fill(m_right, 0, moments[1])
    final_left = dot(left[:picked, :], left[picked:, :]).astype(BF16)
    final_left = jnp.where(most <= count_left, final_left, left[:picked, :])
    by_high = dot(right[:width, :], right[width:, high])
    by_low = dot(right[half:width, :], right[width:, low])
    goes_on = most <= count_right
    upper_right = jnp.where(goes_on, by_high[half:].astype(BF16), right[half:width, high])
    right[half:width, low] = jnp.where(goes_on, by_low.astype(BF16), right[half:width, low])
    right[half:width, high] = upper_right
    right[:half, low] = upper_right.T
    right[:half, high] = jnp.where(goes_on, by_high[:half].astype(BF16), right[:half, high])
    partial_value = dot(final_left, grad[...]).astype(BF16)
    update = dot(partial_value[:, low], right[half:width, :]) + dot(
        partial_value[:, high], right[:half, :]
    )
    keep_ref[...] = update[:rows, :].astype(BF16)
    send_ref[...] = update[rows:, :].astype(BF16)


def root(counts, pieces, rows, most=4):
    width = 4 * pieces[0].shape[0]
    square = pltpu.VMEM((width, width), BF16)
    out = jax.ShapeDtypeStruct((rows, width), BF16)
    return pl.pallas_call(
        functools.partial(root_kernel, most),
        out_shape=[out, out],
        in_specs=[HBM] + [VMEM] * 6,
        out_specs=[VMEM] * 2,
        scratch_shapes=[
            square,
            square,
            pltpu.VMEM((2 * rows + width, width), BF16),
            pltpu.VMEM((2 * width, width), BF16),
            square,
            square,
            square,
            square,
            pltpu.SMEM(counts.shape, jnp.int32),
            pltpu.SemaphoreType.DMA(()),
        ],
        compiler_params=params(40),
    )(pltpu.with_memory_space_constraint(counts, pltpu.HBM), *pieces)


def place_kernel(origins, *refs):
    *pieces, out, sems = refs
    column, group = lax.axis_index("x"), lax.axis_index("group")
    copies = []
    for index, (piece, (turn, flip)) in enumerate(zip(pieces, origins)):
        number = 2 * (group ^ turn) + (column ^ flip)
        copies.append(pltpu.make_async_copy(piece, out.at[number], sems.at[index]))
        copies[-1].start()
    for copy in copies:
        copy.wait()


def place(found):
    origins, pieces = zip(*found.items())
    rows, width = pieces[0].shape
    return pl.pallas_call(
        functools.partial(place_kernel, origins),
        out_shape=jax.ShapeDtypeStruct((len(pieces), rows, width), BF16),
        in_specs=[VMEM] * len(pieces),
        out_specs=HBM,
        scratch_shapes=[pltpu.SemaphoreType.DMA((len(pieces),))],
        compiler_params=params(16),
    )(*pieces)


def shards(line, groups, patches, cotangents, newton_counts):
    blocks, pix, width = patches.shape
    half = width // 2
    rows = half // (2 * line)
    scale = 1.0 / float(pix * 4 * line * width) ** 0.5

    def swap(array, axis, mask=1):
        return lax.ppermute(array, axis, [(i, i ^ mask) for i in range(lax.axis_size(axis))])

    def swap_diagonal(array):
        moves = [(2 * z + x, 2 * (z ^ 1) + (x ^ 1)) for z in range(line) for x in range(2)]
        return lax.ppermute(array, ("z", "x"), moves)

    given_column, given_line, patch, cot = load(scale, patches, cotangents)
    came_column, came_line = swap(given_column, "core"), swap(given_line, "core")
    kept_column, kept_line, given_rest = sums(
        scale,
        patch,
        cot,
        (),
        (F32, ((1, 0, 0),)),
        (F32, ((0, 0, 1),)),
        (BF16, ((1, 1, 1), (0, 1, 0))),
    )
    came_rest = swap(given_rest, "core")
    to_column = add(kept_column, came_column).astype(BF16)
    from_column = swap(to_column, "x")
    to_line = add(kept_line, came_line).astype(BF16)
    from_line = swap(to_line, "z")
    kept_diagonal, own = sums(
        scale, patch, cot, (to_line,), (F32, ((1, 0, 1),)), (F32, ((0, 0, 0),))
    )
    quarter = own.shape[0]
    to_diagonal = add(kept_diagonal, came_rest[:quarter]).astype(BF16)
    own = add(own, came_rest[quarter:])
    from_diagonal = swap_diagonal(to_diagonal)
    left, right, send_left, send_right = collect(
        width // 2, own, from_diagonal, from_column, from_line
    )
    pieces = []
    for own, send in ((left, send_left), (right, send_right)):
        mask = 2
        while mask < line:
            own = add(own, swap(send, "z", mask))
            send = own.astype(BF16)
            mask *= 2
        own = send
        other = swap(own, "z")
        pieces += [own, other, swap(jnp.concatenate([own, other], 0), "core")]
    keep, send = root(newton_counts, pieces, rows)

    def pass_on(turn, flip):
        moves = [
            (c * groups + g, (c ^ flip) * groups + (g ^ turn))
            for c in range(2)
            for g in range(groups)
        ]
        return lax.ppermute(send if flip else keep, ("x", "group"), moves)

    others = [(turn, flip) for turn in range(groups) for flip in range(2) if turn or flip]
    found = {(turn, flip): pass_on(turn, flip) for turn, flip in others}
    found[0, 0] = keep
    return place(found)


def solution(mesh):
    devices, groups = mesh.shape["dp"], mesh.shape["group"]
    line = devices // 4
    cut = jax.sharding.Mesh(
        mesh.devices.reshape(line, 2, 2, groups), ("z", "x", "core", "group")
    )
    dp = ("z", "x", "core")
    placed = (P("group", dp, None), P("group", dp, None), P("group", None))
    return jax.shard_map(
        functools.partial(shards, line, groups),
        mesh=cut,
        in_specs=placed,
        out_specs=P(None, dp, None),
        check_vma=False,
    )
```

```python
import functools

import jax
import jax.numpy as jnp
from jax import lax
from jax.experimental import pallas as pl
from jax.experimental.pallas import tpu as pltpu
from jax.sharding import PartitionSpec as P

F32 = jnp.float32
BF16 = jnp.bfloat16
VMEM = pl.BlockSpec(memory_space=pltpu.VMEM)
SMEM = pl.BlockSpec(memory_space=pltpu.SMEM)
HBM = pl.BlockSpec(memory_space=pltpu.HBM)
ROWS_IN_COLS = (((0,), (0,)), ((), ()))


def params(limit):
    return pltpu.CompilerParams(vmem_limit_bytes=limit << 20)


def half_sum(patch, cot, block, side, scale, part=None):
    quarter = patch.shape[3] // 2
    rows = slice(None) if part is None else slice(part * quarter, (part + 1) * quarter)
    terms = lax.dot_general(
        patch[block, side, :, rows], cot[block], ROWS_IN_COLS, preferred_element_type=F32
    )
    return terms * scale


def load_kernel(scale, patch_hbm, cot_hbm, given_near, given_far, patch, cot, sems):
    half = patch.shape[3]
    width = half // 2
    column, core, parity = lax.axis_index("x"), lax.axis_index("core"), lax.axis_index("z") % 2
    copies = []
    quarter = given_near.shape[0]

    def fetch(source, target):
        copies.append(pltpu.make_async_copy(source, target, sems.at[len(copies)]))
        copies[-1].start()

    def fetch_patch(block, side):
        for quarter in range(2):
            first = (core ^ side) * half + (parity ^ quarter) * width
            fetch(
                patch_hbm.at[column ^ block, :, pl.ds(pl.multiple_of(first, width), width)],
                patch.at[block, side, :, quarter * width : (quarter + 1) * width],
            )

    fetch(cot_hbm.at[column ^ 1], cot.at[1])
    fetch_patch(1, 1)
    needed = len(copies)
    fetch_patch(1, 0)
    fetch(cot_hbm.at[column], cot.at[0])
    fetch_patch(0, 1)
    fetch_patch(0, 0)
    for copy in copies[:needed]:
        copy.wait()
    terms = half_sum(patch, cot, 1, 1, scale).astype(BF16)
    given_near[...] = terms[:quarter]
    given_far[...] = terms[quarter:]
    for copy in copies[needed:]:
        copy.wait()


def load(scale, patches, cotangents):
    blocks, pix, width = patches.shape
    half = width // 2
    return pl.pallas_call(
        functools.partial(load_kernel, scale),
        out_shape=[
            jax.ShapeDtypeStruct((half // 2, width), BF16),
            jax.ShapeDtypeStruct((half // 2, width), BF16),
            jax.ShapeDtypeStruct((blocks, 2, pix, half), BF16),
            jax.ShapeDtypeStruct((blocks, pix, width), BF16),
        ],
        in_specs=[HBM] * 2,
        out_specs=[VMEM] * 4,
        scratch_shapes=[pltpu.SemaphoreType.DMA((10,))],
        compiler_params=params(16),
    )(
        pltpu.with_memory_space_constraint(patches, pltpu.HBM),
        pltpu.with_memory_space_constraint(cotangents, pltpu.HBM),
    )


def sums_kernel(scale, wanted, patch, cot, *refs):
    for (block, side, part, dtype), out in zip(wanted, refs[-len(wanted) :]):
        out[...] = half_sum(patch, cot, block, side, scale, part).astype(dtype)


def sums(scale, patch, cot, after, *wanted):
    pix, half = patch.shape[2:]
    return pl.pallas_call(
        functools.partial(sums_kernel, scale, wanted),
        out_shape=[
            jax.ShapeDtypeStruct((half if part is None else half // 2, 2 * half), dtype)
            for _, _, part, dtype in wanted
        ],
        in_specs=[VMEM] * 2 + [pl.BlockSpec(memory_space=pl.ANY)] * len(after),
        out_specs=[VMEM] * len(wanted),
        compiler_params=params(16),
        cost_estimate=pl.CostEstimate(
            flops=4 * len(wanted) * pix * half * half,
            bytes_accessed=8 * pix * half,
            transcendentals=0,
        ),
    )(patch, cot, *after)


def collect_kernel(own, *refs):
    *came, keep_left, keep_right, send_left, send_right = refs
    split = keep_left.shape[1]
    for columns, keep, send in (
        (slice(0, split), keep_left, send_left),
        (slice(split, own.shape[1]), keep_right, send_right),
    ):
        total = own[: keep.shape[0], columns]
        for ref in came:
            total = total + ref[:, columns].astype(F32)
        keep[...] = total
        send[...] = total.astype(BF16)


def collect(split, own, *came):
    rows, width = came[0].shape
    shapes = [(rows, split), (rows, width - split)]
    return pl.pallas_call(
        collect_kernel,
        out_shape=[jax.ShapeDtypeStruct(shape, F32) for shape in shapes]
        + [jax.ShapeDtypeStruct(shape, BF16) for shape in shapes],
        in_specs=[VMEM] * (1 + len(came)),
        out_specs=[VMEM] * 4,
        compiler_params=params(16),
    )(own, *came)


def add(*values):
    total = values[0]
    for value in values[1:]:
        total = total + value.astype(F32)
    return total


def root_kernel(most, counts_hbm, *refs):
    pieces = refs[:6]
    keep_ref, send_ref, grad, turned, left, right, m_left, m_right, s_left, s_right, counts, sem = refs[6:]
    counts_copy = pltpu.make_async_copy(counts_hbm, counts, sem)
    counts_copy.start()
    width = grad.shape[0]
    half, quarter = width // 2, width // 4
    rows = keep_ref.shape[0]
    low, high = slice(0, half), slice(half, width)
    place, column, core = (lax.axis_index(name) for name in ("z", "x", "core"))
    column_start = 0
    for index in range(2):
        own, other, far = pieces[3 * index : 3 * index + 3]
        columns = slice(column_start, column_start + own.shape[1])
        column_start += own.shape[1]
        grad[:quarter, columns] = own[...]
        grad[quarter:half, columns] = other[...]
        grad[half:, columns] = far[...]
    turned[...] = grad[...].T
    diagonal = lax.broadcasted_iota(jnp.int32, (half, half), 0) == lax.broadcasted_iota(
        jnp.int32, (half, half), 1
    )

    def dot(a, b):
        return jnp.dot(a, b, preferred_element_type=F32)

    def fill(ref, start, tiles):
        upper_left, upper_right, lower_right = (tile.astype(BF16) for tile in tiles)
        ref[start : start + half, low] = upper_left
        ref[start : start + half, high] = upper_right
        ref[start + half : start + width, low] = upper_right.T
        ref[start + half : start + width, high] = lower_right

    def factor(tiles):
        upper_left, upper_right, lower_right = tiles
        five = jnp.where(diagonal, 1.25, 0.0)
        return five - 0.25 * upper_left, -0.25 * upper_right, five - 0.25 * lower_right

    def statistics(first, second):
        tiles = [
            dot(first[a, :], second[:, b]) for a, b in ((low, low), (low, high), (high, high))
        ]
        tenth = jnp.where(diagonal, 0.1, 0.0)
        return tiles[0] + tenth, tiles[1], tiles[2] + tenth

    def spot(flip):
        row = (4 * place + 2 * (column ^ flip) + core) * rows
        part = row // quarter
        return ((part // 2 ^ core) * 2 + (part % 2 ^ place % 2)) * quarter + row % quarter

    line = lax.broadcasted_iota(jnp.int32, (2 * rows, width), 0)
    wanted = jnp.where(line < rows, spot(0) + line, spot(1) + line - rows)
    pick = lax.broadcasted_iota(jnp.int32, (2 * rows, width), 1) == wanted
    pick = jnp.where(pick, 1.0, 0.0).astype(BF16)
    picked = 2 * rows
    stats_left = statistics(grad, turned)
    stats_right = statistics(turned, grad)
    squares = [tile * tile for tile in stats_left]
    norm = jnp.sqrt(jnp.sum(squares[0] + 2.0 * squares[1] + squares[2], keepdims=True))
    scale = 2.5 / norm
    first = jnp.sqrt(jnp.sqrt(scale)).astype(BF16).astype(F32)
    tiles = [scale * tile for tile in stats_left]
    fill(m_left, 0, tiles)
    fill(left, picked, factor(tiles))
    left[:picked, :] = (first * dot(pick, left[picked:, :])).astype(BF16)
    tiles = [scale * tile for tile in stats_right]
    fill(m_right, 0, tiles)
    tiles = [tile.astype(BF16) for tile in factor(tiles)]
    fill(right, width, tiles)
    tiles = [(first * tile.astype(F32)).astype(BF16) for tile in tiles]
    right[half:width, low] = tiles[0]
    right[half:width, high] = tiles[1]
    right[:half, low] = tiles[1].T
    right[:half, high] = tiles[2]

    def square(ref):
        by_high = dot(ref[...], ref[:, high])
        return dot(ref[low, :], ref[:, low]), by_high[low], by_high[high]

    counts_copy.wait()
    count_left, count_right = counts[column, 0], counts[column, 1]
    for index in range(1, most):
        q_left, q_right = left.at[picked:, :], right.at[width:, :]
        if index == 1:
            seconds = square(q_left), square(q_right)
            fill(s_left, 0, seconds[0])
            fill(s_right, 0, seconds[1])
        else:
            by_high = dot(left[...], q_left[:, high])
            by_low = dot(left[: picked + half, :], q_left[:, low])
            right_by_high = dot(right[...], q_right[:, high])
            right_by_low = dot(right[half : width + half, :], q_right[:, low])
            fill(s_left, 0, (by_low[picked:], by_high[picked : picked + half], by_high[picked + half :]))
            fill(
                s_right,
                0,
                (right_by_low[half:], right_by_high[width : width + half], right_by_high[width + half :]),
            )

            def keep_if(ref, value, goes_on):
                value = value.astype(BF16)
                return value if index == 2 else jnp.where(goes_on, value, ref)

            left[:picked, low] = keep_if(left[:picked, low], by_low[:picked], index <= count_left)
            left[:picked, high] = keep_if(left[:picked, high], by_high[:picked], index <= count_left)
            goes_on = index <= count_right
            upper_right = keep_if(right[half:width, high], right_by_high[half:width], goes_on)
            right[half:width, low] = keep_if(right[half:width, low], right_by_low[:half], goes_on)
            right[half:width, high] = upper_right
            right[:half, low] = upper_right.T
            right[:half, high] = keep_if(right[:half, high], right_by_high[:half], goes_on)
        fourths = square(s_left), square(s_right)
        fill(s_left, 0, fourths[0])
        fill(s_right, 0, fourths[1])
        moments = []
        for fourth, moment_ref in ((s_left, m_left), (s_right, m_right)):
            by_high = dot(fourth[...], moment_ref[:, high])
            by_low = dot(fourth[low, :], moment_ref[:, low])
            moments.append((by_low, by_high[low], by_high[high]))
        fill(left, picked, factor(moments[0]))
        fill(right, width, factor(moments[1]))
        if index < most - 1:
            fill(m_left, 0, moments[0])
            fill(m_right, 0, moments[1])
    final_left = dot(left[:picked, :], left[picked:, :]).astype(BF16)
    final_left = jnp.where(most <= count_left, final_left, left[:picked, :])
    by_high = dot(right[:width, :], right[width:, high])
    by_low = dot(right[half:width, :], right[width:, low])
    goes_on = most <= count_right
    upper_right = jnp.where(goes_on, by_high[half:].astype(BF16), right[half:width, high])
    right[half:width, low] = jnp.where(goes_on, by_low.astype(BF16), right[half:width, low])
    right[half:width, high] = upper_right
    right[:half, low] = upper_right.T
    right[:half, high] = jnp.where(goes_on, by_high[:half].astype(BF16), right[:half, high])
    partial_value = dot(final_left, grad[...]).astype(BF16)
    update = dot(partial_value[:, low], right[half:width, :]) + dot(
        partial_value[:, high], right[:half, :]
    )
    keep_ref[...] = update[:rows, :].astype(BF16)
    send_ref[...] = update[rows:, :].astype(BF16)


def root(counts, pieces, rows, most=4):
    width = 4 * pieces[0].shape[0]
    square = pltpu.VMEM((width, width), BF16)
    out = jax.ShapeDtypeStruct((rows, width), BF16)
    return pl.pallas_call(
        functools.partial(root_kernel, most),
        out_shape=[out, out],
        in_specs=[HBM] + [VMEM] * 6,
        out_specs=[VMEM] * 2,
        scratch_shapes=[
            square,
            square,
            pltpu.VMEM((2 * rows + width, width), BF16),
            pltpu.VMEM((2 * width, width), BF16),
            square,
            square,
            square,
            square,
            pltpu.SMEM(counts.shape, jnp.int32),
            pltpu.SemaphoreType.DMA(()),
        ],
        compiler_params=params(40),
    )(pltpu.with_memory_space_constraint(counts, pltpu.HBM), *pieces)


def place_kernel(origins, *refs):
    *pieces, out, sems = refs
    column, group = lax.axis_index("x"), lax.axis_index("group")
    copies = []
    for index, (piece, (turn, flip)) in enumerate(zip(pieces, origins)):
        number = 2 * (group ^ turn) + (column ^ flip)
        copies.append(pltpu.make_async_copy(piece, out.at[number], sems.at[index]))
        copies[-1].start()
    for copy in copies:
        copy.wait()


def place(found):
    origins, pieces = zip(*found.items())
    rows, width = pieces[0].shape
    return pl.pallas_call(
        functools.partial(place_kernel, origins),
        out_shape=jax.ShapeDtypeStruct((len(pieces), rows, width), BF16),
        in_specs=[VMEM] * len(pieces),
        out_specs=HBM,
        scratch_shapes=[pltpu.SemaphoreType.DMA((len(pieces),))],
        compiler_params=params(16),
    )(*pieces)


def shards(line, groups, patches, cotangents, newton_counts):
    blocks, pix, width = patches.shape
    half, quarter = width // 2, width // 4
    rows = half // (2 * line)
    scale = 1.0 / float(pix * 4 * line * width) ** 0.5

    def swap(array, axis, mask=1):
        return lax.ppermute(array, axis, [(i, i ^ mask) for i in range(lax.axis_size(axis))])

    def swap_diagonal(array):
        moves = [(2 * z + x, 2 * (z ^ 1) + (x ^ 1)) for z in range(line) for x in range(2)]
        return lax.ppermute(array, ("z", "x"), moves)

    given_near, given_far, patch, cot = load(scale, patches, cotangents)
    came_near, came_far = swap(given_near, "core"), swap(given_far, "core")
    kept_near, kept_far, given_on = sums(
        scale, patch, cot, (), (1, 0, 0, F32), (1, 0, 1, F32), (0, 1, None, BF16)
    )
    came_on = swap(given_on, "core")
    to_column = add(kept_near, came_near).astype(BF16)
    to_diagonal = add(kept_far, came_far).astype(BF16)
    from_diagonal = swap_diagonal(to_diagonal)
    from_column = swap(to_column, "x")
    (kept_on,) = sums(scale, patch, cot, (to_column,), (0, 0, None, F32))
    own = add(kept_on, came_on)
    from_line = swap(own[quarter:].astype(BF16), "z")
    left, right, send_left, send_right = collect(
        width * 3 // 4, own, from_diagonal, from_column, from_line
    )
    pieces = []
    for own, send in ((left, send_left), (right, send_right)):
        mask = 2
        while mask < line:
            own = add(own, swap(send, "z", mask))
            send = own.astype(BF16)
            mask *= 2
        own = send
        other = swap(own, "z")
        pieces += [own, other, swap(jnp.concatenate([own, other], 0), "core")]
    keep, send = root(newton_counts, pieces, rows)

    def pass_on(turn, flip):
        moves = [
            (c * groups + g, (c ^ flip) * groups + (g ^ turn))
            for c in range(2)
            for g in range(groups)
        ]
        return lax.ppermute(send if flip else keep, ("x", "group"), moves)

    others = [(turn, flip) for turn in range(groups) for flip in range(2) if turn or flip]
    found = {(turn, flip): pass_on(turn, flip) for turn, flip in others}
    found[0, 0] = keep
    return place(found)


def solution(mesh):
    devices, groups = mesh.shape["dp"], mesh.shape["group"]
    line = devices // 4
    cut = jax.sharding.Mesh(
        mesh.devices.reshape(line, 2, 2, groups), ("z", "x", "core", "group")
    )
    dp = ("z", "x", "core")
    placed = (P("group", dp, None), P("group", dp, None), P("group", None))
    return jax.shard_map(
        functools.partial(shards, line, groups),
        mesh=cut,
        in_specs=placed,
        out_specs=P(None, dp, None),
        check_vma=False,
    )
```

```python
import functools

import jax
import jax.numpy as jnp
from jax import lax
from jax.experimental import pallas as pl
from jax.experimental.pallas import tpu as pltpu
from jax.sharding import PartitionSpec as P

F32 = jnp.float32
BF16 = jnp.bfloat16
VMEM = pl.BlockSpec(memory_space=pltpu.VMEM)
SMEM = pl.BlockSpec(memory_space=pltpu.SMEM)
HBM = pl.BlockSpec(memory_space=pltpu.HBM)
ROWS_IN_COLS = (((0,), (0,)), ((), ()))


def params(limit):
    return pltpu.CompilerParams(vmem_limit_bytes=limit << 20)


def piece_sum(patch, cot, scale, block, side, part):
    quarter = patch.shape[3] // 2
    rows = slice(part * quarter, (part + 1) * quarter)
    terms = lax.dot_general(
        patch[block, side, :, rows], cot[block], ROWS_IN_COLS, preferred_element_type=F32
    )
    return terms * scale


def load_kernel(scale, patch_hbm, cot_hbm, given_column, given_line, patch, cot, sems):
    half = patch.shape[3]
    width = half // 2
    column, core, parity = lax.axis_index("x"), lax.axis_index("core"), lax.axis_index("z") % 2
    copies = []

    def fetch(source, target):
        copies.append(pltpu.make_async_copy(source, target, sems.at[len(copies)]))
        copies[-1].start()

    def fetch_patch(block, side, part):
        first = (core ^ side) * half + (parity ^ part) * width
        fetch(
            patch_hbm.at[column ^ block, :, pl.ds(pl.multiple_of(first, width), width)],
            patch.at[block, side, :, part * width : (part + 1) * width],
        )

    fetch(cot_hbm.at[column ^ 1], cot.at[1])
    fetch_patch(1, 1, 0)
    fetch(cot_hbm.at[column], cot.at[0])
    fetch_patch(0, 1, 1)
    needed = len(copies)
    for side in range(2):
        for block, part in ((1, 0), (0, 1), (1, 1), (0, 0)):
            if side == 0 or block == part:
                fetch_patch(block, side, part)
    for copy in copies[:2]:
        copy.wait()
    given_column[...] = piece_sum(patch, cot, scale, 1, 1, 0).astype(BF16)
    for copy in copies[2:needed]:
        copy.wait()
    given_line[...] = piece_sum(patch, cot, scale, 0, 1, 1).astype(BF16)
    for copy in copies[needed:]:
        copy.wait()


def load(scale, patches, cotangents):
    blocks, pix, width = patches.shape
    half = width // 2
    return pl.pallas_call(
        functools.partial(load_kernel, scale),
        out_shape=[
            jax.ShapeDtypeStruct((half // 2, width), BF16),
            jax.ShapeDtypeStruct((half // 2, width), BF16),
            jax.ShapeDtypeStruct((blocks, 2, pix, half), BF16),
            jax.ShapeDtypeStruct((blocks, pix, width), BF16),
        ],
        in_specs=[HBM] * 2,
        out_specs=[VMEM] * 4,
        scratch_shapes=[pltpu.SemaphoreType.DMA((10,))],
        compiler_params=params(16),
    )(
        pltpu.with_memory_space_constraint(patches, pltpu.HBM),
        pltpu.with_memory_space_constraint(cotangents, pltpu.HBM),
    )


def sums_kernel(scale, wanted, patch, cot, *refs):
    for (dtype, pieces), out in zip(wanted, refs[-len(wanted) :]):
        rows = out.shape[0] // len(pieces)
        for index, piece in enumerate(pieces):
            value = piece_sum(patch, cot, scale, *piece).astype(dtype)
            out[index * rows : (index + 1) * rows, :] = value


def sums(scale, patch, cot, after, *wanted):
    pix, half = patch.shape[2:]
    return pl.pallas_call(
        functools.partial(sums_kernel, scale, wanted),
        out_shape=[
            jax.ShapeDtypeStruct((len(pieces) * half // 2, 2 * half), dtype)
            for dtype, pieces in wanted
        ],
        in_specs=[VMEM] * 2 + [pl.BlockSpec(memory_space=pl.ANY)] * len(after),
        out_specs=[VMEM] * len(wanted),
        compiler_params=params(16),
        cost_estimate=pl.CostEstimate(
            flops=4 * len(wanted) * pix * half * half,
            bytes_accessed=8 * pix * half,
            transcendentals=0,
        ),
    )(patch, cot, *after)


def collect_kernel(own, *refs):
    *came, keep_left, keep_right, send_left, send_right = refs
    split = keep_left.shape[1]
    for columns, keep, send in (
        (slice(0, split), keep_left, send_left),
        (slice(split, own.shape[1]), keep_right, send_right),
    ):
        total = own[: keep.shape[0], columns]
        for ref in came:
            total = total + ref[:, columns].astype(F32)
        keep[...] = total
        send[...] = total.astype(BF16)


def collect(split, own, *came):
    rows, width = came[0].shape
    shapes = [(rows, split), (rows, width - split)]
    return pl.pallas_call(
        collect_kernel,
        out_shape=[jax.ShapeDtypeStruct(shape, F32) for shape in shapes]
        + [jax.ShapeDtypeStruct(shape, BF16) for shape in shapes],
        in_specs=[VMEM] * (1 + len(came)),
        out_specs=[VMEM] * 4,
        compiler_params=params(16),
    )(own, *came)


def add(*values):
    total = values[0]
    for value in values[1:]:
        total = total + value.astype(F32)
    return total


def root_kernel(most, counts_hbm, *refs):
    pieces = refs[:6]
    keep_ref, send_ref, grad, turned, left, right, m_left, m_right, s_left, s_right, counts, sem = refs[6:]
    counts_copy = pltpu.make_async_copy(counts_hbm, counts, sem)
    counts_copy.start()
    width = grad.shape[0]
    half, quarter = width // 2, width // 4
    rows = keep_ref.shape[0]
    low, high = slice(0, half), slice(half, width)
    place, column, core = (lax.axis_index(name) for name in ("z", "x", "core"))
    column_start = 0
    for index in range(2):
        own, other, far = pieces[3 * index : 3 * index + 3]
        columns = slice(column_start, column_start + own.shape[1])
        column_start += own.shape[1]
        grad[:quarter, columns] = own[...]
        grad[quarter:half, columns] = other[...]
        grad[half:, columns] = far[...]
    turned[...] = grad[...].T
    diagonal = lax.broadcasted_iota(jnp.int32, (half, half), 0) == lax.broadcasted_iota(
        jnp.int32, (half, half), 1
    )

    def dot(a, b):
        return jnp.dot(a, b, preferred_element_type=F32)

    def fill(ref, start, tiles):
        upper_left, upper_right, lower_right = (tile.astype(BF16) for tile in tiles)
        ref[start : start + half, low] = upper_left
        ref[start : start + half, high] = upper_right
        ref[start + half : start + width, low] = upper_right.T
        ref[start + half : start + width, high] = lower_right

    def factor(tiles):
        upper_left, upper_right, lower_right = tiles
        five = jnp.where(diagonal, 1.25, 0.0)
        return five - 0.25 * upper_left, -0.25 * upper_right, five - 0.25 * lower_right

    def statistics(first, second):
        tiles = [
            dot(first[a, :], second[:, b]) for a, b in ((low, low), (low, high), (high, high))
        ]
        tenth = jnp.where(diagonal, 0.1, 0.0)
        return tiles[0] + tenth, tiles[1], tiles[2] + tenth

    def spot(flip):
        row = (4 * place + 2 * (column ^ flip) + core) * rows
        part = row // quarter
        return ((part // 2 ^ core) * 2 + (part % 2 ^ place % 2)) * quarter + row % quarter

    line = lax.broadcasted_iota(jnp.int32, (2 * rows, width), 0)
    wanted = jnp.where(line < rows, spot(0) + line, spot(1) + line - rows)
    pick = lax.broadcasted_iota(jnp.int32, (2 * rows, width), 1) == wanted
    pick = jnp.where(pick, 1.0, 0.0).astype(BF16)
    picked = 2 * rows
    stats_left = statistics(grad, turned)
    stats_right = statistics(turned, grad)
    squares = [tile * tile for tile in stats_left]
    norm = jnp.sqrt(jnp.sum(squares[0] + 2.0 * squares[1] + squares[2], keepdims=True))
    scale = 2.5 / norm
    first = jnp.sqrt(jnp.sqrt(scale)).astype(BF16).astype(F32)
    tiles = [scale * tile for tile in stats_left]
    fill(m_left, 0, tiles)
    fill(left, picked, factor(tiles))
    left[:picked, :] = (first * dot(pick, left[picked:, :])).astype(BF16)
    tiles = [scale * tile for tile in stats_right]
    fill(m_right, 0, tiles)
    tiles = [tile.astype(BF16) for tile in factor(tiles)]
    fill(right, width, tiles)
    tiles = [(first * tile.astype(F32)).astype(BF16) for tile in tiles]
    right[half:width, low] = tiles[0]
    right[half:width, high] = tiles[1]
    right[:half, low] = tiles[1].T
    right[:half, high] = tiles[2]

    def square(ref):
        by_high = dot(ref[...], ref[:, high])
        return dot(ref[low, :], ref[:, low]), by_high[low], by_high[high]

    counts_copy.wait()
    count_left, count_right = counts[column, 0], counts[column, 1]
    for index in range(1, most):
        q_left, q_right = left.at[picked:, :], right.at[width:, :]
        if index == 1:
            seconds = square(q_left), square(q_right)
            fill(s_left, 0, seconds[0])
            fill(s_right, 0, seconds[1])
        else:
            by_high = dot(left[...], q_left[:, high])
            by_low = dot(left[: picked + half, :], q_left[:, low])
            right_by_high = dot(right[...], q_right[:, high])
            right_by_low = dot(right[half : width + half, :], q_right[:, low])
            fill(s_left, 0, (by_low[picked:], by_high[picked : picked + half], by_high[picked + half :]))
            fill(
                s_right,
                0,
                (right_by_low[half:], right_by_high[width : width + half], right_by_high[width + half :]),
            )

            def keep_if(ref, value, goes_on):
                value = value.astype(BF16)
                return value if index == 2 else jnp.where(goes_on, value, ref)

            left[:picked, low] = keep_if(left[:picked, low], by_low[:picked], index <= count_left)
            left[:picked, high] = keep_if(left[:picked, high], by_high[:picked], index <= count_left)
            goes_on = index <= count_right
            upper_right = keep_if(right[half:width, high], right_by_high[half:width], goes_on)
            right[half:width, low] = keep_if(right[half:width, low], right_by_low[:half], goes_on)
            right[half:width, high] = upper_right
            right[:half, low] = upper_right.T
            right[:half, high] = keep_if(right[:half, high], right_by_high[:half], goes_on)
        fourths = square(s_left), square(s_right)
        fill(s_left, 0, fourths[0])
        fill(s_right, 0, fourths[1])
        moments = []
        for fourth, moment_ref in ((s_left, m_left), (s_right, m_right)):
            by_high = dot(fourth[...], moment_ref[:, high])
            by_low = dot(fourth[low, :], moment_ref[:, low])
            moments.append((by_low, by_high[low], by_high[high]))
        fill(left, picked, factor(moments[0]))
        fill(right, width, factor(moments[1]))
        if index < most - 1:
            fill(m_left, 0, moments[0])
            fill(m_right, 0, moments[1])
    final_left = dot(left[:picked, :], left[picked:, :]).astype(BF16)
    final_left = jnp.where(most <= count_left, final_left, left[:picked, :])
    by_high = dot(right[:width, :], right[width:, high])
    by_low = dot(right[half:width, :], right[width:, low])
    goes_on = most <= count_right
    upper_right = jnp.where(goes_on, by_high[half:].astype(BF16), right[half:width, high])
    right[half:width, low] = jnp.where(goes_on, by_low.astype(BF16), right[half:width, low])
    right[half:width, high] = upper_right
    right[:half, low] = upper_right.T
    right[:half, high] = jnp.where(goes_on, by_high[:half].astype(BF16), right[:half, high])
    partial_value = dot(final_left, grad[...]).astype(BF16)
    update = dot(partial_value[:, low], right[half:width, :]) + dot(
        partial_value[:, high], right[:half, :]
    )
    keep_ref[...] = update[:rows, :].astype(BF16)
    send_ref[...] = update[rows:, :].astype(BF16)


def root(counts, pieces, rows, most=4):
    width = 4 * pieces[0].shape[0]
    square = pltpu.VMEM((width, width), BF16)
    out = jax.ShapeDtypeStruct((rows, width), BF16)
    return pl.pallas_call(
        functools.partial(root_kernel, most),
        out_shape=[out, out],
        in_specs=[HBM] + [VMEM] * 6,
        out_specs=[VMEM] * 2,
        scratch_shapes=[
            square,
            square,
            pltpu.VMEM((2 * rows + width, width), BF16),
            pltpu.VMEM((2 * width, width), BF16),
            square,
            square,
            square,
            square,
            pltpu.SMEM(counts.shape, jnp.int32),
            pltpu.SemaphoreType.DMA(()),
        ],
        compiler_params=params(40),
    )(pltpu.with_memory_space_constraint(counts, pltpu.HBM), *pieces)


def place_kernel(origins, *refs):
    *pieces, out, sems = refs
    column, group = lax.axis_index("x"), lax.axis_index("group")
    core = lax.axis_index("core")
    copies = []
    for index, (piece, (turn, flip, by_core)) in enumerate(zip(pieces, origins)):
        if by_core:
            turn, flip = turn ^ core, flip ^ core
        number = 2 * (group ^ turn) + (column ^ flip)
        copies.append(pltpu.make_async_copy(piece, out.at[number], sems.at[index]))
        copies[-1].start()
    for copy in copies:
        copy.wait()


def place(found):
    origins, pieces = zip(*found.items())
    rows, width = pieces[0].shape
    return pl.pallas_call(
        functools.partial(place_kernel, origins),
        out_shape=jax.ShapeDtypeStruct((len(pieces), rows, width), BF16),
        in_specs=[VMEM] * len(pieces),
        out_specs=HBM,
        scratch_shapes=[pltpu.SemaphoreType.DMA((len(pieces),))],
        compiler_params=params(16),
    )(*pieces)


def shards(line, groups, patches, cotangents, newton_counts):
    blocks, pix, width = patches.shape
    half = width // 2
    rows = half // (2 * line)
    scale = 1.0 / float(pix * 4 * line * width) ** 0.5

    def swap(array, axis, mask=1):
        return lax.ppermute(array, axis, [(i, i ^ mask) for i in range(lax.axis_size(axis))])

    def swap_diagonal(array):
        moves = [(2 * z + x, 2 * (z ^ 1) + (x ^ 1)) for z in range(line) for x in range(2)]
        return lax.ppermute(array, ("z", "x"), moves)

    given_column, given_line, patch, cot = load(scale, patches, cotangents)
    came_column, came_line = swap(given_column, "core"), swap(given_line, "core")
    kept_column, kept_line, given_rest = sums(
        scale,
        patch,
        cot,
        (),
        (F32, ((1, 0, 0),)),
        (F32, ((0, 0, 1),)),
        (BF16, ((1, 1, 1), (0, 1, 0))),
    )
    came_rest = swap(given_rest, "core")
    to_column = add(kept_column, came_column).astype(BF16)
    from_column = swap(to_column, "x")
    to_line = add(kept_line, came_line).astype(BF16)
    from_line = swap(to_line, "z")
    kept_diagonal, own = sums(
        scale, patch, cot, (to_line,), (F32, ((1, 0, 1),)), (F32, ((0, 0, 0),))
    )
    quarter = own.shape[0]
    to_diagonal = add(kept_diagonal, came_rest[:quarter]).astype(BF16)
    own = add(own, came_rest[quarter:])
    from_diagonal = swap_diagonal(to_diagonal)
    left, right, send_left, send_right = collect(
        width * 3 // 4, own, from_diagonal, from_column, from_line
    )
    pieces = []
    for own, send in ((left, send_left), (right, send_right)):
        mask = 2
        while mask < line:
            own = add(own, swap(send, "z", mask))
            send = own.astype(BF16)
            mask *= 2
        own = send
        other = swap(own, "z")
        pieces += [own, other, swap(jnp.concatenate([own, other], 0), "core")]
    keep, send = root(newton_counts, pieces, rows)

    def pass_on(turn, flip):
        moves = [
            (c * groups + g, (c ^ flip) * groups + (g ^ turn))
            for c in range(2)
            for g in range(groups)
        ]
        return lax.ppermute(send if flip else keep, ("x", "group"), moves)

    if groups == 2:
        first_core = lax.axis_index("core") == 0
        payloads = jnp.where(first_core, send, keep), jnp.where(first_core, keep, send)
        found = {(1, 1, False): pass_on(1, 1)}
        for order, payload in enumerate(payloads):
            moves = []
            for c in range(2):
                for core in range(2):
                    for g in range(2):
                        to = (c ^ 1, g) if core == order else (c, g ^ 1)
                        moves.append((4 * c + 2 * core + g, 4 * to[0] + 2 * core + to[1]))
            found[order, 1 - order, True] = lax.ppermute(payload, ("x", "core", "group"), moves)
    else:
        others = [(turn, flip) for turn in range(groups) for flip in range(2) if turn or flip]
        found = {(turn, flip, False): pass_on(turn, flip) for turn, flip in others}
    found[0, 0, False] = keep
    return place(found)


def solution(mesh):
    devices, groups = mesh.shape["dp"], mesh.shape["group"]
    line = devices // 4
    cut = jax.sharding.Mesh(
        mesh.devices.reshape(line, 2, 2, groups), ("z", "x", "core", "group")
    )
    dp = ("z", "x", "core")
    placed = (P("group", dp, None), P("group", dp, None), P("group", None))
    return jax.shard_map(
        functools.partial(shards, line, groups),
        mesh=cut,
        in_specs=placed,
        out_specs=P(None, dp, None),
        check_vma=False,
    )
```

```python
import functools

import jax
import jax.numpy as jnp
from jax import lax
from jax.experimental import pallas as pl
from jax.experimental.pallas import tpu as pltpu
from jax.sharding import PartitionSpec as P

F32 = jnp.float32
BF16 = jnp.bfloat16
VMEM = pl.BlockSpec(memory_space=pltpu.VMEM)
SMEM = pl.BlockSpec(memory_space=pltpu.SMEM)
HBM = pl.BlockSpec(memory_space=pltpu.HBM)
ROWS_IN_COLS = (((0,), (0,)), ((), ()))


def params(limit):
    return pltpu.CompilerParams(vmem_limit_bytes=limit << 20)


def piece_sum(patch, cot, scale, block, side, part):
    quarter = patch.shape[3] // 2
    rows = slice(part * quarter, (part + 1) * quarter)
    terms = lax.dot_general(
        patch[block, side, :, rows], cot[block], ROWS_IN_COLS, preferred_element_type=F32
    )
    return terms * scale


def load_kernel(scale, patch_hbm, cot_hbm, given_column, given_line, patch, cot, sems):
    half = patch.shape[3]
    width = half // 2
    column, core, parity = lax.axis_index("x"), lax.axis_index("core"), lax.axis_index("z") % 2
    copies = []

    def fetch(source, target):
        copies.append(pltpu.make_async_copy(source, target, sems.at[len(copies)]))
        copies[-1].start()

    def fetch_patch(block, side, part):
        first = (core ^ side) * half + (parity ^ part) * width
        fetch(
            patch_hbm.at[column ^ block, :, pl.ds(pl.multiple_of(first, width), width)],
            patch.at[block, side, :, part * width : (part + 1) * width],
        )

    fetch(cot_hbm.at[column ^ 1], cot.at[1])
    fetch_patch(1, 1, 0)
    fetch(cot_hbm.at[column], cot.at[0])
    fetch_patch(0, 1, 1)
    needed = len(copies)
    for side in range(2):
        for block, part in ((1, 0), (0, 1), (1, 1), (0, 0)):
            if side == 0 or block == part:
                fetch_patch(block, side, part)
    for copy in copies[:2]:
        copy.wait()
    given_column[...] = piece_sum(patch, cot, scale, 1, 1, 0).astype(BF16)
    for copy in copies[2:needed]:
        copy.wait()
    given_line[...] = piece_sum(patch, cot, scale, 0, 1, 1).astype(BF16)
    for copy in copies[needed:]:
        copy.wait()


def load(scale, patches, cotangents):
    blocks, pix, width = patches.shape
    half = width // 2
    return pl.pallas_call(
        functools.partial(load_kernel, scale),
        out_shape=[
            jax.ShapeDtypeStruct((half // 2, width), BF16),
            jax.ShapeDtypeStruct((half // 2, width), BF16),
            jax.ShapeDtypeStruct((blocks, 2, pix, half), BF16),
            jax.ShapeDtypeStruct((blocks, pix, width), BF16),
        ],
        in_specs=[HBM] * 2,
        out_specs=[VMEM] * 4,
        scratch_shapes=[pltpu.SemaphoreType.DMA((10,))],
        compiler_params=params(16),
    )(
        pltpu.with_memory_space_constraint(patches, pltpu.HBM),
        pltpu.with_memory_space_constraint(cotangents, pltpu.HBM),
    )


def sums_kernel(scale, wanted, patch, cot, *refs):
    for (dtype, pieces), out in zip(wanted, refs[-len(wanted) :]):
        rows = out.shape[0] // len(pieces)
        for index, piece in enumerate(pieces):
            value = piece_sum(patch, cot, scale, *piece).astype(dtype)
            out[index * rows : (index + 1) * rows, :] = value


def sums(scale, patch, cot, after, *wanted):
    pix, half = patch.shape[2:]
    return pl.pallas_call(
        functools.partial(sums_kernel, scale, wanted),
        out_shape=[
            jax.ShapeDtypeStruct((len(pieces) * half // 2, 2 * half), dtype)
            for dtype, pieces in wanted
        ],
        in_specs=[VMEM] * 2 + [pl.BlockSpec(memory_space=pl.ANY)] * len(after),
        out_specs=[VMEM] * len(wanted),
        compiler_params=params(16),
        cost_estimate=pl.CostEstimate(
            flops=4 * len(wanted) * pix * half * half,
            bytes_accessed=8 * pix * half,
            transcendentals=0,
        ),
    )(patch, cot, *after)


def collect_kernel(own, *refs):
    *came, keep_left, keep_right, send_left, send_right = refs
    split = keep_left.shape[1]
    for columns, keep, send in (
        (slice(0, split), keep_left, send_left),
        (slice(split, own.shape[1]), keep_right, send_right),
    ):
        total = own[: keep.shape[0], columns]
        for ref in came:
            total = total + ref[:, columns].astype(F32)
        keep[...] = total
        send[...] = total.astype(BF16)


def collect(split, own, *came):
    rows, width = came[0].shape
    shapes = [(rows, split), (rows, width - split)]
    return pl.pallas_call(
        collect_kernel,
        out_shape=[jax.ShapeDtypeStruct(shape, F32) for shape in shapes]
        + [jax.ShapeDtypeStruct(shape, BF16) for shape in shapes],
        in_specs=[VMEM] * (1 + len(came)),
        out_specs=[VMEM] * 4,
        compiler_params=params(16),
    )(own, *came)


def add(*values):
    total = values[0]
    for value in values[1:]:
        total = total + value.astype(F32)
    return total


def root_kernel(most, counts_hbm, *refs):
    pieces, far = refs[:4], refs[4]
    keep_ref, send_ref, grad, turned, left, right, m_left, m_right, s_left, s_right, counts, sem = refs[5:]
    counts_copy = pltpu.make_async_copy(counts_hbm, counts, sem)
    counts_copy.start()
    width = grad.shape[0]
    half, quarter = width // 2, width // 4
    rows = keep_ref.shape[0]
    low, high = slice(0, half), slice(half, width)
    place, column, core = (lax.axis_index(name) for name in ("z", "x", "core"))
    column_start = 0
    for own, other in (pieces[:2], pieces[2:]):
        columns = slice(column_start, column_start + own.shape[1])
        column_start += own.shape[1]
        grad[:quarter, columns] = own[...]
        grad[quarter:half, columns] = other[...]
    grad[half:, :] = far[...]
    turned[...] = grad[...].T
    diagonal = lax.broadcasted_iota(jnp.int32, (half, half), 0) == lax.broadcasted_iota(
        jnp.int32, (half, half), 1
    )

    def dot(a, b):
        return jnp.dot(a, b, preferred_element_type=F32)

    def fill(ref, start, tiles):
        upper_left, upper_right, lower_right = (tile.astype(BF16) for tile in tiles)
        ref[start : start + half, low] = upper_left
        ref[start : start + half, high] = upper_right
        ref[start + half : start + width, low] = upper_right.T
        ref[start + half : start + width, high] = lower_right

    def factor(tiles):
        upper_left, upper_right, lower_right = tiles
        five = jnp.where(diagonal, 1.25, 0.0)
        return five - 0.25 * upper_left, -0.25 * upper_right, five - 0.25 * lower_right

    def statistics(first, second):
        tiles = [
            dot(first[a, :], second[:, b]) for a, b in ((low, low), (low, high), (high, high))
        ]
        tenth = jnp.where(diagonal, 0.1, 0.0)
        return tiles[0] + tenth, tiles[1], tiles[2] + tenth

    def spot(flip):
        row = (4 * place + 2 * (column ^ flip) + core) * rows
        part = row // quarter
        return ((part // 2 ^ core) * 2 + (part % 2 ^ place % 2)) * quarter + row % quarter

    line = lax.broadcasted_iota(jnp.int32, (2 * rows, width), 0)
    wanted = jnp.where(line < rows, spot(0) + line, spot(1) + line - rows)
    pick = lax.broadcasted_iota(jnp.int32, (2 * rows, width), 1) == wanted
    pick = jnp.where(pick, 1.0, 0.0).astype(BF16)
    picked = 2 * rows
    stats_left = statistics(grad, turned)
    stats_right = statistics(turned, grad)
    squares = [tile * tile for tile in stats_left]
    norm = jnp.sqrt(jnp.sum(squares[0] + 2.0 * squares[1] + squares[2], keepdims=True))
    scale = 2.5 / norm
    first = jnp.sqrt(jnp.sqrt(scale)).astype(BF16).astype(F32)
    tiles = [scale * tile for tile in stats_left]
    fill(m_left, 0, tiles)
    fill(left, picked, factor(tiles))
    left[:picked, :] = (first * dot(pick, left[picked:, :])).astype(BF16)
    tiles = [scale * tile for tile in stats_right]
    fill(m_right, 0, tiles)
    tiles = [tile.astype(BF16) for tile in factor(tiles)]
    fill(right, width, tiles)
    tiles = [(first * tile.astype(F32)).astype(BF16) for tile in tiles]
    right[half:width, low] = tiles[0]
    right[half:width, high] = tiles[1]
    right[:half, low] = tiles[1].T
    right[:half, high] = tiles[2]

    def square(ref):
        by_high = dot(ref[...], ref[:, high])
        return dot(ref[low, :], ref[:, low]), by_high[low], by_high[high]

    counts_copy.wait()
    count_left, count_right = counts[column, 0], counts[column, 1]
    for index in range(1, most):
        q_left, q_right = left.at[picked:, :], right.at[width:, :]
        if index == 1:
            seconds = square(q_left), square(q_right)
            fill(s_left, 0, seconds[0])
            fill(s_right, 0, seconds[1])
        else:
            by_high = dot(left[...], q_left[:, high])
            by_low = dot(left[: picked + half, :], q_left[:, low])
            right_by_high = dot(right[...], q_right[:, high])
            right_by_low = dot(right[half : width + half, :], q_right[:, low])
            fill(s_left, 0, (by_low[picked:], by_high[picked : picked + half], by_high[picked + half :]))
            fill(
                s_right,
                0,
                (right_by_low[half:], right_by_high[width : width + half], right_by_high[width + half :]),
            )

            def keep_if(ref, value, goes_on):
                value = value.astype(BF16)
                return value if index == 2 else jnp.where(goes_on, value, ref)

            left[:picked, low] = keep_if(left[:picked, low], by_low[:picked], index <= count_left)
            left[:picked, high] = keep_if(left[:picked, high], by_high[:picked], index <= count_left)
            goes_on = index <= count_right
            upper_right = keep_if(right[half:width, high], right_by_high[half:width], goes_on)
            right[half:width, low] = keep_if(right[half:width, low], right_by_low[:half], goes_on)
            right[half:width, high] = upper_right
            right[:half, low] = upper_right.T
            right[:half, high] = keep_if(right[:half, high], right_by_high[:half], goes_on)
        fourths = square(s_left), square(s_right)
        fill(s_left, 0, fourths[0])
        fill(s_right, 0, fourths[1])
        moments = []
        for fourth, moment_ref in ((s_left, m_left), (s_right, m_right)):
            by_high = dot(fourth[...], moment_ref[:, high])
            by_low = dot(fourth[low, :], moment_ref[:, low])
            moments.append((by_low, by_high[low], by_high[high]))
        fill(left, picked, factor(moments[0]))
        fill(right, width, factor(moments[1]))
        if index < most - 1:
            fill(m_left, 0, moments[0])
            fill(m_right, 0, moments[1])
    final_left = dot(left[:picked, :], left[picked:, :]).astype(BF16)
    final_left = jnp.where(most <= count_left, final_left, left[:picked, :])
    by_high = dot(right[:width, :], right[width:, high])
    by_low = dot(right[half:width, :], right[width:, low])
    goes_on = most <= count_right
    upper_right = jnp.where(goes_on, by_high[half:].astype(BF16), right[half:width, high])
    right[half:width, low] = jnp.where(goes_on, by_low.astype(BF16), right[half:width, low])
    right[half:width, high] = upper_right
    right[:half, low] = upper_right.T
    right[:half, high] = jnp.where(goes_on, by_high[:half].astype(BF16), right[:half, high])
    partial_value = dot(final_left, grad[...]).astype(BF16)
    update = dot(partial_value[:, low], right[half:width, :]) + dot(
        partial_value[:, high], right[:half, :]
    )
    keep_ref[...] = update[:rows, :].astype(BF16)
    send_ref[...] = update[rows:, :].astype(BF16)


def root(counts, pieces, rows, most=4):
    width = 4 * pieces[0].shape[0]
    square = pltpu.VMEM((width, width), BF16)
    out = jax.ShapeDtypeStruct((rows, width), BF16)
    return pl.pallas_call(
        functools.partial(root_kernel, most),
        out_shape=[out, out],
        in_specs=[HBM] + [VMEM] * 5,
        out_specs=[VMEM] * 2,
        scratch_shapes=[
            square,
            square,
            pltpu.VMEM((2 * rows + width, width), BF16),
            pltpu.VMEM((2 * width, width), BF16),
            square,
            square,
            square,
            square,
            pltpu.SMEM(counts.shape, jnp.int32),
            pltpu.SemaphoreType.DMA(()),
        ],
        compiler_params=params(40),
    )(pltpu.with_memory_space_constraint(counts, pltpu.HBM), *pieces)


def place_kernel(origins, *refs):
    *pieces, out, sems = refs
    column, group = lax.axis_index("x"), lax.axis_index("group")
    copies = []
    for index, (piece, (turn, flip)) in enumerate(zip(pieces, origins)):
        number = 2 * (group ^ turn) + (column ^ flip)
        copies.append(pltpu.make_async_copy(piece, out.at[number], sems.at[index]))
        copies[-1].start()
    for copy in copies:
        copy.wait()


def place(found):
    origins, pieces = zip(*found.items())
    rows, width = pieces[0].shape
    return pl.pallas_call(
        functools.partial(place_kernel, origins),
        out_shape=jax.ShapeDtypeStruct((len(pieces), rows, width), BF16),
        in_specs=[VMEM] * len(pieces),
        out_specs=HBM,
        scratch_shapes=[pltpu.SemaphoreType.DMA((len(pieces),))],
        compiler_params=params(16),
    )(*pieces)


def shards(line, groups, patches, cotangents, newton_counts):
    blocks, pix, width = patches.shape
    half = width // 2
    rows = half // (2 * line)
    scale = 1.0 / float(pix * 4 * line * width) ** 0.5

    def swap(array, axis, mask=1):
        return lax.ppermute(array, axis, [(i, i ^ mask) for i in range(lax.axis_size(axis))])

    def swap_diagonal(array):
        moves = [(2 * z + x, 2 * (z ^ 1) + (x ^ 1)) for z in range(line) for x in range(2)]
        return lax.ppermute(array, ("z", "x"), moves)

    given_column, given_line, patch, cot = load(scale, patches, cotangents)
    came_column, came_line = swap(given_column, "core"), swap(given_line, "core")
    kept_column, kept_line, given_rest = sums(
        scale,
        patch,
        cot,
        (),
        (F32, ((1, 0, 0),)),
        (F32, ((0, 0, 1),)),
        (BF16, ((1, 1, 1), (0, 1, 0))),
    )
    came_rest = swap(given_rest, "core")
    to_column = add(kept_column, came_column).astype(BF16)
    from_column = swap(to_column, "x")
    to_line = add(kept_line, came_line).astype(BF16)
    from_line = swap(to_line, "z")
    kept_diagonal, own = sums(
        scale, patch, cot, (to_line,), (F32, ((1, 0, 1),)), (F32, ((0, 0, 0),))
    )
    quarter = own.shape[0]
    to_diagonal = add(kept_diagonal, came_rest[:quarter]).astype(BF16)
    own = add(own, came_rest[quarter:])
    from_diagonal = swap_diagonal(to_diagonal)
    left, right, send_left, send_right = collect(
        width * 3 // 4, own, from_diagonal, from_column, from_line
    )
    pieces = []
    for own, send in ((left, send_left), (right, send_right)):
        mask = 2
        while mask < line:
            own = add(own, swap(send, "z", mask))
            send = own.astype(BF16)
            mask *= 2
        own = send
        other = swap(own, "z")
        pieces += [own, other]
    far = swap(jnp.concatenate([jnp.concatenate(pieces[i : i + 2], 0) for i in (0, 2)], 1), "core")
    pieces.append(far)
    keep, send = root(newton_counts, pieces, rows)

    def pass_on(turn, flip):
        moves = [
            (c * groups + g, (c ^ flip) * groups + (g ^ turn))
            for c in range(2)
            for g in range(groups)
        ]
        return lax.ppermute(send if flip else keep, ("x", "group"), moves)

    others = [(turn, flip) for turn in range(groups) for flip in range(2) if turn or flip]
    found = {(turn, flip): pass_on(turn, flip) for turn, flip in others}
    found[0, 0] = keep
    return place(found)


def solution(mesh):
    devices, groups = mesh.shape["dp"], mesh.shape["group"]
    line = devices // 4
    cut = jax.sharding.Mesh(
        mesh.devices.reshape(line, 2, 2, groups), ("z", "x", "core", "group")
    )
    dp = ("z", "x", "core")
    placed = (P("group", dp, None), P("group", dp, None), P("group", None))
    return jax.shard_map(
        functools.partial(shards, line, groups),
        mesh=cut,
        in_specs=placed,
        out_specs=P(None, dp, None),
        check_vma=False,
    )
```

```python
import functools

import jax
import jax.numpy as jnp
from jax import lax
from jax.experimental import pallas as pl
from jax.experimental.pallas import tpu as pltpu
from jax.sharding import PartitionSpec as P

F32 = jnp.float32
BF16 = jnp.bfloat16
VMEM = pl.BlockSpec(memory_space=pltpu.VMEM)
SMEM = pl.BlockSpec(memory_space=pltpu.SMEM)
HBM = pl.BlockSpec(memory_space=pltpu.HBM)
ROWS_IN_COLS = (((0,), (0,)), ((), ()))


def params(limit):
    return pltpu.CompilerParams(vmem_limit_bytes=limit << 20)


def piece_sum(patch, cot, scale, block, side, part):
    quarter = patch.shape[3] // 2
    rows = slice(part * quarter, (part + 1) * quarter)
    terms = lax.dot_general(
        patch[block, side, :, rows], cot[block], ROWS_IN_COLS, preferred_element_type=F32
    )
    return terms * scale


def load_kernel(scale, patch_hbm, cot_hbm, given_column, given_line, patch, cot, sems):
    half = patch.shape[3]
    width = half // 2
    column, core, parity = lax.axis_index("x"), lax.axis_index("core"), lax.axis_index("z") % 2
    copies = []

    def fetch(source, target):
        copies.append(pltpu.make_async_copy(source, target, sems.at[len(copies)]))
        copies[-1].start()

    def fetch_patch(block, side, part):
        first = (core ^ side) * half + (parity ^ part) * width
        fetch(
            patch_hbm.at[column ^ block, :, pl.ds(pl.multiple_of(first, width), width)],
            patch.at[block, side, :, part * width : (part + 1) * width],
        )

    fetch(cot_hbm.at[column ^ 1], cot.at[1])
    fetch_patch(1, 1, 0)
    fetch(cot_hbm.at[column], cot.at[0])
    fetch_patch(0, 1, 1)
    needed = len(copies)
    for side in range(2):
        for block, part in ((1, 0), (0, 1), (1, 1), (0, 0)):
            if side == 0 or block == part:
                fetch_patch(block, side, part)
    for copy in copies[:2]:
        copy.wait()
    given_column[...] = piece_sum(patch, cot, scale, 1, 1, 0).astype(BF16)
    for copy in copies[2:needed]:
        copy.wait()
    given_line[...] = piece_sum(patch, cot, scale, 0, 1, 1).astype(BF16)
    for copy in copies[needed:]:
        copy.wait()


def load(scale, patches, cotangents):
    blocks, pix, width = patches.shape
    half = width // 2
    return pl.pallas_call(
        functools.partial(load_kernel, scale),
        out_shape=[
            jax.ShapeDtypeStruct((half // 2, width), BF16),
            jax.ShapeDtypeStruct((half // 2, width), BF16),
            jax.ShapeDtypeStruct((blocks, 2, pix, half), BF16),
            jax.ShapeDtypeStruct((blocks, pix, width), BF16),
        ],
        in_specs=[HBM] * 2,
        out_specs=[VMEM] * 4,
        scratch_shapes=[pltpu.SemaphoreType.DMA((10,))],
        compiler_params=params(16),
    )(
        pltpu.with_memory_space_constraint(patches, pltpu.HBM),
        pltpu.with_memory_space_constraint(cotangents, pltpu.HBM),
    )


def sums_kernel(scale, wanted, patch, cot, *refs):
    for (dtype, pieces), out in zip(wanted, refs[-len(wanted) :]):
        rows = out.shape[0] // len(pieces)
        for index, piece in enumerate(pieces):
            value = piece_sum(patch, cot, scale, *piece).astype(dtype)
            out[index * rows : (index + 1) * rows, :] = value


def sums(scale, patch, cot, after, *wanted):
    pix, half = patch.shape[2:]
    return pl.pallas_call(
        functools.partial(sums_kernel, scale, wanted),
        out_shape=[
            jax.ShapeDtypeStruct((len(pieces) * half // 2, 2 * half), dtype)
            for dtype, pieces in wanted
        ],
        in_specs=[VMEM] * 2 + [pl.BlockSpec(memory_space=pl.ANY)] * len(after),
        out_specs=[VMEM] * len(wanted),
        compiler_params=params(16),
        cost_estimate=pl.CostEstimate(
            flops=4 * len(wanted) * pix * half * half,
            bytes_accessed=8 * pix * half,
            transcendentals=0,
        ),
    )(patch, cot, *after)


def collect_kernel(own, *refs):
    *came, keep_left, keep_right, send_left, send_right = refs
    split = keep_left.shape[1]
    for columns, keep, send in (
        (slice(0, split), keep_left, send_left),
        (slice(split, own.shape[1]), keep_right, send_right),
    ):
        total = own[: keep.shape[0], columns]
        for ref in came:
            total = total + ref[:, columns].astype(F32)
        keep[...] = total
        send[...] = total.astype(BF16)


def collect(split, own, *came):
    rows, width = came[0].shape
    shapes = [(rows, split), (rows, width - split)]
    return pl.pallas_call(
        collect_kernel,
        out_shape=[jax.ShapeDtypeStruct(shape, F32) for shape in shapes]
        + [jax.ShapeDtypeStruct(shape, BF16) for shape in shapes],
        in_specs=[VMEM] * (1 + len(came)),
        out_specs=[VMEM] * 4,
        compiler_params=params(16),
    )(own, *came)


def add(*values):
    total = values[0]
    for value in values[1:]:
        total = total + value.astype(F32)
    return total


def root_kernel(most, counts_hbm, *refs):
    pieces = refs[:6]
    keep_ref, send_ref, grad, turned, left, right, m_left, m_right, s_left, s_right, counts, sem = refs[6:]
    counts_copy = pltpu.make_async_copy(counts_hbm, counts, sem)
    counts_copy.start()
    width = grad.shape[0]
    half, quarter = width // 2, width // 4
    rows = keep_ref.shape[0]
    low, high = slice(0, half), slice(half, width)
    place, column, core = (lax.axis_index(name) for name in ("z", "x", "core"))
    column_start = 0
    for index in range(2):
        own, other, far = pieces[3 * index : 3 * index + 3]
        columns = slice(column_start, column_start + own.shape[1])
        column_start += own.shape[1]
        grad[:quarter, columns] = own[...]
        grad[quarter:half, columns] = other[...]
        grad[half:, columns] = far[...]
    turned[...] = grad[...].T
    diagonal = lax.broadcasted_iota(jnp.int32, (half, half), 0) == lax.broadcasted_iota(
        jnp.int32, (half, half), 1
    )

    def dot(a, b):
        return jnp.dot(a, b, preferred_element_type=F32)

    def fill(ref, start, tiles):
        upper_left, upper_right, lower_right = (tile.astype(BF16) for tile in tiles)
        ref[start : start + half, low] = upper_left
        ref[start : start + half, high] = upper_right
        ref[start + half : start + width, low] = upper_right.T
        ref[start + half : start + width, high] = lower_right

    def factor(tiles):
        upper_left, upper_right, lower_right = tiles
        five = jnp.where(diagonal, 1.25, 0.0)
        return five - 0.25 * upper_left, -0.25 * upper_right, five - 0.25 * lower_right

    def statistics(first, second):
        tiles = [
            dot(first[a, :], second[:, b]) for a, b in ((low, low), (low, high), (high, high))
        ]
        tenth = jnp.where(diagonal, 0.1, 0.0)
        return tiles[0] + tenth, tiles[1], tiles[2] + tenth

    def spot(flip):
        row = (4 * place + 2 * (column ^ flip) + core) * rows
        part = row // quarter
        return ((part // 2 ^ core) * 2 + (part % 2 ^ place % 2)) * quarter + row % quarter

    line = lax.broadcasted_iota(jnp.int32, (2 * rows, width), 0)
    wanted = jnp.where(line < rows, spot(0) + line, spot(1) + line - rows)
    pick = lax.broadcasted_iota(jnp.int32, (2 * rows, width), 1) == wanted
    pick = jnp.where(pick, 1.0, 0.0).astype(BF16)
    picked = 2 * rows
    stats_left = statistics(grad, turned)
    stats_right = statistics(turned, grad)
    squares = [tile * tile for tile in stats_left]
    norm = jnp.sqrt(jnp.sum(squares[0] + 2.0 * squares[1] + squares[2], keepdims=True))
    scale = 2.5 / norm
    first = jnp.sqrt(jnp.sqrt(scale)).astype(BF16).astype(F32)
    tiles = [scale * tile for tile in stats_left]
    fill(m_left, 0, tiles)
    fill(left, picked, factor(tiles))
    left[:picked, :] = (first * dot(pick, left[picked:, :])).astype(BF16)
    tiles = [scale * tile for tile in stats_right]
    fill(m_right, 0, tiles)
    tiles = [tile.astype(BF16) for tile in factor(tiles)]
    fill(right, width, tiles)
    tiles = [(first * tile.astype(F32)).astype(BF16) for tile in tiles]
    right[half:width, low] = tiles[0]
    right[half:width, high] = tiles[1]
    right[:half, low] = tiles[1].T
    right[:half, high] = tiles[2]

    def square(ref):
        by_high = dot(ref[...], ref[:, high])
        return dot(ref[low, :], ref[:, low]), by_high[low], by_high[high]

    counts_copy.wait()
    count_left, count_right = counts[column, 0], counts[column, 1]
    for index in range(1, most):
        q_left, q_right = left.at[picked:, :], right.at[width:, :]
        if index == 1:
            fill(s_left, 0, square(q_left))
            fill(s_right, 0, square(q_right))
        else:
            by_high = dot(left[...], q_left[:, high])
            by_low = dot(left[: picked + half, :], q_left[:, low])
            right_by_high = dot(right[...], q_right[:, high])
            right_by_low = dot(right[half : width + half, :], q_right[:, low])
            fill(s_left, 0, (by_low[picked:], by_high[picked : picked + half], by_high[picked + half :]))
            fill(
                s_right,
                0,
                (right_by_low[half:], right_by_high[width : width + half], right_by_high[width + half :]),
            )

            def keep_if(ref, value, goes_on):
                value = value.astype(BF16)
                return value if index == 2 else jnp.where(goes_on, value, ref)

            left[:picked, low] = keep_if(left[:picked, low], by_low[:picked], index <= count_left)
            left[:picked, high] = keep_if(left[:picked, high], by_high[:picked], index <= count_left)
            goes_on = index <= count_right
            upper_right = keep_if(right[half:width, high], right_by_high[half:width], goes_on)
            right[half:width, low] = keep_if(right[half:width, low], right_by_low[:half], goes_on)
            right[half:width, high] = upper_right
            right[:half, low] = upper_right.T
            right[:half, high] = keep_if(right[:half, high], right_by_high[:half], goes_on)
        fourths = square(s_left), square(s_right)
        fill(s_left, 0, fourths[0])
        fill(s_right, 0, fourths[1])
        for fourth, moment_ref, ref, start in (
            (s_left, m_left, left, picked),
            (s_right, m_right, right, width),
        ):
            by_high = dot(fourth[...], moment_ref[:, high])
            tiles = (dot(fourth[low, :], moment_ref[:, low]), by_high[low], by_high[high])
            if index < most - 1:
                fill(moment_ref, 0, tiles)
            fill(ref, start, factor(tiles))
    final_left = dot(left[:picked, :], left[picked:, :]).astype(BF16)
    final_left = jnp.where(most <= count_left, final_left, left[:picked, :])
    by_high = dot(right[:width, :], right[width:, high])
    by_low = dot(right[half:width, :], right[width:, low])
    goes_on = most <= count_right
    upper_right = jnp.where(goes_on, by_high[half:].astype(BF16), right[half:width, high])
    right[half:width, low] = jnp.where(goes_on, by_low.astype(BF16), right[half:width, low])
    right[half:width, high] = upper_right
    right[:half, low] = upper_right.T
    right[:half, high] = jnp.where(goes_on, by_high[:half].astype(BF16), right[:half, high])
    partial_value = dot(final_left, grad[...]).astype(BF16)
    update = dot(partial_value[:, low], right[half:width, :]) + dot(
        partial_value[:, high], right[:half, :]
    )
    keep_ref[...] = update[:rows, :].astype(BF16)
    send_ref[...] = update[rows:, :].astype(BF16)


def root(counts, pieces, rows, most=4):
    width = 4 * pieces[0].shape[0]
    square = pltpu.VMEM((width, width), BF16)
    out = jax.ShapeDtypeStruct((rows, width), BF16)
    return pl.pallas_call(
        functools.partial(root_kernel, most),
        out_shape=[out, out],
        in_specs=[HBM] + [VMEM] * 6,
        out_specs=[VMEM] * 2,
        scratch_shapes=[
            square,
            square,
            pltpu.VMEM((2 * rows + width, width), BF16),
            pltpu.VMEM((2 * width, width), BF16),
            square,
            square,
            square,
            square,
            pltpu.SMEM(counts.shape, jnp.int32),
            pltpu.SemaphoreType.DMA(()),
        ],
        compiler_params=params(40),
    )(pltpu.with_memory_space_constraint(counts, pltpu.HBM), *pieces)


def place_kernel(origins, *refs):
    pieces, out, sems = refs[: len(origins)], refs[-2], refs[-1]
    column, group = lax.axis_index("x"), lax.axis_index("group")
    copies = []
    for index, (piece, (turn, flip)) in enumerate(zip(pieces, origins)):
        number = 2 * (group ^ turn) + (column ^ flip)
        copies.append(pltpu.make_async_copy(piece, out.at[number], sems.at[index]))
        copies[-1].start()
    for copy in copies:
        copy.wait()


def place(found, total, begun=()):
    origins, pieces = zip(*found.items())
    rows, width = pieces[0].shape
    return pl.pallas_call(
        functools.partial(place_kernel, origins),
        out_shape=jax.ShapeDtypeStruct((total, rows, width), BF16),
        in_specs=[VMEM] * len(pieces) + [HBM] * len(begun),
        out_specs=HBM,
        input_output_aliases={len(pieces): 0} if begun else {},
        scratch_shapes=[pltpu.SemaphoreType.DMA((len(pieces),))],
        compiler_params=params(16),
    )(*pieces, *begun)


def shards(line, groups, patches, cotangents, newton_counts):
    blocks, pix, width = patches.shape
    half = width // 2
    rows = half // (2 * line)
    scale = 1.0 / float(pix * 4 * line * width) ** 0.5

    def swap(array, axis, mask=1):
        return lax.ppermute(array, axis, [(i, i ^ mask) for i in range(lax.axis_size(axis))])

    def swap_diagonal(array):
        moves = [(2 * z + x, 2 * (z ^ 1) + (x ^ 1)) for z in range(line) for x in range(2)]
        return lax.ppermute(array, ("z", "x"), moves)

    given_column, given_line, patch, cot = load(scale, patches, cotangents)
    came_column, came_line = swap(given_column, "core"), swap(given_line, "core")
    kept_column, kept_line, given_rest = sums(
        scale,
        patch,
        cot,
        (),
        (F32, ((1, 0, 0),)),
        (F32, ((0, 0, 1),)),
        (BF16, ((1, 1, 1), (0, 1, 0))),
    )
    came_rest = swap(given_rest, "core")
    to_column = add(kept_column, came_column).astype(BF16)
    from_column = swap(to_column, "x")
    to_line = add(kept_line, came_line).astype(BF16)
    from_line = swap(to_line, "z")
    kept_diagonal, own = sums(
        scale, patch, cot, (to_line,), (F32, ((1, 0, 1),)), (F32, ((0, 0, 0),))
    )
    quarter = own.shape[0]
    to_diagonal = add(kept_diagonal, came_rest[:quarter]).astype(BF16)
    own = add(own, came_rest[quarter:])
    from_diagonal = swap_diagonal(to_diagonal)
    left, right, send_left, send_right = collect(
        width * 3 // 4, own, from_diagonal, from_column, from_line
    )
    pieces = []
    for own, send in ((left, send_left), (right, send_right)):
        mask = 2
        while mask < line:
            own = add(own, swap(send, "z", mask))
            send = own.astype(BF16)
            mask *= 2
        own = send
        other = swap(own, "z")
        pieces += [own, other, swap(jnp.concatenate([own, other], 0), "core")]
    keep, send = root(newton_counts, pieces, rows)

    def pass_on(turn, flip):
        moves = [
            (c * groups + g, (c ^ flip) * groups + (g ^ turn))
            for c in range(2)
            for g in range(groups)
        ]
        return lax.ppermute(send if flip else keep, ("x", "group"), moves)

    others = [(turn, flip) for turn in range(groups) for flip in range(2) if turn or flip]
    found = {(turn, flip): pass_on(turn, flip) for turn, flip in others}
    last = {(1, 0): found.pop((1, 0))}
    found[0, 0] = keep
    return place(last, 2 * groups, (place(found, 2 * groups),))


def solution(mesh):
    devices, groups = mesh.shape["dp"], mesh.shape["group"]
    line = devices // 4
    cut = jax.sharding.Mesh(
        mesh.devices.reshape(line, 2, 2, groups), ("z", "x", "core", "group")
    )
    dp = ("z", "x", "core")
    placed = (P("group", dp, None), P("group", dp, None), P("group", None))
    return jax.shard_map(
        functools.partial(shards, line, groups),
        mesh=cut,
        in_specs=placed,
        out_specs=P(None, dp, None),
        check_vma=False,
    )
```

```python
import functools

import jax
import jax.numpy as jnp
from jax import lax
from jax.experimental import pallas as pl
from jax.experimental.pallas import tpu as pltpu
from jax.sharding import PartitionSpec as P

F32 = jnp.float32
BF16 = jnp.bfloat16
VMEM = pl.BlockSpec(memory_space=pltpu.VMEM)
SMEM = pl.BlockSpec(memory_space=pltpu.SMEM)
HBM = pl.BlockSpec(memory_space=pltpu.HBM)
ROWS_IN_COLS = (((0,), (0,)), ((), ()))


def params(limit):
    return pltpu.CompilerParams(vmem_limit_bytes=limit << 20)


def piece_sum(patch, cot, scale, block, side, part):
    quarter = patch.shape[3] // 2
    rows = slice(part * quarter, (part + 1) * quarter)
    terms = lax.dot_general(
        patch[block, side, :, rows], cot[block], ROWS_IN_COLS, preferred_element_type=F32
    )
    return terms * scale


def load_kernel(scale, patch_hbm, cot_hbm, given_column, given_line, patch, cot, sems):
    half = patch.shape[3]
    width = half // 2
    column, core, parity = lax.axis_index("x"), lax.axis_index("core"), lax.axis_index("z") % 2
    copies = []

    def fetch(source, target):
        copies.append(pltpu.make_async_copy(source, target, sems.at[len(copies)]))
        copies[-1].start()

    def fetch_patch(block, side, part):
        first = (core ^ side) * half + (parity ^ part) * width
        fetch(
            patch_hbm.at[column ^ block, :, pl.ds(pl.multiple_of(first, width), width)],
            patch.at[block, side, :, part * width : (part + 1) * width],
        )

    fetch(cot_hbm.at[column ^ 1], cot.at[1])
    fetch_patch(1, 1, 0)
    fetch(cot_hbm.at[column], cot.at[0])
    fetch_patch(0, 1, 1)
    needed = len(copies)
    for side in range(2):
        for block, part in ((1, 0), (0, 1), (1, 1), (0, 0)):
            if side == 0 or block == part:
                fetch_patch(block, side, part)
    for copy in copies[:2]:
        copy.wait()
    given_column[...] = piece_sum(patch, cot, scale, 1, 1, 0).astype(BF16)
    for copy in copies[2:needed]:
        copy.wait()
    given_line[...] = piece_sum(patch, cot, scale, 0, 1, 1).astype(BF16)
    for copy in copies[needed:]:
        copy.wait()


def load(scale, patches, cotangents):
    blocks, pix, width = patches.shape
    half = width // 2
    return pl.pallas_call(
        functools.partial(load_kernel, scale),
        out_shape=[
            jax.ShapeDtypeStruct((half // 2, width), BF16),
            jax.ShapeDtypeStruct((half // 2, width), BF16),
            jax.ShapeDtypeStruct((blocks, 2, pix, half), BF16),
            jax.ShapeDtypeStruct((blocks, pix, width), BF16),
        ],
        in_specs=[HBM] * 2,
        out_specs=[VMEM] * 4,
        scratch_shapes=[pltpu.SemaphoreType.DMA((10,))],
        compiler_params=params(16),
    )(
        pltpu.with_memory_space_constraint(patches, pltpu.HBM),
        pltpu.with_memory_space_constraint(cotangents, pltpu.HBM),
    )


def sums_kernel(scale, wanted, patch, cot, *refs):
    for (dtype, pieces), out in zip(wanted, refs[-len(wanted) :]):
        rows = out.shape[0] // len(pieces)
        for index, piece in enumerate(pieces):
            value = piece_sum(patch, cot, scale, *piece).astype(dtype)
            out[index * rows : (index + 1) * rows, :] = value


def sums(scale, patch, cot, after, *wanted):
    pix, half = patch.shape[2:]
    return pl.pallas_call(
        functools.partial(sums_kernel, scale, wanted),
        out_shape=[
            jax.ShapeDtypeStruct((len(pieces) * half // 2, 2 * half), dtype)
            for dtype, pieces in wanted
        ],
        in_specs=[VMEM] * 2 + [pl.BlockSpec(memory_space=pl.ANY)] * len(after),
        out_specs=[VMEM] * len(wanted),
        compiler_params=params(16),
        cost_estimate=pl.CostEstimate(
            flops=4 * len(wanted) * pix * half * half,
            bytes_accessed=8 * pix * half,
            transcendentals=0,
        ),
    )(patch, cot, *after)


def collect_kernel(own, *refs):
    *came, keep_left, keep_right, send_left, send_right = refs
    split = keep_left.shape[1]
    for columns, keep, send in (
        (slice(0, split), keep_left, send_left),
        (slice(split, own.shape[1]), keep_right, send_right),
    ):
        total = own[: keep.shape[0], columns]
        for ref in came:
            total = total + ref[:, columns].astype(F32)
        keep[...] = total
        send[...] = total.astype(BF16)


def collect(split, own, *came):
    rows, width = came[0].shape
    shapes = [(rows, split), (rows, width - split)]
    return pl.pallas_call(
        collect_kernel,
        out_shape=[jax.ShapeDtypeStruct(shape, F32) for shape in shapes]
        + [jax.ShapeDtypeStruct(shape, BF16) for shape in shapes],
        in_specs=[VMEM] * (1 + len(came)),
        out_specs=[VMEM] * 4,
        compiler_params=params(16),
    )(own, *came)


def add(*values):
    total = values[0]
    for value in values[1:]:
        total = total + value.astype(F32)
    return total


def root_kernel(most, counts_hbm, *refs):
    pieces = refs[:6]
    keep_ref, send_ref, grad, turned, left, right, m_left, m_right, s_left, s_right, counts, sem = refs[6:]
    counts_copy = pltpu.make_async_copy(counts_hbm, counts, sem)
    counts_copy.start()
    width = grad.shape[0]
    half, quarter = width // 2, width // 4
    rows = keep_ref.shape[0]
    low, high = slice(0, half), slice(half, width)
    place, column, core = (lax.axis_index(name) for name in ("z", "x", "core"))
    column_start = 0
    for index in range(2):
        own, other, far = pieces[3 * index : 3 * index + 3]
        columns = slice(column_start, column_start + own.shape[1])
        column_start += own.shape[1]
        grad[:quarter, columns] = own[...]
        grad[quarter:half, columns] = other[...]
        grad[half:, columns] = far[...]
    turned[...] = grad[...].T
    diagonal = lax.broadcasted_iota(jnp.int32, (half, half), 0) == lax.broadcasted_iota(
        jnp.int32, (half, half), 1
    )

    def dot(a, b):
        return jnp.dot(a, b, preferred_element_type=F32)

    def fill(ref, start, tiles):
        upper_left, upper_right, lower_right = (tile.astype(BF16) for tile in tiles)
        ref[start : start + half, low] = upper_left
        ref[start : start + half, high] = upper_right
        ref[start + half : start + width, low] = upper_right.T
        ref[start + half : start + width, high] = lower_right

    def factor(tiles):
        upper_left, upper_right, lower_right = tiles
        five = jnp.where(diagonal, 1.25, 0.0)
        return five - 0.25 * upper_left, -0.25 * upper_right, five - 0.25 * lower_right

    def statistics(first, second):
        tiles = [
            dot(first[a, :], second[:, b]) for a, b in ((low, low), (low, high), (high, high))
        ]
        tenth = jnp.where(diagonal, 0.1, 0.0)
        return tiles[0] + tenth, tiles[1], tiles[2] + tenth

    def spot(flip):
        row = (4 * place + 2 * (column ^ flip) + core) * rows
        part = row // quarter
        return ((part // 2 ^ core) * 2 + (part % 2 ^ place % 2)) * quarter + row % quarter

    line = lax.broadcasted_iota(jnp.int32, (2 * rows, width), 0)
    wanted = jnp.where(line < rows, spot(0) + line, spot(1) + line - rows)
    pick = lax.broadcasted_iota(jnp.int32, (2 * rows, width), 1) == wanted
    pick = jnp.where(pick, 1.0, 0.0).astype(BF16)
    picked = 2 * rows
    stats_left = statistics(grad, turned)
    stats_right = statistics(turned, grad)
    squares = [tile * tile for tile in stats_left]
    norm = jnp.sqrt(jnp.sum(squares[0] + 2.0 * squares[1] + squares[2], keepdims=True))
    scale = 2.5 / norm
    first = jnp.sqrt(jnp.sqrt(scale)).astype(BF16).astype(F32)
    tiles = [scale * tile for tile in stats_left]
    fill(m_left, 0, tiles)
    fill(left, picked, factor(tiles))
    left[:picked, :] = (first * dot(pick, left[picked:, :])).astype(BF16)
    tiles = [scale * tile for tile in stats_right]
    fill(m_right, 0, tiles)
    tiles = [tile.astype(BF16) for tile in factor(tiles)]
    fill(right, width, tiles)
    tiles = [(first * tile.astype(F32)).astype(BF16) for tile in tiles]
    right[half:width, low] = tiles[0]
    right[half:width, high] = tiles[1]
    right[:half, low] = tiles[1].T
    right[:half, high] = tiles[2]

    def square(ref):
        by_high = dot(ref[...], ref[:, high])
        return dot(ref[low, :], ref[:, low]), by_high[low], by_high[high]

    counts_copy.wait()
    count_left, count_right = counts[column, 0], counts[column, 1]
    for index in range(1, most):
        q_left, q_right = left.at[picked:, :], right.at[width:, :]
        if index == 1:
            fill(s_left, 0, square(q_left))
            fill(s_right, 0, square(q_right))
        else:
            by_high = dot(left[...], q_left[:, high])
            by_low = dot(left[: picked + half, :], q_left[:, low])
            right_by_high = dot(right[...], q_right[:, high])
            right_by_low = dot(right[half : width + half, :], q_right[:, low])
            fill(s_left, 0, (by_low[picked:], by_high[picked : picked + half], by_high[picked + half :]))
            fill(
                s_right,
                0,
                (right_by_low[half:], right_by_high[width : width + half], right_by_high[width + half :]),
            )

            def keep_if(ref, value, goes_on):
                value = value.astype(BF16)
                return value if index == 2 else jnp.where(goes_on, value, ref)

            left[:picked, low] = keep_if(left[:picked, low], by_low[:picked], index <= count_left)
            left[:picked, high] = keep_if(left[:picked, high], by_high[:picked], index <= count_left)
            goes_on = index <= count_right
            upper_right = keep_if(right[half:width, high], right_by_high[half:width], goes_on)
            right[half:width, low] = keep_if(right[half:width, low], right_by_low[:half], goes_on)
            right[half:width, high] = upper_right
            right[:half, low] = upper_right.T
            right[:half, high] = keep_if(right[:half, high], right_by_high[:half], goes_on)
        fourths = square(s_left), square(s_right)
        fill(s_left, 0, fourths[0])
        fill(s_right, 0, fourths[1])
        for fourth, moment_ref, ref, start in (
            (s_left, m_left, left, picked),
            (s_right, m_right, right, width),
        ):
            by_high = dot(fourth[...], moment_ref[:, high])
            tiles = (dot(fourth[low, :], moment_ref[:, low]), by_high[low], by_high[high])
            if index < most - 1:
                fill(moment_ref, 0, tiles)
            fill(ref, start, factor(tiles))
    final_left = dot(left[:picked, :], left[picked:, :]).astype(BF16)
    final_left = jnp.where(most <= count_left, final_left, left[:picked, :])
    partial_value = dot(final_left, grad[...]).astype(BF16)
    update = dot(partial_value[:, low], right[half:width, :]) + dot(
        partial_value[:, high], right[:half, :]
    )
    update = jnp.where(most <= count_right, dot(update.astype(BF16), right[width:, :]), update)
    keep_ref[...] = update[:rows, :].astype(BF16)
    send_ref[...] = update[rows:, :].astype(BF16)


def root(counts, pieces, rows, most=4):
    width = 4 * pieces[0].shape[0]
    square = pltpu.VMEM((width, width), BF16)
    out = jax.ShapeDtypeStruct((rows, width), BF16)
    return pl.pallas_call(
        functools.partial(root_kernel, most),
        out_shape=[out, out],
        in_specs=[HBM] + [VMEM] * 6,
        out_specs=[VMEM] * 2,
        scratch_shapes=[
            square,
            square,
            pltpu.VMEM((2 * rows + width, width), BF16),
            pltpu.VMEM((2 * width, width), BF16),
            square,
            square,
            square,
            square,
            pltpu.SMEM(counts.shape, jnp.int32),
            pltpu.SemaphoreType.DMA(()),
        ],
        compiler_params=params(40),
    )(pltpu.with_memory_space_constraint(counts, pltpu.HBM), *pieces)


def place_kernel(origins, *refs):
    *pieces, out, sems = refs
    column, group = lax.axis_index("x"), lax.axis_index("group")
    copies = []
    for index, (piece, (turn, flip)) in enumerate(zip(pieces, origins)):
        number = 2 * (group ^ turn) + (column ^ flip)
        copies.append(pltpu.make_async_copy(piece, out.at[number], sems.at[index]))
        copies[-1].start()
    for copy in copies:
        copy.wait()


def place(found):
    origins, pieces = zip(*found.items())
    rows, width = pieces[0].shape
    return pl.pallas_call(
        functools.partial(place_kernel, origins),
        out_shape=jax.ShapeDtypeStruct((len(pieces), rows, width), BF16),
        in_specs=[VMEM] * len(pieces),
        out_specs=HBM,
        scratch_shapes=[pltpu.SemaphoreType.DMA((len(pieces),))],
        compiler_params=params(16),
    )(*pieces)


def shards(line, groups, patches, cotangents, newton_counts):
    blocks, pix, width = patches.shape
    half = width // 2
    rows = half // (2 * line)
    scale = 1.0 / float(pix * 4 * line * width) ** 0.5

    def swap(array, axis, mask=1):
        return lax.ppermute(array, axis, [(i, i ^ mask) for i in range(lax.axis_size(axis))])

    def swap_diagonal(array):
        moves = [(2 * z + x, 2 * (z ^ 1) + (x ^ 1)) for z in range(line) for x in range(2)]
        return lax.ppermute(array, ("z", "x"), moves)

    given_column, given_line, patch, cot = load(scale, patches, cotangents)
    came_column, came_line = swap(given_column, "core"), swap(given_line, "core")
    kept_column, kept_line, given_rest = sums(
        scale,
        patch,
        cot,
        (),
        (F32, ((1, 0, 0),)),
        (F32, ((0, 0, 1),)),
        (BF16, ((1, 1, 1), (0, 1, 0))),
    )
    came_rest = swap(given_rest, "core")
    to_column = add(kept_column, came_column).astype(BF16)
    from_column = swap(to_column, "x")
    to_line = add(kept_line, came_line).astype(BF16)
    from_line = swap(to_line, "z")
    kept_diagonal, own = sums(
        scale, patch, cot, (to_line,), (F32, ((1, 0, 1),)), (F32, ((0, 0, 0),))
    )
    quarter = own.shape[0]
    to_diagonal = add(kept_diagonal, came_rest[:quarter]).astype(BF16)
    own = add(own, came_rest[quarter:])
    from_diagonal = swap_diagonal(to_diagonal)
    left, right, send_left, send_right = collect(
        width * 3 // 4, own, from_diagonal, from_column, from_line
    )
    pieces = []
    for own, send in ((left, send_left), (right, send_right)):
        mask = 2
        while mask < line:
            own = add(own, swap(send, "z", mask))
            send = own.astype(BF16)
            mask *= 2
        own = send
        other = swap(own, "z")
        pieces += [own, other, swap(jnp.concatenate([own, other], 0), "core")]
    keep, send = root(newton_counts, pieces, rows)

    def pass_on(turn, flip):
        moves = [
            (c * groups + g, (c ^ flip) * groups + (g ^ turn))
            for c in range(2)
            for g in range(groups)
        ]
        return lax.ppermute(send if flip else keep, ("x", "group"), moves)

    others = [(turn, flip) for turn in range(groups) for flip in range(2) if turn or flip]
    found = {(turn, flip): pass_on(turn, flip) for turn, flip in others}
    found[0, 0] = keep
    return place(found)


def solution(mesh):
    devices, groups = mesh.shape["dp"], mesh.shape["group"]
    line = devices // 4
    cut = jax.sharding.Mesh(
        mesh.devices.reshape(line, 2, 2, groups), ("z", "x", "core", "group")
    )
    dp = ("z", "x", "core")
    placed = (P("group", dp, None), P("group", dp, None), P("group", None))
    return jax.shard_map(
        functools.partial(shards, line, groups),
        mesh=cut,
        in_specs=placed,
        out_specs=P(None, dp, None),
        check_vma=False,
    )
```

```python
import functools

import jax
import jax.numpy as jnp
from jax import lax
from jax.experimental import pallas as pl
from jax.experimental.pallas import tpu as pltpu
from jax.sharding import PartitionSpec as P

F32 = jnp.float32
BF16 = jnp.bfloat16
VMEM = pl.BlockSpec(memory_space=pltpu.VMEM)
SMEM = pl.BlockSpec(memory_space=pltpu.SMEM)
HBM = pl.BlockSpec(memory_space=pltpu.HBM)
ROWS_IN_COLS = (((0,), (0,)), ((), ()))


def params(limit):
    return pltpu.CompilerParams(vmem_limit_bytes=limit << 20)


def piece_sum(patch, cot, scale, block, side, part):
    quarter = patch.shape[3] // 2
    rows = slice(part * quarter, (part + 1) * quarter)
    terms = lax.dot_general(
        patch[block, side, :, rows], cot[block], ROWS_IN_COLS, preferred_element_type=F32
    )
    return terms * scale


def load_kernel(scale, patch_hbm, cot_hbm, given_column, given_line, patch, cot, sems):
    half = patch.shape[3]
    width = half // 2
    column, core, parity = lax.axis_index("x"), lax.axis_index("core"), lax.axis_index("z") % 2
    copies = []

    def fetch(source, target):
        copies.append(pltpu.make_async_copy(source, target, sems.at[len(copies)]))
        copies[-1].start()

    def fetch_patch(block, side, part):
        first = (core ^ side) * half + (parity ^ part) * width
        fetch(
            patch_hbm.at[column ^ block, :, pl.ds(pl.multiple_of(first, width), width)],
            patch.at[block, side, :, part * width : (part + 1) * width],
        )

    fetch(cot_hbm.at[column ^ 1], cot.at[1])
    fetch_patch(1, 1, 0)
    fetch(cot_hbm.at[column], cot.at[0])
    fetch_patch(0, 1, 1)
    needed = len(copies)
    for side in range(2):
        for block, part in ((1, 0), (0, 1), (1, 1), (0, 0)):
            if side == 0 or block == part:
                fetch_patch(block, side, part)
    for copy in copies[:2]:
        copy.wait()
    given_column[...] = piece_sum(patch, cot, scale, 1, 1, 0).astype(BF16)
    for copy in copies[2:needed]:
        copy.wait()
    given_line[...] = piece_sum(patch, cot, scale, 0, 1, 1).astype(BF16)
    for copy in copies[needed:]:
        copy.wait()


def load(scale, patches, cotangents):
    blocks, pix, width = patches.shape
    half = width // 2
    return pl.pallas_call(
        functools.partial(load_kernel, scale),
        out_shape=[
            jax.ShapeDtypeStruct((half // 2, width), BF16),
            jax.ShapeDtypeStruct((half // 2, width), BF16),
            jax.ShapeDtypeStruct((blocks, 2, pix, half), BF16),
            jax.ShapeDtypeStruct((blocks, pix, width), BF16),
        ],
        in_specs=[HBM] * 2,
        out_specs=[VMEM] * 4,
        scratch_shapes=[pltpu.SemaphoreType.DMA((10,))],
        compiler_params=params(16),
    )(
        pltpu.with_memory_space_constraint(patches, pltpu.HBM),
        pltpu.with_memory_space_constraint(cotangents, pltpu.HBM),
    )


def sums_kernel(scale, wanted, patch, cot, *refs):
    for (dtype, pieces), out in zip(wanted, refs[-len(wanted) :]):
        rows = out.shape[0] // len(pieces)
        for index, piece in enumerate(pieces):
            value = piece_sum(patch, cot, scale, *piece).astype(dtype)
            out[index * rows : (index + 1) * rows, :] = value


def sums(scale, patch, cot, after, *wanted):
    pix, half = patch.shape[2:]
    return pl.pallas_call(
        functools.partial(sums_kernel, scale, wanted),
        out_shape=[
            jax.ShapeDtypeStruct((len(pieces) * half // 2, 2 * half), dtype)
            for dtype, pieces in wanted
        ],
        in_specs=[VMEM] * 2 + [pl.BlockSpec(memory_space=pl.ANY)] * len(after),
        out_specs=[VMEM] * len(wanted),
        compiler_params=params(16),
        cost_estimate=pl.CostEstimate(
            flops=4 * len(wanted) * pix * half * half,
            bytes_accessed=8 * pix * half,
            transcendentals=0,
        ),
    )(patch, cot, *after)


def collect_kernel(own, *refs):
    *came, keep_left, keep_right, send_left, send_right = refs
    split = keep_left.shape[1]
    for columns, keep, send in (
        (slice(0, split), keep_left, send_left),
        (slice(split, own.shape[1]), keep_right, send_right),
    ):
        total = own[: keep.shape[0], columns]
        for ref in came:
            total = total + ref[:, columns].astype(F32)
        keep[...] = total
        send[...] = total.astype(BF16)


def collect(split, own, *came):
    rows, width = came[0].shape
    shapes = [(rows, split), (rows, width - split)]
    return pl.pallas_call(
        collect_kernel,
        out_shape=[jax.ShapeDtypeStruct(shape, F32) for shape in shapes]
        + [jax.ShapeDtypeStruct(shape, BF16) for shape in shapes],
        in_specs=[VMEM] * (1 + len(came)),
        out_specs=[VMEM] * 4,
        compiler_params=params(16),
    )(own, *came)


def add(*values):
    total = values[0]
    for value in values[1:]:
        total = total + value.astype(F32)
    return total


def root_kernel(most, counts_hbm, *refs):
    pieces = refs[:6]
    keep_ref, send_ref, grad, turned, left, right, m_left, m_right, s_left, s_right, counts, sem = refs[6:]
    counts_copy = pltpu.make_async_copy(counts_hbm, counts, sem)
    counts_copy.start()
    width = grad.shape[0]
    half, quarter = width // 2, width // 4
    rows = keep_ref.shape[0]
    low, high = slice(0, half), slice(half, width)
    place, column, core = (lax.axis_index(name) for name in ("z", "x", "core"))
    column_start = 0
    for index in range(2):
        own, other, far = pieces[3 * index : 3 * index + 3]
        columns = slice(column_start, column_start + own.shape[1])
        column_start += own.shape[1]
        grad[:quarter, columns] = own[...]
        grad[quarter:half, columns] = other[...]
        grad[half:, columns] = far[...]
    turned[...] = grad[...].T
    diagonal = lax.broadcasted_iota(jnp.int32, (half, half), 0) == lax.broadcasted_iota(
        jnp.int32, (half, half), 1
    )

    def dot(a, b):
        return jnp.dot(a, b, preferred_element_type=F32)

    def fill(ref, start, tiles):
        upper_left, upper_right, lower_right = (tile.astype(BF16) for tile in tiles)
        ref[start : start + half, low] = upper_left
        ref[start : start + half, high] = upper_right
        ref[start + half : start + width, low] = upper_right.T
        ref[start + half : start + width, high] = lower_right

    def factor(tiles):
        upper_left, upper_right, lower_right = tiles
        five = jnp.where(diagonal, 1.25, 0.0)
        return five - 0.25 * upper_left, -0.25 * upper_right, five - 0.25 * lower_right

    def statistics(first, second):
        tiles = [
            dot(first[a, :], second[:, b]) for a, b in ((low, low), (low, high), (high, high))
        ]
        tenth = jnp.where(diagonal, 0.1, 0.0)
        return tiles[0] + tenth, tiles[1], tiles[2] + tenth

    def spot(flip):
        row = (4 * place + 2 * (column ^ flip) + core) * rows
        part = row // quarter
        return ((part // 2 ^ core) * 2 + (part % 2 ^ place % 2)) * quarter + row % quarter

    line = lax.broadcasted_iota(jnp.int32, (2 * rows, width), 0)
    wanted = jnp.where(line < rows, spot(0) + line, spot(1) + line - rows)
    pick = lax.broadcasted_iota(jnp.int32, (2 * rows, width), 1) == wanted
    pick = jnp.where(pick, 1.0, 0.0).astype(BF16)
    picked = 2 * rows
    stats_left = statistics(grad, turned)
    stats_right = statistics(turned, grad)
    squares = [tile * tile for tile in stats_left]
    norm = jnp.sqrt(jnp.sum(squares[0] + 2.0 * squares[1] + squares[2], keepdims=True))
    scale = 2.5 / norm
    first = jnp.sqrt(jnp.sqrt(scale)).astype(BF16).astype(F32)
    tiles = [scale * tile for tile in stats_left]
    fill(m_left, 0, tiles)
    fill(left, picked, factor(tiles))
    left[:picked, :] = (first * dot(pick, left[picked:, :])).astype(BF16)
    tiles = [scale * tile for tile in stats_right]
    fill(m_right, 0, tiles)
    tiles = [tile.astype(BF16) for tile in factor(tiles)]
    fill(right, width, tiles)
    tiles = [(first * tile.astype(F32)).astype(BF16) for tile in tiles]
    right[half:width, low] = tiles[0]
    right[half:width, high] = tiles[1]
    right[:half, low] = tiles[1].T
    right[:half, high] = tiles[2]

    def square(ref):
        by_high = dot(ref[...], ref[:, high])
        return dot(ref[low, :], ref[:, low]), by_high[low], by_high[high]

    counts_copy.wait()
    count_left, count_right = counts[column, 0], counts[column, 1]
    for index in range(1, most):
        q_left, q_right = left.at[picked:, :], right.at[width:, :]
        if index == 1:
            fill(s_left, 0, square(q_left))
            fill(s_right, 0, square(q_right))
        else:
            by_high = dot(left[...], q_left[:, high])
            by_low = dot(left[: picked + half, :], q_left[:, low])
            right_by_high = dot(right[...], q_right[:, high])
            right_by_low = dot(right[half : width + half, :], q_right[:, low])
            fill(s_left, 0, (by_low[picked:], by_high[picked : picked + half], by_high[picked + half :]))
            fill(
                s_right,
                0,
                (right_by_low[half:], right_by_high[width : width + half], right_by_high[width + half :]),
            )

            def keep_if(ref, value, goes_on):
                value = value.astype(BF16)
                return value if index == 2 else jnp.where(goes_on, value, ref)

            left[:picked, low] = keep_if(left[:picked, low], by_low[:picked], index <= count_left)
            left[:picked, high] = keep_if(left[:picked, high], by_high[:picked], index <= count_left)
            goes_on = index <= count_right
            upper_right = keep_if(right[half:width, high], right_by_high[half:width], goes_on)
            right[half:width, low] = keep_if(right[half:width, low], right_by_low[:half], goes_on)
            right[half:width, high] = upper_right
            right[:half, low] = upper_right.T
            right[:half, high] = keep_if(right[:half, high], right_by_high[:half], goes_on)
        fourths = square(s_left), square(s_right)
        fill(s_left, 0, fourths[0])
        fill(s_right, 0, fourths[1])
        for fourth, moment_ref, ref, start in (
            (s_left, m_left, left, picked),
            (s_right, m_right, right, width),
        ):
            by_high = dot(fourth[...], moment_ref[:, high])
            tiles = (dot(fourth[low, :], moment_ref[:, low]), by_high[low], by_high[high])
            if index < most - 1:
                fill(moment_ref, 0, tiles)
            elif ref is right:
                final_left = dot(left[:picked, :], left[picked:, :]).astype(BF16)
                final_left = jnp.where(most <= count_left, final_left, left[:picked, :])
                partial_value = dot(final_left, grad[...]).astype(BF16)
            fill(ref, start, factor(tiles))
    update = dot(partial_value[:, low], right[half:width, :]) + dot(
        partial_value[:, high], right[:half, :]
    )
    update = jnp.where(most <= count_right, dot(update.astype(BF16), right[width:, :]), update)
    keep_ref[...] = update[:rows, :].astype(BF16)
    send_ref[...] = update[rows:, :].astype(BF16)


def root(counts, pieces, rows, most=4):
    width = 4 * pieces[0].shape[0]
    square = pltpu.VMEM((width, width), BF16)
    out = jax.ShapeDtypeStruct((rows, width), BF16)
    return pl.pallas_call(
        functools.partial(root_kernel, most),
        out_shape=[out, out],
        in_specs=[HBM] + [VMEM] * 6,
        out_specs=[VMEM] * 2,
        scratch_shapes=[
            square,
            square,
            pltpu.VMEM((2 * rows + width, width), BF16),
            pltpu.VMEM((2 * width, width), BF16),
            square,
            square,
            square,
            square,
            pltpu.SMEM(counts.shape, jnp.int32),
            pltpu.SemaphoreType.DMA(()),
        ],
        compiler_params=params(40),
    )(pltpu.with_memory_space_constraint(counts, pltpu.HBM), *pieces)


def place_kernel(origins, *refs):
    *pieces, out, sems = refs
    column, group = lax.axis_index("x"), lax.axis_index("group")
    copies = []
    for index, (piece, (turn, flip)) in enumerate(zip(pieces, origins)):
        number = 2 * (group ^ turn) + (column ^ flip)
        copies.append(pltpu.make_async_copy(piece, out.at[number], sems.at[index]))
        copies[-1].start()
    for copy in copies:
        copy.wait()


def place(found):
    origins, pieces = zip(*found.items())
    rows, width = pieces[0].shape
    return pl.pallas_call(
        functools.partial(place_kernel, origins),
        out_shape=jax.ShapeDtypeStruct((len(pieces), rows, width), BF16),
        in_specs=[VMEM] * len(pieces),
        out_specs=HBM,
        scratch_shapes=[pltpu.SemaphoreType.DMA((len(pieces),))],
        compiler_params=params(16),
    )(*pieces)


def shards(line, groups, patches, cotangents, newton_counts):
    blocks, pix, width = patches.shape
    half = width // 2
    rows = half // (2 * line)
    scale = 1.0 / float(pix * 4 * line * width) ** 0.5

    def swap(array, axis, mask=1):
        return lax.ppermute(array, axis, [(i, i ^ mask) for i in range(lax.axis_size(axis))])

    def swap_diagonal(array):
        moves = [(2 * z + x, 2 * (z ^ 1) + (x ^ 1)) for z in range(line) for x in range(2)]
        return lax.ppermute(array, ("z", "x"), moves)

    given_column, given_line, patch, cot = load(scale, patches, cotangents)
    came_column, came_line = swap(given_column, "core"), swap(given_line, "core")
    kept_column, kept_line, given_rest = sums(
        scale,
        patch,
        cot,
        (),
        (F32, ((1, 0, 0),)),
        (F32, ((0, 0, 1),)),
        (BF16, ((1, 1, 1), (0, 1, 0))),
    )
    came_rest = swap(given_rest, "core")
    to_column = add(kept_column, came_column).astype(BF16)
    from_column = swap(to_column, "x")
    to_line = add(kept_line, came_line).astype(BF16)
    from_line = swap(to_line, "z")
    kept_diagonal, own = sums(
        scale, patch, cot, (to_line,), (F32, ((1, 0, 1),)), (F32, ((0, 0, 0),))
    )
    quarter = own.shape[0]
    to_diagonal = add(kept_diagonal, came_rest[:quarter]).astype(BF16)
    own = add(own, came_rest[quarter:])
    from_diagonal = swap_diagonal(to_diagonal)
    left, right, send_left, send_right = collect(
        width * 3 // 4, own, from_diagonal, from_column, from_line
    )
    pieces = []
    for own, send in ((left, send_left), (right, send_right)):
        mask = 2
        while mask < line:
            own = add(own, swap(send, "z", mask))
            send = own.astype(BF16)
            mask *= 2
        own = send
        other = swap(own, "z")
        pieces += [own, other, swap(jnp.concatenate([own, other], 0), "core")]
    keep, send = root(newton_counts, pieces, rows)

    def pass_on(turn, flip):
        moves = [
            (c * groups + g, (c ^ flip) * groups + (g ^ turn))
            for c in range(2)
            for g in range(groups)
        ]
        return lax.ppermute(send if flip else keep, ("x", "group"), moves)

    others = [(turn, flip) for turn in range(groups) for flip in range(2) if turn or flip]
    found = {(turn, flip): pass_on(turn, flip) for turn, flip in others}
    found[0, 0] = keep
    return place(found)


def solution(mesh):
    devices, groups = mesh.shape["dp"], mesh.shape["group"]
    line = devices // 4
    cut = jax.sharding.Mesh(
        mesh.devices.reshape(line, 2, 2, groups), ("z", "x", "core", "group")
    )
    dp = ("z", "x", "core")
    placed = (P("group", dp, None), P("group", dp, None), P("group", None))
    return jax.shard_map(
        functools.partial(shards, line, groups),
        mesh=cut,
        in_specs=placed,
        out_specs=P(None, dp, None),
        check_vma=False,
    )
```

```python
import functools

import jax
import jax.numpy as jnp
from jax import lax
from jax.experimental import pallas as pl
from jax.experimental.pallas import tpu as pltpu
from jax.sharding import PartitionSpec as P

F32 = jnp.float32
BF16 = jnp.bfloat16
VMEM = pl.BlockSpec(memory_space=pltpu.VMEM)
SMEM = pl.BlockSpec(memory_space=pltpu.SMEM)
HBM = pl.BlockSpec(memory_space=pltpu.HBM)
ROWS_IN_COLS = (((0,), (0,)), ((), ()))


def params(limit):
    return pltpu.CompilerParams(vmem_limit_bytes=limit << 20)


def piece_sum(patch, cot, scale, block, side, part):
    quarter = patch.shape[3] // 2
    rows = slice(part * quarter, (part + 1) * quarter)
    terms = lax.dot_general(
        patch[block, side, :, rows], cot[block], ROWS_IN_COLS, preferred_element_type=F32
    )
    return terms * scale


def load_kernel(scale, patch_hbm, cot_hbm, given_column, given_line, patch, cot, sems):
    half = patch.shape[3]
    width = half // 2
    column, core, parity = lax.axis_index("x"), lax.axis_index("core"), lax.axis_index("z") % 2
    copies = []

    def fetch(source, target):
        copies.append(pltpu.make_async_copy(source, target, sems.at[len(copies)]))
        copies[-1].start()

    def fetch_patch(block, side, part):
        first = (core ^ side) * half + (parity ^ part) * width
        fetch(
            patch_hbm.at[column ^ block, :, pl.ds(pl.multiple_of(first, width), width)],
            patch.at[block, side, :, part * width : (part + 1) * width],
        )

    fetch(cot_hbm.at[column ^ 1], cot.at[1])
    fetch_patch(1, 1, 0)
    fetch(cot_hbm.at[column], cot.at[0])
    fetch_patch(0, 1, 1)
    needed = len(copies)
    for side in range(2):
        for block, part in ((1, 0), (0, 1), (1, 1), (0, 0)):
            if side == 0 or block == part:
                fetch_patch(block, side, part)
    for copy in copies[:2]:
        copy.wait()
    given_column[...] = piece_sum(patch, cot, scale, 1, 1, 0).astype(BF16)
    for copy in copies[2:needed]:
        copy.wait()
    given_line[...] = piece_sum(patch, cot, scale, 0, 1, 1).astype(BF16)
    for copy in copies[needed:]:
        copy.wait()


def load(scale, patches, cotangents):
    blocks, pix, width = patches.shape
    half = width // 2
    return pl.pallas_call(
        functools.partial(load_kernel, scale),
        out_shape=[
            jax.ShapeDtypeStruct((half // 2, width), BF16),
            jax.ShapeDtypeStruct((half // 2, width), BF16),
            jax.ShapeDtypeStruct((blocks, 2, pix, half), BF16),
            jax.ShapeDtypeStruct((blocks, pix, width), BF16),
        ],
        in_specs=[HBM] * 2,
        out_specs=[VMEM] * 4,
        scratch_shapes=[pltpu.SemaphoreType.DMA((10,))],
        compiler_params=params(16),
    )(
        pltpu.with_memory_space_constraint(patches, pltpu.HBM),
        pltpu.with_memory_space_constraint(cotangents, pltpu.HBM),
    )


def sums_kernel(scale, wanted, patch, cot, *refs):
    for (dtype, pieces), out in zip(wanted, refs[-len(wanted) :]):
        rows = out.shape[0] // len(pieces)
        for index, piece in enumerate(pieces):
            value = piece_sum(patch, cot, scale, *piece).astype(dtype)
            out[index * rows : (index + 1) * rows, :] = value


def sums(scale, patch, cot, after, *wanted):
    pix, half = patch.shape[2:]
    return pl.pallas_call(
        functools.partial(sums_kernel, scale, wanted),
        out_shape=[
            jax.ShapeDtypeStruct((len(pieces) * half // 2, 2 * half), dtype)
            for dtype, pieces in wanted
        ],
        in_specs=[VMEM] * 2 + [pl.BlockSpec(memory_space=pl.ANY)] * len(after),
        out_specs=[VMEM] * len(wanted),
        compiler_params=params(16),
        cost_estimate=pl.CostEstimate(
            flops=4 * len(wanted) * pix * half * half,
            bytes_accessed=8 * pix * half,
            transcendentals=0,
        ),
    )(patch, cot, *after)


def collect_kernel(own, *refs):
    *came, keep_left, keep_right, send_left, send_right = refs
    split = keep_left.shape[1]
    for columns, keep, send in (
        (slice(0, split), keep_left, send_left),
        (slice(split, own.shape[1]), keep_right, send_right),
    ):
        total = own[: keep.shape[0], columns]
        for ref in came:
            total = total + ref[:, columns].astype(F32)
        keep[...] = total
        send[...] = total.astype(BF16)


def collect(split, own, *came):
    rows, width = came[0].shape
    shapes = [(rows, split), (rows, width - split)]
    return pl.pallas_call(
        collect_kernel,
        out_shape=[jax.ShapeDtypeStruct(shape, F32) for shape in shapes]
        + [jax.ShapeDtypeStruct(shape, BF16) for shape in shapes],
        in_specs=[VMEM] * (1 + len(came)),
        out_specs=[VMEM] * 4,
        compiler_params=params(16),
    )(own, *came)


def add(*values):
    total = values[0]
    for value in values[1:]:
        total = total + value.astype(F32)
    return total


def root_kernel(most, counts_hbm, *refs):
    pieces = refs[:6]
    keep_ref, send_ref, grad, turned, left, right, m_left, m_right, s_left, s_right, counts, sem = refs[6:]
    counts_copy = pltpu.make_async_copy(counts_hbm, counts, sem)
    counts_copy.start()
    width = grad.shape[0]
    half, quarter = width // 2, width // 4
    rows = keep_ref.shape[0]
    low, high = slice(0, half), slice(half, width)
    place, column, core = (lax.axis_index(name) for name in ("z", "x", "core"))
    column_start = 0
    for index in range(2):
        own, other, far = pieces[3 * index : 3 * index + 3]
        columns = slice(column_start, column_start + own.shape[1])
        column_start += own.shape[1]
        grad[:quarter, columns] = own[...]
        grad[quarter:half, columns] = other[...]
        grad[half:, columns] = far[...]
    turned[...] = grad[...].T
    diagonal = lax.broadcasted_iota(jnp.int32, (half, half), 0) == lax.broadcasted_iota(
        jnp.int32, (half, half), 1
    )

    def dot(a, b):
        return jnp.dot(a, b, preferred_element_type=F32)

    def fill(ref, start, tiles):
        upper_left, upper_right, lower_right = (tile.astype(BF16) for tile in tiles)
        ref[start : start + half, low] = upper_left
        ref[start : start + half, high] = upper_right
        ref[start + half : start + width, low] = upper_right.T
        ref[start + half : start + width, high] = lower_right

    def factor(tiles):
        upper_left, upper_right, lower_right = tiles
        five = jnp.where(diagonal, 1.25, 0.0)
        return five - 0.25 * upper_left, -0.25 * upper_right, five - 0.25 * lower_right

    def statistics(first, second):
        tiles = [
            dot(first[a, :], second[:, b]) for a, b in ((low, low), (low, high), (high, high))
        ]
        tenth = jnp.where(diagonal, 0.1, 0.0)
        return tiles[0] + tenth, tiles[1], tiles[2] + tenth

    def spot(flip):
        row = (4 * place + 2 * (column ^ flip) + core) * rows
        part = row // quarter
        return ((part // 2 ^ core) * 2 + (part % 2 ^ place % 2)) * quarter + row % quarter

    line = lax.broadcasted_iota(jnp.int32, (2 * rows, width), 0)
    wanted = jnp.where(line < rows, spot(0) + line, spot(1) + line - rows)
    pick = lax.broadcasted_iota(jnp.int32, (2 * rows, width), 1) == wanted
    pick = jnp.where(pick, 1.0, 0.0).astype(BF16)
    picked = 2 * rows
    stats_left = statistics(grad, turned)
    stats_right = statistics(turned, grad)
    squares = [tile * tile for tile in stats_left]
    norm = jnp.sqrt(jnp.sum(squares[0] + 2.0 * squares[1] + squares[2], keepdims=True))
    scale = 2.5 / norm
    first = jnp.sqrt(jnp.sqrt(scale)).astype(BF16).astype(F32)
    tiles = [scale * tile for tile in stats_left]
    fill(m_left, 0, tiles)
    fill(left, picked, factor(tiles))
    left[:picked, :] = (first * dot(pick, left[picked:, :])).astype(BF16)
    tiles = [scale * tile for tile in stats_right]
    fill(m_right, 0, tiles)
    tiles = [tile.astype(BF16) for tile in factor(tiles)]
    fill(right, width, tiles)
    tiles = [(first * tile.astype(F32)).astype(BF16) for tile in tiles]
    right[half:width, low] = tiles[0]
    right[half:width, high] = tiles[1]
    right[:half, low] = tiles[1].T
    right[:half, high] = tiles[2]

    def square(ref):
        by_high = dot(ref[...], ref[:, high])
        return dot(ref[low, :], ref[:, low]), by_high[low], by_high[high]

    counts_copy.wait()
    count_left, count_right = counts[column, 0], counts[column, 1]
    for index in range(1, most):
        q_left, q_right = left.at[picked:, :], right.at[width:, :]
        if index == 1:
            seconds = square(q_left), square(q_right)
            fill(s_left, 0, seconds[0])
            fill(s_right, 0, seconds[1])
        else:
            by_high = dot(left[...], q_left[:, high])
            by_low = dot(left[: picked + half, :], q_left[:, low])
            right_by_high = dot(right[...], q_right[:, high])
            right_by_low = dot(right[half : width + half, :], q_right[:, low])
            fill(s_left, 0, (by_low[picked:], by_high[picked : picked + half], by_high[picked + half :]))
            fill(
                s_right,
                0,
                (right_by_low[half:], right_by_high[width : width + half], right_by_high[width + half :]),
            )

            def keep_if(ref, value, goes_on):
                value = value.astype(BF16)
                return value if index == 2 else jnp.where(goes_on, value, ref)

            left[:picked, low] = keep_if(left[:picked, low], by_low[:picked], index <= count_left)
            left[:picked, high] = keep_if(left[:picked, high], by_high[:picked], index <= count_left)
            goes_on = index <= count_right
            upper_right = keep_if(right[half:width, high], right_by_high[half:width], goes_on)
            right[half:width, low] = keep_if(right[half:width, low], right_by_low[:half], goes_on)
            right[half:width, high] = upper_right
            right[:half, low] = upper_right.T
            right[:half, high] = keep_if(right[:half, high], right_by_high[:half], goes_on)
        fourths = square(s_left), square(s_right)
        fill(s_left, 0, fourths[0])
        fill(s_right, 0, fourths[1])
        for fourth, moment_ref, ref, start in (
            (s_left, m_left, left, picked),
            (s_right, m_right, right, width),
        ):
            by_high = dot(fourth[...], moment_ref[:, high])
            tiles = (dot(fourth[low, :], moment_ref[:, low]), by_high[low], by_high[high])
            if index < most - 1:
                fill(moment_ref, 0, tiles)
            fill(ref, start, factor(tiles))
    final_left = dot(left[:picked, :], left[picked:, :]).astype(BF16)
    final_left = jnp.where(most <= count_left, final_left, left[:picked, :])
    partial_value = dot(final_left, grad[...]).astype(BF16)
    update = dot(partial_value[:, low], right[half:width, :]) + dot(
        partial_value[:, high], right[:half, :]
    )
    update = jnp.where(most <= count_right, dot(update.astype(BF16), right[width:, :]), update)
    keep_ref[...] = update[:rows, :].astype(BF16)
    send_ref[...] = update[rows:, :].astype(BF16)


def root(counts, pieces, rows, most=4):
    width = 4 * pieces[0].shape[0]
    square = pltpu.VMEM((width, width), BF16)
    out = jax.ShapeDtypeStruct((rows, width), BF16)
    return pl.pallas_call(
        functools.partial(root_kernel, most),
        out_shape=[out, out],
        in_specs=[HBM] + [VMEM] * 6,
        out_specs=[VMEM] * 2,
        scratch_shapes=[
            square,
            square,
            pltpu.VMEM((2 * rows + width, width), BF16),
            pltpu.VMEM((2 * width, width), BF16),
            square,
            square,
            square,
            square,
            pltpu.SMEM(counts.shape, jnp.int32),
            pltpu.SemaphoreType.DMA(()),
        ],
        compiler_params=params(40),
    )(pltpu.with_memory_space_constraint(counts, pltpu.HBM), *pieces)


def place_kernel(origins, *refs):
    *pieces, out, sems = refs
    column, group = lax.axis_index("x"), lax.axis_index("group")
    copies = []
    for index, (piece, (turn, flip)) in enumerate(zip(pieces, origins)):
        number = 2 * (group ^ turn) + (column ^ flip)
        copies.append(pltpu.make_async_copy(piece, out.at[number], sems.at[index]))
        copies[-1].start()
    for copy in copies:
        copy.wait()


def place(found):
    origins, pieces = zip(*found.items())
    rows, width = pieces[0].shape
    return pl.pallas_call(
        functools.partial(place_kernel, origins),
        out_shape=jax.ShapeDtypeStruct((len(pieces), rows, width), BF16),
        in_specs=[VMEM] * len(pieces),
        out_specs=HBM,
        scratch_shapes=[pltpu.SemaphoreType.DMA((len(pieces),))],
        compiler_params=params(16),
    )(*pieces)


def shards(line, groups, patches, cotangents, newton_counts):
    blocks, pix, width = patches.shape
    half = width // 2
    rows = half // (2 * line)
    scale = 1.0 / float(pix * 4 * line * width) ** 0.5

    def swap(array, axis, mask=1):
        return lax.ppermute(array, axis, [(i, i ^ mask) for i in range(lax.axis_size(axis))])

    def swap_diagonal(array):
        moves = [(2 * z + x, 2 * (z ^ 1) + (x ^ 1)) for z in range(line) for x in range(2)]
        return lax.ppermute(array, ("z", "x"), moves)

    given_column, given_line, patch, cot = load(scale, patches, cotangents)
    came_column, came_line = swap(given_column, "core"), swap(given_line, "core")
    kept_column, kept_line, given_rest = sums(
        scale,
        patch,
        cot,
        (),
        (F32, ((1, 0, 0),)),
        (F32, ((0, 0, 1),)),
        (BF16, ((1, 1, 1), (0, 1, 0))),
    )
    came_rest = swap(given_rest, "core")
    to_column = add(kept_column, came_column).astype(BF16)
    from_column = swap(to_column, "x")
    to_line = add(kept_line, came_line).astype(BF16)
    from_line = swap(to_line, "z")
    kept_diagonal, own = sums(
        scale, patch, cot, (to_line,), (F32, ((1, 0, 1),)), (F32, ((0, 0, 0),))
    )
    quarter = own.shape[0]
    to_diagonal = add(kept_diagonal, came_rest[:quarter]).astype(BF16)
    own = add(own, came_rest[quarter:])
    from_diagonal = swap_diagonal(to_diagonal)
    left, right, send_left, send_right = collect(
        width * 3 // 4, own, from_diagonal, from_column, from_line
    )
    pieces = []
    for own, send in ((left, send_left), (right, send_right)):
        mask = 2
        while mask < line:
            own = add(own, swap(send, "z", mask))
            send = own.astype(BF16)
            mask *= 2
        own = send
        other = swap(own, "z")
        pieces += [own, other, swap(jnp.concatenate([own, other], 0), "core")]
    keep, send = root(newton_counts, pieces, rows)

    def pass_on(turn, flip):
        moves = [
            (c * groups + g, (c ^ flip) * groups + (g ^ turn))
            for c in range(2)
            for g in range(groups)
        ]
        return lax.ppermute(send if flip else keep, ("x", "group"), moves)

    others = [(turn, flip) for turn in range(groups) for flip in range(2) if turn or flip]
    found = {(turn, flip): pass_on(turn, flip) for turn, flip in others}
    found[0, 0] = keep
    return place(found)


def solution(mesh):
    devices, groups = mesh.shape["dp"], mesh.shape["group"]
    line = devices // 4
    cut = jax.sharding.Mesh(
        mesh.devices.reshape(line, 2, 2, groups), ("z", "x", "core", "group")
    )
    dp = ("z", "x", "core")
    placed = (P("group", dp, None), P("group", dp, None), P("group", None))
    return jax.shard_map(
        functools.partial(shards, line, groups),
        mesh=cut,
        in_specs=placed,
        out_specs=P(None, dp, None),
        check_vma=False,
    )
```
